32 devices in a mesh: grp: 2 (over y), tchunk: 2 (over x), ha: 4 (over z), wa: 2 (over core).
Axes of the slice: x: 2, y: 2, z: 4, core: 2. Of those that a mesh axis runs over, the one named last changes fastest.
Arguments:
- features: bfloat16 [32, 32, 16, 192], P(('grp', 'tchunk'), 'ha', 'wa'), parts along dimension 0, may hold values from -6 to 6
- frame_counts: int32 [4], P(('grp', 'tchunk')), parts along dimension 0, may hold values from 0 to 8, as said below
- gain_first: float32 [192], replicated, may hold values from 0.25 to 1.75
- conv_first: bfloat16 [3, 3, 3, 192, 192], replicated, may hold values from -0.078125 to 0.078125
- bias_first: float32 [192], replicated, may hold values from -1.8 to 1.8
- gain_second: float32 [192], replicated, may hold values from 0.25 to 1.75
- conv_second: bfloat16 [3, 3, 3, 192, 192], replicated, may hold values from -0.078125 to 0.078125
- bias_second: float32 [192], replicated, may hold values from -1.8 to 1.8
Outputs:
- decoded: bfloat16 [32, 32, 16, 192], P(('grp', 'tchunk'), 'ha', 'wa'), parts along dimension 0
The draws below stay inside these ranges and needn't reach their ends.
There are 2 independent parts, one for each index of `grp`. The reference program is written for one: setup_inputs(seed, part) draws one part's arguments, and reference() takes and returns one part's arrays. A program takes and returns all parts, laid end to end along the dimension named above; an argument that names none is the same for every part. Nothing has to cross between parts.
Inputs may be any that keep to these rules, and one draw needn't show every extreme that they name: `frame_counts`: in every draw some temporal block has all 8 slots live; any block may have none.
All inputs are finite; a program needn't handle non-finite values.
Results may differ from the reference program's by a relative error of at most 0.0039.
Values may be sent and summed in bfloat16 or wider, within the bound.
No kernel may reach another device: no remote copies, remote signals or barrier semaphores. Data moves between devices by JAX's collectives and lax.ppermute only.
A program may use at most 64 MiB of HBM per device.

```python
import jax
import jax.numpy as jnp
from jax import lax

C = 192
F = 8
FRAMES = 16
HEIGHT = 32
WIDTH = 16
N_TCHUNK = 2


def draw_frame_counts(key, part):
    totals = jax.random.randint(key, (N_TCHUNK,), 0, F + 1)
    chosen = jax.random.randint(jax.random.fold_in(key, 11), (), 0, N_TCHUNK)
    return jnp.where(jnp.arange(N_TCHUNK) == chosen, F, totals).astype(jnp.int32)


def block_scale(rng, extent, shards, low, largest):
    loudness, own = 1.0, jax.random.fold_in(rng, 6)
    for position, blocks in shards:
        heights = jnp.exp(jax.random.uniform(jax.random.fold_in(own, position), (blocks,), jnp.float32, low / len(shards), largest / len(shards)))
        loudness = loudness * jnp.repeat(heights, extent[position] // blocks).reshape([-1 if axis == position else 1 for axis in range(len(extent))])
    return loudness


def bell_draw(key, extent, spread, reach, cuts=(), held_as=jnp.bfloat16):
    values = spread * jax.random.normal(key, extent, jnp.float32)
    if cuts:
        values = values * block_scale(key, extent, cuts, -0.22, 0.18)
    return jnp.clip(values, -reach, reach).astype(held_as)


def setup_inputs(seed: int = 0, part: int = 0) -> dict:
    key_of = jax.random.split(jax.random.key(seed), 9)
    own_keys = jax.random.split(jax.random.fold_in(key_of[8], part), 9)
    return {
        "features": bell_draw(own_keys[0], (FRAMES, HEIGHT, WIDTH, C), 1.0, 6.0, ((0, 2), (1, 4), (2, 2))),
        "frame_counts": draw_frame_counts(jax.random.fold_in(jax.random.fold_in(key_of[8], part), 71), part),
        "gain_first": jnp.clip(1.0 + 0.15 * jax.random.normal(key_of[2], (C,), jnp.float32), 0.25, 1.75),
        "conv_first": bell_draw(key_of[3], (3, 3, 3, C, C), (27 * C) ** -0.5, 0.078125),
        "bias_first": bell_draw(key_of[4], (C,), 0.3, 1.8, (), jnp.float32),
        "gain_second": jnp.clip(1.0 + 0.15 * jax.random.normal(key_of[5], (C,), jnp.float32), 0.25, 1.75),
        "conv_second": bell_draw(key_of[6], (3, 3, 3, C, C), (27 * C) ** -0.5, 0.078125),
        "bias_second": bell_draw(key_of[7], (C,), 0.3, 1.8, (), jnp.float32),
    }


epsilon = 1e-06

def activate(values, gain):
    values = values.astype(jnp.float32)
    inverse = lax.rsqrt(lax.optimization_barrier(jnp.mean(values * values, axis=-1, keepdims=True)) + epsilon)
    return jax.nn.silu(values * inverse * gain).astype(jnp.bfloat16)

def convolve(stacked, kernel, bias_term):
    padded = jnp.pad(stacked.astype(jnp.float32), ((0, 0), (1, 1), (1, 1), (0, 0)))
    result = lax.conv_general_dilated(padded[None], kernel.astype(jnp.float32), (1, 1, 1), 'VALID', dimension_numbers=('NDHWC', 'DHWIO', 'NDHWC'), precision=lax.Precision.HIGHEST)
    return result[0] + bias_term

def reference(features, frame_counts, gain_first, conv_first, bias_first, gain_second, conv_second, bias_second):
    blocks = features.reshape(N_TCHUNK, F, HEIGHT, WIDTH, C)

    def advance(carry, inputs):
        cache_first, cache_second = carry
        block_frames, frame_total = inputs
        valid_mask = (jnp.arange(F) < frame_total)[:, None, None, None]
        first_input = jnp.where(valid_mask, activate(block_frames, gain_first), jnp.zeros_like(block_frames))
        joined_first = jnp.concatenate([cache_first, first_input], axis=0)
        hidden = convolve(joined_first, conv_first, bias_first)
        second_input = jnp.where(valid_mask, activate(hidden, gain_second), jnp.zeros_like(block_frames))
        joined_second = jnp.concatenate([cache_second, second_input], axis=0)
        result = convolve(joined_second, conv_second, bias_second)
        outcome = jnp.where(valid_mask, block_frames.astype(jnp.float32) + result, jnp.zeros((), jnp.float32)).astype(jnp.bfloat16)
        start = frame_total.astype(jnp.int32)
        new_first = lax.dynamic_slice_in_dim(joined_first, start, 2, 0)
        new_second = lax.dynamic_slice_in_dim(joined_second, start, 2, 0)
        return ((new_first, new_second), outcome)
    empty = jnp.zeros((2, HEIGHT, WIDTH, C), jnp.bfloat16)
    final_caches, decoded = lax.scan(advance, (empty, empty), (blocks, frame_counts))
    return decoded.reshape(FRAMES, HEIGHT, WIDTH, C)
```

```python
import functools

import jax
import jax.numpy as jnp
from jax import lax
from jax.experimental import pallas as pl
from jax.experimental.pallas import tpu as pltpu
from jax.sharding import PartitionSpec as P

epsilon = 1e-06
CACHE = 4
HALO = 2
TAPS = 3


def earlier_frames(tail, lanes_used):
    count = lax.axis_size("tchunk")

    def moved(value, step):
        return lax.ppermute(value, "tchunk", [(k, k + step) for k in range(count - step)])

    frames = moved(tail, 1)
    step = 1
    while step < count - 1:
        early = moved(frames, step)
        held = jnp.sum(frames[:, 0, 0, lanes_used].astype(jnp.int32))
        shifted = lax.dynamic_slice_in_dim(
            jnp.concatenate([early, jnp.zeros_like(early)], axis=0), held, CACHE, 0
        )
        frames = shifted + frames
        step *= 2
    return frames


def normalised(values, gain, flag, channels):
    total = jnp.sum(values * values, axis=-1, keepdims=True)
    inverse = lax.rsqrt(total * (1.0 / channels) + epsilon)
    if flag is not None:
        inverse = inverse * flag
    scaled = values * inverse * gain
    return scaled * (0.5 + 0.5 * jnp.tanh(0.5 * scaled))


def block_kernel(
    core_ref, mine_ref, other_ref, edge_ref,
    gain1_ref, w1_ref, bias1_ref, gain2_ref, w2_ref, bias2_ref,
    keep_ref, send_ref,
    plane1, cols1, plane2, cols2, total_ref,
):
    core = core_ref[0]
    slots, rows, side, lanes = mine_ref.shape
    channels = w1_ref.shape[-1]
    width = 2 * side
    high = rows + HALO
    half = high - 2 * HALO
    deep = cols1.shape[-1]

    plane1[:, :, 0:8, :] = jnp.zeros((slots, high, 8, lanes), jnp.float32)
    plane1[:, :, 8 + width:16 + width, :] = jnp.zeros((slots, high, 8, lanes), jnp.float32)
    lane = lax.broadcasted_iota(jnp.int32, (1, 1, 1, lanes), 3)
    gain1 = gain1_ref[...].reshape(1, 1, 1, lanes)

    def first(raw):
        values = raw.astype(jnp.float32)
        inner = jnp.where(lane < channels, values, 0.0)
        return jnp.where(lane < channels, normalised(inner, gain1, None, channels), values)

    here = pl.ds(pl.multiple_of(8 + side * core, 8), side)
    there = pl.ds(pl.multiple_of(8 + side * (1 - core), 8), side)
    main_rows = pl.ds(HALO * (1 - core), rows)
    edge_rows = pl.ds(rows * core, HALO)
    plane1[:, main_rows, here, :] = first(mine_ref[...])
    plane1[:, main_rows, there, :] = first(other_ref[...])
    plane1[:, edge_rows, here, :] = first(edge_ref[1])
    plane1[:, edge_rows, there, :] = first(edge_ref[0])

    def spread(plane, cols):
        parts = [plane[:, :, 7 + j:7 + j + width, 0:channels].astype(jnp.bfloat16) for j in range(TAPS)]
        rest = jnp.zeros(parts[0].shape[:-1] + (deep - TAPS * channels,), jnp.bfloat16)
        cols[...] = jnp.concatenate(parts + [rest], axis=-1)

    def convolved(cols, weights_ref, frame, frames, out_rows):
        total = None
        pairs = [(a, i) for a in range(TAPS) for i in range(TAPS)]
        blank = jnp.zeros((deep - TAPS * channels, channels), jnp.bfloat16)
        for start in range(0, len(pairs), 2):
            left, right = [], []
            for a, i in pairs[start:start + 2]:
                window = cols[frame + a:frame + a + frames, i:i + out_rows]
                left.append(window.reshape(frames * out_rows * width, deep))
                right += [weights_ref[a, i].reshape(TAPS * channels, channels), blank]
            product = jnp.dot(
                jnp.concatenate(left, axis=-1), jnp.concatenate(right, axis=0),
                preferred_element_type=jnp.float32,
            )
            total = product if total is None else total + product
        return total

    spread(plane1, cols1)

    hidden_rows = high - 2
    hidden_slots = slots - 2
    plane2[:, :, 0:8, :] = jnp.zeros((hidden_slots, hidden_rows, 8, channels), jnp.float32)
    plane2[:, :, 8 + width:16 + width, :] = jnp.zeros((hidden_slots, hidden_rows, 8, channels), jnp.float32)
    gain2 = gain2_ref[...].reshape(1, 1, 1, channels)
    step = 2
    for frame in range(0, hidden_slots, step):
        hidden = convolved(cols1, w1_ref, frame, step, hidden_rows) + bias1_ref[...].reshape(1, channels)
        hidden = hidden.reshape(step, hidden_rows, width, channels)
        flag = plane1[frame + 2:frame + 2 + step, 1:1 + hidden_rows, 8:8 + width, channels:channels + 1]
        plane2[frame:frame + step, :, 8:8 + width, :] = normalised(hidden, gain2, flag, channels)

    spread(plane2, cols2)

    frames = slots - CACHE
    step = 4
    for frame in range(0, frames, step):
        result = convolved(cols2, w2_ref, frame, step, half) + bias2_ref[...].reshape(1, channels)
        total_ref[frame:frame + step] = result.reshape(step, half, width, channels)

    own_rows = pl.ds(HALO * core, half)
    for source, columns, target in (
        (mine_ref, pl.ds(pl.multiple_of(side * core, 8), side), keep_ref),
        (other_ref, pl.ds(pl.multiple_of(side * (1 - core), 8), side), send_ref),
    ):
        raw = source[CACHE:, own_rows].astype(jnp.float32)
        value = raw[..., 0:channels] + total_ref[:, :, columns, :]
        target[...] = jnp.where(raw[..., channels:channels + 1] > 0, value, 0.0).astype(target.dtype)


def shards(features, frame_counts, gain_first, conv_first, bias_first, gain_second, conv_second, bias_second):
    frames, rows, side, channels = features.shape
    half = rows // 2
    core = lax.axis_index("wa")
    tall, cores = lax.axis_size("ha"), lax.axis_size("wa")
    live_total = frame_counts[0]
    lanes = (channels // 128 + 1) * 128

    live = (jnp.arange(frames) < live_total)[:, None, None, None]
    marked = jnp.concatenate(
        [features, jnp.ones(features.shape[:-1] + (lanes - channels,), features.dtype)], axis=-1
    )
    marked = jnp.where(live, marked, jnp.zeros((), marked.dtype))
    tail = lax.dynamic_slice_in_dim(
        jnp.concatenate([jnp.zeros((CACHE,) + marked.shape[1:], marked.dtype), marked], axis=0),
        live_total, CACHE, 0,
    )
    joined = jnp.concatenate([earlier_frames(tail, channels), marked], axis=0)

    swap = [(0, 1), (1, 0)]
    away = half - HALO
    mine = lax.dynamic_slice_in_dim(joined, away * core, half + HALO, 1)
    theirs = lax.dynamic_slice_in_dim(joined, away * (1 - core), half + HALO, 1)
    other = lax.ppermute(theirs, "wa", swap)
    edge = lax.dynamic_slice_in_dim(jnp.stack([mine, other]), half * core, HALO, 2)
    pairs = []
    for h in range(tall - 1):
        lower, upper = h * cores + 1, (h + 1) * cores
        pairs += [(lower, upper), (upper, lower)]
    edge = lax.ppermute(edge, ("ha", "wa"), pairs)

    slots = frames + CACHE
    high, width = half + 2 * HALO, 2 * side
    deep = -(-TAPS * channels // 128) * 128
    part = jax.ShapeDtypeStruct((frames, half, side, channels), features.dtype)
    vmem = pl.BlockSpec(memory_space=pltpu.VMEM)
    keep, send = pl.pallas_call(
        block_kernel,
        out_shape=(part, part),
        in_specs=[pl.BlockSpec(memory_space=pltpu.SMEM)] + [vmem] * 9,
        out_specs=(vmem, vmem),
        scratch_shapes=[
            pltpu.VMEM((slots, high, width + 16, lanes), jnp.float32),
            pltpu.VMEM((slots, high, width, deep), jnp.bfloat16),
            pltpu.VMEM((slots - 2, high - 2, width + 16, channels), jnp.float32),
            pltpu.VMEM((slots - 2, high - 2, width, deep), jnp.bfloat16),
            pltpu.VMEM((frames, half, width, channels), jnp.float32),
        ],
        compiler_params=pltpu.CompilerParams(vmem_limit_bytes=40 * 2**20),
    )(
        core.astype(jnp.int32).reshape(1), mine, other, edge,
        jnp.pad(gain_first, (0, lanes - channels)).reshape(1, lanes), conv_first, bias_first.reshape(1, channels),
        gain_second.reshape(1, channels), conv_second, bias_second.reshape(1, channels),
    )
    got = lax.ppermute(send, "wa", swap)
    upper = jnp.where(core == 0, keep, got)
    lower = jnp.where(core == 0, got, keep)
    return jnp.concatenate([upper, lower], axis=1)


def solution(mesh):
    return jax.shard_map(
        shards,
        mesh=mesh,
        in_specs=(
            P(("grp", "tchunk"), "ha", "wa", None),
            P(("grp", "tchunk")),
            P(), P(), P(), P(), P(), P(),
        ),
        out_specs=P(("grp", "tchunk"), "ha", "wa", None),
        check_vma=False,
    )
```

```python
import jax
import jax.numpy as jnp
from jax import lax
from jax.experimental import pallas as pl
from jax.experimental.pallas import tpu as pltpu
from jax.sharding import PartitionSpec as P

epsilon = 1e-06
CACHE = 4
TAPS = 3
LANES = 128


def prepare_kernel(total_ref, features_ref, tail_ref, own_ref, held):
    frames, rows, side, channels = features_ref.shape
    total = total_ref[0]
    for frame in range(frames):
        for pair in range(rows // 2):
            first, second = features_ref[frame, 2 * pair], features_ref[frame, 2 * pair + 1]
            packed = jnp.concatenate(
                [first[:, :LANES], second[:, :LANES], first[:, LANES:], second[:, LANES:]], axis=-1
            )
            held[frame, pair] = packed
            own_ref[frame, pair] = jnp.where(frame < total, packed, jnp.zeros_like(packed))
    pairs = rows // 2
    for slot in range(CACHE):
        frame = total - CACHE + slot
        packed = held[jnp.maximum(frame, 0)]
        tail_ref[slot * pairs:(slot + 1) * pairs] = jnp.where(frame >= 0, packed, jnp.zeros_like(packed))
    slot = lax.broadcasted_iota(jnp.int32, tail_ref.shape[1:], 0)
    tail_ref[CACHE * pairs] = jnp.where((slot < CACHE) & (total - CACHE + slot >= 0), 1.0, 0.0).astype(tail_ref.dtype)


def earlier_frames(tail, pairs):
    count = lax.axis_size("tchunk")

    def moved(value, step):
        return lax.ppermute(value, "tchunk", [(k, k + step) for k in range(count - step)])

    def pushed(value, held):
        zeros = jnp.zeros_like(value)
        return lax.dynamic_slice_in_dim(jnp.concatenate([value, zeros], axis=0), held, CACHE, 0)

    frames = moved(tail, 1)
    step = 1
    while step < count - 1:
        early = moved(frames, step)
        held = jnp.sum(frames[-1, :CACHE, 0].astype(jnp.int32))
        body = pushed(early[:-1].reshape((CACHE, pairs) + early.shape[1:]), held).reshape(early[:-1].shape)
        marks = jnp.pad(pushed(early[-1, :CACHE], held), ((0, early.shape[1] - CACHE), (0, 0)))
        frames = frames + jnp.concatenate([body, marks[None]], axis=0)
        step *= 2
    return frames


def silu(values):
    return values * (0.5 + 0.5 * jnp.tanh(0.5 * values))


def lane_mask():
    return lax.broadcasted_iota(jnp.int32, (1, 1, 1, LANES), 3) < LANES // 2


def gains(gain_ref):
    low, high = gain_ref[:, :LANES], gain_ref[:, LANES:]
    return low.reshape(1, 1, 1, LANES), jnp.concatenate([high, high], axis=-1).reshape(1, 1, 1, LANES)


def rolled(values):
    shape = values.shape
    return pltpu.roll(values.reshape(-1, LANES), LANES // 2, 1).reshape(shape)


def first_rows(left, right, gain_ref, channels):
    raw = jnp.concatenate([left.astype(jnp.float32), right.astype(jnp.float32)], axis=2)
    front, back, high = raw[..., :LANES], raw[..., LANES:2 * LANES], raw[..., 2 * LANES:]
    lower = lane_mask()
    squared = high * high

    def inverse(low, mask):
        total = jnp.sum(low * low + jnp.where(mask, squared, 0.0), axis=-1, keepdims=True)
        return lax.rsqrt(total * (1.0 / channels) + epsilon)

    scale_front, scale_back = inverse(front, lower), inverse(back, jnp.logical_not(lower))
    gain_low, gain_high = gains(gain_ref)
    front = silu(front * scale_front * gain_low)
    back = silu(back * scale_back * gain_low)
    high = silu(high * jnp.where(lower, scale_front, scale_back) * gain_high)
    turned = rolled(high)
    one = [front, jnp.where(lower, high, 0.0), jnp.where(lower, 0.0, turned)]
    two = [back, jnp.where(lower, turned, 0.0), jnp.where(lower, 0.0, high)]
    return [jnp.concatenate([part.astype(jnp.bfloat16) for part in row], axis=-1) for row in (one, two)]


def second_rows(hidden, flag, gain_ref, channels):
    gain = gain_ref[...].reshape(1, 1, 1, channels)
    total = jnp.sum(hidden * hidden, axis=-1, keepdims=True)
    inverse = lax.rsqrt(total * (1.0 / channels) + epsilon) * flag
    values = silu(hidden * inverse * gain)
    rest = jnp.zeros(values.shape[:-1] + (LANES // 2,), jnp.float32)
    high = jnp.concatenate([values[..., LANES:], rest], axis=-1)
    parts = [values[..., :LANES], high, rolled(high)]
    return jnp.concatenate([part.astype(jnp.bfloat16) for part in parts], axis=-1)


def convolved(operand, weights_ref, bias_ref, frame, frames, rows):
    width = operand.shape[2]
    channels = weights_ref.shape[-1]
    taps = [(a, i) for a in range(TAPS) for i in range(TAPS)]
    groups = [taps[start:start + 2] for start in range(0, len(taps), 2)]

    def window(tap, part):
        a, i = tap
        value = operand[frame + a:frame + a + frames, i:i + rows, :, part * LANES:(part + 1) * LANES]
        return value.reshape(frames * rows * width, LANES)

    pieces = []
    for group in groups:
        pieces += [window(tap, 0) for tap in group]
        high = window(group[0], 1)
        pieces.append(high + window(group[1], 2) if len(group) > 1 else high)
    left = jnp.concatenate(pieces, axis=-1)
    products = []
    for j in range(TAPS):
        rights = []
        for group in groups:
            held = [weights_ref[a, i, j] for a, i in group]
            rights += [weight[:LANES] for weight in held] + [weight[LANES:] for weight in held]
        rights.append(jnp.zeros((left.shape[1] - sum(r.shape[0] for r in rights), channels), jnp.bfloat16))
        product = jnp.dot(left, jnp.concatenate(rights, axis=0), preferred_element_type=jnp.float32)
        products.append(product.reshape(frames * rows, width, channels))
    column = lax.broadcasted_iota(jnp.int32, (1, width, 1), 1)
    before = jnp.where(column == 0, 0.0, pltpu.roll(products[0], 1, 1))
    after = jnp.where(column == width - 1, 0.0, pltpu.roll(products[2], width - 1, 1))
    result = products[1] + before + after + bias_ref[...].reshape(1, 1, channels)
    return result.reshape(frames, rows, width, channels)


def halves(core, mine, other):
    return jnp.where(core == 0, mine, other), jnp.where(core == 0, other, mine)


def frame_flags(total_ref, marks_ref, slots):
    marks = marks_ref[...].astype(jnp.float32)
    flags = [marks[k:k + 1, 0:1].reshape(1, 1, 1, 1) for k in range(CACHE - (TAPS - 1), CACHE)]
    own = [
        jnp.where(frame < total_ref[0], 1.0, 0.0) * jnp.ones((1, 1, 1, 1), jnp.float32)
        for frame in range(slots - CACHE)
    ]
    return jnp.concatenate(flags + own, axis=0)


def inner_kernel(
    core_ref, total_ref, marks_ref, mine_ref, other_ref, gain1_ref, w1_ref, bias1_ref, gain2_ref,
    inner_ref, near_ref, operand,
):
    core = core_ref[0]
    slots, pairs = mine_ref.shape[:2]
    channels = w1_ref.shape[-1]
    rows = 2 * pairs
    left, right = halves(core, mine_ref[...], other_ref[...])
    upper, lower = first_rows(left, right, gain1_ref, channels)
    for pair in range(pairs):
        operand[:, 2 * pair] = upper[:, pair]
        operand[:, 2 * pair + 1] = lower[:, pair]
    near_ref[...] = operand[:, pl.ds((rows - 2) * core, 2)]
    flags = frame_flags(total_ref, marks_ref, slots)
    hidden_slots = slots - 2
    step = hidden_slots // 2
    for frame in range(0, hidden_slots, step):
        hidden = convolved(operand, w1_ref, bias1_ref, frame, step, rows - 2)
        inner_ref[frame:frame + step] = second_rows(hidden, flags[frame:frame + step], gain2_ref, channels)


def outer_kernel(
    core_ref, total_ref, inside_ref, marks_ref, mine_ref, other_ref, edge_ref, inner_ref, near_ref,
    gain1_ref, w1_ref, bias1_ref, gain2_ref, w2_ref, bias2_ref,
    keep_ref, send_ref, strip, operand,
):
    core = core_ref[0]
    slots, _, side, _ = mine_ref.shape
    hidden_slots, inner_rows = inner_ref.shape[:2]
    channels = w1_ref.shape[-1]
    frames = slots - CACHE

    left, right = halves(core, edge_ref[1], edge_ref[0])
    upper, lower = first_rows(left[:, None], right[:, None], gain1_ref, channels)
    strip[:, pl.ds(2 * core, 1)] = upper
    strip[:, pl.ds(2 * core + 1, 1)] = lower
    strip[:, pl.ds(2 * (1 - core), 2)] = near_ref[...]
    flags = frame_flags(total_ref, marks_ref, slots)
    hidden = convolved(strip, w1_ref, bias1_ref, 0, hidden_slots, 2)
    inside = inside_ref[0].astype(jnp.float32)
    row = lax.broadcasted_iota(jnp.int32, (1, 2, 1, 1), 1)
    row_flag = jnp.where(row == core, inside, 1.0)
    operand[:, pl.ds(2 * (1 - core), inner_rows)] = inner_ref[...]
    operand[:, pl.ds(inner_rows * core, 2)] = second_rows(hidden, flags * row_flag, gain2_ref, channels)

    lane = lane_mask()
    step = frames // 2
    for frame in range(0, frames, step):
        result = convolved(operand, w2_ref, bias2_ref, frame, step, inner_rows)
        near, far = halves(core, result[:, :, :side], result[:, :, side:])
        for source, value, target in ((mine_ref, near, keep_ref), (other_ref, far, send_ref)):
            raw = source[CACHE + frame:CACHE + frame + step, pl.ds(core, inner_rows // 2)].astype(jnp.float32)
            high = raw[..., 2 * LANES:]
            turned = rolled(high)
            for pair in range(inner_rows // 2):
                for row, tail in ((0, high), (1, turned)):
                    low = raw[:, pair, :, row * LANES:(row + 1) * LANES]
                    features = jnp.concatenate([low, tail[:, pair, :, :channels - LANES]], axis=-1)
                    summed = features + value[:, 2 * pair + row]
                    for k in range(step):
                        live = frame + k < total_ref[0]
                        target[frame + k, 2 * pair + row] = jnp.where(live, summed[k], 0.0).astype(target.dtype)


def shards(features, frame_counts, gain_first, conv_first, bias_first, gain_second, conv_second, bias_second):
    frames, rows, side, channels = features.shape
    pairs, half = rows // 2, rows // 2
    core = lax.axis_index("wa")
    tall, cores = lax.axis_size("ha"), lax.axis_size("wa")
    packed = 3 * LANES
    bf16 = jnp.bfloat16
    vmem, smem = pl.BlockSpec(memory_space=pltpu.VMEM), pl.BlockSpec(memory_space=pltpu.SMEM)
    limit = pltpu.CompilerParams(vmem_limit_bytes=24 * 2**20)

    def shape(*extent):
        return jax.ShapeDtypeStruct(extent, bf16)

    tail, own = pl.pallas_call(
        prepare_kernel,
        out_shape=(shape(CACHE * pairs + 1, side, packed), shape(frames, pairs, side, packed)),
        in_specs=[smem, vmem],
        out_specs=(vmem, vmem),
        scratch_shapes=[pltpu.VMEM((frames, pairs, side, packed), bf16)],
        compiler_params=limit,
    )(frame_counts, features)
    earlier = earlier_frames(tail, pairs)
    marks = earlier[-1]
    joined = jnp.concatenate([earlier[:-1].reshape(CACHE, pairs, side, packed), own], axis=0)

    swap = [(0, 1), (1, 0)]
    held = half // 2 + 1
    mine = lax.dynamic_slice_in_dim(joined, core * (pairs - held), held, 1)
    theirs = lax.dynamic_slice_in_dim(joined, (1 - core) * (pairs - held), held, 1)
    other = lax.ppermute(theirs, "wa", swap)
    edge = lax.dynamic_index_in_dim(jnp.stack([mine, other]), core * (held - 1), 2, keepdims=False)
    across = []
    for h in range(tall - 1):
        lower, upper = h * cores + 1, (h + 1) * cores
        across += [(lower, upper), (upper, lower)]
    edge = lax.ppermute(edge, ("ha", "wa"), across)
    place = lax.axis_index("ha")
    inside = jnp.where(core == 0, place > 0, place < tall - 1)

    slots = frames + CACHE
    width = 2 * side
    core_word = core.astype(jnp.int32).reshape(1)
    weights = (
        gain_first.reshape(1, channels), conv_first, bias_first.reshape(1, channels),
        gain_second.reshape(1, channels),
    )
    work = 2 * TAPS**3 * channels * channels * width
    inner, near = pl.pallas_call(
        inner_kernel,
        out_shape=(shape(slots - 2, half, width, packed), shape(slots, 2, width, packed)),
        in_specs=[smem, smem] + [vmem] * 7,
        out_specs=(vmem, vmem),
        scratch_shapes=[pltpu.VMEM((slots, half + 2, width, packed), bf16)],
        compiler_params=limit,
        cost_estimate=pl.CostEstimate(
            flops=work * (slots - 2) * half, bytes_accessed=8 * 2**20, transcendentals=0
        ),
    )(core_word, frame_counts, marks, mine, other, *weights)
    keep, send = pl.pallas_call(
        outer_kernel,
        out_shape=(shape(frames, half, side, channels), shape(frames, half, side, channels)),
        in_specs=[smem, smem, smem] + [vmem] * 12,
        out_specs=(vmem, vmem),
        scratch_shapes=[
            pltpu.VMEM((slots, 4, width, packed), bf16),
            pltpu.VMEM((slots - 2, half + 2, width, packed), bf16),
        ],
        compiler_params=limit,
        cost_estimate=pl.CostEstimate(
            flops=work * ((slots - 2) * 2 + frames * half), bytes_accessed=8 * 2**20, transcendentals=0
        ),
    )(
        core_word, frame_counts, inside.astype(jnp.int32).reshape(1), marks, mine, other, edge, inner, near,
        *weights, conv_second, bias_second.reshape(1, channels),
    )
    got = lax.ppermute(send, "wa", swap)
    upper, lower = halves(core, keep, got)
    return jnp.concatenate([upper, lower], axis=1)


def solution(mesh):
    return jax.shard_map(
        shards,
        mesh=mesh,
        in_specs=(
            P(("grp", "tchunk"), "ha", "wa", None),
            P(("grp", "tchunk")),
            P(), P(), P(), P(), P(), P(),
        ),
        out_specs=P(("grp", "tchunk"), "ha", "wa", None),
        check_vma=False,
    )
```

```python
import jax
import jax.numpy as jnp
from jax import lax
from jax.experimental import pallas as pl
from jax.experimental.pallas import tpu as pltpu
from jax.sharding import PartitionSpec as P

epsilon = 1e-06
CACHE = 4
TAPS = 3
LANES = 128


def prepare_kernel(
    total_ref, features_hbm, tail_mine_ref, tail_other_ref, own_mine_ref, own_other_ref, marks_ref,
    raw, pack, arrived,
):
    fetch = pltpu.make_async_copy(features_hbm, raw, arrived)
    fetch.start()
    fetch.wait()
    frames, rows = raw.shape[:2]
    pairs, held = rows // 2, own_mine_ref.shape[1]
    core = lax.axis_index("wa")
    total = total_ref[0]
    for frame in range(frames):
        for pair in range(pairs):
            first, second = raw[frame, 2 * pair], raw[frame, 2 * pair + 1]
            packed = jnp.concatenate(
                [first[:, :LANES], second[:, :LANES], first[:, LANES:], second[:, LANES:]], axis=-1
            )
            pack[frame, pair] = packed
    for place, own_ref, tail_ref in ((core, own_mine_ref, tail_mine_ref), (1 - core, own_other_ref, tail_other_ref)):
        chosen = pl.ds(place * (pairs - held), held)
        for frame in range(frames):
            value = pack[frame, chosen]
            own_ref[frame] = jnp.where(frame < total, value, jnp.zeros_like(value))
        for slot in range(CACHE):
            frame = total - CACHE + slot
            value = pack[jnp.maximum(frame, 0), chosen]
            tail_ref[slot * held:(slot + 1) * held] = jnp.where(frame >= 0, value, jnp.zeros_like(value))
    slot = lax.broadcasted_iota(jnp.int32, marks_ref.shape, 0)
    tail_mine_ref[CACHE * held] = jnp.where(
        (slot < CACHE) & (total - CACHE + slot >= 0), 1.0, 0.0
    ).astype(tail_mine_ref.dtype)
    marks_ref[...] = jnp.where(slot < total, 1.0, 0.0).astype(marks_ref.dtype)


def joined_tails(mine, other):
    count = lax.axis_size("tchunk")
    if count <= 2:
        return mine, other
    tiles = other.shape[0]
    value = jnp.concatenate([mine, other], axis=0)

    def apart(value):
        return jnp.concatenate([
            value[:tiles].reshape((CACHE, -1) + value.shape[1:]),
            value[tiles + 1:].reshape((CACHE, -1) + value.shape[1:]),
        ], axis=1), value[tiles, :CACHE]

    def pushed(value, held):
        return lax.dynamic_slice_in_dim(jnp.concatenate([value, jnp.zeros_like(value)], axis=0), held, CACHE, 0)

    step = 1
    while step < count - 1:
        early = lax.ppermute(value, "tchunk", [(k, k + step) for k in range(count - step)])
        held = jnp.sum(value[tiles, :CACHE, 0].astype(jnp.int32))
        body, marks = apart(early)
        body, marks = pushed(body, held), pushed(marks, held)
        half = body.shape[1] // 2
        marks = jnp.pad(marks, ((0, value.shape[1] - CACHE), (0, 0)))[None]
        shape = (tiles,) + value.shape[1:]
        value = value + jnp.concatenate([body[:, :half].reshape(shape), marks, body[:, half:].reshape(shape)], axis=0)
        step *= 2
    return value[:tiles + 1], value[tiles + 1:]


def fetch_kernel(ready_ref, *refs):
    count = (len(refs) - 1) // 2
    arrived = refs[-1]
    fetches = [
        pltpu.make_async_copy(refs[k], refs[count + k], arrived.at[k]) for k in range(count)
    ]
    for fetch in fetches:
        fetch.start()
    for fetch in fetches:
        fetch.wait()


def silu(values):
    return values * (0.5 + 0.5 * jnp.tanh(0.5 * values))


def lane_mask():
    return lax.broadcasted_iota(jnp.int32, (1, 1, 1, LANES), 3) < LANES // 2


def gains(gain_ref):
    low, high = gain_ref[:, :LANES], gain_ref[:, LANES:]
    return low.reshape(1, 1, 1, LANES), jnp.concatenate([high, high], axis=-1).reshape(1, 1, 1, LANES)


def rolled(values):
    shape = values.shape
    return pltpu.roll(values.reshape(-1, LANES), LANES // 2, 1).reshape(shape)


def first_rows(left, right, gain_ref, channels):
    raw = jnp.concatenate([left.astype(jnp.float32), right.astype(jnp.float32)], axis=2)
    front, back, high = raw[..., :LANES], raw[..., LANES:2 * LANES], raw[..., 2 * LANES:]
    lower = lane_mask()
    squared = high * high

    def inverse(low, mask):
        total = jnp.sum(low * low + jnp.where(mask, squared, 0.0), axis=-1, keepdims=True)
        return lax.rsqrt(total * (1.0 / channels) + epsilon)

    scale_front, scale_back = inverse(front, lower), inverse(back, jnp.logical_not(lower))
    gain_low, gain_high = gains(gain_ref)
    front = silu(front * scale_front * gain_low)
    back = silu(back * scale_back * gain_low)
    high = silu(high * jnp.where(lower, scale_front, scale_back) * gain_high)
    turned = rolled(high)
    one = [front, jnp.where(lower, high, 0.0), jnp.where(lower, 0.0, turned)]
    two = [back, jnp.where(lower, turned, 0.0), jnp.where(lower, 0.0, high)]
    return [jnp.concatenate([part.astype(jnp.bfloat16) for part in row], axis=-1) for row in (one, two)]


def second_rows(hidden, flag, gain_ref, channels):
    gain = gain_ref[...].reshape(1, 1, 1, channels)
    total = jnp.sum(hidden * hidden, axis=-1, keepdims=True)
    inverse = lax.rsqrt(total * (1.0 / channels) + epsilon) * flag
    values = silu(hidden * inverse * gain)
    rest = jnp.zeros(values.shape[:-1] + (LANES // 2,), jnp.float32)
    high = jnp.concatenate([values[..., LANES:], rest], axis=-1)
    parts = [values[..., :LANES], high, rolled(high)]
    return jnp.concatenate([part.astype(jnp.bfloat16) for part in parts], axis=-1)


def convolved(operand, weights_ref, bias_ref, frame, frames, rows):
    width = operand.shape[2]
    channels = weights_ref.shape[-1]
    taps = [(a, i) for a in range(TAPS) for i in range(TAPS)]
    groups = [taps[start:start + 2] for start in range(0, len(taps), 2)]

    def window(tap, part):
        a, i = tap
        value = operand[frame + a:frame + a + frames, i:i + rows, :, part * LANES:(part + 1) * LANES]
        return value.reshape(frames * rows * width, LANES)

    pieces = []
    for group in groups:
        pieces += [window(tap, 0) for tap in group]
        high = window(group[0], 1)
        pieces.append(high + window(group[1], 2) if len(group) > 1 else high)
    left = jnp.concatenate(pieces, axis=-1)
    products = []
    for j in range(TAPS):
        rights = []
        for group in groups:
            held = [weights_ref[a, i, j] for a, i in group]
            rights += [weight[:LANES] for weight in held] + [weight[LANES:] for weight in held]
        rights.append(jnp.zeros((left.shape[1] - sum(r.shape[0] for r in rights), channels), jnp.bfloat16))
        product = jnp.dot(left, jnp.concatenate(rights, axis=0), preferred_element_type=jnp.float32)
        products.append(product.reshape(frames * rows, width, channels))
    column = lax.broadcasted_iota(jnp.int32, (1, width, 1), 1)
    before = jnp.where(column == 0, 0.0, pltpu.roll(products[0], 1, 1))
    after = jnp.where(column == width - 1, 0.0, pltpu.roll(products[2], width - 1, 1))
    result = products[1] + before + after + bias_ref[...].reshape(1, 1, channels)
    return result.reshape(frames, rows, width, channels)


def halves(core, mine, other):
    return jnp.where(core == 0, mine, other), jnp.where(core == 0, other, mine)


def frame_flags(marks, frames):
    values = marks.astype(jnp.float32)
    return [values[k:k + 1, 0:1].reshape(1, 1, 1, 1) for k in frames]


def fill_rows(operand, frame, mine, other, gain_ref, channels):
    left, right = halves(lax.axis_index("wa"), mine, other)
    frames, pairs = mine.shape[:2]
    upper, lower = first_rows(left, right, gain_ref, channels)
    for pair in range(pairs):
        operand[frame:frame + frames, 2 * pair] = upper[:, pair]
        operand[frame:frame + frames, 2 * pair + 1] = lower[:, pair]


def own_kernel(
    marks_ref, mine_ref, other_ref, gain1_ref, w1_ref, bias1_ref, gain2_ref, w2_hbm,
    first_ref, inner_ref, edge_ref, w2_ref, arrived,
):
    fetch = pltpu.make_async_copy(w2_hbm, w2_ref, arrived)
    fetch.start()
    core = lax.axis_index("wa")
    frames, pairs = mine_ref.shape[:2]
    channels = w1_ref.shape[-1]
    fill_rows(first_ref, 0, mine_ref[...], other_ref[...], gain1_ref, channels)
    for k, source in enumerate((mine_ref, other_ref)):
        edge_ref[k] = source[:, pl.ds((pairs - 1) * core, 1)].reshape(edge_ref.shape[1:])
    hidden = convolved(first_ref, w1_ref, bias1_ref, 0, frames - 2, 2 * pairs - 2)
    flags = jnp.concatenate(frame_flags(marks_ref[...], range(2, frames)), axis=0)
    inner_ref[...] = second_rows(hidden, flags, gain2_ref, channels)
    fetch.wait()


def edge_kernel(tail_mine_ref, tail_other_ref, own_ref, edge_ref):
    held = tail_other_ref.shape[0] // CACHE
    pair = lax.axis_index("wa") * (held - 1)
    for k, source in enumerate((tail_mine_ref, tail_other_ref)):
        for slot in range(CACHE):
            edge_ref[k, slot] = source[slot * held + pair]
    edge_ref[:, CACHE:] = own_ref[...]


def early_kernel(
    marks_ref, tail_mine_ref, tail_other_ref, first_ref, gain1_ref, w1_ref, bias1_ref, gain2_ref,
    near_ref, inner_ref, operand,
):
    core = lax.axis_index("wa")
    rows = first_ref.shape[1]
    pairs = rows // 2
    channels = w1_ref.shape[-1]
    tiles = CACHE * pairs

    def unpacked(ref):
        return ref[0:tiles].reshape((CACHE, pairs) + ref.shape[1:])

    fill_rows(operand, 0, unpacked(tail_mine_ref), unpacked(tail_other_ref), gain1_ref, channels)
    operand[CACHE:CACHE + 2] = first_ref[0:2]
    near_ref[...] = operand[0:CACHE, pl.ds((rows - 2) * core, 2)]
    hidden = convolved(operand, w1_ref, bias1_ref, 0, CACHE, rows - 2)
    flags = frame_flags(tail_mine_ref[tiles], range(CACHE - 2, CACHE)) + frame_flags(marks_ref[...], range(2))
    inner_ref[...] = second_rows(hidden, jnp.concatenate(flags, axis=0), gain2_ref, channels)


def outer_kernel(
    marks_ref, tail_mine_ref, mine_ref, other_ref, edge_ref, near_ref, first_ref, early_ref, inner_ref,
    gain1_ref, w1_ref, bias1_ref, gain2_ref, w2_ref, bias2_ref,
    keep_ref, send_ref, strip, operand,
):
    core, place = lax.axis_index("wa"), lax.axis_index("ha")
    frames, pairs, side, _ = mine_ref.shape
    inner_rows = inner_ref.shape[1]
    channels = w1_ref.shape[-1]

    left, right = halves(core, edge_ref[1], edge_ref[0])
    upper, lower = first_rows(left[:, None], right[:, None], gain1_ref, channels)
    strip[:, pl.ds(2 * core, 1)] = upper
    strip[:, pl.ds(2 * core + 1, 1)] = lower
    near = pl.ds(2 * (1 - core), 2)
    strip[0:CACHE, near] = near_ref[...]
    strip[CACHE:, near] = first_ref[:, pl.ds((2 * pairs - 2) * core, 2)]
    hidden = convolved(strip, w1_ref, bias1_ref, 0, frames + 2, 2)
    inside = jnp.where(core == 0, place > 0, place < lax.axis_size("ha") - 1)
    row = lax.broadcasted_iota(jnp.int32, (1, 2, 1, 1), 1)
    row_flag = jnp.where((row == core) & jnp.logical_not(inside), 0.0, 1.0)
    marks = marks_ref[...]
    live = frame_flags(marks, range(frames))
    flags = frame_flags(tail_mine_ref[CACHE * pairs], range(CACHE - 2, CACHE)) + live
    middle = pl.ds(2 * (1 - core), inner_rows)
    operand[0:CACHE, middle] = early_ref[...]
    operand[CACHE:, middle] = inner_ref[...]
    operand[:, pl.ds(inner_rows * core, 2)] = second_rows(
        hidden, jnp.concatenate(flags, axis=0) * row_flag, gain2_ref, channels
    )

    step = frames // 2
    for frame in range(0, frames, step):
        result = convolved(operand, w2_ref, bias2_ref, frame, step, inner_rows)
        near, far = halves(core, result[:, :, :side], result[:, :, side:])
        for source, value, target in ((mine_ref, near, keep_ref), (other_ref, far, send_ref)):
            raw = source[frame:frame + step, pl.ds(core, inner_rows // 2)].astype(jnp.float32)
            high = raw[..., 2 * LANES:]
            turned = rolled(high)
            for pair in range(inner_rows // 2):
                for row, tail in ((0, high), (1, turned)):
                    low = raw[:, pair, :, row * LANES:(row + 1) * LANES]
                    features = jnp.concatenate([low, tail[:, pair, :, :channels - LANES]], axis=-1)
                    summed = features + value[:, 2 * pair + row]
                    for k in range(step):
                        kept = jnp.where(live[frame + k].reshape(1, 1) > 0.5, summed[k], 0.0)
                        target[frame + k, 2 * pair + row] = kept.astype(target.dtype)


def shards(features, frame_counts, gain_first, conv_first, bias_first, gain_second, conv_second, bias_second):
    frames, rows, side, channels = features.shape
    pairs, half = rows // 2, rows // 2
    held = half // 2 + 1
    tall, cores, blocks = lax.axis_size("ha"), lax.axis_size("wa"), lax.axis_size("tchunk")
    packed, width = 3 * LANES, 2 * side
    bf16 = jnp.bfloat16
    hbm, vmem = pl.BlockSpec(memory_space=pltpu.HBM), pl.BlockSpec(memory_space=pltpu.VMEM)
    limit = pltpu.CompilerParams(vmem_limit_bytes=20 * 2**20)
    work = 2 * TAPS**3 * channels * channels * width

    def shape(*extent):
        return jax.ShapeDtypeStruct(extent, bf16)

    def placed(value):
        return pltpu.with_memory_space_constraint(value, pltpu.HBM)

    def cost(flops, fetched):
        return pl.CostEstimate(flops=flops, bytes_accessed=fetched, transcendentals=0)

    tail_mine, tail_other, mine, theirs, marks = pl.pallas_call(
        prepare_kernel,
        out_shape=(
            shape(CACHE * held + 1, side, packed), shape(CACHE * held, side, packed),
            shape(frames, held, side, packed), shape(frames, held, side, packed), shape(side, packed),
        ),
        in_specs=[pl.BlockSpec(memory_space=pltpu.SMEM), hbm],
        out_specs=(vmem,) * 5,
        scratch_shapes=[
            pltpu.VMEM(features.shape, bf16),
            pltpu.VMEM((frames, pairs, side, packed), bf16),
            pltpu.SemaphoreType.DMA,
        ],
        compiler_params=limit,
    )(frame_counts, placed(features))

    tail_mine, tail_other = joined_tails(tail_mine, tail_other)
    straight, crossed = [], []
    for k in range(blocks - 1):
        for core in range(cores):
            straight.append((k * cores + core, (k + 1) * cores + core))
            crossed.append((k * cores + core, (k + 1) * cores + 1 - core))
    tail_mine = lax.ppermute(tail_mine, ("tchunk", "wa"), straight)
    tail_other = lax.ppermute(tail_other, ("tchunk", "wa"), crossed)
    swap = [(0, 1), (1, 0)]
    other = lax.ppermute(theirs, "wa", swap)

    sources = (
        gain_first.reshape(1, channels), conv_first, bias_first.reshape(1, channels),
        gain_second.reshape(1, channels), bias_second.reshape(1, channels),
    )
    gain1, w1, bias1, gain2, bias2 = pl.pallas_call(
        fetch_kernel,
        out_shape=tuple(jax.ShapeDtypeStruct(source.shape, source.dtype) for source in sources),
        in_specs=[vmem] + [hbm] * len(sources),
        out_specs=(vmem,) * len(sources),
        scratch_shapes=[pltpu.SemaphoreType.DMA((len(sources),))],
        compiler_params=limit,
        cost_estimate=cost(0, 4 * 2**20),
    )(marks, *map(placed, sources))
    first, inner, edge_own, w2 = pl.pallas_call(
        own_kernel,
        out_shape=(
            shape(frames, half + 2, width, packed), shape(frames - 2, half, width, packed),
            shape(2, frames, side, packed), jax.ShapeDtypeStruct(conv_second.shape, conv_second.dtype),
        ),
        in_specs=[vmem] * 7 + [hbm],
        out_specs=(vmem,) * 4,
        scratch_shapes=[pltpu.SemaphoreType.DMA],
        compiler_params=limit,
        cost_estimate=cost(work * (frames - 2) * half, 8 * 2**20),
    )(marks, mine, other, gain1, w1, bias1, gain2, placed(conv_second))

    edge = pl.pallas_call(
        edge_kernel,
        out_shape=shape(2, CACHE + frames, side, packed),
        in_specs=[vmem] * 3,
        out_specs=vmem,
        compiler_params=limit,
        cost_estimate=cost(0, 2**18),
    )(tail_mine, tail_other, edge_own)
    across = []
    for h in range(tall - 1):
        lower, upper = h * cores + 1, (h + 1) * cores
        across += [(lower, upper), (upper, lower)]
    edge = lax.ppermute(edge, ("ha", "wa"), across)
    near, early = pl.pallas_call(
        early_kernel,
        out_shape=(shape(CACHE, 2, width, packed), shape(CACHE, half, width, packed)),
        in_specs=[vmem] * 8,
        out_specs=(vmem, vmem),
        scratch_shapes=[pltpu.VMEM((CACHE + 2, half + 2, width, packed), bf16)],
        compiler_params=limit,
        cost_estimate=cost(work * CACHE * half, 4 * 2**20),
    )(marks, tail_mine, tail_other, first, gain1, w1, bias1, gain2)
    keep, send = pl.pallas_call(
        outer_kernel,
        out_shape=(shape(frames, half, side, channels), shape(frames, half, side, channels)),
        in_specs=[vmem] * 15,
        out_specs=(vmem, vmem),
        scratch_shapes=[
            pltpu.VMEM((frames + CACHE, 4, width, packed), bf16),
            pltpu.VMEM((frames + 2, half + 2, width, packed), bf16),
        ],
        compiler_params=limit,
        cost_estimate=cost(work * ((frames + 2) * 2 + frames * half), 8 * 2**20),
    )(marks, tail_mine, mine, other, edge, near, first, early, inner, gain1, w1, bias1, gain2, w2, bias2)
    got = lax.ppermute(send, "wa", swap)
    upper, lower = halves(lax.axis_index("wa"), keep, got)
    return jnp.concatenate([upper, lower], axis=1)


def solution(mesh):
    return jax.shard_map(
        shards,
        mesh=mesh,
        in_specs=(
            P(("grp", "tchunk"), "ha", "wa", None),
            P(("grp", "tchunk")),
            P(), P(), P(), P(), P(), P(),
        ),
        out_specs=P(("grp", "tchunk"), "ha", "wa", None),
        check_vma=False,
    )
```

```python
import jax
import jax.numpy as jnp
from jax import lax
from jax.experimental import pallas as pl
from jax.experimental.pallas import tpu as pltpu
from jax.sharding import PartitionSpec as P

epsilon = 1e-06
CACHE = 4
TAPS = 3
LANES = 128


def prepare_kernel(total_ref, features_hbm, tail_ref, mine_ref, theirs_ref, marks_ref, raw, pack, arrived):
    fetch = pltpu.make_async_copy(features_hbm, raw, arrived)
    fetch.start()
    fetch.wait()
    frames, rows = raw.shape[:2]
    pairs, held = rows // 2, mine_ref.shape[1]
    core = lax.axis_index("wa")
    total = total_ref[0]
    for frame in range(frames):
        for pair in range(pairs):
            first, second = raw[frame, 2 * pair], raw[frame, 2 * pair + 1]
            packed = jnp.concatenate(
                [first[:, :LANES], second[:, :LANES], first[:, LANES:], second[:, LANES:]], axis=-1
            )
            pack[frame, pair] = packed
    for place, ref in ((core, tail_ref), (1 - core, theirs_ref)):
        for slot in range(CACHE):
            frame = total - CACHE + slot
            value = pack[jnp.maximum(frame, 0), pl.ds(place * (pairs - held), held)]
            ref[slot * held:(slot + 1) * held] = jnp.where(frame >= 0, value, jnp.zeros_like(value))
    for frame in range(frames):
        start = (CACHE + frame) * held
        value = pack[frame, pl.ds(core * (pairs - held), held)]
        mine_ref[frame] = jnp.where(frame < total, value, jnp.zeros_like(value))
        value = pack[frame, pl.ds((1 - core) * (pairs - held), held)]
        theirs_ref[start:start + held] = jnp.where(frame < total, value, jnp.zeros_like(value))
    slot = lax.broadcasted_iota(jnp.int32, marks_ref.shape, 0)
    tail_ref[CACHE * held] = jnp.where(
        (slot < CACHE) & (total - CACHE + slot >= 0), 1.0, 0.0
    ).astype(tail_ref.dtype)
    marks_ref[...] = jnp.where(slot < total, 1.0, 0.0).astype(marks_ref.dtype)


def joined_tails(mine, other):
    count = lax.axis_size("tchunk")
    if count <= 2:
        return mine, other
    tiles = other.shape[0]
    value = jnp.concatenate([mine, other], axis=0)

    def apart(value):
        return jnp.concatenate([
            value[:tiles].reshape((CACHE, -1) + value.shape[1:]),
            value[tiles + 1:].reshape((CACHE, -1) + value.shape[1:]),
        ], axis=1), value[tiles, :CACHE]

    def pushed(value, held):
        return lax.dynamic_slice_in_dim(jnp.concatenate([value, jnp.zeros_like(value)], axis=0), held, CACHE, 0)

    step = 1
    while step < count - 1:
        early = lax.ppermute(value, "tchunk", [(k, k + step) for k in range(count - step)])
        held = jnp.sum(value[tiles, :CACHE, 0].astype(jnp.int32))
        body, marks = apart(early)
        body, marks = pushed(body, held), pushed(marks, held)
        half = body.shape[1] // 2
        marks = jnp.pad(marks, ((0, value.shape[1] - CACHE), (0, 0)))[None]
        shape = (tiles,) + value.shape[1:]
        value = value + jnp.concatenate([body[:, :half].reshape(shape), marks, body[:, half:].reshape(shape)], axis=0)
        step *= 2
    return value[:tiles + 1], value[tiles + 1:]


def silu(values):
    return values * (0.5 + 0.5 * jnp.tanh(0.5 * values))


def lane_mask():
    return lax.broadcasted_iota(jnp.int32, (1, 1, 1, LANES), 3) < LANES // 2


def gains(gain_ref):
    low, high = gain_ref[:, :LANES], gain_ref[:, LANES:]
    return low.reshape(1, 1, 1, LANES), jnp.concatenate([high, high], axis=-1).reshape(1, 1, 1, LANES)


def rolled(values):
    shape = values.shape
    return pltpu.roll(values.reshape(-1, LANES), LANES // 2, 1).reshape(shape)


def first_rows(left, right, gain_ref, channels):
    raw = jnp.concatenate([left.astype(jnp.float32), right.astype(jnp.float32)], axis=2)
    front, back, high = raw[..., :LANES], raw[..., LANES:2 * LANES], raw[..., 2 * LANES:]
    lower = lane_mask()
    squared = high * high

    def inverse(low, mask):
        total = jnp.sum(low * low + jnp.where(mask, squared, 0.0), axis=-1, keepdims=True)
        return lax.rsqrt(total * (1.0 / channels) + epsilon)

    scale_front, scale_back = inverse(front, lower), inverse(back, jnp.logical_not(lower))
    gain_low, gain_high = gains(gain_ref)
    front = silu(front * scale_front * gain_low)
    back = silu(back * scale_back * gain_low)
    high = silu(high * jnp.where(lower, scale_front, scale_back) * gain_high)
    turned = rolled(high)
    one = [front, jnp.where(lower, high, 0.0), jnp.where(lower, 0.0, turned)]
    two = [back, jnp.where(lower, turned, 0.0), jnp.where(lower, 0.0, high)]
    return [jnp.concatenate([part.astype(jnp.bfloat16) for part in row], axis=-1) for row in (one, two)]


def second_rows(hidden, flag, gain_ref, channels):
    gain = gain_ref[...].reshape(1, 1, 1, channels)
    total = jnp.sum(hidden * hidden, axis=-1, keepdims=True)
    inverse = lax.rsqrt(total * (1.0 / channels) + epsilon) * flag
    values = silu(hidden * inverse * gain)
    rest = jnp.zeros(values.shape[:-1] + (LANES // 2,), jnp.float32)
    high = jnp.concatenate([values[..., LANES:], rest], axis=-1)
    parts = [values[..., :LANES], high, rolled(high)]
    return jnp.concatenate([part.astype(jnp.bfloat16) for part in parts], axis=-1)


def convolved(operand, weights_ref, bias_ref, frame, frames, rows):
    width = operand.shape[2]
    channels = weights_ref.shape[-1]
    taps = [(a, i) for a in range(TAPS) for i in range(TAPS)]
    groups = [taps[start:start + 2] for start in range(0, len(taps), 2)]

    def window(tap, part):
        a, i = tap
        value = operand[frame + a:frame + a + frames, i:i + rows, :, part * LANES:(part + 1) * LANES]
        return value.reshape(frames * rows * width, LANES)

    pieces = []
    for group in groups:
        pieces += [window(tap, 0) for tap in group]
        high = window(group[0], 1)
        pieces.append(high + window(group[1], 2) if len(group) > 1 else high)
    left = jnp.concatenate(pieces, axis=-1)
    products = []
    for j in range(TAPS):
        rights = []
        for group in groups:
            held = [weights_ref[a, i, j] for a, i in group]
            rights += [weight[:LANES] for weight in held] + [weight[LANES:] for weight in held]
        rights.append(jnp.zeros((left.shape[1] - sum(r.shape[0] for r in rights), channels), jnp.bfloat16))
        product = jnp.dot(left, jnp.concatenate(rights, axis=0), preferred_element_type=jnp.float32)
        products.append(product.reshape(frames * rows, width, channels))
    column = lax.broadcasted_iota(jnp.int32, (1, width, 1), 1)
    before = jnp.where(column == 0, 0.0, pltpu.roll(products[0], 1, 1))
    after = jnp.where(column == width - 1, 0.0, pltpu.roll(products[2], width - 1, 1))
    result = products[1] + before + after + bias_ref[...].reshape(1, 1, channels)
    return result.reshape(frames, rows, width, channels)


def halves(core, mine, other):
    return jnp.where(core == 0, mine, other), jnp.where(core == 0, other, mine)


def frame_flags(marks, frames):
    values = marks.astype(jnp.float32)
    return [values[k:k + 1, 0:1].reshape(1, 1, 1, 1) for k in frames]


def fill_rows(operand, frame, mine, other, gain_ref, channels):
    left, right = halves(lax.axis_index("wa"), mine, other)
    frames, pairs = mine.shape[:2]
    upper, lower = first_rows(left, right, gain_ref, channels)
    for pair in range(pairs):
        operand[frame:frame + frames, 2 * pair] = upper[:, pair]
        operand[frame:frame + frames, 2 * pair + 1] = lower[:, pair]


def border_kernel(tail_ref, mine_ref, other_ref, tail_edge_ref, own_edge_ref):
    frames, held = mine_ref.shape[:2]
    pair = lax.axis_index("wa") * (held - 1)
    for slot in range(CACHE):
        tail_edge_ref[0, slot] = tail_ref[slot * held + pair]
        tail_edge_ref[1, slot] = other_ref[slot * held + pair]
    for frame in range(frames):
        own_edge_ref[0, frame] = mine_ref[frame, pair]
        own_edge_ref[1, frame] = other_ref[(CACHE + frame) * held + pair]


def finish(mine_ref, other_ref, live, pairs, value, targets):
    frames, held, side, _ = mine_ref.shape
    channels = value.shape[-1]
    start, count = pairs
    near, far = halves(lax.axis_index("wa"), value[:, :, :side], value[:, :, side:])
    for mine, value, target in ((True, near, targets[0]), (False, far, targets[1])):
        for frame in range(frames):
            for k in range(count):
                if mine:
                    raw = mine_ref[frame, start + k]
                else:
                    raw = other_ref[(CACHE + frame) * held + start + k]
                raw = raw.astype(jnp.float32)
                high = raw[:, 2 * LANES:]
                for row, tail in ((0, high), (1, pltpu.roll(high, LANES // 2, 1))):
                    low = raw[:, row * LANES:(row + 1) * LANES]
                    features = jnp.concatenate([low, tail[:, :channels - LANES]], axis=-1)
                    summed = features + value[frame, 2 * k + row]
                    kept = jnp.where(live[frame].reshape(1, 1) > 0.5, summed, 0.0)
                    target(frame, 2 * k + row, kept.astype(jnp.bfloat16))


def middle_kernel(
    marks_ref, tail_mine_ref, tail_other_ref, mine_ref, other_ref,
    gain1_ref, w1_ref, bias1_ref, gain2_ref, w2_ref, bias2_ref,
    near_ref, inner_ref, keep_ref, send_ref, operand,
):
    core = lax.axis_index("wa")
    frames, pairs, side, packed = mine_ref.shape
    channels = w1_ref.shape[-1]
    rows = 2 * pairs
    tiles = CACHE * pairs
    live = frame_flags(marks_ref[...], range(frames))
    earlier = lax.axis_index("tchunk") > 0

    def unpacked(ref, start, count):
        return ref[start:start + count * pairs].reshape(count, pairs, side, packed)

    @pl.when(earlier)
    def _():
        fill_rows(
            operand, 0, unpacked(tail_mine_ref, 0, CACHE), unpacked(tail_other_ref, 0, CACHE), gain1_ref, channels
        )
        hidden = convolved(operand, w1_ref, bias1_ref, 0, 2, rows - 2)
        flags = frame_flags(tail_mine_ref[tiles], range(CACHE - 2, CACHE))
        inner_ref[0:2] = second_rows(hidden, jnp.concatenate(flags, axis=0), gain2_ref, channels)

    @pl.when(jnp.logical_not(earlier))
    def _():
        operand[0:CACHE] = jnp.zeros((CACHE,) + operand.shape[1:], operand.dtype)
        inner_ref[0:2] = jnp.zeros((2,) + inner_ref.shape[1:], inner_ref.dtype)

    fill_rows(operand, CACHE, mine_ref[...], unpacked(other_ref, tiles, frames), gain1_ref, channels)
    near_ref[...] = operand[:, pl.ds((rows - 2) * core, 2)]
    step = frames // 2
    for frame in range(2, frames + 2, step):
        hidden = convolved(operand, w1_ref, bias1_ref, frame, step, rows - 2)
        flags = jnp.concatenate(live[frame - 2:frame - 2 + step], axis=0)
        inner_ref[frame:frame + step] = second_rows(hidden, flags, gain2_ref, channels)
    result = convolved(inner_ref, w2_ref, bias2_ref, 0, frames, rows - 4)

    def put(ref):
        def store(frame, row, value):
            ref[frame, row] = value
        return store

    finish(mine_ref, other_ref, live, (1, pairs - 2), result, (put(keep_ref), put(send_ref)))


def outer_kernel(
    marks_ref, tail_mine_ref, mine_ref, other_ref, tail_edge_ref, own_edge_ref, near_ref, inner_ref,
    keep_mid_ref, send_mid_ref, gain1_ref, w1_ref, bias1_ref, gain2_ref, w2_ref, bias2_ref,
    keep_ref, send_ref, strip, operand,
):
    core, place = lax.axis_index("wa"), lax.axis_index("ha")
    frames, pairs = mine_ref.shape[:2]
    inner_rows = inner_ref.shape[1]
    channels = w1_ref.shape[-1]
    outward, inward = pl.ds(2 * core, 2), pl.ds(2 * (1 - core), 2)

    for start, ref in ((0, tail_edge_ref), (CACHE, own_edge_ref)):
        left, right = halves(core, ref[1], ref[0])
        upper, lower = first_rows(left[:, None], right[:, None], gain1_ref, channels)
        strip[start:start + ref.shape[1], pl.ds(2 * core, 1)] = upper
        strip[start:start + ref.shape[1], pl.ds(2 * core + 1, 1)] = lower
    strip[:, inward] = near_ref[...]
    hidden = convolved(strip, w1_ref, bias1_ref, 0, frames + 2, 2)
    inside = jnp.where(core == 0, place > 0, place < lax.axis_size("ha") - 1)
    row = lax.broadcasted_iota(jnp.int32, (1, 2, 1, 1), 1)
    row_flag = jnp.where((row == core) & jnp.logical_not(inside), 0.0, 1.0)
    live = frame_flags(marks_ref[...], range(frames))
    flags = frame_flags(tail_mine_ref[CACHE * pairs], range(CACHE - 2, CACHE)) + live
    operand[:, inward] = inner_ref[:, pl.ds((inner_rows - 2) * core, 2)]
    operand[:, outward] = second_rows(hidden, jnp.concatenate(flags, axis=0) * row_flag, gain2_ref, channels)
    result = convolved(operand, w2_ref, bias2_ref, 0, frames, 2)

    def put(ref):
        def store(frame, row, value):
            ref[frame, (inner_rows - 2) * core + row] = value
        return store

    finish(mine_ref, other_ref, live, ((pairs - 1) * core, 1), result, (put(keep_ref), put(send_ref)))
    for source, target in ((keep_mid_ref, keep_ref), (send_mid_ref, send_ref)):
        target[:, pl.ds(2 * (1 - core), inner_rows - 2)] = source[...]


def shards(features, frame_counts, gain_first, conv_first, bias_first, gain_second, conv_second, bias_second):
    frames, rows, side, channels = features.shape
    pairs, half = rows // 2, rows // 2
    held = half // 2 + 1
    tall, cores, blocks = lax.axis_size("ha"), lax.axis_size("wa"), lax.axis_size("tchunk")
    packed, width, tiles = 3 * LANES, 2 * side, CACHE * held
    bf16 = jnp.bfloat16
    hbm, vmem = pl.BlockSpec(memory_space=pltpu.HBM), pl.BlockSpec(memory_space=pltpu.VMEM)
    limit = pltpu.CompilerParams(vmem_limit_bytes=20 * 2**20)
    work = 2 * TAPS**3 * channels * channels * width

    def shape(*extent):
        return jax.ShapeDtypeStruct(extent, bf16)

    def cost(flops, fetched):
        return pl.CostEstimate(flops=flops, bytes_accessed=fetched, transcendentals=0)

    tail, mine, theirs, marks = pl.pallas_call(
        prepare_kernel,
        out_shape=(
            shape(tiles + 1, side, packed), shape(frames, held, side, packed),
            shape((CACHE + frames) * held, side, packed), shape(side, packed),
        ),
        in_specs=[pl.BlockSpec(memory_space=pltpu.SMEM), hbm],
        out_specs=(vmem,) * 4,
        scratch_shapes=[
            pltpu.VMEM(features.shape, bf16),
            pltpu.VMEM((frames, pairs, side, packed), bf16),
            pltpu.SemaphoreType.DMA,
        ],
        compiler_params=limit,
    )(frame_counts, pltpu.with_memory_space_constraint(features, pltpu.HBM))

    tail, tail_theirs = joined_tails(tail, theirs[:tiles])
    if blocks > 2:
        theirs = jnp.concatenate([tail_theirs, theirs[tiles:]], axis=0)
    straight, crossed, diagonal, across = [], [], [], []

    def index(block, h, core):
        return (block * tall + h) * cores + core

    for h in range(tall):
        for k in range(blocks - 1):
            for core in range(cores):
                straight.append((index(k, h, core), index(k + 1, h, core)))
                crossed.append((index(k, h, core), index(k + 1, h, 1 - core)))
    for h in range(tall - 1):
        for k in range(blocks):
            lower, upper = index(k, h, 1), index(k, h + 1, 0)
            across += [(lower, upper), (upper, lower)]
            if k + 1 < blocks:
                lower_next, upper_next = index(k + 1, h, 1), index(k + 1, h + 1, 0)
                diagonal += [(lower, upper_next), (upper, lower_next)]
    axes = ("tchunk", "ha", "wa")
    swap = [(0, 1), (1, 0)]
    tail_mine = lax.ppermute(tail, axes, straight)
    tail_other = lax.ppermute(tail_theirs, axes, crossed)
    other = lax.ppermute(theirs, "wa", swap)
    tail_edge, own_edge = pl.pallas_call(
        border_kernel,
        out_shape=(shape(2, CACHE, side, packed), shape(2, frames, side, packed)),
        in_specs=[vmem] * 3,
        out_specs=(vmem, vmem),
        compiler_params=limit,
        cost_estimate=cost(2**34, 2**20),
    )(tail, mine, other)
    own_edge = lax.ppermute(own_edge, axes, across)
    tail_edge = lax.ppermute(tail_edge, axes, diagonal)

    weights = (
        gain_first.reshape(1, channels), conv_first, bias_first.reshape(1, channels),
        gain_second.reshape(1, channels), conv_second, bias_second.reshape(1, channels),
    )
    near, inner, keep, send = pl.pallas_call(
        middle_kernel,
        out_shape=(
            shape(frames + CACHE, 2, width, packed), shape(frames + 2, half, width, packed),
            shape(frames, half - 2, side, channels), shape(frames, half - 2, side, channels),
        ),
        in_specs=[vmem] * 11,
        out_specs=(vmem,) * 4,
        scratch_shapes=[pltpu.VMEM((frames + CACHE, half + 2, width, packed), bf16)],
        compiler_params=limit,
        cost_estimate=cost(work * ((frames + 2) * half + frames * (half - 2)), 8 * 2**20),
    )(marks, tail_mine, tail_other, mine, other, *weights)
    keep, send = pl.pallas_call(
        outer_kernel,
        out_shape=(shape(frames, half, side, channels), shape(frames, half, side, channels)),
        in_specs=[vmem] * 16,
        out_specs=(vmem, vmem),
        scratch_shapes=[
            pltpu.VMEM((frames + CACHE, 4, width, packed), bf16),
            pltpu.VMEM((frames + 2, 4, width, packed), bf16),
        ],
        compiler_params=limit,
        cost_estimate=cost(work * 2 * (2 * frames + 2), 8 * 2**20),
    )(marks, tail_mine, mine, other, tail_edge, own_edge, near, inner, keep, send, *weights)
    got = lax.ppermute(send, "wa", swap)
    upper, lower = halves(lax.axis_index("wa"), keep, got)
    return jnp.concatenate([upper, lower], axis=1)


def solution(mesh):
    return jax.shard_map(
        shards,
        mesh=mesh,
        in_specs=(
            P(("grp", "tchunk"), "ha", "wa", None),
            P(("grp", "tchunk")),
            P(), P(), P(), P(), P(), P(),
        ),
        out_specs=P(("grp", "tchunk"), "ha", "wa", None),
        check_vma=False,
    )
```

```python
import jax
import jax.numpy as jnp
from jax import lax
from jax.experimental import pallas as pl
from jax.experimental.pallas import tpu as pltpu
from jax.sharding import PartitionSpec as P

epsilon = 1e-06
CACHE = 4
TAPS = 3
LANES = 128


def slots_kernel(slots_ref):
    slots_ref[...] = lax.broadcasted_iota(jnp.int32, slots_ref.shape, 0)


def prepare_kernel(total_ref, slots_ref, raw, tail_ref, mine_ref, theirs_ref, marks_ref, pack):
    frames, rows = raw.shape[:2]
    pairs, held = rows // 2, mine_ref.shape[1]
    core = lax.axis_index("wa")
    total = total_ref[0]
    for frame in range(frames):
        for pair in range(pairs):
            first, second = raw[frame, 2 * pair], raw[frame, 2 * pair + 1]
            packed = jnp.concatenate(
                [first[:, :LANES], second[:, :LANES], first[:, LANES:], second[:, LANES:]], axis=-1
            )
            pack[frame, pair] = packed
    for place, ref in ((core, tail_ref), (1 - core, theirs_ref)):
        for slot in range(CACHE):
            frame = total - CACHE + slot
            value = pack[jnp.maximum(frame, 0), pl.ds(place * (pairs - held), held)]
            ref[slot * held:(slot + 1) * held] = jnp.where(frame >= 0, value, jnp.zeros_like(value))
    for frame in range(frames):
        start = (CACHE + frame) * held
        value = pack[frame, pl.ds(core * (pairs - held), held)]
        mine_ref[frame] = jnp.where(frame < total, value, jnp.zeros_like(value))
        value = pack[frame, pl.ds((1 - core) * (pairs - held), held)]
        theirs_ref[start:start + held] = jnp.where(frame < total, value, jnp.zeros_like(value))
    slot = slots_ref[...]
    tail_ref[CACHE * held] = jnp.where(
        (slot < CACHE) & (total - CACHE + slot >= 0), 1.0, 0.0
    ).astype(tail_ref.dtype)
    marks_ref[...] = jnp.where(slot < total, 1.0, 0.0).astype(marks_ref.dtype)


def joined_tails(mine, other):
    count = lax.axis_size("tchunk")
    if count <= 2:
        return mine, other
    tiles = other.shape[0]
    value = jnp.concatenate([mine, other], axis=0)

    def apart(value):
        return jnp.concatenate([
            value[:tiles].reshape((CACHE, -1) + value.shape[1:]),
            value[tiles + 1:].reshape((CACHE, -1) + value.shape[1:]),
        ], axis=1), value[tiles, :CACHE]

    def pushed(value, held):
        return lax.dynamic_slice_in_dim(jnp.concatenate([value, jnp.zeros_like(value)], axis=0), held, CACHE, 0)

    step = 1
    while step < count - 1:
        early = lax.ppermute(value, "tchunk", [(k, k + step) for k in range(count - step)])
        held = jnp.sum(value[tiles, :CACHE, 0].astype(jnp.int32))
        body, marks = apart(early)
        body, marks = pushed(body, held), pushed(marks, held)
        half = body.shape[1] // 2
        marks = jnp.pad(marks, ((0, value.shape[1] - CACHE), (0, 0)))[None]
        shape = (tiles,) + value.shape[1:]
        value = value + jnp.concatenate([body[:, :half].reshape(shape), marks, body[:, half:].reshape(shape)], axis=0)
        step *= 2
    return value[:tiles + 1], value[tiles + 1:]


def silu(half):
    return half + half * jnp.tanh(half)


def lane_mask():
    return lax.broadcasted_iota(jnp.int32, (1, 1, 1, LANES), 3) < LANES // 2


def gains(gain_ref):
    low, high = 0.5 * gain_ref[:, :LANES], 0.5 * gain_ref[:, LANES:]
    return low.reshape(1, 1, 1, LANES), jnp.concatenate([high, high], axis=-1).reshape(1, 1, 1, LANES)


def rolled(values):
    shape = values.shape
    return pltpu.roll(values.reshape(-1, LANES), LANES // 2, 1).reshape(shape)


def first_rows(left, right, gain_ref, channels):
    raw = jnp.concatenate([left.astype(jnp.float32), right.astype(jnp.float32)], axis=2)
    front, back, high = raw[..., :LANES], raw[..., LANES:2 * LANES], raw[..., 2 * LANES:]
    lower = lane_mask()
    squared = high * high

    def inverse(low, mask):
        total = jnp.sum(low * low + jnp.where(mask, squared, 0.0), axis=-1, keepdims=True)
        return lax.rsqrt(total * (1.0 / channels) + epsilon)

    scale_front, scale_back = inverse(front, lower), inverse(back, jnp.logical_not(lower))
    gain_low, gain_high = gains(gain_ref)
    front = silu(front * scale_front * gain_low)
    back = silu(back * scale_back * gain_low)
    high = silu(high * jnp.where(lower, scale_front, scale_back) * gain_high)
    turned = rolled(high)
    one = [front, jnp.where(lower, high, 0.0), jnp.where(lower, 0.0, turned)]
    two = [back, jnp.where(lower, turned, 0.0), jnp.where(lower, 0.0, high)]
    return [jnp.concatenate([part.astype(jnp.bfloat16) for part in row], axis=-1) for row in (one, two)]


def second_rows(hidden, flag, gain_ref, channels):
    gain = 0.5 * gain_ref[...].reshape(1, 1, 1, channels)
    total = jnp.sum(hidden * hidden, axis=-1, keepdims=True)
    inverse = lax.rsqrt(total * (1.0 / channels) + epsilon) * flag
    values = silu(hidden * inverse * gain)
    rest = jnp.zeros(values.shape[:-1] + (LANES // 2,), jnp.float32)
    high = jnp.concatenate([values[..., LANES:], rest], axis=-1)
    parts = [values[..., :LANES], high, rolled(high)]
    return jnp.concatenate([part.astype(jnp.bfloat16) for part in parts], axis=-1)


def convolved(operand, weights_ref, bias_ref, frame, frames, rows):
    width = operand.shape[2]
    channels = weights_ref.shape[-1]
    taps = [(a, i) for a in range(TAPS) for i in range(TAPS)]
    groups = [taps[start:start + 2] for start in range(0, len(taps), 2)]

    def window(tap, part):
        a, i = tap
        value = operand[frame + a:frame + a + frames, i:i + rows, :, part * LANES:(part + 1) * LANES]
        return value.reshape(frames * rows * width, LANES)

    pieces = []
    for group in groups:
        pieces += [window(tap, 0) for tap in group]
        high = window(group[0], 1)
        pieces.append(high + window(group[1], 2) if len(group) > 1 else high)
    left = jnp.concatenate(pieces, axis=-1)
    products = []
    for j in range(TAPS):
        rights = []
        for group in groups:
            held = [weights_ref[a, i, j] for a, i in group]
            rights += [weight[:LANES] for weight in held] + [weight[LANES:] for weight in held]
        rights.append(jnp.zeros((left.shape[1] - sum(r.shape[0] for r in rights), channels), jnp.bfloat16))
        product = jnp.dot(left, jnp.concatenate(rights, axis=0), preferred_element_type=jnp.float32)
        products.append(product.reshape(frames * rows, width, channels))
    column = lax.broadcasted_iota(jnp.int32, (1, width, 1), 1)
    before = jnp.where(column == 0, 0.0, pltpu.roll(products[0], 1, 1))
    after = jnp.where(column == width - 1, 0.0, pltpu.roll(products[2], width - 1, 1))
    result = products[1] + before + after + bias_ref[...].reshape(1, 1, channels)
    return result.reshape(frames, rows, width, channels)


def halves(core, mine, other):
    return jnp.where(core == 0, mine, other), jnp.where(core == 0, other, mine)


def frame_flags(marks, frames):
    values = marks.astype(jnp.float32)
    return [values[k:k + 1, 0:1].reshape(1, 1, 1, 1) for k in frames]


def fill_rows(operand, frame, mine, other, gain_ref, channels):
    left, right = halves(lax.axis_index("wa"), mine, other)
    frames, pairs = mine.shape[:2]
    upper, lower = first_rows(left, right, gain_ref, channels)
    for pair in range(pairs):
        operand[frame:frame + frames, 2 * pair] = upper[:, pair]
        operand[frame:frame + frames, 2 * pair + 1] = lower[:, pair]


def border_kernel(tail_ref, mine_ref, other_ref, tail_edge_ref, own_edge_ref):
    frames, held = mine_ref.shape[:2]
    pair = lax.axis_index("wa") * (held - 1)
    for slot in range(CACHE):
        tail_edge_ref[0, slot] = tail_ref[slot * held + pair]
        tail_edge_ref[1, slot] = other_ref[slot * held + pair]
    for frame in range(frames):
        own_edge_ref[0, frame] = mine_ref[frame, pair]
        own_edge_ref[1, frame] = other_ref[(CACHE + frame) * held + pair]


def finish(mine_ref, other_ref, live, pairs, value, targets):
    frames, held, side, _ = mine_ref.shape
    channels = value.shape[-1]
    start, count = pairs
    near, far = halves(lax.axis_index("wa"), value[:, :, :side], value[:, :, side:])
    for mine, value, target in ((True, near, targets[0]), (False, far, targets[1])):
        for frame in range(frames):
            for k in range(count):
                if mine:
                    raw = mine_ref[frame, start + k]
                else:
                    raw = other_ref[(CACHE + frame) * held + start + k]
                raw = raw.astype(jnp.float32)
                high = raw[:, 2 * LANES:]
                for row, tail in ((0, high), (1, pltpu.roll(high, LANES // 2, 1))):
                    low = raw[:, row * LANES:(row + 1) * LANES]
                    features = jnp.concatenate([low, tail[:, :channels - LANES]], axis=-1)
                    summed = features + value[frame, 2 * k + row]
                    kept = jnp.where(live[frame].reshape(1, 1) > 0.5, summed, 0.0)
                    target(frame, 2 * k + row, kept.astype(jnp.bfloat16))


def middle_kernel(
    marks_ref, tail_mine_ref, tail_other_ref, mine_ref, other_ref,
    gain1_ref, w1_ref, bias1_ref, gain2_ref, w2_ref, bias2_ref,
    near_ref, inner_ref, keep_ref, send_ref, operand,
):
    core = lax.axis_index("wa")
    frames, pairs, side, packed = mine_ref.shape
    channels = w1_ref.shape[-1]
    rows = 2 * pairs
    tiles = CACHE * pairs
    live = frame_flags(marks_ref[...], range(frames))
    earlier = lax.axis_index("tchunk") > 0

    def unpacked(ref, start, count):
        return ref[start:start + count * pairs].reshape(count, pairs, side, packed)

    @pl.when(earlier)
    def _():
        fill_rows(
            operand, 0, unpacked(tail_mine_ref, 0, CACHE), unpacked(tail_other_ref, 0, CACHE), gain1_ref, channels
        )
        hidden = convolved(operand, w1_ref, bias1_ref, 0, 2, rows - 2)
        flags = frame_flags(tail_mine_ref[tiles], range(CACHE - 2, CACHE))
        inner_ref[0:2] = second_rows(hidden, jnp.concatenate(flags, axis=0), gain2_ref, channels)

    @pl.when(jnp.logical_not(earlier))
    def _():
        operand[0:CACHE] = jnp.zeros((CACHE,) + operand.shape[1:], operand.dtype)
        inner_ref[0:2] = jnp.zeros((2,) + inner_ref.shape[1:], inner_ref.dtype)

    fill_rows(operand, CACHE, mine_ref[...], unpacked(other_ref, tiles, frames), gain1_ref, channels)
    near_ref[...] = operand[:, pl.ds((rows - 2) * core, 2)]
    hidden = convolved(operand, w1_ref, bias1_ref, 2, frames, rows - 2)
    inner_ref[2:] = second_rows(hidden, jnp.concatenate(live, axis=0), gain2_ref, channels)
    result = convolved(inner_ref, w2_ref, bias2_ref, 0, frames, rows - 4)

    def put(ref):
        def store(frame, row, value):
            ref[frame, row] = value
        return store

    finish(mine_ref, other_ref, live, (1, pairs - 2), result, (put(keep_ref), put(send_ref)))


def outer_kernel(
    marks_ref, tail_mine_ref, mine_ref, other_ref, tail_edge_ref, own_edge_ref, near_ref, inner_ref,
    keep_mid_ref, send_mid_ref, gain1_ref, w1_ref, bias1_ref, gain2_ref, w2_ref, bias2_ref,
    keep_ref, send_ref, strip, operand,
):
    core, place = lax.axis_index("wa"), lax.axis_index("ha")
    frames, pairs = mine_ref.shape[:2]
    inner_rows = inner_ref.shape[1]
    channels = w1_ref.shape[-1]
    outward, inward = pl.ds(2 * core, 2), pl.ds(2 * (1 - core), 2)

    for start, ref in ((0, tail_edge_ref), (CACHE, own_edge_ref)):
        left, right = halves(core, ref[1], ref[0])
        upper, lower = first_rows(left[:, None], right[:, None], gain1_ref, channels)
        strip[start:start + ref.shape[1], pl.ds(2 * core, 1)] = upper
        strip[start:start + ref.shape[1], pl.ds(2 * core + 1, 1)] = lower
    strip[:, inward] = near_ref[...]
    hidden = convolved(strip, w1_ref, bias1_ref, 0, frames + 2, 2)
    inside = jnp.where(core == 0, place > 0, place < lax.axis_size("ha") - 1)
    row = lax.broadcasted_iota(jnp.int32, (1, 2, 1, 1), 1)
    row_flag = jnp.where((row == core) & jnp.logical_not(inside), 0.0, 1.0)
    live = frame_flags(marks_ref[...], range(frames))
    flags = frame_flags(tail_mine_ref[CACHE * pairs], range(CACHE - 2, CACHE)) + live
    operand[:, inward] = inner_ref[:, pl.ds((inner_rows - 2) * core, 2)]
    operand[:, outward] = second_rows(hidden, jnp.concatenate(flags, axis=0) * row_flag, gain2_ref, channels)
    result = convolved(operand, w2_ref, bias2_ref, 0, frames, 2)

    def put(ref):
        def store(frame, row, value):
            ref[frame, (inner_rows - 2) * core + row] = value
        return store

    finish(mine_ref, other_ref, live, ((pairs - 1) * core, 1), result, (put(keep_ref), put(send_ref)))
    for source, target in ((keep_mid_ref, keep_ref), (send_mid_ref, send_ref)):
        target[:, pl.ds(2 * (1 - core), inner_rows - 2)] = source[...]


def shards(features, frame_counts, gain_first, conv_first, bias_first, gain_second, conv_second, bias_second):
    frames, rows, side, channels = features.shape
    pairs, half = rows // 2, rows // 2
    held = half // 2 + 1
    tall, cores, blocks = lax.axis_size("ha"), lax.axis_size("wa"), lax.axis_size("tchunk")
    packed, width, tiles = 3 * LANES, 2 * side, CACHE * held
    bf16 = jnp.bfloat16
    vmem = pl.BlockSpec(memory_space=pltpu.VMEM)
    limit = pltpu.CompilerParams(vmem_limit_bytes=20 * 2**20)
    work = 2 * TAPS**3 * channels * channels * width

    def shape(*extent):
        return jax.ShapeDtypeStruct(extent, bf16)

    def cost(flops, fetched):
        return pl.CostEstimate(flops=flops, bytes_accessed=fetched, transcendentals=0)

    slots = pl.pallas_call(
        slots_kernel,
        out_shape=jax.ShapeDtypeStruct((side, packed), jnp.int32),
        out_specs=vmem,
        compiler_params=limit,
        cost_estimate=cost(2**34, 2**20),
    )()
    slots, frame_counts = lax.optimization_barrier((slots, frame_counts))
    tail, mine, theirs, marks = pl.pallas_call(
        prepare_kernel,
        out_shape=(
            shape(tiles + 1, side, packed), shape(frames, held, side, packed),
            shape((CACHE + frames) * held, side, packed), shape(side, packed),
        ),
        in_specs=[pl.BlockSpec(memory_space=pltpu.SMEM), vmem, vmem],
        out_specs=(vmem,) * 4,
        scratch_shapes=[pltpu.VMEM((frames, pairs, side, packed), bf16)],
        compiler_params=limit,
    )(frame_counts, slots, features)

    tail, tail_theirs = joined_tails(tail, theirs[:tiles])
    if blocks > 2:
        theirs = jnp.concatenate([tail_theirs, theirs[tiles:]], axis=0)
    straight, crossed, diagonal, across = [], [], [], []

    def index(block, h, core):
        return (block * tall + h) * cores + core

    for h in range(tall):
        for k in range(blocks - 1):
            for core in range(cores):
                straight.append((index(k, h, core), index(k + 1, h, core)))
                crossed.append((index(k, h, core), index(k + 1, h, 1 - core)))
    for h in range(tall - 1):
        for k in range(blocks):
            lower, upper = index(k, h, 1), index(k, h + 1, 0)
            across += [(lower, upper), (upper, lower)]
            if k + 1 < blocks:
                lower_next, upper_next = index(k + 1, h, 1), index(k + 1, h + 1, 0)
                diagonal += [(lower, upper_next), (upper, lower_next)]
    axes = ("tchunk", "ha", "wa")
    swap = [(0, 1), (1, 0)]
    tail_mine = lax.ppermute(tail, axes, straight)
    tail_other = lax.ppermute(tail_theirs, axes, crossed)
    other = lax.ppermute(theirs, "wa", swap)
    tail_edge, own_edge = pl.pallas_call(
        border_kernel,
        out_shape=(shape(2, CACHE, side, packed), shape(2, frames, side, packed)),
        in_specs=[vmem] * 3,
        out_specs=(vmem, vmem),
        compiler_params=limit,
        cost_estimate=cost(2**34, 2**20),
    )(tail, mine, other)
    own_edge = lax.ppermute(own_edge, axes, across)
    tail_edge = lax.ppermute(tail_edge, axes, diagonal)

    weights = (
        gain_first.reshape(1, channels), conv_first, bias_first.reshape(1, channels),
        gain_second.reshape(1, channels), conv_second, bias_second.reshape(1, channels),
    )
    near, inner, keep, send = pl.pallas_call(
        middle_kernel,
        out_shape=(
            shape(frames + CACHE, 2, width, packed), shape(frames + 2, half, width, packed),
            shape(frames, half - 2, side, channels), shape(frames, half - 2, side, channels),
        ),
        in_specs=[vmem] * 11,
        out_specs=(vmem,) * 4,
        scratch_shapes=[pltpu.VMEM((frames + CACHE, half + 2, width, packed), bf16)],
        compiler_params=limit,
        cost_estimate=cost(work * ((frames + 2) * half + frames * (half - 2)), 8 * 2**20),
    )(marks, tail_mine, tail_other, mine, other, *weights)
    keep, send = pl.pallas_call(
        outer_kernel,
        out_shape=(shape(frames, half, side, channels), shape(frames, half, side, channels)),
        in_specs=[vmem] * 16,
        out_specs=(vmem, vmem),
        scratch_shapes=[
            pltpu.VMEM((frames + CACHE, 4, width, packed), bf16),
            pltpu.VMEM((frames + 2, 4, width, packed), bf16),
        ],
        compiler_params=limit,
        cost_estimate=cost(work * 2 * (2 * frames + 2), 8 * 2**20),
    )(marks, tail_mine, mine, other, tail_edge, own_edge, near, inner, keep, send, *weights)
    got = lax.ppermute(send, "wa", swap)
    upper, lower = halves(lax.axis_index("wa"), keep, got)
    return jnp.concatenate([upper, lower], axis=1)


def solution(mesh):
    return jax.shard_map(
        shards,
        mesh=mesh,
        in_specs=(
            P(("grp", "tchunk"), "ha", "wa", None),
            P(("grp", "tchunk")),
            P(), P(), P(), P(), P(), P(),
        ),
        out_specs=P(("grp", "tchunk"), "ha", "wa", None),
        check_vma=False,
    )
```

```python
import jax
import jax.numpy as jnp
from jax import lax
from jax.experimental import pallas as pl
from jax.experimental.pallas import tpu as pltpu
from jax.sharding import PartitionSpec as P

epsilon = 1e-06
CACHE = 4
TAPS = 3
LANES = 128
PRODUCT = 128


def slots_kernel(slots_ref):
    slots_ref[...] = lax.broadcasted_iota(jnp.int32, slots_ref.shape, 0)


def prepare_kernel(total_ref, slots_ref, raw, tail_ref, mine_ref, theirs_ref, marks_ref, pack):
    frames, rows = raw.shape[:2]
    pairs, held = rows // 2, mine_ref.shape[1]
    core = lax.axis_index("wa")
    total = total_ref[0]
    for frame in range(frames):
        for pair in range(pairs):
            first, second = raw[frame, 2 * pair], raw[frame, 2 * pair + 1]
            packed = jnp.concatenate(
                [first[:, :LANES], second[:, :LANES], first[:, LANES:], second[:, LANES:]], axis=-1
            )
            pack[frame, pair] = packed
    for place, ref in ((core, tail_ref), (1 - core, theirs_ref)):
        for slot in range(CACHE):
            frame = total - CACHE + slot
            value = pack[jnp.maximum(frame, 0), pl.ds(place * (pairs - held), held)]
            ref[slot * held:(slot + 1) * held] = jnp.where(frame >= 0, value, jnp.zeros_like(value))
    for frame in range(frames):
        start = (CACHE + frame) * held
        value = pack[frame, pl.ds(core * (pairs - held), held)]
        mine_ref[frame] = jnp.where(frame < total, value, jnp.zeros_like(value))
        value = pack[frame, pl.ds((1 - core) * (pairs - held), held)]
        theirs_ref[start:start + held] = jnp.where(frame < total, value, jnp.zeros_like(value))
    slot = slots_ref[...]
    tail_ref[CACHE * held] = jnp.where(
        (slot < CACHE) & (total - CACHE + slot >= 0), 1.0, 0.0
    ).astype(tail_ref.dtype)
    marks_ref[...] = jnp.where(slot < total, 1.0, 0.0).astype(marks_ref.dtype)


def joined_tails(mine, other):
    count = lax.axis_size("tchunk")
    if count <= 2:
        return mine, other
    tiles = other.shape[0]
    value = jnp.concatenate([mine, other], axis=0)

    def apart(value):
        return jnp.concatenate([
            value[:tiles].reshape((CACHE, -1) + value.shape[1:]),
            value[tiles + 1:].reshape((CACHE, -1) + value.shape[1:]),
        ], axis=1), value[tiles, :CACHE]

    def pushed(value, held):
        return lax.dynamic_slice_in_dim(jnp.concatenate([value, jnp.zeros_like(value)], axis=0), held, CACHE, 0)

    step = 1
    while step < count - 1:
        early = lax.ppermute(value, "tchunk", [(k, k + step) for k in range(count - step)])
        held = jnp.sum(value[tiles, :CACHE, 0].astype(jnp.int32))
        body, marks = apart(early)
        body, marks = pushed(body, held), pushed(marks, held)
        half = body.shape[1] // 2
        marks = jnp.pad(marks, ((0, value.shape[1] - CACHE), (0, 0)))[None]
        shape = (tiles,) + value.shape[1:]
        value = value + jnp.concatenate([body[:, :half].reshape(shape), marks, body[:, half:].reshape(shape)], axis=0)
        step *= 2
    return value[:tiles + 1], value[tiles + 1:]


def silu(half):
    return half + half * jnp.tanh(half)


def lane_mask():
    return lax.broadcasted_iota(jnp.int32, (1, 1, 1, LANES), 3) < LANES // 2


def gains(gain_ref):
    low, high = 0.5 * gain_ref[:, :LANES], 0.5 * gain_ref[:, LANES:]
    return low.reshape(1, 1, 1, LANES), jnp.concatenate([high, high], axis=-1).reshape(1, 1, 1, LANES)


def rolled(values):
    shape = values.shape
    return pltpu.roll(values.reshape(-1, LANES), LANES // 2, 1).reshape(shape)


def first_rows(left, right, gain_ref, channels):
    raw = jnp.concatenate([left.astype(jnp.float32), right.astype(jnp.float32)], axis=2)
    front, back, high = raw[..., :LANES], raw[..., LANES:2 * LANES], raw[..., 2 * LANES:]
    lower = lane_mask()
    squared = high * high

    def inverse(low, mask):
        total = jnp.sum(low * low + jnp.where(mask, squared, 0.0), axis=-1, keepdims=True)
        return lax.rsqrt(total * (1.0 / channels) + epsilon)

    scale_front, scale_back = inverse(front, lower), inverse(back, jnp.logical_not(lower))
    gain_low, gain_high = gains(gain_ref)
    front = silu(front * scale_front * gain_low)
    back = silu(back * scale_back * gain_low)
    high = silu(high * jnp.where(lower, scale_front, scale_back) * gain_high)
    turned = rolled(high)
    one = [front, jnp.where(lower, high, 0.0), jnp.where(lower, 0.0, turned)]
    two = [back, jnp.where(lower, turned, 0.0), jnp.where(lower, 0.0, high)]
    return [jnp.concatenate([part.astype(jnp.bfloat16) for part in row], axis=-1) for row in (one, two)]


def second_rows(hidden, flag, gain_ref, channels):
    gain = 0.5 * gain_ref[...].reshape(1, 1, 1, channels)
    total = jnp.sum(hidden * hidden, axis=-1, keepdims=True)
    inverse = lax.rsqrt(total * (1.0 / channels) + epsilon) * flag
    values = silu(hidden * inverse * gain)
    rest = jnp.zeros(values.shape[:-1] + (LANES // 2,), jnp.float32)
    high = jnp.concatenate([values[..., LANES:], rest], axis=-1)
    parts = [values[..., :LANES], high, rolled(high)]
    return jnp.concatenate([part.astype(jnp.bfloat16) for part in parts], axis=-1)


def convolved(operand, weights_ref, bias_ref, frame, frames, rows, then):
    step = max(1, PRODUCT // (rows * operand.shape[2]))
    for start in range(0, frames, step):
        count = min(step, frames - start)
        then(start, count, convolved_part(operand, weights_ref, bias_ref, frame + start, count, rows))


def convolved_part(operand, weights_ref, bias_ref, frame, frames, rows):
    width = operand.shape[2]
    channels = weights_ref.shape[-1]
    taps = [(a, i) for a in range(TAPS) for i in range(TAPS)]
    groups = [taps[start:start + 2] for start in range(0, len(taps), 2)]

    def window(tap, part):
        a, i = tap
        value = operand[frame + a:frame + a + frames, i:i + rows, :, part * LANES:(part + 1) * LANES]
        return value.reshape(frames * rows * width, LANES)

    pieces = []
    for group in groups:
        pieces += [window(tap, 0) for tap in group]
        high = window(group[0], 1)
        pieces.append(high + window(group[1], 2) if len(group) > 1 else high)
    left = jnp.concatenate(pieces, axis=-1)
    products = []
    for j in range(TAPS):
        rights = []
        for group in groups:
            held = [weights_ref[a, i, j] for a, i in group]
            rights += [weight[:LANES] for weight in held] + [weight[LANES:] for weight in held]
        rights.append(jnp.zeros((left.shape[1] - sum(r.shape[0] for r in rights), channels), jnp.bfloat16))
        product = jnp.dot(left, jnp.concatenate(rights, axis=0), preferred_element_type=jnp.float32)
        products.append(product.reshape(frames * rows, width, channels))
    column = lax.broadcasted_iota(jnp.int32, (1, width, 1), 1)
    before = jnp.where(column == 0, 0.0, pltpu.roll(products[0], 1, 1))
    after = jnp.where(column == width - 1, 0.0, pltpu.roll(products[2], width - 1, 1))
    result = products[1] + before + after + bias_ref[...].reshape(1, 1, channels)
    return result.reshape(frames, rows, width, channels)


def halves(core, mine, other):
    return jnp.where(core == 0, mine, other), jnp.where(core == 0, other, mine)


def frame_flags(marks, frames):
    values = marks.astype(jnp.float32)
    return [values[k:k + 1, 0:1].reshape(1, 1, 1, 1) for k in frames]


def fill_rows(operand, frame, mine, other, gain_ref, channels):
    left, right = halves(lax.axis_index("wa"), mine, other)
    frames, pairs = mine.shape[:2]
    upper, lower = first_rows(left, right, gain_ref, channels)
    for pair in range(pairs):
        operand[frame:frame + frames, 2 * pair] = upper[:, pair]
        operand[frame:frame + frames, 2 * pair + 1] = lower[:, pair]


def border_kernel(tail_ref, mine_ref, other_ref, tail_edge_ref, own_edge_ref):
    frames, held = mine_ref.shape[:2]
    pair = lax.axis_index("wa") * (held - 1)
    for slot in range(CACHE):
        tail_edge_ref[0, slot] = tail_ref[slot * held + pair]
        tail_edge_ref[1, slot] = other_ref[slot * held + pair]
    for frame in range(frames):
        own_edge_ref[0, frame] = mine_ref[frame, pair]
        own_edge_ref[1, frame] = other_ref[(CACHE + frame) * held + pair]


def finish(mine_ref, other_ref, live, first, pairs, value, targets):
    _, held, side, _ = mine_ref.shape
    frames, channels = value.shape[0], value.shape[-1]
    start, count = pairs
    near, far = halves(lax.axis_index("wa"), value[:, :, :side], value[:, :, side:])
    for mine, value, target in ((True, near, targets[0]), (False, far, targets[1])):
        for frame in range(frames):
            for k in range(count):
                if mine:
                    raw = mine_ref[first + frame, start + k]
                else:
                    raw = other_ref[(CACHE + first + frame) * held + start + k]
                raw = raw.astype(jnp.float32)
                high = raw[:, 2 * LANES:]
                for row, tail in ((0, high), (1, pltpu.roll(high, LANES // 2, 1))):
                    low = raw[:, row * LANES:(row + 1) * LANES]
                    features = jnp.concatenate([low, tail[:, :channels - LANES]], axis=-1)
                    summed = features + value[frame, 2 * k + row]
                    kept = jnp.where(live[first + frame].reshape(1, 1) > 0.5, summed, 0.0)
                    target(first + frame, 2 * k + row, kept.astype(jnp.bfloat16))


def middle_kernel(
    marks_ref, tail_mine_ref, tail_other_ref, mine_ref, other_ref,
    gain1_ref, w1_ref, bias1_ref, gain2_ref, w2_ref, bias2_ref,
    near_ref, inner_ref, keep_ref, send_ref, operand,
):
    core = lax.axis_index("wa")
    frames, pairs, side, packed = mine_ref.shape
    channels = w1_ref.shape[-1]
    rows = 2 * pairs
    tiles = CACHE * pairs
    live = frame_flags(marks_ref[...], range(frames))
    earlier = lax.axis_index("tchunk") > 0

    def unpacked(ref, start, count):
        return ref[start:start + count * pairs].reshape(count, pairs, side, packed)

    def hide(first, count, flags):
        def then(start, part, hidden):
            flag = jnp.concatenate(flags[start:start + part], axis=0)
            inner_ref[first + start:first + start + part] = second_rows(hidden, flag, gain2_ref, channels)

        convolved(operand, w1_ref, bias1_ref, first, count, rows - 2, then)

    @pl.when(earlier)
    def _():
        fill_rows(
            operand, 0, unpacked(tail_mine_ref, 0, CACHE), unpacked(tail_other_ref, 0, CACHE), gain1_ref, channels
        )
        hide(0, 2, frame_flags(tail_mine_ref[tiles], range(CACHE - 2, CACHE)))

    @pl.when(jnp.logical_not(earlier))
    def _():
        operand[0:CACHE] = jnp.zeros((CACHE,) + operand.shape[1:], operand.dtype)
        inner_ref[0:2] = jnp.zeros((2,) + inner_ref.shape[1:], inner_ref.dtype)

    fill_rows(operand, CACHE, mine_ref[...], unpacked(other_ref, tiles, frames), gain1_ref, channels)
    near_ref[...] = operand[:, pl.ds((rows - 2) * core, 2)]
    hide(2, frames, live)

    def put(ref):
        def store(frame, row, value):
            ref[frame, row] = value
        return store

    def then(start, part, result):
        finish(mine_ref, other_ref, live, start, (1, pairs - 2), result, (put(keep_ref), put(send_ref)))

    convolved(inner_ref, w2_ref, bias2_ref, 0, frames, rows - 4, then)


def outer_kernel(
    marks_ref, tail_mine_ref, mine_ref, other_ref, tail_edge_ref, own_edge_ref, near_ref, inner_ref,
    keep_mid_ref, send_mid_ref, gain1_ref, w1_ref, bias1_ref, gain2_ref, w2_ref, bias2_ref,
    keep_ref, send_ref, strip, operand,
):
    core, place = lax.axis_index("wa"), lax.axis_index("ha")
    frames, pairs = mine_ref.shape[:2]
    inner_rows = inner_ref.shape[1]
    channels = w1_ref.shape[-1]
    outward, inward = pl.ds(2 * core, 2), pl.ds(2 * (1 - core), 2)

    for start, ref in ((0, tail_edge_ref), (CACHE, own_edge_ref)):
        left, right = halves(core, ref[1], ref[0])
        upper, lower = first_rows(left[:, None], right[:, None], gain1_ref, channels)
        strip[start:start + ref.shape[1], pl.ds(2 * core, 1)] = upper
        strip[start:start + ref.shape[1], pl.ds(2 * core + 1, 1)] = lower
    strip[:, inward] = near_ref[...]
    inside = jnp.where(core == 0, place > 0, place < lax.axis_size("ha") - 1)
    row = lax.broadcasted_iota(jnp.int32, (1, 2, 1, 1), 1)
    row_flag = jnp.where((row == core) & jnp.logical_not(inside), 0.0, 1.0)
    live = frame_flags(marks_ref[...], range(frames))
    flags = frame_flags(tail_mine_ref[CACHE * pairs], range(CACHE - 2, CACHE)) + live
    operand[:, inward] = inner_ref[:, pl.ds((inner_rows - 2) * core, 2)]

    def hide(start, part, hidden):
        flag = jnp.concatenate(flags[start:start + part], axis=0) * row_flag
        operand[start:start + part, outward] = second_rows(hidden, flag, gain2_ref, channels)

    convolved(strip, w1_ref, bias1_ref, 0, frames + 2, 2, hide)

    def put(ref):
        def store(frame, row, value):
            ref[frame, (inner_rows - 2) * core + row] = value
        return store

    def then(start, part, result):
        finish(mine_ref, other_ref, live, start, ((pairs - 1) * core, 1), result, (put(keep_ref), put(send_ref)))

    convolved(operand, w2_ref, bias2_ref, 0, frames, 2, then)
    for source, target in ((keep_mid_ref, keep_ref), (send_mid_ref, send_ref)):
        target[:, pl.ds(2 * (1 - core), inner_rows - 2)] = source[...]


def shards(features, frame_counts, gain_first, conv_first, bias_first, gain_second, conv_second, bias_second):
    frames, rows, side, channels = features.shape
    pairs, half = rows // 2, rows // 2
    held = half // 2 + 1
    tall, cores, blocks = lax.axis_size("ha"), lax.axis_size("wa"), lax.axis_size("tchunk")
    packed, width, tiles = 3 * LANES, 2 * side, CACHE * held
    bf16 = jnp.bfloat16
    vmem = pl.BlockSpec(memory_space=pltpu.VMEM)
    limit = pltpu.CompilerParams(vmem_limit_bytes=20 * 2**20)
    work = 2 * TAPS**3 * channels * channels * width

    def shape(*extent):
        return jax.ShapeDtypeStruct(extent, bf16)

    def cost(flops, fetched):
        return pl.CostEstimate(flops=flops, bytes_accessed=fetched, transcendentals=0)

    slots = pl.pallas_call(
        slots_kernel,
        out_shape=jax.ShapeDtypeStruct((side, packed), jnp.int32),
        out_specs=vmem,
        compiler_params=limit,
        cost_estimate=cost(2**34, 2**20),
    )()
    slots, frame_counts = lax.optimization_barrier((slots, frame_counts))
    tail, mine, theirs, marks = pl.pallas_call(
        prepare_kernel,
        out_shape=(
            shape(tiles + 1, side, packed), shape(frames, held, side, packed),
            shape((CACHE + frames) * held, side, packed), shape(side, packed),
        ),
        in_specs=[pl.BlockSpec(memory_space=pltpu.SMEM), vmem, vmem],
        out_specs=(vmem,) * 4,
        scratch_shapes=[pltpu.VMEM((frames, pairs, side, packed), bf16)],
        compiler_params=limit,
    )(frame_counts, slots, features)

    tail, tail_theirs = joined_tails(tail, theirs[:tiles])
    if blocks > 2:
        theirs = jnp.concatenate([tail_theirs, theirs[tiles:]], axis=0)
    straight, crossed, diagonal, across = [], [], [], []

    def index(block, h, core):
        return (block * tall + h) * cores + core

    for h in range(tall):
        for k in range(blocks - 1):
            for core in range(cores):
                straight.append((index(k, h, core), index(k + 1, h, core)))
                crossed.append((index(k, h, core), index(k + 1, h, 1 - core)))
    for h in range(tall - 1):
        for k in range(blocks):
            lower, upper = index(k, h, 1), index(k, h + 1, 0)
            across += [(lower, upper), (upper, lower)]
            if k + 1 < blocks:
                lower_next, upper_next = index(k + 1, h, 1), index(k + 1, h + 1, 0)
                diagonal += [(lower, upper_next), (upper, lower_next)]
    axes = ("tchunk", "ha", "wa")
    swap = [(0, 1), (1, 0)]
    tail_mine = lax.ppermute(tail, axes, straight)
    tail_other = lax.ppermute(tail_theirs, axes, crossed)
    other = lax.ppermute(theirs, "wa", swap)
    tail_edge, own_edge = pl.pallas_call(
        border_kernel,
        out_shape=(shape(2, CACHE, side, packed), shape(2, frames, side, packed)),
        in_specs=[vmem] * 3,
        out_specs=(vmem, vmem),
        compiler_params=limit,
        cost_estimate=cost(2**34, 2**20),
    )(tail, mine, other)
    own_edge = lax.ppermute(own_edge, axes, across)
    tail_edge = lax.ppermute(tail_edge, axes, diagonal)

    weights = (
        gain_first.reshape(1, channels), conv_first, bias_first.reshape(1, channels),
        gain_second.reshape(1, channels), conv_second, bias_second.reshape(1, channels),
    )
    near, inner, keep, send = pl.pallas_call(
        middle_kernel,
        out_shape=(
            shape(frames + CACHE, 2, width, packed), shape(frames + 2, half, width, packed),
            shape(frames, half - 2, side, channels), shape(frames, half - 2, side, channels),
        ),
        in_specs=[vmem] * 11,
        out_specs=(vmem,) * 4,
        scratch_shapes=[pltpu.VMEM((frames + CACHE, half + 2, width, packed), bf16)],
        compiler_params=limit,
        cost_estimate=cost(work * ((frames + 2) * half + frames * (half - 2)), 8 * 2**20),
    )(marks, tail_mine, tail_other, mine, other, *weights)
    keep, send = pl.pallas_call(
        outer_kernel,
        out_shape=(shape(frames, half, side, channels), shape(frames, half, side, channels)),
        in_specs=[vmem] * 16,
        out_specs=(vmem, vmem),
        scratch_shapes=[
            pltpu.VMEM((frames + CACHE, 4, width, packed), bf16),
            pltpu.VMEM((frames + 2, 4, width, packed), bf16),
        ],
        compiler_params=limit,
        cost_estimate=cost(work * 2 * (2 * frames + 2), 8 * 2**20),
    )(marks, tail_mine, mine, other, tail_edge, own_edge, near, inner, keep, send, *weights)
    got = lax.ppermute(send, "wa", swap)
    upper, lower = halves(lax.axis_index("wa"), keep, got)
    return jnp.concatenate([upper, lower], axis=1)


def solution(mesh):
    return jax.shard_map(
        shards,
        mesh=mesh,
        in_specs=(
            P(("grp", "tchunk"), "ha", "wa", None),
            P(("grp", "tchunk")),
            P(), P(), P(), P(), P(), P(),
        ),
        out_specs=P(("grp", "tchunk"), "ha", "wa", None),
        check_vma=False,
    )
```

```python
import jax
import jax.numpy as jnp
from jax import lax
from jax.experimental import pallas as pl
from jax.experimental.pallas import tpu as pltpu
from jax.sharding import PartitionSpec as P

epsilon = 1e-06
CACHE = 4
TAPS = 3
LANES = 128
PRODUCT = 64


def slots_kernel(slots_ref):
    slots_ref[...] = lax.broadcasted_iota(jnp.int32, slots_ref.shape, 0)


def prepare_kernel(total_ref, slots_ref, raw, tail_ref, mine_ref, theirs_ref, marks_ref, pack):
    frames, rows = raw.shape[:2]
    pairs, held = rows // 2, mine_ref.shape[1]
    core = lax.axis_index("wa")
    total = total_ref[0]
    for frame in range(frames):
        for pair in range(pairs):
            first, second = raw[frame, 2 * pair], raw[frame, 2 * pair + 1]
            packed = jnp.concatenate(
                [first[:, :LANES], second[:, :LANES], first[:, LANES:], second[:, LANES:]], axis=-1
            )
            pack[frame, pair] = packed
    for place, ref in ((core, tail_ref), (1 - core, theirs_ref)):
        for slot in range(CACHE):
            frame = total - CACHE + slot
            value = pack[jnp.maximum(frame, 0), pl.ds(place * (pairs - held), held)]
            ref[slot * held:(slot + 1) * held] = jnp.where(frame >= 0, value, jnp.zeros_like(value))
    for frame in range(frames):
        start = (CACHE + frame) * held
        value = pack[frame, pl.ds(core * (pairs - held), held)]
        mine_ref[frame] = jnp.where(frame < total, value, jnp.zeros_like(value))
        value = pack[frame, pl.ds((1 - core) * (pairs - held), held)]
        theirs_ref[start:start + held] = jnp.where(frame < total, value, jnp.zeros_like(value))
    slot = slots_ref[...]
    tail_ref[CACHE * held] = jnp.where(
        (slot < CACHE) & (total - CACHE + slot >= 0), 1.0, 0.0
    ).astype(tail_ref.dtype)
    marks_ref[...] = jnp.where(slot < total, 1.0, 0.0).astype(marks_ref.dtype)


def joined_tails(mine, other):
    count = lax.axis_size("tchunk")
    if count <= 2:
        return mine, other
    tiles = other.shape[0]
    value = jnp.concatenate([mine, other], axis=0)

    def apart(value):
        return jnp.concatenate([
            value[:tiles].reshape((CACHE, -1) + value.shape[1:]),
            value[tiles + 1:].reshape((CACHE, -1) + value.shape[1:]),
        ], axis=1), value[tiles, :CACHE]

    def pushed(value, held):
        return lax.dynamic_slice_in_dim(jnp.concatenate([value, jnp.zeros_like(value)], axis=0), held, CACHE, 0)

    step = 1
    while step < count - 1:
        early = lax.ppermute(value, "tchunk", [(k, k + step) for k in range(count - step)])
        held = jnp.sum(value[tiles, :CACHE, 0].astype(jnp.int32))
        body, marks = apart(early)
        body, marks = pushed(body, held), pushed(marks, held)
        half = body.shape[1] // 2
        marks = jnp.pad(marks, ((0, value.shape[1] - CACHE), (0, 0)))[None]
        shape = (tiles,) + value.shape[1:]
        value = value + jnp.concatenate([body[:, :half].reshape(shape), marks, body[:, half:].reshape(shape)], axis=0)
        step *= 2
    return value[:tiles + 1], value[tiles + 1:]


def silu(half):
    return half + half * jnp.tanh(half)


def lane_mask():
    return lax.broadcasted_iota(jnp.int32, (1, 1, 1, LANES), 3) < LANES // 2


def gains(gain_ref):
    low, high = 0.5 * gain_ref[:, :LANES], 0.5 * gain_ref[:, LANES:]
    return low.reshape(1, 1, 1, LANES), jnp.concatenate([high, high], axis=-1).reshape(1, 1, 1, LANES)


def rolled(values):
    shape = values.shape
    return pltpu.roll(values.reshape(-1, LANES), LANES // 2, 1).reshape(shape)


def first_rows(left, right, gain_ref, channels):
    raw = jnp.concatenate([left.astype(jnp.float32), right.astype(jnp.float32)], axis=2)
    front, back, high = raw[..., :LANES], raw[..., LANES:2 * LANES], raw[..., 2 * LANES:]
    lower = lane_mask()
    squared = high * high

    def inverse(low, mask):
        total = jnp.sum(low * low + jnp.where(mask, squared, 0.0), axis=-1, keepdims=True)
        return lax.rsqrt(total * (1.0 / channels) + epsilon)

    scale_front, scale_back = inverse(front, lower), inverse(back, jnp.logical_not(lower))
    gain_low, gain_high = gains(gain_ref)
    front = silu(front * scale_front * gain_low)
    back = silu(back * scale_back * gain_low)
    high = silu(high * jnp.where(lower, scale_front, scale_back) * gain_high)
    turned = rolled(high)
    one = [front, jnp.where(lower, high, 0.0), jnp.where(lower, 0.0, turned)]
    two = [back, jnp.where(lower, turned, 0.0), jnp.where(lower, 0.0, high)]
    return [jnp.concatenate([part.astype(jnp.bfloat16) for part in row], axis=-1) for row in (one, two)]


def second_rows(hidden, flag, gain_ref, channels):
    gain = 0.5 * gain_ref[...].reshape(1, 1, 1, channels)
    total = jnp.sum(hidden * hidden, axis=-1, keepdims=True)
    inverse = lax.rsqrt(total * (1.0 / channels) + epsilon) * flag
    values = silu(hidden * inverse * gain)
    rest = jnp.zeros(values.shape[:-1] + (LANES // 2,), jnp.float32)
    high = jnp.concatenate([values[..., LANES:], rest], axis=-1)
    parts = [values[..., :LANES], high, rolled(high)]
    return jnp.concatenate([part.astype(jnp.bfloat16) for part in parts], axis=-1)


def convolved(operand, weights_ref, bias_ref, frame, frames, rows, then):
    step = max(1, PRODUCT // (rows * operand.shape[2]))
    for start in range(0, frames, step):
        count = min(step, frames - start)
        then(start, count, convolved_part(operand, weights_ref, bias_ref, frame + start, count, rows))


def convolved_part(operand, weights_ref, bias_ref, frame, frames, rows):
    width = operand.shape[2]
    channels = weights_ref.shape[-1]
    taps = [(a, i) for a in range(TAPS) for i in range(TAPS)]
    groups = [taps[start:start + 2] for start in range(0, len(taps), 2)]

    def window(tap, part):
        a, i = tap
        value = operand[frame + a:frame + a + frames, i:i + rows, :, part * LANES:(part + 1) * LANES]
        return value.reshape(frames * rows * width, LANES)

    pieces = []
    for group in groups:
        pieces += [window(tap, 0) for tap in group]
        high = window(group[0], 1)
        pieces.append(high + window(group[1], 2) if len(group) > 1 else high)
    left = jnp.concatenate(pieces, axis=-1)
    products = []
    for j in range(TAPS):
        rights = []
        for group in groups:
            held = [weights_ref[a, i, j] for a, i in group]
            rights += [weight[:LANES] for weight in held] + [weight[LANES:] for weight in held]
        rights.append(jnp.zeros((left.shape[1] - sum(r.shape[0] for r in rights), channels), jnp.bfloat16))
        product = jnp.dot(left, jnp.concatenate(rights, axis=0), preferred_element_type=jnp.float32)
        products.append(product.reshape(frames * rows, width, channels))
    column = lax.broadcasted_iota(jnp.int32, (1, width, 1), 1)
    before = jnp.where(column == 0, 0.0, pltpu.roll(products[0], 1, 1))
    after = jnp.where(column == width - 1, 0.0, pltpu.roll(products[2], width - 1, 1))
    result = products[1] + before + after + bias_ref[...].reshape(1, 1, channels)
    return result.reshape(frames, rows, width, channels)


def halves(core, mine, other):
    return jnp.where(core == 0, mine, other), jnp.where(core == 0, other, mine)


def frame_flags(marks, frames):
    values = marks.astype(jnp.float32)
    return [values[k:k + 1, 0:1].reshape(1, 1, 1, 1) for k in frames]


def fill_rows(operand, frame, mine, other, gain_ref, channels):
    left, right = halves(lax.axis_index("wa"), mine, other)
    frames, pairs = mine.shape[:2]
    upper, lower = first_rows(left, right, gain_ref, channels)
    for pair in range(pairs):
        operand[frame:frame + frames, 2 * pair] = upper[:, pair]
        operand[frame:frame + frames, 2 * pair + 1] = lower[:, pair]


def border_kernel(tail_ref, mine_ref, other_ref, tail_edge_ref, own_edge_ref):
    frames, held = mine_ref.shape[:2]
    pair = lax.axis_index("wa") * (held - 1)
    for slot in range(CACHE):
        tail_edge_ref[0, slot] = tail_ref[slot * held + pair]
        tail_edge_ref[1, slot] = other_ref[slot * held + pair]
    for frame in range(frames):
        own_edge_ref[0, frame] = mine_ref[frame, pair]
        own_edge_ref[1, frame] = other_ref[(CACHE + frame) * held + pair]


def finish(mine_ref, other_ref, live, first, pairs, value, targets):
    _, held, side, _ = mine_ref.shape
    frames, channels = value.shape[0], value.shape[-1]
    start, count = pairs
    near, far = halves(lax.axis_index("wa"), value[:, :, :side], value[:, :, side:])
    for mine, value, target in ((True, near, targets[0]), (False, far, targets[1])):
        for frame in range(frames):
            for k in range(count):
                if mine:
                    raw = mine_ref[first + frame, start + k]
                else:
                    raw = other_ref[(CACHE + first + frame) * held + start + k]
                raw = raw.astype(jnp.float32)
                high = raw[:, 2 * LANES:]
                for row, tail in ((0, high), (1, pltpu.roll(high, LANES // 2, 1))):
                    low = raw[:, row * LANES:(row + 1) * LANES]
                    features = jnp.concatenate([low, tail[:, :channels - LANES]], axis=-1)
                    summed = features + value[frame, 2 * k + row]
                    kept = jnp.where(live[first + frame].reshape(1, 1) > 0.5, summed, 0.0)
                    target(first + frame, 2 * k + row, kept.astype(jnp.bfloat16))


def middle_kernel(
    marks_ref, tail_mine_ref, tail_other_ref, mine_ref, other_ref,
    gain1_ref, w1_ref, bias1_ref, gain2_ref, w2_ref, bias2_ref,
    near_ref, inner_ref, keep_ref, send_ref, operand,
):
    core = lax.axis_index("wa")
    frames, pairs, side, packed = mine_ref.shape
    channels = w1_ref.shape[-1]
    rows = 2 * pairs
    tiles = CACHE * pairs
    live = frame_flags(marks_ref[...], range(frames))
    earlier = lax.axis_index("tchunk") > 0

    def unpacked(ref, start, count):
        return ref[start:start + count * pairs].reshape(count, pairs, side, packed)

    def hide(first, count, flags):
        def then(start, part, hidden):
            flag = jnp.concatenate(flags[start:start + part], axis=0)
            inner_ref[first + start:first + start + part] = second_rows(hidden, flag, gain2_ref, channels)

        convolved(operand, w1_ref, bias1_ref, first, count, rows - 2, then)

    @pl.when(earlier)
    def _():
        fill_rows(
            operand, 0, unpacked(tail_mine_ref, 0, CACHE), unpacked(tail_other_ref, 0, CACHE), gain1_ref, channels
        )
        hide(0, 2, frame_flags(tail_mine_ref[tiles], range(CACHE - 2, CACHE)))

    @pl.when(jnp.logical_not(earlier))
    def _():
        operand[0:CACHE] = jnp.zeros((CACHE,) + operand.shape[1:], operand.dtype)
        inner_ref[0:2] = jnp.zeros((2,) + inner_ref.shape[1:], inner_ref.dtype)

    fill_rows(operand, CACHE, mine_ref[...], unpacked(other_ref, tiles, frames), gain1_ref, channels)
    near_ref[...] = operand[:, pl.ds((rows - 2) * core, 2)]
    hide(2, frames, live)

    def put(ref):
        def store(frame, row, value):
            ref[frame, row] = value
        return store

    def then(start, part, result):
        finish(mine_ref, other_ref, live, start, (1, pairs - 2), result, (put(keep_ref), put(send_ref)))

    convolved(inner_ref, w2_ref, bias2_ref, 0, frames, rows - 4, then)


def outer_kernel(
    marks_ref, tail_mine_ref, mine_ref, other_ref, tail_edge_ref, own_edge_ref, near_ref, inner_ref,
    keep_mid_ref, send_mid_ref, gain1_ref, w1_ref, bias1_ref, gain2_ref, w2_ref, bias2_ref,
    keep_ref, send_ref, strip, operand,
):
    core, place = lax.axis_index("wa"), lax.axis_index("ha")
    frames, pairs = mine_ref.shape[:2]
    inner_rows = inner_ref.shape[1]
    channels = w1_ref.shape[-1]
    outward, inward = pl.ds(2 * core, 2), pl.ds(2 * (1 - core), 2)

    for start, ref in ((0, tail_edge_ref), (CACHE, own_edge_ref)):
        left, right = halves(core, ref[1], ref[0])
        upper, lower = first_rows(left[:, None], right[:, None], gain1_ref, channels)
        strip[start:start + ref.shape[1], pl.ds(2 * core, 1)] = upper
        strip[start:start + ref.shape[1], pl.ds(2 * core + 1, 1)] = lower
    strip[:, inward] = near_ref[...]
    inside = jnp.where(core == 0, place > 0, place < lax.axis_size("ha") - 1)
    row = lax.broadcasted_iota(jnp.int32, (1, 2, 1, 1), 1)
    row_flag = jnp.where((row == core) & jnp.logical_not(inside), 0.0, 1.0)
    live = frame_flags(marks_ref[...], range(frames))
    flags = frame_flags(tail_mine_ref[CACHE * pairs], range(CACHE - 2, CACHE)) + live
    operand[:, inward] = inner_ref[:, pl.ds((inner_rows - 2) * core, 2)]

    def hide(start, part, hidden):
        flag = jnp.concatenate(flags[start:start + part], axis=0) * row_flag
        operand[start:start + part, outward] = second_rows(hidden, flag, gain2_ref, channels)

    convolved(strip, w1_ref, bias1_ref, 0, frames + 2, 2, hide)

    def put(ref):
        def store(frame, row, value):
            ref[frame, (inner_rows - 2) * core + row] = value
        return store

    def then(start, part, result):
        finish(mine_ref, other_ref, live, start, ((pairs - 1) * core, 1), result, (put(keep_ref), put(send_ref)))

    convolved(operand, w2_ref, bias2_ref, 0, frames, 2, then)
    for source, target in ((keep_mid_ref, keep_ref), (send_mid_ref, send_ref)):
        target[:, pl.ds(2 * (1 - core), inner_rows - 2)] = source[...]


def shards(features, frame_counts, gain_first, conv_first, bias_first, gain_second, conv_second, bias_second):
    frames, rows, side, channels = features.shape
    pairs, half = rows // 2, rows // 2
    held = half // 2 + 1
    tall, cores, blocks = lax.axis_size("ha"), lax.axis_size("wa"), lax.axis_size("tchunk")
    packed, width, tiles = 3 * LANES, 2 * side, CACHE * held
    bf16 = jnp.bfloat16
    vmem = pl.BlockSpec(memory_space=pltpu.VMEM)
    limit = pltpu.CompilerParams(vmem_limit_bytes=20 * 2**20)
    work = 2 * TAPS**3 * channels * channels * width

    def shape(*extent):
        return jax.ShapeDtypeStruct(extent, bf16)

    def cost(flops, fetched):
        return pl.CostEstimate(flops=flops, bytes_accessed=fetched, transcendentals=0)

    slots = pl.pallas_call(
        slots_kernel,
        out_shape=jax.ShapeDtypeStruct((side, packed), jnp.int32),
        out_specs=vmem,
        compiler_params=limit,
        cost_estimate=cost(2**34, 2**20),
    )()
    slots, frame_counts = lax.optimization_barrier((slots, frame_counts))
    tail, mine, theirs, marks = pl.pallas_call(
        prepare_kernel,
        out_shape=(
            shape(tiles + 1, side, packed), shape(frames, held, side, packed),
            shape((CACHE + frames) * held, side, packed), shape(side, packed),
        ),
        in_specs=[pl.BlockSpec(memory_space=pltpu.SMEM), vmem, vmem],
        out_specs=(vmem,) * 4,
        scratch_shapes=[pltpu.VMEM((frames, pairs, side, packed), bf16)],
        compiler_params=limit,
    )(frame_counts, slots, features)

    tail, tail_theirs = joined_tails(tail, theirs[:tiles])
    if blocks > 2:
        theirs = jnp.concatenate([tail_theirs, theirs[tiles:]], axis=0)
    straight, crossed, diagonal, across = [], [], [], []

    def index(block, h, core):
        return (block * tall + h) * cores + core

    for h in range(tall):
        for k in range(blocks - 1):
            for core in range(cores):
                straight.append((index(k, h, core), index(k + 1, h, core)))
                crossed.append((index(k, h, core), index(k + 1, h, 1 - core)))
    for h in range(tall - 1):
        for k in range(blocks):
            lower, upper = index(k, h, 1), index(k, h + 1, 0)
            across += [(lower, upper), (upper, lower)]
            if k + 1 < blocks:
                lower_next, upper_next = index(k + 1, h, 1), index(k + 1, h + 1, 0)
                diagonal += [(lower, upper_next), (upper, lower_next)]
    axes = ("tchunk", "ha", "wa")
    swap = [(0, 1), (1, 0)]
    tail_mine = lax.ppermute(tail, axes, straight)
    tail_other = lax.ppermute(tail_theirs, axes, crossed)
    other = lax.ppermute(theirs, "wa", swap)
    tail_edge, own_edge = pl.pallas_call(
        border_kernel,
        out_shape=(shape(2, CACHE, side, packed), shape(2, frames, side, packed)),
        in_specs=[vmem] * 3,
        out_specs=(vmem, vmem),
        compiler_params=limit,
        cost_estimate=cost(2**34, 2**20),
    )(tail, mine, other)
    own_edge = lax.ppermute(own_edge, axes, across)
    tail_edge = lax.ppermute(tail_edge, axes, diagonal)

    weights = (
        gain_first.reshape(1, channels), conv_first, bias_first.reshape(1, channels),
        gain_second.reshape(1, channels), conv_second, bias_second.reshape(1, channels),
    )
    near, inner, keep, send = pl.pallas_call(
        middle_kernel,
        out_shape=(
            shape(frames + CACHE, 2, width, packed), shape(frames + 2, half, width, packed),
            shape(frames, half - 2, side, channels), shape(frames, half - 2, side, channels),
        ),
        in_specs=[vmem] * 11,
        out_specs=(vmem,) * 4,
        scratch_shapes=[pltpu.VMEM((frames + CACHE, half + 2, width, packed), bf16)],
        compiler_params=limit,
        cost_estimate=cost(work * ((frames + 2) * half + frames * (half - 2)), 8 * 2**20),
    )(marks, tail_mine, tail_other, mine, other, *weights)
    keep, send = pl.pallas_call(
        outer_kernel,
        out_shape=(shape(frames, half, side, channels), shape(frames, half, side, channels)),
        in_specs=[vmem] * 16,
        out_specs=(vmem, vmem),
        scratch_shapes=[
            pltpu.VMEM((frames + CACHE, 4, width, packed), bf16),
            pltpu.VMEM((frames + 2, 4, width, packed), bf16),
        ],
        compiler_params=limit,
        cost_estimate=cost(work * 2 * (2 * frames + 2), 8 * 2**20),
    )(marks, tail_mine, mine, other, tail_edge, own_edge, near, inner, keep, send, *weights)
    got = lax.ppermute(send, "wa", swap)
    upper, lower = halves(lax.axis_index("wa"), keep, got)
    return jnp.concatenate([upper, lower], axis=1)


def solution(mesh):
    return jax.shard_map(
        shards,
        mesh=mesh,
        in_specs=(
            P(("grp", "tchunk"), "ha", "wa", None),
            P(("grp", "tchunk")),
            P(), P(), P(), P(), P(), P(),
        ),
        out_specs=P(("grp", "tchunk"), "ha", "wa", None),
        check_vma=False,
    )
```

```python
import jax
import jax.numpy as jnp
from jax import lax
from jax.experimental import pallas as pl
from jax.experimental.pallas import tpu as pltpu
from jax.sharding import PartitionSpec as P

epsilon = 1e-06
CACHE = 4
TAPS = 3
LANES = 128
PRODUCT = 192


def slots_kernel(slots_ref):
    slots_ref[...] = lax.broadcasted_iota(jnp.int32, slots_ref.shape, 0)


def prepare_kernel(total_ref, slots_ref, raw, tail_ref, mine_ref, theirs_ref, marks_ref, pack):
    frames, rows = raw.shape[:2]
    pairs, held = rows // 2, mine_ref.shape[1]
    core = lax.axis_index("wa")
    total = total_ref[0]
    for frame in range(frames):
        for pair in range(pairs):
            first, second = raw[frame, 2 * pair], raw[frame, 2 * pair + 1]
            packed = jnp.concatenate(
                [first[:, :LANES], second[:, :LANES], first[:, LANES:], second[:, LANES:]], axis=-1
            )
            pack[frame, pair] = packed
    for place, ref in ((core, tail_ref), (1 - core, theirs_ref)):
        for slot in range(CACHE):
            frame = total - CACHE + slot
            value = pack[jnp.maximum(frame, 0), pl.ds(place * (pairs - held), held)]
            ref[slot * held:(slot + 1) * held] = jnp.where(frame >= 0, value, jnp.zeros_like(value))
    for frame in range(frames):
        start = (CACHE + frame) * held
        value = pack[frame, pl.ds(core * (pairs - held), held)]
        mine_ref[frame] = jnp.where(frame < total, value, jnp.zeros_like(value))
        value = pack[frame, pl.ds((1 - core) * (pairs - held), held)]
        theirs_ref[start:start + held] = jnp.where(frame < total, value, jnp.zeros_like(value))
    slot = slots_ref[...]
    tail_ref[CACHE * held] = jnp.where(
        (slot < CACHE) & (total - CACHE + slot >= 0), 1.0, 0.0
    ).astype(tail_ref.dtype)
    marks_ref[...] = jnp.where(slot < total, 1.0, 0.0).astype(marks_ref.dtype)


def joined_tails(mine, other):
    count = lax.axis_size("tchunk")
    if count <= 2:
        return mine, other
    tiles = other.shape[0]
    value = jnp.concatenate([mine, other], axis=0)

    def apart(value):
        return jnp.concatenate([
            value[:tiles].reshape((CACHE, -1) + value.shape[1:]),
            value[tiles + 1:].reshape((CACHE, -1) + value.shape[1:]),
        ], axis=1), value[tiles, :CACHE]

    def pushed(value, held):
        return lax.dynamic_slice_in_dim(jnp.concatenate([value, jnp.zeros_like(value)], axis=0), held, CACHE, 0)

    step = 1
    while step < count - 1:
        early = lax.ppermute(value, "tchunk", [(k, k + step) for k in range(count - step)])
        held = jnp.sum(value[tiles, :CACHE, 0].astype(jnp.int32))
        body, marks = apart(early)
        body, marks = pushed(body, held), pushed(marks, held)
        half = body.shape[1] // 2
        marks = jnp.pad(marks, ((0, value.shape[1] - CACHE), (0, 0)))[None]
        shape = (tiles,) + value.shape[1:]
        value = value + jnp.concatenate([body[:, :half].reshape(shape), marks, body[:, half:].reshape(shape)], axis=0)
        step *= 2
    return value[:tiles + 1], value[tiles + 1:]


def silu(half):
    return half + half * jnp.tanh(half)


def lane_mask():
    return lax.broadcasted_iota(jnp.int32, (1, 1, 1, LANES), 3) < LANES // 2


def gains(gain_ref):
    low, high = 0.5 * gain_ref[:, :LANES], 0.5 * gain_ref[:, LANES:]
    return low.reshape(1, 1, 1, LANES), jnp.concatenate([high, high], axis=-1).reshape(1, 1, 1, LANES)


def rolled(values):
    shape = values.shape
    return pltpu.roll(values.reshape(-1, LANES), LANES // 2, 1).reshape(shape)


def first_rows(left, right, gain_ref, channels):
    raw = jnp.concatenate([left.astype(jnp.float32), right.astype(jnp.float32)], axis=2)
    front, back, high = raw[..., :LANES], raw[..., LANES:2 * LANES], raw[..., 2 * LANES:]
    lower = lane_mask()
    squared = high * high

    def inverse(low, mask):
        total = jnp.sum(low * low + jnp.where(mask, squared, 0.0), axis=-1, keepdims=True)
        return lax.rsqrt(total * (1.0 / channels) + epsilon)

    scale_front, scale_back = inverse(front, lower), inverse(back, jnp.logical_not(lower))
    gain_low, gain_high = gains(gain_ref)
    front = silu(front * scale_front * gain_low)
    back = silu(back * scale_back * gain_low)
    high = silu(high * jnp.where(lower, scale_front, scale_back) * gain_high)
    turned = rolled(high)
    one = [front, jnp.where(lower, high, 0.0), jnp.where(lower, 0.0, turned)]
    two = [back, jnp.where(lower, turned, 0.0), jnp.where(lower, 0.0, high)]
    return [jnp.concatenate([part.astype(jnp.bfloat16) for part in row], axis=-1) for row in (one, two)]


def second_rows(hidden, flag, gain_ref, channels):
    gain = 0.5 * gain_ref[...].reshape(1, 1, 1, channels)
    total = jnp.sum(hidden * hidden, axis=-1, keepdims=True)
    inverse = lax.rsqrt(total * (1.0 / channels) + epsilon) * flag
    values = silu(hidden * inverse * gain)
    rest = jnp.zeros(values.shape[:-1] + (LANES // 2,), jnp.float32)
    high = jnp.concatenate([values[..., LANES:], rest], axis=-1)
    parts = [values[..., :LANES], high, rolled(high)]
    return jnp.concatenate([part.astype(jnp.bfloat16) for part in parts], axis=-1)


def convolved(operand, weights_ref, bias_ref, frame, frames, rows, then):
    products = -(-frames * rows * operand.shape[2] // PRODUCT)
    step = -(-frames // products)
    for start in range(0, frames, step):
        count = min(step, frames - start)
        then(start, count, convolved_part(operand, weights_ref, bias_ref, frame + start, count, rows))


def convolved_part(operand, weights_ref, bias_ref, frame, frames, rows):
    width = operand.shape[2]
    channels = weights_ref.shape[-1]
    taps = [(a, i) for a in range(TAPS) for i in range(TAPS)]
    groups = [taps[start:start + 2] for start in range(0, len(taps), 2)]

    def window(tap, part):
        a, i = tap
        value = operand[frame + a:frame + a + frames, i:i + rows, :, part * LANES:(part + 1) * LANES]
        return value.reshape(frames * rows * width, LANES)

    pieces = []
    for group in groups:
        pieces += [window(tap, 0) for tap in group]
        high = window(group[0], 1)
        pieces.append(high + window(group[1], 2) if len(group) > 1 else high)
    left = jnp.concatenate(pieces, axis=-1)
    products = []
    for j in range(TAPS):
        rights = []
        for group in groups:
            held = [weights_ref[a, i, j] for a, i in group]
            rights += [weight[:LANES] for weight in held] + [weight[LANES:] for weight in held]
        rights.append(jnp.zeros((left.shape[1] - sum(r.shape[0] for r in rights), channels), jnp.bfloat16))
        product = jnp.dot(left, jnp.concatenate(rights, axis=0), preferred_element_type=jnp.float32)
        products.append(product.reshape(frames * rows, width, channels))
    column = lax.broadcasted_iota(jnp.int32, (1, width, 1), 1)
    before = jnp.where(column == 0, 0.0, pltpu.roll(products[0], 1, 1))
    after = jnp.where(column == width - 1, 0.0, pltpu.roll(products[2], width - 1, 1))
    result = products[1] + before + after + bias_ref[...].reshape(1, 1, channels)
    return result.reshape(frames, rows, width, channels)


def halves(core, mine, other):
    return jnp.where(core == 0, mine, other), jnp.where(core == 0, other, mine)


def frame_flags(marks, frames):
    values = marks.astype(jnp.float32)
    return [values[k:k + 1, 0:1].reshape(1, 1, 1, 1) for k in frames]


def fill_rows(operand, frame, mine, other, gain_ref, channels):
    left, right = halves(lax.axis_index("wa"), mine, other)
    frames, pairs = mine.shape[:2]
    upper, lower = first_rows(left, right, gain_ref, channels)
    for pair in range(pairs):
        operand[frame:frame + frames, 2 * pair] = upper[:, pair]
        operand[frame:frame + frames, 2 * pair + 1] = lower[:, pair]


def border_kernel(tail_ref, mine_ref, other_ref, tail_edge_ref, own_edge_ref):
    frames, held = mine_ref.shape[:2]
    pair = lax.axis_index("wa") * (held - 1)
    for slot in range(CACHE):
        tail_edge_ref[0, slot] = tail_ref[slot * held + pair]
        tail_edge_ref[1, slot] = other_ref[slot * held + pair]
    for frame in range(frames):
        own_edge_ref[0, frame] = mine_ref[frame, pair]
        own_edge_ref[1, frame] = other_ref[(CACHE + frame) * held + pair]


def finish(mine_ref, other_ref, live, first, pairs, value, targets):
    _, held, side, _ = mine_ref.shape
    frames, channels = value.shape[0], value.shape[-1]
    start, count = pairs
    near, far = halves(lax.axis_index("wa"), value[:, :, :side], value[:, :, side:])
    for mine, value, target in ((True, near, targets[0]), (False, far, targets[1])):
        for frame in range(frames):
            for k in range(count):
                if mine:
                    raw = mine_ref[first + frame, start + k]
                else:
                    raw = other_ref[(CACHE + first + frame) * held + start + k]
                raw = raw.astype(jnp.float32)
                high = raw[:, 2 * LANES:]
                for row, tail in ((0, high), (1, pltpu.roll(high, LANES // 2, 1))):
                    low = raw[:, row * LANES:(row + 1) * LANES]
                    features = jnp.concatenate([low, tail[:, :channels - LANES]], axis=-1)
                    summed = features + value[frame, 2 * k + row]
                    kept = jnp.where(live[first + frame].reshape(1, 1) > 0.5, summed, 0.0)
                    target(first + frame, 2 * k + row, kept.astype(jnp.bfloat16))


def middle_kernel(
    marks_ref, tail_mine_ref, tail_other_ref, mine_ref, other_ref,
    gain1_ref, w1_ref, bias1_ref, gain2_ref, w2_ref, bias2_ref,
    near_ref, inner_ref, keep_ref, send_ref, operand,
):
    core = lax.axis_index("wa")
    frames, pairs, side, packed = mine_ref.shape
    channels = w1_ref.shape[-1]
    rows = 2 * pairs
    tiles = CACHE * pairs
    live = frame_flags(marks_ref[...], range(frames))
    earlier = lax.axis_index("tchunk") > 0

    def unpacked(ref, start, count):
        return ref[start:start + count * pairs].reshape(count, pairs, side, packed)

    def hide(first, count, flags):
        def then(start, part, hidden):
            flag = jnp.concatenate(flags[start:start + part], axis=0)
            inner_ref[first + start:first + start + part] = second_rows(hidden, flag, gain2_ref, channels)

        convolved(operand, w1_ref, bias1_ref, first, count, rows - 2, then)

    @pl.when(earlier)
    def _():
        fill_rows(
            operand, 0, unpacked(tail_mine_ref, 0, CACHE), unpacked(tail_other_ref, 0, CACHE), gain1_ref, channels
        )
        hide(0, 2, frame_flags(tail_mine_ref[tiles], range(CACHE - 2, CACHE)))

    @pl.when(jnp.logical_not(earlier))
    def _():
        operand[0:CACHE] = jnp.zeros((CACHE,) + operand.shape[1:], operand.dtype)
        inner_ref[0:2] = jnp.zeros((2,) + inner_ref.shape[1:], inner_ref.dtype)

    fill_rows(operand, CACHE, mine_ref[...], unpacked(other_ref, tiles, frames), gain1_ref, channels)
    near_ref[...] = operand[:, pl.ds((rows - 2) * core, 2)]
    hide(2, frames, live)

    def put(ref):
        def store(frame, row, value):
            ref[frame, row] = value
        return store

    def then(start, part, result):
        finish(mine_ref, other_ref, live, start, (1, pairs - 2), result, (put(keep_ref), put(send_ref)))

    convolved(inner_ref, w2_ref, bias2_ref, 0, frames, rows - 4, then)


def outer_kernel(
    marks_ref, tail_mine_ref, mine_ref, other_ref, tail_edge_ref, own_edge_ref, near_ref, inner_ref,
    keep_mid_ref, send_mid_ref, gain1_ref, w1_ref, bias1_ref, gain2_ref, w2_ref, bias2_ref,
    keep_ref, send_ref, strip, operand,
):
    core, place = lax.axis_index("wa"), lax.axis_index("ha")
    frames, pairs = mine_ref.shape[:2]
    inner_rows = inner_ref.shape[1]
    channels = w1_ref.shape[-1]
    outward, inward = pl.ds(2 * core, 2), pl.ds(2 * (1 - core), 2)

    for start, ref in ((0, tail_edge_ref), (CACHE, own_edge_ref)):
        left, right = halves(core, ref[1], ref[0])
        upper, lower = first_rows(left[:, None], right[:, None], gain1_ref, channels)
        strip[start:start + ref.shape[1], pl.ds(2 * core, 1)] = upper
        strip[start:start + ref.shape[1], pl.ds(2 * core + 1, 1)] = lower
    strip[:, inward] = near_ref[...]
    inside = jnp.where(core == 0, place > 0, place < lax.axis_size("ha") - 1)
    row = lax.broadcasted_iota(jnp.int32, (1, 2, 1, 1), 1)
    row_flag = jnp.where((row == core) & jnp.logical_not(inside), 0.0, 1.0)
    live = frame_flags(marks_ref[...], range(frames))
    flags = frame_flags(tail_mine_ref[CACHE * pairs], range(CACHE - 2, CACHE)) + live
    operand[:, inward] = inner_ref[:, pl.ds((inner_rows - 2) * core, 2)]

    def hide(start, part, hidden):
        flag = jnp.concatenate(flags[start:start + part], axis=0) * row_flag
        operand[start:start + part, outward] = second_rows(hidden, flag, gain2_ref, channels)

    convolved(strip, w1_ref, bias1_ref, 0, frames + 2, 2, hide)

    def put(ref):
        def store(frame, row, value):
            ref[frame, (inner_rows - 2) * core + row] = value
        return store

    def then(start, part, result):
        finish(mine_ref, other_ref, live, start, ((pairs - 1) * core, 1), result, (put(keep_ref), put(send_ref)))

    convolved(operand, w2_ref, bias2_ref, 0, frames, 2, then)
    for source, target in ((keep_mid_ref, keep_ref), (send_mid_ref, send_ref)):
        target[:, pl.ds(2 * (1 - core), inner_rows - 2)] = source[...]


def shards(features, frame_counts, gain_first, conv_first, bias_first, gain_second, conv_second, bias_second):
    frames, rows, side, channels = features.shape
    pairs, half = rows // 2, rows // 2
    held = half // 2 + 1
    tall, cores, blocks = lax.axis_size("ha"), lax.axis_size("wa"), lax.axis_size("tchunk")
    packed, width, tiles = 3 * LANES, 2 * side, CACHE * held
    bf16 = jnp.bfloat16
    vmem = pl.BlockSpec(memory_space=pltpu.VMEM)
    limit = pltpu.CompilerParams(vmem_limit_bytes=20 * 2**20)
    work = 2 * TAPS**3 * channels * channels * width

    def shape(*extent):
        return jax.ShapeDtypeStruct(extent, bf16)

    def cost(flops, fetched):
        return pl.CostEstimate(flops=flops, bytes_accessed=fetched, transcendentals=0)

    slots = pl.pallas_call(
        slots_kernel,
        out_shape=jax.ShapeDtypeStruct((side, packed), jnp.int32),
        out_specs=vmem,
        compiler_params=limit,
        cost_estimate=cost(2**34, 2**20),
    )()
    slots, frame_counts = lax.optimization_barrier((slots, frame_counts))
    tail, mine, theirs, marks = pl.pallas_call(
        prepare_kernel,
        out_shape=(
            shape(tiles + 1, side, packed), shape(frames, held, side, packed),
            shape((CACHE + frames) * held, side, packed), shape(side, packed),
        ),
        in_specs=[pl.BlockSpec(memory_space=pltpu.SMEM), vmem, vmem],
        out_specs=(vmem,) * 4,
        scratch_shapes=[pltpu.VMEM((frames, pairs, side, packed), bf16)],
        compiler_params=limit,
    )(frame_counts, slots, features)

    tail, tail_theirs = joined_tails(tail, theirs[:tiles])
    if blocks > 2:
        theirs = jnp.concatenate([tail_theirs, theirs[tiles:]], axis=0)
    straight, crossed, diagonal, across = [], [], [], []

    def index(block, h, core):
        return (block * tall + h) * cores + core

    for h in range(tall):
        for k in range(blocks - 1):
            for core in range(cores):
                straight.append((index(k, h, core), index(k + 1, h, core)))
                crossed.append((index(k, h, core), index(k + 1, h, 1 - core)))
    for h in range(tall - 1):
        for k in range(blocks):
            lower, upper = index(k, h, 1), index(k, h + 1, 0)
            across += [(lower, upper), (upper, lower)]
            if k + 1 < blocks:
                lower_next, upper_next = index(k + 1, h, 1), index(k + 1, h + 1, 0)
                diagonal += [(lower, upper_next), (upper, lower_next)]
    axes = ("tchunk", "ha", "wa")
    swap = [(0, 1), (1, 0)]
    tail_mine = lax.ppermute(tail, axes, straight)
    tail_other = lax.ppermute(tail_theirs, axes, crossed)
    other = lax.ppermute(theirs, "wa", swap)
    tail_edge, own_edge = pl.pallas_call(
        border_kernel,
        out_shape=(shape(2, CACHE, side, packed), shape(2, frames, side, packed)),
        in_specs=[vmem] * 3,
        out_specs=(vmem, vmem),
        compiler_params=limit,
        cost_estimate=cost(2**34, 2**20),
    )(tail, mine, other)
    own_edge = lax.ppermute(own_edge, axes, across)
    tail_edge = lax.ppermute(tail_edge, axes, diagonal)

    weights = (
        gain_first.reshape(1, channels), conv_first, bias_first.reshape(1, channels),
        gain_second.reshape(1, channels), conv_second, bias_second.reshape(1, channels),
    )
    near, inner, keep, send = pl.pallas_call(
        middle_kernel,
        out_shape=(
            shape(frames + CACHE, 2, width, packed), shape(frames + 2, half, width, packed),
            shape(frames, half - 2, side, channels), shape(frames, half - 2, side, channels),
        ),
        in_specs=[vmem] * 11,
        out_specs=(vmem,) * 4,
        scratch_shapes=[pltpu.VMEM((frames + CACHE, half + 2, width, packed), bf16)],
        compiler_params=limit,
        cost_estimate=cost(work * ((frames + 2) * half + frames * (half - 2)), 8 * 2**20),
    )(marks, tail_mine, tail_other, mine, other, *weights)
    keep, send = pl.pallas_call(
        outer_kernel,
        out_shape=(shape(frames, half, side, channels), shape(frames, half, side, channels)),
        in_specs=[vmem] * 16,
        out_specs=(vmem, vmem),
        scratch_shapes=[
            pltpu.VMEM((frames + CACHE, 4, width, packed), bf16),
            pltpu.VMEM((frames + 2, 4, width, packed), bf16),
        ],
        compiler_params=limit,
        cost_estimate=cost(work * 2 * (2 * frames + 2), 8 * 2**20),
    )(marks, tail_mine, mine, other, tail_edge, own_edge, near, inner, keep, send, *weights)
    got = lax.ppermute(send, "wa", swap)
    upper, lower = halves(lax.axis_index("wa"), keep, got)
    return jnp.concatenate([upper, lower], axis=1)


def solution(mesh):
    return jax.shard_map(
        shards,
        mesh=mesh,
        in_specs=(
            P(("grp", "tchunk"), "ha", "wa", None),
            P(("grp", "tchunk")),
            P(), P(), P(), P(), P(), P(),
        ),
        out_specs=P(("grp", "tchunk"), "ha", "wa", None),
        check_vma=False,
    )
```

```python
import jax
import jax.numpy as jnp
from jax import lax
from jax.experimental import pallas as pl
from jax.experimental.pallas import tpu as pltpu
from jax.sharding import PartitionSpec as P

epsilon = 1e-06
CACHE = 4
TAPS = 3
LANES = 128
PRODUCT = 160


def slots_kernel(slots_ref):
    slots_ref[...] = lax.broadcasted_iota(jnp.int32, slots_ref.shape, 0)


def prepare_kernel(total_ref, slots_ref, raw, tail_ref, mine_ref, theirs_ref, marks_ref, pack):
    frames, rows = raw.shape[:2]
    pairs, held = rows // 2, mine_ref.shape[1]
    core = lax.axis_index("wa")
    total = total_ref[0]
    for frame in range(frames):
        for pair in range(pairs):
            first, second = raw[frame, 2 * pair], raw[frame, 2 * pair + 1]
            packed = jnp.concatenate(
                [first[:, :LANES], second[:, :LANES], first[:, LANES:], second[:, LANES:]], axis=-1
            )
            pack[frame, pair] = packed
    for place, ref in ((core, tail_ref), (1 - core, theirs_ref)):
        for slot in range(CACHE):
            frame = total - CACHE + slot
            value = pack[jnp.maximum(frame, 0), pl.ds(place * (pairs - held), held)]
            ref[slot * held:(slot + 1) * held] = jnp.where(frame >= 0, value, jnp.zeros_like(value))
    for frame in range(frames):
        start = (CACHE + frame) * held
        value = pack[frame, pl.ds(core * (pairs - held), held)]
        mine_ref[frame] = jnp.where(frame < total, value, jnp.zeros_like(value))
        value = pack[frame, pl.ds((1 - core) * (pairs - held), held)]
        theirs_ref[start:start + held] = jnp.where(frame < total, value, jnp.zeros_like(value))
    slot = slots_ref[...]
    tail_ref[CACHE * held] = jnp.where(
        (slot < CACHE) & (total - CACHE + slot >= 0), 1.0, 0.0
    ).astype(tail_ref.dtype)
    marks_ref[...] = jnp.where(slot < total, 1.0, 0.0).astype(marks_ref.dtype)


def joined_tails(mine, other):
    count = lax.axis_size("tchunk")
    if count <= 2:
        return mine, other
    tiles = other.shape[0]
    value = jnp.concatenate([mine, other], axis=0)

    def apart(value):
        return jnp.concatenate([
            value[:tiles].reshape((CACHE, -1) + value.shape[1:]),
            value[tiles + 1:].reshape((CACHE, -1) + value.shape[1:]),
        ], axis=1), value[tiles, :CACHE]

    def pushed(value, held):
        return lax.dynamic_slice_in_dim(jnp.concatenate([value, jnp.zeros_like(value)], axis=0), held, CACHE, 0)

    step = 1
    while step < count - 1:
        early = lax.ppermute(value, "tchunk", [(k, k + step) for k in range(count - step)])
        held = jnp.sum(value[tiles, :CACHE, 0].astype(jnp.int32))
        body, marks = apart(early)
        body, marks = pushed(body, held), pushed(marks, held)
        half = body.shape[1] // 2
        marks = jnp.pad(marks, ((0, value.shape[1] - CACHE), (0, 0)))[None]
        shape = (tiles,) + value.shape[1:]
        value = value + jnp.concatenate([body[:, :half].reshape(shape), marks, body[:, half:].reshape(shape)], axis=0)
        step *= 2
    return value[:tiles + 1], value[tiles + 1:]


def silu(half):
    return half + half * jnp.tanh(half)


def lane_mask():
    return lax.broadcasted_iota(jnp.int32, (1, 1, 1, LANES), 3) < LANES // 2


def gains(gain_ref):
    low, high = 0.5 * gain_ref[:, :LANES], 0.5 * gain_ref[:, LANES:]
    return low.reshape(1, 1, 1, LANES), jnp.concatenate([high, high], axis=-1).reshape(1, 1, 1, LANES)


def rolled(values):
    shape = values.shape
    return pltpu.roll(values.reshape(-1, LANES), LANES // 2, 1).reshape(shape)


def shifted(values):
    width = values.shape[2]
    column = lax.broadcasted_iota(jnp.int32, (1, 1, width, 1), 2)
    before = jnp.where(column == 0, 0.0, pltpu.roll(values, 1, 2))
    after = jnp.where(column == width - 1, 0.0, pltpu.roll(values, width - 1, 2))
    return before, values, after


def first_rows(left, right, gain_ref, channels):
    raw = jnp.concatenate([left.astype(jnp.float32), right.astype(jnp.float32)], axis=2)
    front, back, high = raw[..., :LANES], raw[..., LANES:2 * LANES], raw[..., 2 * LANES:]
    lower = lane_mask()
    squared = high * high

    def inverse(low, mask):
        total = jnp.sum(low * low + jnp.where(mask, squared, 0.0), axis=-1, keepdims=True)
        return lax.rsqrt(total * (1.0 / channels) + epsilon)

    scale_front, scale_back = inverse(front, lower), inverse(back, jnp.logical_not(lower))
    gain_low, gain_high = gains(gain_ref)
    front = silu(front * scale_front * gain_low)
    back = silu(back * scale_back * gain_low)
    high = silu(high * jnp.where(lower, scale_front, scale_back) * gain_high)
    one, two = [], []
    for front, back, high in zip(shifted(front), shifted(back), shifted(high)):
        turned = rolled(high)
        one += [front, jnp.where(lower, high, 0.0), jnp.where(lower, 0.0, turned)]
        two += [back, jnp.where(lower, turned, 0.0), jnp.where(lower, 0.0, high)]
    return [jnp.concatenate([part.astype(jnp.bfloat16) for part in row], axis=-1) for row in (one, two)]


def second_rows(hidden, flag, gain_ref, channels):
    gain = 0.5 * gain_ref[...].reshape(1, 1, 1, channels)
    total = jnp.sum(hidden * hidden, axis=-1, keepdims=True)
    inverse = lax.rsqrt(total * (1.0 / channels) + epsilon) * flag
    values = silu(hidden * inverse * gain)
    rest = jnp.zeros(values.shape[:-1] + (LANES // 2,), jnp.float32)
    high = jnp.concatenate([values[..., LANES:], rest], axis=-1)
    parts = []
    for low, high in zip(shifted(values[..., :LANES]), shifted(high)):
        parts += [low, high, rolled(high)]
    return jnp.concatenate([part.astype(jnp.bfloat16) for part in parts], axis=-1)


def convolved(operand, weights_ref, bias_ref, frame, frames, rows, then):
    products = -(-frames * rows * operand.shape[2] // PRODUCT)
    step = -(-frames // products)
    for start in range(0, frames, step):
        count = min(step, frames - start)
        then(start, count, convolved_part(operand, weights_ref, bias_ref, frame + start, count, rows))


def convolved_part(operand, weights_ref, bias_ref, frame, frames, rows):
    width = operand.shape[2]
    channels = weights_ref.shape[-1]
    taps = [(a, i, j) for a in range(TAPS) for i in range(TAPS) for j in range(TAPS)]
    lefts, rights = [], []

    def window(tap, part):
        a, i, j = tap
        lane = (3 * j + part) * LANES
        value = operand[frame + a:frame + a + frames, i:i + rows, :, lane:lane + LANES]
        return value.reshape(frames * rows * width, LANES)

    for start in range(0, len(taps), 2):
        group = taps[start:start + 2]
        lefts += [window(tap, 0) for tap in group]
        high = window(group[0], 1)
        lefts.append(high + window(group[1], 2) if len(group) > 1 else high)
        held = [weights_ref[a, i, j] for a, i, j in group]
        rights += [weight[:LANES] for weight in held] + [weight[LANES:] for weight in held]
    left = jnp.concatenate(lefts, axis=-1)
    rights.append(jnp.zeros((left.shape[1] - sum(r.shape[0] for r in rights), channels), jnp.bfloat16))
    result = jnp.dot(left, jnp.concatenate(rights, axis=0), preferred_element_type=jnp.float32)
    return (result + bias_ref[...]).reshape(frames, rows, width, channels)


def halves(core, mine, other):
    return jnp.where(core == 0, mine, other), jnp.where(core == 0, other, mine)


def frame_flags(marks, frames):
    values = marks.astype(jnp.float32)
    return [values[k:k + 1, 0:1].reshape(1, 1, 1, 1) for k in frames]


def fill_rows(operand, frame, mine, other, gain_ref, channels):
    left, right = halves(lax.axis_index("wa"), mine, other)
    frames, pairs = mine.shape[:2]
    upper, lower = first_rows(left, right, gain_ref, channels)
    for pair in range(pairs):
        operand[frame:frame + frames, 2 * pair] = upper[:, pair]
        operand[frame:frame + frames, 2 * pair + 1] = lower[:, pair]


def border_kernel(tail_ref, mine_ref, other_ref, tail_edge_ref, own_edge_ref):
    frames, held = mine_ref.shape[:2]
    pair = lax.axis_index("wa") * (held - 1)
    for slot in range(CACHE):
        tail_edge_ref[0, slot] = tail_ref[slot * held + pair]
        tail_edge_ref[1, slot] = other_ref[slot * held + pair]
    for frame in range(frames):
        own_edge_ref[0, frame] = mine_ref[frame, pair]
        own_edge_ref[1, frame] = other_ref[(CACHE + frame) * held + pair]


def finish(mine_ref, other_ref, live, first, pairs, value, targets):
    _, held, side, _ = mine_ref.shape
    frames, channels = value.shape[0], value.shape[-1]
    start, count = pairs
    near, far = halves(lax.axis_index("wa"), value[:, :, :side], value[:, :, side:])
    for mine, value, target in ((True, near, targets[0]), (False, far, targets[1])):
        for frame in range(frames):
            for k in range(count):
                if mine:
                    raw = mine_ref[first + frame, start + k]
                else:
                    raw = other_ref[(CACHE + first + frame) * held + start + k]
                raw = raw.astype(jnp.float32)
                high = raw[:, 2 * LANES:]
                for row, tail in ((0, high), (1, pltpu.roll(high, LANES // 2, 1))):
                    low = raw[:, row * LANES:(row + 1) * LANES]
                    features = jnp.concatenate([low, tail[:, :channels - LANES]], axis=-1)
                    summed = features + value[frame, 2 * k + row]
                    kept = jnp.where(live[first + frame].reshape(1, 1) > 0.5, summed, 0.0)
                    target(first + frame, 2 * k + row, kept.astype(jnp.bfloat16))


def middle_kernel(
    marks_ref, tail_mine_ref, tail_other_ref, mine_ref, other_ref,
    gain1_ref, w1_ref, bias1_ref, gain2_ref, w2_ref, bias2_ref,
    near_ref, inner_ref, keep_ref, send_ref, operand,
):
    core = lax.axis_index("wa")
    frames, pairs, side, packed = mine_ref.shape
    channels = w1_ref.shape[-1]
    rows = 2 * pairs
    tiles = CACHE * pairs
    live = frame_flags(marks_ref[...], range(frames))
    earlier = lax.axis_index("tchunk") > 0

    def unpacked(ref, start, count):
        return ref[start:start + count * pairs].reshape(count, pairs, side, packed)

    def hide(first, count, flags):
        def then(start, part, hidden):
            flag = jnp.concatenate(flags[start:start + part], axis=0)
            inner_ref[first + start:first + start + part] = second_rows(hidden, flag, gain2_ref, channels)

        convolved(operand, w1_ref, bias1_ref, first, count, rows - 2, then)

    @pl.when(earlier)
    def _():
        fill_rows(
            operand, 0, unpacked(tail_mine_ref, 0, CACHE), unpacked(tail_other_ref, 0, CACHE), gain1_ref, channels
        )
        hide(0, 2, frame_flags(tail_mine_ref[tiles], range(CACHE - 2, CACHE)))

    @pl.when(jnp.logical_not(earlier))
    def _():
        operand[0:CACHE] = jnp.zeros((CACHE,) + operand.shape[1:], operand.dtype)
        inner_ref[0:2] = jnp.zeros((2,) + inner_ref.shape[1:], inner_ref.dtype)

    fill_rows(operand, CACHE, mine_ref[...], unpacked(other_ref, tiles, frames), gain1_ref, channels)
    near_ref[...] = operand[:, pl.ds((rows - 2) * core, 2)]
    hide(2, frames, live)

    def put(ref):
        def store(frame, row, value):
            ref[frame, row] = value
        return store

    def then(start, part, result):
        finish(mine_ref, other_ref, live, start, (1, pairs - 2), result, (put(keep_ref), put(send_ref)))

    convolved(inner_ref, w2_ref, bias2_ref, 0, frames, rows - 4, then)


def outer_kernel(
    marks_ref, tail_mine_ref, mine_ref, other_ref, tail_edge_ref, own_edge_ref, near_ref, inner_ref,
    keep_mid_ref, send_mid_ref, gain1_ref, w1_ref, bias1_ref, gain2_ref, w2_ref, bias2_ref,
    keep_ref, send_ref, strip, operand,
):
    core, place = lax.axis_index("wa"), lax.axis_index("ha")
    frames, pairs = mine_ref.shape[:2]
    inner_rows = inner_ref.shape[1]
    channels = w1_ref.shape[-1]
    outward, inward = pl.ds(2 * core, 2), pl.ds(2 * (1 - core), 2)

    for start, ref in ((0, tail_edge_ref), (CACHE, own_edge_ref)):
        left, right = halves(core, ref[1], ref[0])
        upper, lower = first_rows(left[:, None], right[:, None], gain1_ref, channels)
        strip[start:start + ref.shape[1], pl.ds(2 * core, 1)] = upper
        strip[start:start + ref.shape[1], pl.ds(2 * core + 1, 1)] = lower
    strip[:, inward] = near_ref[...]
    inside = jnp.where(core == 0, place > 0, place < lax.axis_size("ha") - 1)
    row = lax.broadcasted_iota(jnp.int32, (1, 2, 1, 1), 1)
    row_flag = jnp.where((row == core) & jnp.logical_not(inside), 0.0, 1.0)
    live = frame_flags(marks_ref[...], range(frames))
    flags = frame_flags(tail_mine_ref[CACHE * pairs], range(CACHE - 2, CACHE)) + live
    operand[:, inward] = inner_ref[:, pl.ds((inner_rows - 2) * core, 2)]

    def hide(start, part, hidden):
        flag = jnp.concatenate(flags[start:start + part], axis=0) * row_flag
        operand[start:start + part, outward] = second_rows(hidden, flag, gain2_ref, channels)

    convolved(strip, w1_ref, bias1_ref, 0, frames + 2, 2, hide)

    def put(ref):
        def store(frame, row, value):
            ref[frame, (inner_rows - 2) * core + row] = value
        return store

    def then(start, part, result):
        finish(mine_ref, other_ref, live, start, ((pairs - 1) * core, 1), result, (put(keep_ref), put(send_ref)))

    convolved(operand, w2_ref, bias2_ref, 0, frames, 2, then)
    for source, target in ((keep_mid_ref, keep_ref), (send_mid_ref, send_ref)):
        target[:, pl.ds(2 * (1 - core), inner_rows - 2)] = source[...]


def place_kernel(keep_ref, got_ref, result_ref, arrived):
    core, half = lax.axis_index("wa"), keep_ref.shape[1]
    copies = [
        pltpu.make_async_copy(keep_ref, result_ref.at[:, pl.ds(half * core, half)], arrived.at[0]),
        pltpu.make_async_copy(got_ref, result_ref.at[:, pl.ds(half * (1 - core), half)], arrived.at[1]),
    ]
    for copy in copies:
        copy.start()
    for copy in copies:
        copy.wait()


def shards(features, frame_counts, gain_first, conv_first, bias_first, gain_second, conv_second, bias_second):
    frames, rows, side, channels = features.shape
    pairs, half = rows // 2, rows // 2
    held = half // 2 + 1
    tall, cores, blocks = lax.axis_size("ha"), lax.axis_size("wa"), lax.axis_size("tchunk")
    packed, width, tiles = 3 * LANES, 2 * side, CACHE * held
    deep = TAPS * packed
    bf16 = jnp.bfloat16
    vmem = pl.BlockSpec(memory_space=pltpu.VMEM)
    limit = pltpu.CompilerParams(vmem_limit_bytes=20 * 2**20)
    work = 2 * TAPS**3 * channels * channels * width

    def shape(*extent):
        return jax.ShapeDtypeStruct(extent, bf16)

    def cost(flops, fetched):
        return pl.CostEstimate(flops=flops, bytes_accessed=fetched, transcendentals=0)

    slots = pl.pallas_call(
        slots_kernel,
        out_shape=jax.ShapeDtypeStruct((side, packed), jnp.int32),
        out_specs=vmem,
        compiler_params=limit,
        cost_estimate=cost(2**34, 2**20),
    )()
    slots, frame_counts = lax.optimization_barrier((slots, frame_counts))
    tail, mine, theirs, marks = pl.pallas_call(
        prepare_kernel,
        out_shape=(
            shape(tiles + 1, side, packed), shape(frames, held, side, packed),
            shape((CACHE + frames) * held, side, packed), shape(side, packed),
        ),
        in_specs=[pl.BlockSpec(memory_space=pltpu.SMEM), vmem, vmem],
        out_specs=(vmem,) * 4,
        scratch_shapes=[pltpu.VMEM((frames, pairs, side, packed), bf16)],
        compiler_params=limit,
    )(frame_counts, slots, features)

    tail, tail_theirs = joined_tails(tail, theirs[:tiles])
    if blocks > 2:
        theirs = jnp.concatenate([tail_theirs, theirs[tiles:]], axis=0)
    straight, crossed, diagonal, across = [], [], [], []

    def index(block, h, core):
        return (block * tall + h) * cores + core

    for h in range(tall):
        for k in range(blocks - 1):
            for core in range(cores):
                straight.append((index(k, h, core), index(k + 1, h, core)))
                crossed.append((index(k, h, core), index(k + 1, h, 1 - core)))
    for h in range(tall - 1):
        for k in range(blocks):
            lower, upper = index(k, h, 1), index(k, h + 1, 0)
            across += [(lower, upper), (upper, lower)]
            if k + 1 < blocks:
                lower_next, upper_next = index(k + 1, h, 1), index(k + 1, h + 1, 0)
                diagonal += [(lower, upper_next), (upper, lower_next)]
    axes = ("tchunk", "ha", "wa")
    swap = [(0, 1), (1, 0)]
    tail_mine = lax.ppermute(tail, axes, straight)
    tail_other = lax.ppermute(tail_theirs, axes, crossed)
    other = lax.ppermute(theirs, "wa", swap)
    tail_edge, own_edge = pl.pallas_call(
        border_kernel,
        out_shape=(shape(2, CACHE, side, packed), shape(2, frames, side, packed)),
        in_specs=[vmem] * 3,
        out_specs=(vmem, vmem),
        compiler_params=limit,
        cost_estimate=cost(2**34, 2**20),
    )(tail, mine, other)
    own_edge = lax.ppermute(own_edge, axes, across)
    tail_edge = lax.ppermute(tail_edge, axes, diagonal)

    weights = (
        gain_first.reshape(1, channels), conv_first, bias_first.reshape(1, channels),
        gain_second.reshape(1, channels), conv_second, bias_second.reshape(1, channels),
    )
    near, inner, keep, send = pl.pallas_call(
        middle_kernel,
        out_shape=(
            shape(frames + CACHE, 2, width, deep), shape(frames + 2, half, width, deep),
            shape(frames, half - 2, side, channels), shape(frames, half - 2, side, channels),
        ),
        in_specs=[vmem] * 11,
        out_specs=(vmem,) * 4,
        scratch_shapes=[pltpu.VMEM((frames + CACHE, half + 2, width, deep), bf16)],
        compiler_params=limit,
        cost_estimate=cost(work * ((frames + 2) * half + frames * (half - 2)), 8 * 2**20),
    )(marks, tail_mine, tail_other, mine, other, *weights)
    keep, send = pl.pallas_call(
        outer_kernel,
        out_shape=(shape(frames, half, side, channels), shape(frames, half, side, channels)),
        in_specs=[vmem] * 16,
        out_specs=(vmem, vmem),
        scratch_shapes=[
            pltpu.VMEM((frames + CACHE, 4, width, deep), bf16),
            pltpu.VMEM((frames + 2, 4, width, deep), bf16),
        ],
        compiler_params=limit,
        cost_estimate=cost(work * 2 * (2 * frames + 2), 8 * 2**20),
    )(marks, tail_mine, mine, other, tail_edge, own_edge, near, inner, keep, send, *weights)
    got = lax.ppermute(send, "wa", swap)
    return pl.pallas_call(
        place_kernel,
        out_shape=shape(*features.shape),
        in_specs=[vmem, vmem],
        out_specs=pl.BlockSpec(memory_space=pltpu.HBM),
        scratch_shapes=[pltpu.SemaphoreType.DMA((2,))],
        compiler_params=limit,
    )(keep, got)


def solution(mesh):
    return jax.shard_map(
        shards,
        mesh=mesh,
        in_specs=(
            P(("grp", "tchunk"), "ha", "wa", None),
            P(("grp", "tchunk")),
            P(), P(), P(), P(), P(), P(),
        ),
        out_specs=P(("grp", "tchunk"), "ha", "wa", None),
        check_vma=False,
    )
```

```python
import jax
import jax.numpy as jnp
from jax import lax
from jax.experimental import pallas as pl
from jax.experimental.pallas import tpu as pltpu
from jax.sharding import PartitionSpec as P

epsilon = 1e-06
CACHE = 4
TAPS = 3
LANES = 128
PRODUCT = 160


def slots_kernel(slots_ref):
    slots_ref[...] = lax.broadcasted_iota(jnp.int32, slots_ref.shape, 0)


def prepare_kernel(total_ref, slots_ref, raw, tail_ref, mine_ref, theirs_ref, marks_ref, pack):
    frames, rows = raw.shape[:2]
    pairs, held = rows // 2, mine_ref.shape[1]
    core = lax.axis_index("wa")
    total = total_ref[0]
    for frame in range(frames):
        for pair in range(pairs):
            first, second = raw[frame, 2 * pair], raw[frame, 2 * pair + 1]
            packed = jnp.concatenate(
                [first[:, :LANES], second[:, :LANES], first[:, LANES:], second[:, LANES:]], axis=-1
            )
            pack[frame, pair] = packed
    for place, ref in ((core, tail_ref), (1 - core, theirs_ref)):
        for slot in range(CACHE):
            frame = total - CACHE + slot
            value = pack[jnp.maximum(frame, 0), pl.ds(place * (pairs - held), held)]
            ref[slot * held:(slot + 1) * held] = jnp.where(frame >= 0, value, jnp.zeros_like(value))
    for frame in range(frames):
        start = (CACHE + frame) * held
        value = pack[frame, pl.ds(core * (pairs - held), held)]
        mine_ref[frame] = jnp.where(frame < total, value, jnp.zeros_like(value))
        value = pack[frame, pl.ds((1 - core) * (pairs - held), held)]
        theirs_ref[start:start + held] = jnp.where(frame < total, value, jnp.zeros_like(value))
    slot = slots_ref[...]
    tail_ref[CACHE * held] = jnp.where(
        (slot < CACHE) & (total - CACHE + slot >= 0), 1.0, 0.0
    ).astype(tail_ref.dtype)
    marks_ref[...] = jnp.where(slot < total, 1.0, 0.0).astype(marks_ref.dtype)


def joined_tails(mine, other):
    count = lax.axis_size("tchunk")
    if count <= 2:
        return mine, other
    tiles = other.shape[0]
    value = jnp.concatenate([mine, other], axis=0)

    def apart(value):
        return jnp.concatenate([
            value[:tiles].reshape((CACHE, -1) + value.shape[1:]),
            value[tiles + 1:].reshape((CACHE, -1) + value.shape[1:]),
        ], axis=1), value[tiles, :CACHE]

    def pushed(value, held):
        return lax.dynamic_slice_in_dim(jnp.concatenate([value, jnp.zeros_like(value)], axis=0), held, CACHE, 0)

    step = 1
    while step < count - 1:
        early = lax.ppermute(value, "tchunk", [(k, k + step) for k in range(count - step)])
        held = jnp.sum(value[tiles, :CACHE, 0].astype(jnp.int32))
        body, marks = apart(early)
        body, marks = pushed(body, held), pushed(marks, held)
        half = body.shape[1] // 2
        marks = jnp.pad(marks, ((0, value.shape[1] - CACHE), (0, 0)))[None]
        shape = (tiles,) + value.shape[1:]
        value = value + jnp.concatenate([body[:, :half].reshape(shape), marks, body[:, half:].reshape(shape)], axis=0)
        step *= 2
    return value[:tiles + 1], value[tiles + 1:]


def silu(half):
    return half + half * jnp.tanh(half)


def lane_mask():
    return lax.broadcasted_iota(jnp.int32, (1, 1, 1, LANES), 3) < LANES // 2


def gains(gain_ref):
    low, high = 0.5 * gain_ref[:, :LANES], 0.5 * gain_ref[:, LANES:]
    return low.reshape(1, 1, 1, LANES), jnp.concatenate([high, high], axis=-1).reshape(1, 1, 1, LANES)


def rolled(values):
    shape = values.shape
    return pltpu.roll(values.reshape(-1, LANES), LANES // 2, 1).reshape(shape)


def first_rows(left, right, gain_ref, channels):
    raw = jnp.concatenate([left.astype(jnp.float32), right.astype(jnp.float32)], axis=2)
    front, back, high = raw[..., :LANES], raw[..., LANES:2 * LANES], raw[..., 2 * LANES:]
    lower = lane_mask()
    squared = high * high

    def inverse(low, mask):
        total = jnp.sum(low * low + jnp.where(mask, squared, 0.0), axis=-1, keepdims=True)
        return lax.rsqrt(total * (1.0 / channels) + epsilon)

    scale_front, scale_back = inverse(front, lower), inverse(back, jnp.logical_not(lower))
    gain_low, gain_high = gains(gain_ref)
    front = silu(front * scale_front * gain_low)
    back = silu(back * scale_back * gain_low)
    high = silu(high * jnp.where(lower, scale_front, scale_back) * gain_high)
    turned = rolled(high)
    one = [front, jnp.where(lower, high, 0.0), jnp.where(lower, 0.0, turned)]
    two = [back, jnp.where(lower, turned, 0.0), jnp.where(lower, 0.0, high)]
    return [[part.astype(jnp.bfloat16) for part in row] for row in (one, two)]


def second_rows(hidden, flag, gain_ref, channels):
    gain = 0.5 * gain_ref[...].reshape(1, 1, 1, channels)
    total = jnp.sum(hidden * hidden, axis=-1, keepdims=True)
    inverse = lax.rsqrt(total * (1.0 / channels) + epsilon) * flag
    values = silu(hidden * inverse * gain)
    rest = jnp.zeros(values.shape[:-1] + (LANES // 2,), jnp.float32)
    high = jnp.concatenate([values[..., LANES:], rest], axis=-1)
    parts = [values[..., :LANES], high, rolled(high)]
    return jnp.stack([part.astype(jnp.bfloat16) for part in parts])


def convolved(operand, weights_ref, bias_ref, frame, frames, rows, then):
    products = -(-frames * rows * operand.shape[3] // PRODUCT)
    step = -(-frames // products)
    for start in range(0, frames, step):
        count = min(step, frames - start)
        then(start, count, convolved_part(operand, weights_ref, bias_ref, frame + start, count, rows))


def convolved_part(operand, weights_ref, bias_ref, frame, frames, rows):
    width = operand.shape[3]
    channels = weights_ref.shape[-1]
    taps = [(a, i) for a in range(TAPS) for i in range(TAPS)]
    groups = [taps[start:start + 2] for start in range(0, len(taps), 2)]

    def window(tap, part):
        a, i = tap
        value = operand[part, frame + a:frame + a + frames, i:i + rows]
        return value.reshape(frames * rows * width, LANES)

    pieces = []
    for group in groups:
        pieces += [window(tap, 0) for tap in group]
        high = window(group[0], 1)
        pieces.append(high + window(group[1], 2) if len(group) > 1 else high)
    left = jnp.concatenate(pieces, axis=-1)
    products = []
    for j in range(TAPS):
        rights = []
        for group in groups:
            held = [weights_ref[a, i, j] for a, i in group]
            rights += [weight[:LANES] for weight in held] + [weight[LANES:] for weight in held]
        rights.append(jnp.zeros((left.shape[1] - sum(r.shape[0] for r in rights), channels), jnp.bfloat16))
        product = jnp.dot(left, jnp.concatenate(rights, axis=0), preferred_element_type=jnp.float32)
        products.append(product.reshape(frames * rows, width, channels))
    column = lax.broadcasted_iota(jnp.int32, (1, width, 1), 1)
    before = jnp.where(column == 0, 0.0, pltpu.roll(products[0], 1, 1))
    after = jnp.where(column == width - 1, 0.0, pltpu.roll(products[2], width - 1, 1))
    result = products[1] + before + after + bias_ref[...].reshape(1, 1, channels)
    return result.reshape(frames, rows, width, channels)


def halves(core, mine, other):
    return jnp.where(core == 0, mine, other), jnp.where(core == 0, other, mine)


def frame_flags(marks, frames):
    values = marks.astype(jnp.float32)
    return [values[k:k + 1, 0:1].reshape(1, 1, 1, 1) for k in frames]


def fill_rows(operand, frame, mine, other, gain_ref, channels):
    left, right = halves(lax.axis_index("wa"), mine, other)
    frames, pairs = mine.shape[:2]
    upper, lower = first_rows(left, right, gain_ref, channels)
    for part in range(len(upper)):
        for pair in range(pairs):
            operand[part, frame:frame + frames, 2 * pair] = upper[part][:, pair]
            operand[part, frame:frame + frames, 2 * pair + 1] = lower[part][:, pair]


def border_kernel(tail_ref, mine_ref, other_ref, tail_edge_ref, own_edge_ref):
    frames, held = mine_ref.shape[:2]
    pair = lax.axis_index("wa") * (held - 1)
    for slot in range(CACHE):
        tail_edge_ref[0, slot] = tail_ref[slot * held + pair]
        tail_edge_ref[1, slot] = other_ref[slot * held + pair]
    for frame in range(frames):
        own_edge_ref[0, frame] = mine_ref[frame, pair]
        own_edge_ref[1, frame] = other_ref[(CACHE + frame) * held + pair]


def finish(mine_ref, other_ref, live, first, pairs, value, targets):
    _, held, side, _ = mine_ref.shape
    frames, channels = value.shape[0], value.shape[-1]
    start, count = pairs
    near, far = halves(lax.axis_index("wa"), value[:, :, :side], value[:, :, side:])
    for mine, value, target in ((True, near, targets[0]), (False, far, targets[1])):
        for frame in range(frames):
            for k in range(count):
                if mine:
                    raw = mine_ref[first + frame, start + k]
                else:
                    raw = other_ref[(CACHE + first + frame) * held + start + k]
                raw = raw.astype(jnp.float32)
                high = raw[:, 2 * LANES:]
                for row, tail in ((0, high), (1, pltpu.roll(high, LANES // 2, 1))):
                    low = raw[:, row * LANES:(row + 1) * LANES]
                    features = jnp.concatenate([low, tail[:, :channels - LANES]], axis=-1)
                    summed = features + value[frame, 2 * k + row]
                    kept = jnp.where(live[first + frame].reshape(1, 1) > 0.5, summed, 0.0)
                    target(first + frame, 2 * k + row, kept.astype(jnp.bfloat16))


def middle_kernel(
    marks_ref, tail_mine_ref, tail_other_ref, mine_ref, other_ref,
    gain1_ref, w1_ref, bias1_ref, gain2_ref, w2_ref, bias2_ref,
    near_ref, inner_ref, keep_ref, send_ref, operand,
):
    core = lax.axis_index("wa")
    frames, pairs, side, packed = mine_ref.shape
    channels = w1_ref.shape[-1]
    rows = 2 * pairs
    tiles = CACHE * pairs
    live = frame_flags(marks_ref[...], range(frames))
    earlier = lax.axis_index("tchunk") > 0

    def unpacked(ref, start, count):
        return ref[start:start + count * pairs].reshape(count, pairs, side, packed)

    def hide(first, count, flags):
        def then(start, part, hidden):
            flag = jnp.concatenate(flags[start:start + part], axis=0)
            inner_ref[:, first + start:first + start + part] = second_rows(hidden, flag, gain2_ref, channels)

        convolved(operand, w1_ref, bias1_ref, first, count, rows - 2, then)

    @pl.when(earlier)
    def _():
        fill_rows(
            operand, 0, unpacked(tail_mine_ref, 0, CACHE), unpacked(tail_other_ref, 0, CACHE), gain1_ref, channels
        )
        hide(0, 2, frame_flags(tail_mine_ref[tiles], range(CACHE - 2, CACHE)))

    @pl.when(jnp.logical_not(earlier))
    def _():
        operand[:, 0:CACHE] = jnp.zeros(operand.shape[:1] + (CACHE,) + operand.shape[2:], operand.dtype)
        inner_ref[:, 0:2] = jnp.zeros(inner_ref.shape[:1] + (2,) + inner_ref.shape[2:], inner_ref.dtype)

    fill_rows(operand, CACHE, mine_ref[...], unpacked(other_ref, tiles, frames), gain1_ref, channels)
    near_ref[...] = operand[:, :, pl.ds((rows - 2) * core, 2)]
    hide(2, frames, live)

    def put(ref):
        def store(frame, row, value):
            ref[frame, row] = value
        return store

    def then(start, part, result):
        finish(mine_ref, other_ref, live, start, (1, pairs - 2), result, (put(keep_ref), put(send_ref)))

    convolved(inner_ref, w2_ref, bias2_ref, 0, frames, rows - 4, then)


def outer_kernel(
    marks_ref, tail_mine_ref, mine_ref, other_ref, tail_edge_ref, own_edge_ref, near_ref, inner_ref,
    keep_mid_ref, send_mid_ref, gain1_ref, w1_ref, bias1_ref, gain2_ref, w2_ref, bias2_ref,
    keep_ref, send_ref, strip, operand,
):
    core, place = lax.axis_index("wa"), lax.axis_index("ha")
    frames, pairs = mine_ref.shape[:2]
    inner_rows = inner_ref.shape[2]
    channels = w1_ref.shape[-1]
    outward, inward = pl.ds(2 * core, 2), pl.ds(2 * (1 - core), 2)

    for start, ref in ((0, tail_edge_ref), (CACHE, own_edge_ref)):
        left, right = halves(core, ref[1], ref[0])
        upper, lower = first_rows(left[:, None], right[:, None], gain1_ref, channels)
        for part in range(len(upper)):
            strip[part, start:start + ref.shape[1], pl.ds(2 * core, 1)] = upper[part]
            strip[part, start:start + ref.shape[1], pl.ds(2 * core + 1, 1)] = lower[part]
    strip[:, :, inward] = near_ref[...]
    inside = jnp.where(core == 0, place > 0, place < lax.axis_size("ha") - 1)
    row = lax.broadcasted_iota(jnp.int32, (1, 2, 1, 1), 1)
    row_flag = jnp.where((row == core) & jnp.logical_not(inside), 0.0, 1.0)
    live = frame_flags(marks_ref[...], range(frames))
    flags = frame_flags(tail_mine_ref[CACHE * pairs], range(CACHE - 2, CACHE)) + live
    operand[:, :, inward] = inner_ref[:, :, pl.ds((inner_rows - 2) * core, 2)]

    def hide(start, part, hidden):
        flag = jnp.concatenate(flags[start:start + part], axis=0) * row_flag
        operand[:, start:start + part, outward] = second_rows(hidden, flag, gain2_ref, channels)

    convolved(strip, w1_ref, bias1_ref, 0, frames + 2, 2, hide)

    def put(ref):
        def store(frame, row, value):
            ref[frame, (inner_rows - 2) * core + row] = value
        return store

    def then(start, part, result):
        finish(mine_ref, other_ref, live, start, ((pairs - 1) * core, 1), result, (put(keep_ref), put(send_ref)))

    convolved(operand, w2_ref, bias2_ref, 0, frames, 2, then)
    for source, target in ((keep_mid_ref, keep_ref), (send_mid_ref, send_ref)):
        target[:, pl.ds(2 * (1 - core), inner_rows - 2)] = source[...]


def place_kernel(keep_ref, got_ref, result_ref, arrived):
    core, half = lax.axis_index("wa"), keep_ref.shape[1]
    copies = [
        pltpu.make_async_copy(keep_ref, result_ref.at[:, pl.ds(half * core, half)], arrived.at[0]),
        pltpu.make_async_copy(got_ref, result_ref.at[:, pl.ds(half * (1 - core), half)], arrived.at[1]),
    ]
    for copy in copies:
        copy.start()
    for copy in copies:
        copy.wait()


def shards(features, frame_counts, gain_first, conv_first, bias_first, gain_second, conv_second, bias_second):
    frames, rows, side, channels = features.shape
    pairs, half = rows // 2, rows // 2
    held = half // 2 + 1
    tall, cores, blocks = lax.axis_size("ha"), lax.axis_size("wa"), lax.axis_size("tchunk")
    packed, width, tiles = 3 * LANES, 2 * side, CACHE * held
    bf16 = jnp.bfloat16
    vmem = pl.BlockSpec(memory_space=pltpu.VMEM)
    limit = pltpu.CompilerParams(vmem_limit_bytes=20 * 2**20)
    work = 2 * TAPS**3 * channels * channels * width

    def shape(*extent):
        return jax.ShapeDtypeStruct(extent, bf16)

    def cost(flops, fetched):
        return pl.CostEstimate(flops=flops, bytes_accessed=fetched, transcendentals=0)

    slots = pl.pallas_call(
        slots_kernel,
        out_shape=jax.ShapeDtypeStruct((side, packed), jnp.int32),
        out_specs=vmem,
        compiler_params=limit,
        cost_estimate=cost(2**34, 2**20),
    )()
    slots, frame_counts = lax.optimization_barrier((slots, frame_counts))
    tail, mine, theirs, marks = pl.pallas_call(
        prepare_kernel,
        out_shape=(
            shape(tiles + 1, side, packed), shape(frames, held, side, packed),
            shape((CACHE + frames) * held, side, packed), shape(side, packed),
        ),
        in_specs=[pl.BlockSpec(memory_space=pltpu.SMEM), vmem, vmem],
        out_specs=(vmem,) * 4,
        scratch_shapes=[pltpu.VMEM((frames, pairs, side, packed), bf16)],
        compiler_params=limit,
    )(frame_counts, slots, features)

    tail, tail_theirs = joined_tails(tail, theirs[:tiles])
    if blocks > 2:
        theirs = jnp.concatenate([tail_theirs, theirs[tiles:]], axis=0)
    straight, crossed, diagonal, across = [], [], [], []

    def index(block, h, core):
        return (block * tall + h) * cores + core

    for h in range(tall):
        for k in range(blocks - 1):
            for core in range(cores):
                straight.append((index(k, h, core), index(k + 1, h, core)))
                crossed.append((index(k, h, core), index(k + 1, h, 1 - core)))
    for h in range(tall - 1):
        for k in range(blocks):
            lower, upper = index(k, h, 1), index(k, h + 1, 0)
            across += [(lower, upper), (upper, lower)]
            if k + 1 < blocks:
                lower_next, upper_next = index(k + 1, h, 1), index(k + 1, h + 1, 0)
                diagonal += [(lower, upper_next), (upper, lower_next)]
    axes = ("tchunk", "ha", "wa")
    swap = [(0, 1), (1, 0)]
    tail_mine = lax.ppermute(tail, axes, straight)
    tail_other = lax.ppermute(tail_theirs, axes, crossed)
    other = lax.ppermute(theirs, "wa", swap)
    tail_edge, own_edge = pl.pallas_call(
        border_kernel,
        out_shape=(shape(2, CACHE, side, packed), shape(2, frames, side, packed)),
        in_specs=[vmem] * 3,
        out_specs=(vmem, vmem),
        compiler_params=limit,
        cost_estimate=cost(2**34, 2**20),
    )(tail, mine, other)
    own_edge = lax.ppermute(own_edge, axes, across)
    tail_edge = lax.ppermute(tail_edge, axes, diagonal)

    weights = (
        gain_first.reshape(1, channels), conv_first, bias_first.reshape(1, channels),
        gain_second.reshape(1, channels), conv_second, bias_second.reshape(1, channels),
    )
    near, inner, keep, send = pl.pallas_call(
        middle_kernel,
        out_shape=(
            shape(3, frames + CACHE, 2, width, LANES), shape(3, frames + 2, half, width, LANES),
            shape(frames, half - 2, side, channels), shape(frames, half - 2, side, channels),
        ),
        in_specs=[vmem] * 11,
        out_specs=(vmem,) * 4,
        scratch_shapes=[pltpu.VMEM((3, frames + CACHE, half + 2, width, LANES), bf16)],
        compiler_params=limit,
        cost_estimate=cost(work * ((frames + 2) * half + frames * (half - 2)), 8 * 2**20),
    )(marks, tail_mine, tail_other, mine, other, *weights)
    keep, send = pl.pallas_call(
        outer_kernel,
        out_shape=(shape(frames, half, side, channels), shape(frames, half, side, channels)),
        in_specs=[vmem] * 16,
        out_specs=(vmem, vmem),
        scratch_shapes=[
            pltpu.VMEM((3, frames + CACHE, 4, width, LANES), bf16),
            pltpu.VMEM((3, frames + 2, 4, width, LANES), bf16),
        ],
        compiler_params=limit,
        cost_estimate=cost(work * 2 * (2 * frames + 2), 8 * 2**20),
    )(marks, tail_mine, mine, other, tail_edge, own_edge, near, inner, keep, send, *weights)
    got = lax.ppermute(send, "wa", swap)
    return pl.pallas_call(
        place_kernel,
        out_shape=shape(*features.shape),
        in_specs=[vmem, vmem],
        out_specs=pl.BlockSpec(memory_space=pltpu.HBM),
        scratch_shapes=[pltpu.SemaphoreType.DMA((2,))],
        compiler_params=limit,
    )(keep, got)


def solution(mesh):
    return jax.shard_map(
        shards,
        mesh=mesh,
        in_specs=(
            P(("grp", "tchunk"), "ha", "wa", None),
            P(("grp", "tchunk")),
            P(), P(), P(), P(), P(), P(),
        ),
        out_specs=P(("grp", "tchunk"), "ha", "wa", None),
        check_vma=False,
    )
```

```python
import jax
import jax.numpy as jnp
from jax import lax
from jax.experimental import pallas as pl
from jax.experimental.pallas import tpu as pltpu
from jax.sharding import PartitionSpec as P

epsilon = 1e-06
CACHE = 4
TAPS = 3
LANES = 128
PRODUCT = 192


def slots_kernel(slots_ref):
    slots_ref[...] = lax.broadcasted_iota(jnp.int32, slots_ref.shape, 0)


def prepare_kernel(total_ref, slots_ref, raw, tail_ref, mine_ref, theirs_ref, marks_ref, pack):
    frames, rows = raw.shape[:2]
    pairs, held = rows // 2, mine_ref.shape[1]
    core = lax.axis_index("wa")
    total = total_ref[0]
    for frame in range(frames):
        for pair in range(pairs):
            first, second = raw[frame, 2 * pair], raw[frame, 2 * pair + 1]
            packed = jnp.concatenate(
                [first[:, :LANES], second[:, :LANES], first[:, LANES:], second[:, LANES:]], axis=-1
            )
            pack[frame, pair] = packed
    for slot in range(CACHE):
        frame = total - CACHE + slot
        value = pack[jnp.maximum(frame, 0)]
        tail_ref[slot * pairs:(slot + 1) * pairs] = jnp.where(frame >= 0, value, jnp.zeros_like(value))
        value = pack[jnp.maximum(frame, 0), pl.ds((1 - core) * (pairs - held), held)]
        theirs_ref[slot * held:(slot + 1) * held] = jnp.where(frame >= 0, value, jnp.zeros_like(value))
    for frame in range(frames):
        start = (CACHE + frame) * held
        value = pack[frame, pl.ds(core * (pairs - held), held)]
        mine_ref[frame] = jnp.where(frame < total, value, jnp.zeros_like(value))
        value = pack[frame, pl.ds((1 - core) * (pairs - held), held)]
        theirs_ref[start:start + held] = jnp.where(frame < total, value, jnp.zeros_like(value))
    slot = slots_ref[...]
    tail_ref[CACHE * pairs] = jnp.where(
        (slot < CACHE) & (total - CACHE + slot >= 0), 1.0, 0.0
    ).astype(tail_ref.dtype)
    marks_ref[...] = jnp.where(slot < total, 1.0, 0.0).astype(marks_ref.dtype)


def joined_tail(tail):
    count = lax.axis_size("tchunk")

    def pushed(value, held):
        return lax.dynamic_slice_in_dim(jnp.concatenate([value, jnp.zeros_like(value)], axis=0), held, CACHE, 0)

    step = 1
    while step < count - 1:
        early = lax.ppermute(tail, "tchunk", [(k, k + step) for k in range(count - step)])
        held = jnp.sum(tail[-1, :CACHE, 0].astype(jnp.int32))
        body = pushed(early[:-1].reshape((CACHE, -1) + tail.shape[1:]), held).reshape(tail[:-1].shape)
        marks = jnp.pad(pushed(early[-1, :CACHE], held), ((0, tail.shape[1] - CACHE), (0, 0)))
        tail = tail + jnp.concatenate([body, marks[None]], axis=0)
        step *= 2
    return tail


def silu(half):
    return half + half * jnp.tanh(half)


def lane_mask():
    return lax.broadcasted_iota(jnp.int32, (1, 1, 1, LANES), 3) < LANES // 2


def gains(gain_ref):
    low, high = 0.5 * gain_ref[:, :LANES], 0.5 * gain_ref[:, LANES:]
    return low.reshape(1, 1, 1, LANES), jnp.concatenate([high, high], axis=-1).reshape(1, 1, 1, LANES)


def rolled(values):
    shape = values.shape
    return pltpu.roll(values.reshape(-1, LANES), LANES // 2, 1).reshape(shape)


def first_rows(left, right, gain_ref, channels):
    raw = jnp.concatenate([left.astype(jnp.float32), right.astype(jnp.float32)], axis=2)
    front, back, high = raw[..., :LANES], raw[..., LANES:2 * LANES], raw[..., 2 * LANES:]
    lower = lane_mask()
    squared = high * high

    def inverse(low, mask):
        total = jnp.sum(low * low + jnp.where(mask, squared, 0.0), axis=-1, keepdims=True)
        return lax.rsqrt(total * (1.0 / channels) + epsilon)

    scale_front, scale_back = inverse(front, lower), inverse(back, jnp.logical_not(lower))
    gain_low, gain_high = gains(gain_ref)
    front = silu(front * scale_front * gain_low)
    back = silu(back * scale_back * gain_low)
    high = silu(high * jnp.where(lower, scale_front, scale_back) * gain_high)
    turned = rolled(high)
    one = [front, jnp.where(lower, high, 0.0), jnp.where(lower, 0.0, turned)]
    two = [back, jnp.where(lower, turned, 0.0), jnp.where(lower, 0.0, high)]
    return [[part.astype(jnp.bfloat16) for part in row] for row in (one, two)]


def second_rows(hidden, flag, gain_ref, channels):
    gain = 0.5 * gain_ref[...].reshape(1, 1, 1, channels)
    total = jnp.sum(hidden * hidden, axis=-1, keepdims=True)
    inverse = lax.rsqrt(total * (1.0 / channels) + epsilon) * flag
    values = silu(hidden * inverse * gain)
    rest = jnp.zeros(values.shape[:-1] + (LANES // 2,), jnp.float32)
    high = jnp.concatenate([values[..., LANES:], rest], axis=-1)
    parts = [values[..., :LANES], high, rolled(high)]
    return jnp.stack([part.astype(jnp.bfloat16) for part in parts])


def convolved(operand, weights_ref, bias_ref, frame, frames, rows, then):
    products = -(-frames * rows * operand.shape[3] // PRODUCT)
    step = -(-frames // products)
    for start in range(0, frames, step):
        count = min(step, frames - start)
        then(start, count, convolved_part(operand, weights_ref, bias_ref, frame + start, count, rows))


def convolved_part(operand, weights_ref, bias_ref, frame, frames, rows):
    width = operand.shape[3]
    channels = weights_ref.shape[-1]
    taps = [(a, i) for a in range(TAPS) for i in range(TAPS)]
    groups = [taps[start:start + 2] for start in range(0, len(taps), 2)]

    def window(tap, part):
        a, i = tap
        value = operand[part, frame + a:frame + a + frames, i:i + rows]
        return value.reshape(frames * rows * width, LANES)

    pieces = []
    for group in groups:
        pieces += [window(tap, 0) for tap in group]
        high = window(group[0], 1)
        pieces.append(high + window(group[1], 2) if len(group) > 1 else high)
    left = jnp.concatenate(pieces, axis=-1)
    products = []
    for j in range(TAPS):
        rights = []
        for group in groups:
            held = [weights_ref[a, i, j] for a, i in group]
            rights += [weight[:LANES] for weight in held] + [weight[LANES:] for weight in held]
        rights.append(jnp.zeros((left.shape[1] - sum(r.shape[0] for r in rights), channels), jnp.bfloat16))
        product = jnp.dot(left, jnp.concatenate(rights, axis=0), preferred_element_type=jnp.float32)
        products.append(product.reshape(frames * rows, width, channels))
    column = lax.broadcasted_iota(jnp.int32, (1, width, 1), 1)
    before = jnp.where(column == 0, 0.0, pltpu.roll(products[0], 1, 1))
    after = jnp.where(column == width - 1, 0.0, pltpu.roll(products[2], width - 1, 1))
    result = products[1] + before + after + bias_ref[...].reshape(1, 1, channels)
    return result.reshape(frames, rows, width, channels)


def halves(core, mine, other):
    return jnp.where(core == 0, mine, other), jnp.where(core == 0, other, mine)


def frame_flags(marks, frames):
    values = marks.astype(jnp.float32)
    return [values[k:k + 1, 0:1].reshape(1, 1, 1, 1) for k in frames]


def fill_rows(operand, frame, row, mine, other, gain_ref):
    left, right = halves(lax.axis_index("wa"), mine, other)
    frames, pairs = mine.shape[:2]
    upper, lower = first_rows(left, right, gain_ref, gain_ref.shape[-1])
    for part in range(len(upper)):
        for pair in range(pairs):
            operand[part, frame:frame + frames, pl.ds(row + 2 * pair, 1)] = upper[part][:, pair:pair + 1]
            operand[part, frame:frame + frames, pl.ds(row + 2 * pair + 1, 1)] = lower[part][:, pair:pair + 1]


def border_kernel(tail_ref, mine_ref, other_ref, tail_edge_ref, own_edge_ref):
    frames, held = mine_ref.shape[:2]
    pairs = tail_ref.shape[0] // CACHE
    core = lax.axis_index("wa")
    pair = core * (held - 1)
    for slot in range(CACHE):
        tail_edge_ref[0, slot] = tail_ref[slot * pairs + core * (pairs - 1)]
        tail_edge_ref[1, slot] = other_ref[slot * held + pair]
    for frame in range(frames):
        own_edge_ref[0, frame] = mine_ref[frame, pair]
        own_edge_ref[1, frame] = other_ref[(CACHE + frame) * held + pair]


def finish(mine_ref, other_ref, live, first, pairs, value, targets):
    _, held, side, _ = mine_ref.shape
    frames, channels = value.shape[0], value.shape[-1]
    start, count = pairs
    near, far = halves(lax.axis_index("wa"), value[:, :, :side], value[:, :, side:])
    for mine, value, target in ((True, near, targets[0]), (False, far, targets[1])):
        for frame in range(frames):
            for k in range(count):
                if mine:
                    raw = mine_ref[first + frame, start + k]
                else:
                    raw = other_ref[(CACHE + first + frame) * held + start + k]
                raw = raw.astype(jnp.float32)
                high = raw[:, 2 * LANES:]
                for row, tail in ((0, high), (1, pltpu.roll(high, LANES // 2, 1))):
                    low = raw[:, row * LANES:(row + 1) * LANES]
                    features = jnp.concatenate([low, tail[:, :channels - LANES]], axis=-1)
                    summed = features + value[frame, 2 * k + row]
                    kept = jnp.where(live[first + frame].reshape(1, 1) > 0.5, summed, 0.0)
                    target(first + frame, 2 * k + row, kept.astype(jnp.bfloat16))


def hide(operand, weights_ref, bias_ref, gain_ref, first, count, rows, flags, store):
    channels = weights_ref.shape[-1]

    def then(begin, part, hidden):
        flag = jnp.concatenate(flags[begin:begin + part], axis=0)
        store(begin, begin + part, second_rows(hidden, flag, gain_ref, channels))

    convolved(operand, weights_ref, bias_ref, first, count, rows, then)


def inside_flags(rows):
    core, place = lax.axis_index("wa"), lax.axis_index("ha")
    inside = jnp.where(core == 0, place > 0, place < lax.axis_size("ha") - 1)
    row = lax.broadcasted_iota(jnp.int32, (1, rows, 1, 1), 1)
    return jnp.where((row == (rows - 1) * core) & jnp.logical_not(inside), 0.0, 1.0)


def own_kernel(
    marks_ref, mine_ref, other_ref, gain1_ref, w1_ref, bias1_ref, gain2_ref, first_ref, late_ref
):
    frames, pairs, side, packed = mine_ref.shape
    other = other_ref[CACHE * pairs:].reshape(frames, pairs, side, packed)
    fill_rows(first_ref, 0, 0, mine_ref[...], other, gain1_ref)
    live = frame_flags(marks_ref[...], range(2, frames))

    def store(begin, end, rows):
        late_ref[:, begin:end] = rows

    hide(first_ref, w1_ref, bias1_ref, gain2_ref, 0, frames - 2, 2 * pairs - 2, live, store)


def edge_kernel(
    marks_ref, mine_ref, other_ref, edge_ref, tail_edge_ref, first_ref, late_ref,
    gain1_ref, w1_ref, bias1_ref, gain2_ref, w2_ref, bias2_ref,
    strip_ref, hidden_ref, keep_ref, send_ref, strip, operand,
):
    core = lax.axis_index("wa")
    frames, pairs = mine_ref.shape[:2]
    rows = 2 * pairs
    fill_rows(strip, 0, 2 * core, edge_ref[1][:, None], edge_ref[0][:, None], gain1_ref)
    strip[:, :, pl.ds(2 * (1 - core), 2)] = first_ref[:, :, pl.ds((rows - 2) * core, 2)]
    live = frame_flags(marks_ref[...], range(frames))
    inside = inside_flags(2)

    def store(begin, end, values):
        operand[:, begin:end, pl.ds((rows - 2) * core, 2)] = values

    hide(strip, w1_ref, bias1_ref, gain2_ref, 0, frames - 2, 2, [flag * inside for flag in live[2:]], store)
    operand[:, :, pl.ds(2 * (1 - core), rows - 2)] = late_ref[...]
    fill_rows(strip_ref, 0, 0, tail_edge_ref[1][:, None], tail_edge_ref[0][:, None], gain1_ref)
    strip_ref[:, CACHE:] = strip[:, 0:2, pl.ds(2 * core, 2)]
    hidden_ref[...] = operand[:, 0:2]

    def put(ref):
        def store(frame, row, value):
            ref[frame - CACHE, row] = value
        return store

    def then(start, part, result):
        finish(
            mine_ref, other_ref, live, CACHE + start, (core, pairs - 1), result, (put(keep_ref), put(send_ref))
        )

    convolved(operand, w2_ref, bias2_ref, 0, frames - CACHE, rows - 2, then)


def early_kernel(
    marks_ref, tail_mine_ref, tail_other_ref, mine_ref, other_ref, first_ref, strip_ref, hidden_ref,
    late_keep_ref, late_send_ref, gain1_ref, w1_ref, bias1_ref, gain2_ref, w2_ref, bias2_ref,
    keep_ref, send_ref, plane, operand,
):
    core = lax.axis_index("wa")
    held = mine_ref.shape[1]
    rows = 2 * held
    pairs = tail_mine_ref.shape[0] // CACHE
    live = frame_flags(marks_ref[...], range(CACHE))
    inside = inside_flags(rows)
    earlier = lax.axis_index("tchunk") > 0
    middle, border = 2 * (1 - core), rows * core

    def unpacked(ref):
        return jnp.stack([ref[pl.ds(slot * pairs + core * (pairs - held), held)] for slot in range(CACHE)])

    plane[:, CACHE:, pl.ds(middle, rows)] = first_ref[:, 0:2]
    plane[:, :, pl.ds(border, 2)] = strip_ref[...]
    operand[:, CACHE:] = hidden_ref[...]

    def fill(first, flags):
        def store(begin, end, values):
            operand[:, first + begin:first + end] = values

        flags = [flag * inside for flag in flags]
        hide(plane, w1_ref, bias1_ref, gain2_ref, first, CACHE - first, rows, flags, store)

    @pl.when(earlier)
    def _():
        fill_rows(plane, 0, middle, unpacked(tail_mine_ref), unpacked(tail_other_ref), gain1_ref)
        fill(0, frame_flags(tail_mine_ref[CACHE * pairs], range(CACHE - 2, CACHE)) + live[0:2])

    @pl.when(jnp.logical_not(earlier))
    def _():
        plane[:, 0:CACHE, pl.ds(middle, rows)] = jnp.zeros(
            plane.shape[:1] + (CACHE, rows) + plane.shape[3:], plane.dtype
        )
        operand[:, 0:2] = jnp.zeros(operand.shape[:1] + (2,) + operand.shape[2:], operand.dtype)
        fill(2, live[0:2])

    def put(ref):
        def store(frame, row, value):
            ref[frame, row] = value
        return store

    def then(start, part, result):
        finish(mine_ref, other_ref, live, start, (core, held - 1), result, (put(keep_ref), put(send_ref)))

    convolved(operand, w2_ref, bias2_ref, 0, CACHE, rows - 2, then)
    keep_ref[CACHE:] = late_keep_ref[...]
    send_ref[CACHE:] = late_send_ref[...]


def place_kernel(keep_ref, got_ref, result_ref, arrived):
    core, half = lax.axis_index("wa"), keep_ref.shape[1]
    copies = [
        pltpu.make_async_copy(keep_ref, result_ref.at[:, pl.ds(half * core, half)], arrived.at[0]),
        pltpu.make_async_copy(got_ref, result_ref.at[:, pl.ds(half * (1 - core), half)], arrived.at[1]),
    ]
    for copy in copies:
        copy.start()
    for copy in copies:
        copy.wait()


def shards(features, frame_counts, gain_first, conv_first, bias_first, gain_second, conv_second, bias_second):
    frames, rows, side, channels = features.shape
    pairs, half = rows // 2, rows // 2
    held = half // 2 + 1
    tall, cores, blocks = lax.axis_size("ha"), lax.axis_size("wa"), lax.axis_size("tchunk")
    packed, width, tiles = 3 * LANES, 2 * side, CACHE * held
    bf16 = jnp.bfloat16
    vmem = pl.BlockSpec(memory_space=pltpu.VMEM)
    limit = pltpu.CompilerParams(vmem_limit_bytes=20 * 2**20)
    work = 2 * TAPS**3 * channels * channels * width

    def shape(*extent):
        return jax.ShapeDtypeStruct(extent, bf16)

    def cost(flops, fetched):
        return pl.CostEstimate(flops=flops, bytes_accessed=fetched, transcendentals=0)

    slots = pl.pallas_call(
        slots_kernel,
        out_shape=jax.ShapeDtypeStruct((side, packed), jnp.int32),
        out_specs=vmem,
        compiler_params=limit,
        cost_estimate=cost(2**34, 2**20),
    )()
    slots, frame_counts = lax.optimization_barrier((slots, frame_counts))
    tail, mine, theirs, marks = pl.pallas_call(
        prepare_kernel,
        out_shape=(
            shape(CACHE * pairs + 1, side, packed), shape(frames, held, side, packed),
            shape((CACHE + frames) * held, side, packed), shape(side, packed),
        ),
        in_specs=[pl.BlockSpec(memory_space=pltpu.SMEM), vmem, vmem],
        out_specs=(vmem,) * 4,
        scratch_shapes=[pltpu.VMEM((frames, pairs, side, packed), bf16)],
        compiler_params=limit,
    )(frame_counts, slots, features)

    if blocks > 2:
        tail = joined_tail(tail)
        rest = lax.dynamic_slice_in_dim(
            tail[:-1].reshape(CACHE, pairs, side, packed), (1 - lax.axis_index("wa")) * (pairs - held), held, 1
        )
        theirs = jnp.concatenate([rest.reshape(tiles, side, packed), theirs[tiles:]], axis=0)
    straight, diagonal, across = [], [], []

    def index(block, h, core):
        return (block * tall + h) * cores + core

    for k in range(blocks - 1):
        for h in range(tall):
            for core in range(cores):
                straight.append((index(k, h, core), index(k + 1, h, core)))
    for h in range(tall - 1):
        for k in range(blocks):
            lower, upper = index(k, h, 1), index(k, h + 1, 0)
            across += [(lower, upper), (upper, lower)]
            if k + 1 < blocks:
                lower_next, upper_next = index(k + 1, h, 1), index(k + 1, h + 1, 0)
                diagonal += [(lower, upper_next), (upper, lower_next)]
    axes = ("tchunk", "ha", "wa")
    swap = [(0, 1), (1, 0)]
    tail_mine = lax.ppermute(tail, axes, straight)
    tail_other = lax.ppermute(tail_mine, "wa", swap)
    other = lax.ppermute(theirs, "wa", swap)
    tail_edge, own_edge = pl.pallas_call(
        border_kernel,
        out_shape=(shape(2, CACHE, side, packed), shape(2, frames, side, packed)),
        in_specs=[vmem] * 3,
        out_specs=(vmem, vmem),
        compiler_params=limit,
        cost_estimate=cost(2**34, 2**20),
    )(tail, mine, other)
    own_edge = lax.ppermute(own_edge, axes, across)
    tail_edge = lax.ppermute(tail_edge, axes, diagonal)

    weights = (
        gain_first.reshape(1, channels), conv_first, bias_first.reshape(1, channels),
        gain_second.reshape(1, channels), conv_second, bias_second.reshape(1, channels),
    )
    first, late = pl.pallas_call(
        own_kernel,
        out_shape=(shape(3, frames, half + 2, width, LANES), shape(3, frames - 2, half, width, LANES)),
        in_specs=[vmem] * 7,
        out_specs=(vmem,) * 2,
        compiler_params=limit,
        cost_estimate=cost(work * (frames - 2) * half, 4 * 2**20),
    )(marks, mine, other, *weights[:4])
    strip, hidden, keep, send = pl.pallas_call(
        edge_kernel,
        out_shape=(
            shape(3, CACHE + 2, 2, width, LANES), shape(3, 2, half + 2, width, LANES),
            shape(frames - CACHE, half, side, channels), shape(frames - CACHE, half, side, channels),
        ),
        in_specs=[vmem] * 13,
        out_specs=(vmem,) * 4,
        scratch_shapes=[
            pltpu.VMEM((3, frames, 4, width, LANES), bf16),
            pltpu.VMEM((3, frames - 2, half + 2, width, LANES), bf16),
        ],
        compiler_params=limit,
        cost_estimate=cost(work * ((frames - 2) * 2 + (frames - CACHE) * half), 8 * 2**20),
    )(marks, mine, other, own_edge, tail_edge, first, late, *weights)
    keep, send = pl.pallas_call(
        early_kernel,
        out_shape=(shape(frames, half, side, channels), shape(frames, half, side, channels)),
        in_specs=[vmem] * 16,
        out_specs=(vmem, vmem),
        scratch_shapes=[
            pltpu.VMEM((3, CACHE + 2, half + 4, width, LANES), bf16),
            pltpu.VMEM((3, CACHE + 2, half + 2, width, LANES), bf16),
        ],
        compiler_params=limit,
        cost_estimate=cost(work * CACHE * (2 * half + 2), 8 * 2**20),
    )(marks, tail_mine, tail_other, mine, other, first, strip, hidden, keep, send, *weights)
    got = lax.ppermute(send, "wa", swap)
    return pl.pallas_call(
        place_kernel,
        out_shape=shape(*features.shape),
        in_specs=[vmem, vmem],
        out_specs=pl.BlockSpec(memory_space=pltpu.HBM),
        scratch_shapes=[pltpu.SemaphoreType.DMA((2,))],
        compiler_params=limit,
    )(keep, got)


def solution(mesh):
    return jax.shard_map(
        shards,
        mesh=mesh,
        in_specs=(
            P(("grp", "tchunk"), "ha", "wa", None),
            P(("grp", "tchunk")),
            P(), P(), P(), P(), P(), P(),
        ),
        out_specs=P(("grp", "tchunk"), "ha", "wa", None),
        check_vma=False,
    )
```

```python
import jax
import jax.numpy as jnp
from jax import lax
from jax.experimental import pallas as pl
from jax.experimental.pallas import tpu as pltpu
from jax.sharding import PartitionSpec as P

epsilon = 1e-06
CACHE = 4
TAPS = 3
LANES = 128
PRODUCT = 192


def slots_kernel(slots_ref):
    slots_ref[...] = lax.broadcasted_iota(jnp.int32, slots_ref.shape, 0)


def prepare_kernel(total_ref, slots_ref, raw, tail_ref, mine_ref, theirs_ref, marks_ref, pack):
    frames, rows = raw.shape[:2]
    pairs, held = rows // 2, mine_ref.shape[1]
    core = lax.axis_index("wa")
    total = total_ref[0]
    for frame in range(frames):
        for pair in range(pairs):
            first, second = raw[frame, 2 * pair], raw[frame, 2 * pair + 1]
            packed = jnp.concatenate(
                [first[:, :LANES], second[:, :LANES], first[:, LANES:], second[:, LANES:]], axis=-1
            )
            pack[frame, pair] = packed
    for slot in range(CACHE):
        frame = total - CACHE + slot
        value = pack[jnp.maximum(frame, 0)]
        tail_ref[slot * pairs:(slot + 1) * pairs] = jnp.where(frame >= 0, value, jnp.zeros_like(value))
        value = pack[jnp.maximum(frame, 0), pl.ds((1 - core) * (pairs - held), held)]
        theirs_ref[slot * held:(slot + 1) * held] = jnp.where(frame >= 0, value, jnp.zeros_like(value))
    for frame in range(frames):
        start = (CACHE + frame) * held
        value = pack[frame, pl.ds(core * (pairs - held), held)]
        mine_ref[frame] = jnp.where(frame < total, value, jnp.zeros_like(value))
        value = pack[frame, pl.ds((1 - core) * (pairs - held), held)]
        theirs_ref[start:start + held] = jnp.where(frame < total, value, jnp.zeros_like(value))
    slot = slots_ref[...]
    tail_ref[CACHE * pairs] = jnp.where(
        (slot < CACHE) & (total - CACHE + slot >= 0), 1.0, 0.0
    ).astype(tail_ref.dtype)
    marks_ref[...] = jnp.where(slot < total, 1.0, 0.0).astype(marks_ref.dtype)


def joined_tail(tail):
    count = lax.axis_size("tchunk")

    def pushed(value, held):
        return lax.dynamic_slice_in_dim(jnp.concatenate([value, jnp.zeros_like(value)], axis=0), held, CACHE, 0)

    step = 1
    while step < count - 1:
        early = lax.ppermute(tail, "tchunk", [(k, k + step) for k in range(count - step)])
        held = jnp.sum(tail[-1, :CACHE, 0].astype(jnp.int32))
        body = pushed(early[:-1].reshape((CACHE, -1) + tail.shape[1:]), held).reshape(tail[:-1].shape)
        marks = jnp.pad(pushed(early[-1, :CACHE], held), ((0, tail.shape[1] - CACHE), (0, 0)))
        tail = tail + jnp.concatenate([body, marks[None]], axis=0)
        step *= 2
    return tail


def silu(half):
    return half + half * jnp.tanh(half)


def lane_mask():
    return lax.broadcasted_iota(jnp.int32, (1, 1, 1, LANES), 3) < LANES // 2


def gains(gain_ref):
    low, high = 0.5 * gain_ref[:, :LANES], 0.5 * gain_ref[:, LANES:]
    return low.reshape(1, 1, 1, LANES), jnp.concatenate([high, high], axis=-1).reshape(1, 1, 1, LANES)


def rolled(values):
    shape = values.shape
    return pltpu.roll(values.reshape(-1, LANES), LANES // 2, 1).reshape(shape)


def first_rows(left, right, gain_ref, channels):
    raw = jnp.concatenate([left.astype(jnp.float32), right.astype(jnp.float32)], axis=2)
    front, back, high = raw[..., :LANES], raw[..., LANES:2 * LANES], raw[..., 2 * LANES:]
    lower = lane_mask()
    squared = high * high

    def inverse(low, mask):
        total = jnp.sum(low * low + jnp.where(mask, squared, 0.0), axis=-1, keepdims=True)
        return lax.rsqrt(total * (1.0 / channels) + epsilon)

    scale_front, scale_back = inverse(front, lower), inverse(back, jnp.logical_not(lower))
    gain_low, gain_high = gains(gain_ref)
    front = silu(front * scale_front * gain_low)
    back = silu(back * scale_back * gain_low)
    high = silu(high * jnp.where(lower, scale_front, scale_back) * gain_high)
    turned = rolled(high)
    one = [front, jnp.where(lower, high, 0.0), jnp.where(lower, 0.0, turned)]
    two = [back, jnp.where(lower, turned, 0.0), jnp.where(lower, 0.0, high)]
    return [[part.astype(jnp.bfloat16) for part in row] for row in (one, two)]


def second_rows(hidden, flag, gain_ref, channels):
    gain = 0.5 * gain_ref[...].reshape(1, 1, 1, channels)
    total = jnp.sum(hidden * hidden, axis=-1, keepdims=True)
    inverse = lax.rsqrt(total * (1.0 / channels) + epsilon) * flag
    values = silu(hidden * inverse * gain)
    rest = jnp.zeros(values.shape[:-1] + (LANES // 2,), jnp.float32)
    high = jnp.concatenate([values[..., LANES:], rest], axis=-1)
    parts = [values[..., :LANES], high, rolled(high)]
    return jnp.stack([part.astype(jnp.bfloat16) for part in parts])


def convolved(operand, weights_ref, bias_ref, frame, frames, rows, then):
    products = -(-frames * rows * operand.shape[3] // PRODUCT)
    step = -(-frames // products)
    for start in range(0, frames, step):
        count = min(step, frames - start)
        then(start, count, convolved_part(operand, weights_ref, bias_ref, frame + start, count, rows))


def convolved_part(operand, weights_ref, bias_ref, frame, frames, rows):
    width = operand.shape[3]
    channels = weights_ref.shape[-1]
    taps = [(a, i) for a in range(TAPS) for i in range(TAPS)]
    groups = [taps[start:start + 2] for start in range(0, len(taps), 2)]

    def window(tap, part):
        a, i = tap
        value = operand[part, frame + a:frame + a + frames, i:i + rows]
        return value.reshape(frames * rows * width, LANES)

    pieces = []
    for group in groups:
        pieces += [window(tap, 0) for tap in group]
        high = window(group[0], 1)
        pieces.append(high + window(group[1], 2) if len(group) > 1 else high)
    left = jnp.concatenate(pieces, axis=-1)
    products = []
    for j in range(TAPS):
        rights = []
        for group in groups:
            held = [weights_ref[a, i, j] for a, i in group]
            rights += [weight[:LANES] for weight in held] + [weight[LANES:] for weight in held]
        rights.append(jnp.zeros((left.shape[1] - sum(r.shape[0] for r in rights), channels), jnp.bfloat16))
        product = jnp.dot(left, jnp.concatenate(rights, axis=0), preferred_element_type=jnp.float32)
        products.append(product.reshape(frames * rows, width, channels))
    column = lax.broadcasted_iota(jnp.int32, (1, width, 1), 1)
    before = jnp.where(column == 0, 0.0, pltpu.roll(products[0], 1, 1))
    after = jnp.where(column == width - 1, 0.0, pltpu.roll(products[2], width - 1, 1))
    result = products[1] + before + after + bias_ref[...].reshape(1, 1, channels)
    return result.reshape(frames, rows, width, channels)


def halves(core, mine, other):
    return jnp.where(core == 0, mine, other), jnp.where(core == 0, other, mine)


def frame_flags(marks, frames):
    values = marks.astype(jnp.float32)
    return [values[k:k + 1, 0:1].reshape(1, 1, 1, 1) for k in frames]


def fill_rows(operand, frame, row, mine, other, gain_ref):
    left, right = halves(lax.axis_index("wa"), mine, other)
    frames, pairs = mine.shape[:2]
    upper, lower = first_rows(left, right, gain_ref, gain_ref.shape[-1])
    for part in range(len(upper)):
        for pair in range(pairs):
            operand[part, frame:frame + frames, pl.ds(row + 2 * pair, 1)] = upper[part][:, pair:pair + 1]
            operand[part, frame:frame + frames, pl.ds(row + 2 * pair + 1, 1)] = lower[part][:, pair:pair + 1]


def border_kernel(tail_ref, mine_ref, other_ref, tail_edge_ref, own_edge_ref):
    frames, held = mine_ref.shape[:2]
    pairs = tail_ref.shape[0] // CACHE
    core = lax.axis_index("wa")
    pair = core * (held - 1)
    for slot in range(CACHE):
        tail_edge_ref[0, slot] = tail_ref[slot * pairs + core * (pairs - 1)]
        tail_edge_ref[1, slot] = other_ref[slot * held + pair]
    for frame in range(frames):
        own_edge_ref[0, frame] = mine_ref[frame, pair]
        own_edge_ref[1, frame] = other_ref[(CACHE + frame) * held + pair]


def finish(mine_ref, other_ref, live, first, pairs, value, targets):
    _, held, side, _ = mine_ref.shape
    frames, channels = value.shape[0], value.shape[-1]
    start, count = pairs
    near, far = halves(lax.axis_index("wa"), value[:, :, :side], value[:, :, side:])
    for mine, value, target in ((True, near, targets[0]), (False, far, targets[1])):
        for frame in range(frames):
            for k in range(count):
                if mine:
                    raw = mine_ref[first + frame, start + k]
                else:
                    raw = other_ref[(CACHE + first + frame) * held + start + k]
                raw = raw.astype(jnp.float32)
                high = raw[:, 2 * LANES:]
                for row, tail in ((0, high), (1, pltpu.roll(high, LANES // 2, 1))):
                    low = raw[:, row * LANES:(row + 1) * LANES]
                    features = jnp.concatenate([low, tail[:, :channels - LANES]], axis=-1)
                    summed = features + value[frame, 2 * k + row]
                    kept = jnp.where(live[first + frame].reshape(1, 1) > 0.5, summed, 0.0)
                    target(first + frame, 2 * k + row, kept.astype(jnp.bfloat16))


def hide(operand, weights_ref, bias_ref, gain_ref, first, count, rows, flags, store):
    channels = weights_ref.shape[-1]

    def then(begin, part, hidden):
        flag = jnp.concatenate(flags[begin:begin + part], axis=0)
        store(begin, begin + part, second_rows(hidden, flag, gain_ref, channels))

    convolved(operand, weights_ref, bias_ref, first, count, rows, then)


def inside_flags(rows):
    core, place = lax.axis_index("wa"), lax.axis_index("ha")
    inside = jnp.where(core == 0, place > 0, place < lax.axis_size("ha") - 1)
    row = lax.broadcasted_iota(jnp.int32, (1, rows, 1, 1), 1)
    return jnp.where((row == (rows - 1) * core) & jnp.logical_not(inside), 0.0, 1.0)


def own_kernel(
    marks_ref, mine_ref, other_ref, gain1_ref, w1_ref, bias1_ref, gain2_ref, first_ref, late_ref
):
    frames, pairs, side, packed = mine_ref.shape
    other = other_ref[CACHE * pairs:].reshape(frames, pairs, side, packed)
    fill_rows(first_ref, 0, 0, mine_ref[...], other, gain1_ref)
    live = frame_flags(marks_ref[...], range(2, frames))

    def store(begin, end, rows):
        late_ref[:, begin:end] = rows

    hide(first_ref, w1_ref, bias1_ref, gain2_ref, 0, frames - 2, 2 * pairs - 2, live, store)


def edge_kernel(
    marks_ref, mine_ref, other_ref, edge_ref, tail_edge_ref, first_ref, late_ref,
    gain1_ref, w1_ref, bias1_ref, gain2_ref, w2_ref, bias2_ref,
    strip_ref, hidden_ref, keep_ref, send_ref, strip, operand,
):
    core = lax.axis_index("wa")
    frames, pairs = mine_ref.shape[:2]
    rows = 2 * pairs
    fill_rows(strip, 0, 2 * core, edge_ref[1][:, None], edge_ref[0][:, None], gain1_ref)
    strip[:, :, pl.ds(2 * (1 - core), 2)] = first_ref[:, :, pl.ds((rows - 2) * core, 2)]
    live = frame_flags(marks_ref[...], range(frames))
    inside = inside_flags(2)

    def store(begin, end, values):
        operand[:, begin:end, pl.ds((rows - 2) * core, 2)] = values

    hide(strip, w1_ref, bias1_ref, gain2_ref, 0, frames - 2, 2, [flag * inside for flag in live[2:]], store)
    operand[:, :, pl.ds(2 * (1 - core), rows - 2)] = late_ref[...]
    fill_rows(strip_ref, 0, 0, tail_edge_ref[1][:, None], tail_edge_ref[0][:, None], gain1_ref)
    strip_ref[:, CACHE:] = strip[:, 0:2, pl.ds(2 * core, 2)]
    hidden_ref[...] = operand[:, 0:2]

    def put(ref):
        def store(frame, row, value):
            ref[frame - CACHE, row] = value
        return store

    def then(start, part, result):
        finish(
            mine_ref, other_ref, live, CACHE + start, (core, pairs - 1), result, (put(keep_ref), put(send_ref))
        )

    convolved(operand, w2_ref, bias2_ref, 0, frames - CACHE, rows - 2, then)


def early_kernel(
    marks_ref, tail_mine_ref, tail_other_ref, mine_ref, other_ref, first_ref, strip_ref, hidden_ref,
    late_keep_ref, late_send_ref, gain1_ref, w1_ref, bias1_ref, gain2_ref, w2_ref, bias2_ref,
    keep_ref, send_ref, plane, operand,
):
    core = lax.axis_index("wa")
    held = mine_ref.shape[1]
    rows = 2 * held
    pairs = tail_mine_ref.shape[0] // CACHE
    live = frame_flags(marks_ref[...], range(CACHE))
    inside = inside_flags(rows)
    earlier = lax.axis_index("tchunk") > 0
    middle, border = 2 * (1 - core), rows * core

    def unpacked(ref):
        return jnp.stack([ref[pl.ds(slot * pairs + core * (pairs - held), held)] for slot in range(CACHE)])

    plane[:, CACHE:, pl.ds(middle, rows)] = first_ref[:, 0:2]
    plane[:, :, pl.ds(border, 2)] = strip_ref[...]
    operand[:, CACHE:] = hidden_ref[...]

    def fill(first, flags):
        def store(begin, end, values):
            operand[:, first + begin:first + end] = values

        flags = [flag * inside for flag in flags]
        hide(plane, w1_ref, bias1_ref, gain2_ref, first, CACHE - first, rows, flags, store)

    @pl.when(earlier)
    def _():
        fill_rows(plane, 0, middle, unpacked(tail_mine_ref), unpacked(tail_other_ref), gain1_ref)
        fill(0, frame_flags(tail_mine_ref[CACHE * pairs], range(CACHE - 2, CACHE)) + live[0:2])

    @pl.when(jnp.logical_not(earlier))
    def _():
        plane[:, 0:CACHE, pl.ds(middle, rows)] = jnp.zeros(
            plane.shape[:1] + (CACHE, rows) + plane.shape[3:], plane.dtype
        )
        operand[:, 0:2] = jnp.zeros(operand.shape[:1] + (2,) + operand.shape[2:], operand.dtype)
        fill(2, live[0:2])

    def put(ref):
        def store(frame, row, value):
            ref[frame, row] = value
        return store

    def then(start, part, result):
        finish(mine_ref, other_ref, live, start, (core, held - 1), result, (put(keep_ref), put(send_ref)))

    convolved(operand, w2_ref, bias2_ref, 0, CACHE, rows - 2, then)
    keep_ref[CACHE:] = late_keep_ref[...]
    send_ref[CACHE:] = late_send_ref[...]


def place_kernel(keep_ref, got_ref, result_ref, arrived):
    core, half = lax.axis_index("wa"), keep_ref.shape[1]
    copies = [
        pltpu.make_async_copy(keep_ref, result_ref.at[:, pl.ds(half * core, half)], arrived.at[0]),
        pltpu.make_async_copy(got_ref, result_ref.at[:, pl.ds(half * (1 - core), half)], arrived.at[1]),
    ]
    for copy in copies:
        copy.start()
    for copy in copies:
        copy.wait()


def shards(features, frame_counts, gain_first, conv_first, bias_first, gain_second, conv_second, bias_second):
    frames, rows, side, channels = features.shape
    pairs, half = rows // 2, rows // 2
    held = half // 2 + 1
    tall, cores, blocks = lax.axis_size("ha"), lax.axis_size("wa"), lax.axis_size("tchunk")
    packed, width, tiles = 3 * LANES, 2 * side, CACHE * held
    bf16 = jnp.bfloat16
    vmem = pl.BlockSpec(memory_space=pltpu.VMEM)
    limit = pltpu.CompilerParams(vmem_limit_bytes=20 * 2**20)
    work = 2 * TAPS**3 * channels * channels * width

    def shape(*extent):
        return jax.ShapeDtypeStruct(extent, bf16)

    def cost(flops, fetched):
        return pl.CostEstimate(flops=flops, bytes_accessed=fetched, transcendentals=0)

    slots = pl.pallas_call(
        slots_kernel,
        out_shape=jax.ShapeDtypeStruct((side, packed), jnp.int32),
        out_specs=vmem,
        compiler_params=limit,
        cost_estimate=cost(2**34, 2**20),
    )()
    slots, frame_counts = lax.optimization_barrier((slots, frame_counts))
    tail, mine, theirs, marks = pl.pallas_call(
        prepare_kernel,
        out_shape=(
            shape(CACHE * pairs + 1, side, packed), shape(frames, held, side, packed),
            shape((CACHE + frames) * held, side, packed), shape(side, packed),
        ),
        in_specs=[pl.BlockSpec(memory_space=pltpu.SMEM), vmem, vmem],
        out_specs=(vmem,) * 4,
        scratch_shapes=[pltpu.VMEM((frames, pairs, side, packed), bf16)],
        compiler_params=limit,
    )(frame_counts, slots, features)

    if blocks > 2:
        tail = joined_tail(tail)
        rest = lax.dynamic_slice_in_dim(
            tail[:-1].reshape(CACHE, pairs, side, packed), (1 - lax.axis_index("wa")) * (pairs - held), held, 1
        )
        theirs = jnp.concatenate([rest.reshape(tiles, side, packed), theirs[tiles:]], axis=0)
    straight, diagonal, across = [], [], []

    def index(block, h, core):
        return (block * tall + h) * cores + core

    for k in range(blocks - 1):
        for h in range(tall):
            for core in range(cores):
                straight.append((index(k, h, core), index(k + 1, h, core)))
    for h in range(tall - 1):
        for k in range(blocks):
            lower, upper = index(k, h, 1), index(k, h + 1, 0)
            across += [(lower, upper), (upper, lower)]
            if k + 1 < blocks:
                lower_next, upper_next = index(k + 1, h, 1), index(k + 1, h + 1, 0)
                diagonal += [(lower, upper_next), (upper, lower_next)]
    axes = ("tchunk", "ha", "wa")
    swap = [(0, 1), (1, 0)]
    tail_mine = lax.ppermute(tail, axes, straight)
    other = lax.ppermute(theirs, "wa", swap)
    tail_edge, own_edge = pl.pallas_call(
        border_kernel,
        out_shape=(shape(2, CACHE, side, packed), shape(2, frames, side, packed)),
        in_specs=[vmem] * 3,
        out_specs=(vmem, vmem),
        compiler_params=limit,
        cost_estimate=cost(2**34, 2**20),
    )(tail, mine, other)
    own_edge = lax.ppermute(own_edge, axes, across)
    tail_edge = lax.ppermute(tail_edge, axes, diagonal)

    weights = (
        gain_first.reshape(1, channels), conv_first, bias_first.reshape(1, channels),
        gain_second.reshape(1, channels), conv_second, bias_second.reshape(1, channels),
    )
    first, late = pl.pallas_call(
        own_kernel,
        out_shape=(shape(3, frames, half + 2, width, LANES), shape(3, frames - 2, half, width, LANES)),
        in_specs=[vmem] * 7,
        out_specs=(vmem,) * 2,
        compiler_params=limit,
        cost_estimate=cost(work * (frames - 2) * half, 4 * 2**20),
    )(marks, mine, other, *weights[:4])
    late, tail_mine = lax.optimization_barrier((late, tail_mine))
    tail_other = lax.ppermute(tail_mine, "wa", swap)
    strip, hidden, keep, send = pl.pallas_call(
        edge_kernel,
        out_shape=(
            shape(3, CACHE + 2, 2, width, LANES), shape(3, 2, half + 2, width, LANES),
            shape(frames - CACHE, half, side, channels), shape(frames - CACHE, half, side, channels),
        ),
        in_specs=[vmem] * 13,
        out_specs=(vmem,) * 4,
        scratch_shapes=[
            pltpu.VMEM((3, frames, 4, width, LANES), bf16),
            pltpu.VMEM((3, frames - 2, half + 2, width, LANES), bf16),
        ],
        compiler_params=limit,
        cost_estimate=cost(work * ((frames - 2) * 2 + (frames - CACHE) * half), 8 * 2**20),
    )(marks, mine, other, own_edge, tail_edge, first, late, *weights)
    keep, send = pl.pallas_call(
        early_kernel,
        out_shape=(shape(frames, half, side, channels), shape(frames, half, side, channels)),
        in_specs=[vmem] * 16,
        out_specs=(vmem, vmem),
        scratch_shapes=[
            pltpu.VMEM((3, CACHE + 2, half + 4, width, LANES), bf16),
            pltpu.VMEM((3, CACHE + 2, half + 2, width, LANES), bf16),
        ],
        compiler_params=limit,
        cost_estimate=cost(work * CACHE * (2 * half + 2), 8 * 2**20),
    )(marks, tail_mine, tail_other, mine, other, first, strip, hidden, keep, send, *weights)
    got = lax.ppermute(send, "wa", swap)
    return pl.pallas_call(
        place_kernel,
        out_shape=shape(*features.shape),
        in_specs=[vmem, vmem],
        out_specs=pl.BlockSpec(memory_space=pltpu.HBM),
        scratch_shapes=[pltpu.SemaphoreType.DMA((2,))],
        compiler_params=limit,
    )(keep, got)


def solution(mesh):
    return jax.shard_map(
        shards,
        mesh=mesh,
        in_specs=(
            P(("grp", "tchunk"), "ha", "wa", None),
            P(("grp", "tchunk")),
            P(), P(), P(), P(), P(), P(),
        ),
        out_specs=P(("grp", "tchunk"), "ha", "wa", None),
        check_vma=False,
    )
```

```python
import jax
import jax.numpy as jnp
from jax import lax
from jax.experimental import pallas as pl
from jax.experimental.pallas import tpu as pltpu
from jax.sharding import PartitionSpec as P

epsilon = 1e-06
CACHE = 4
TAPS = 3
LANES = 128
PRODUCT = 192


def slots_kernel(slots_ref):
    slots_ref[...] = lax.broadcasted_iota(jnp.int32, slots_ref.shape, 0)


def prepare_kernel(total_ref, slots_ref, raw, tail_ref, mine_ref, theirs_ref, marks_ref, pack):
    frames, rows = raw.shape[:2]
    pairs, held = rows // 2, mine_ref.shape[1]
    core = lax.axis_index("wa")
    total = total_ref[0]
    for frame in range(frames):
        for pair in range(pairs):
            first, second = raw[frame, 2 * pair], raw[frame, 2 * pair + 1]
            packed = jnp.concatenate(
                [first[:, :LANES], second[:, :LANES], first[:, LANES:], second[:, LANES:]], axis=-1
            )
            pack[frame, pair] = packed
    for slot in range(CACHE):
        frame = total - CACHE + slot
        value = pack[jnp.maximum(frame, 0)]
        tail_ref[slot * pairs:(slot + 1) * pairs] = jnp.where(frame >= 0, value, jnp.zeros_like(value))
        value = pack[jnp.maximum(frame, 0), pl.ds((1 - core) * (pairs - held), held)]
        theirs_ref[slot * held:(slot + 1) * held] = jnp.where(frame >= 0, value, jnp.zeros_like(value))
    for frame in range(frames):
        start = (CACHE + frame) * held
        value = pack[frame, pl.ds(core * (pairs - held), held)]
        mine_ref[frame] = jnp.where(frame < total, value, jnp.zeros_like(value))
        value = pack[frame, pl.ds((1 - core) * (pairs - held), held)]
        theirs_ref[start:start + held] = jnp.where(frame < total, value, jnp.zeros_like(value))
    slot = slots_ref[...]
    tail_ref[CACHE * pairs] = jnp.where(
        (slot < CACHE) & (total - CACHE + slot >= 0), 1.0, 0.0
    ).astype(tail_ref.dtype)
    marks_ref[...] = jnp.where(slot < total, 1.0, 0.0).astype(marks_ref.dtype)


def joined_tail(tail):
    count = lax.axis_size("tchunk")

    def pushed(value, held):
        return lax.dynamic_slice_in_dim(jnp.concatenate([value, jnp.zeros_like(value)], axis=0), held, CACHE, 0)

    step = 1
    while step < count - 1:
        early = lax.ppermute(tail, "tchunk", [(k, k + step) for k in range(count - step)])
        held = jnp.sum(tail[-1, :CACHE, 0].astype(jnp.int32))
        body = pushed(early[:-1].reshape((CACHE, -1) + tail.shape[1:]), held).reshape(tail[:-1].shape)
        marks = jnp.pad(pushed(early[-1, :CACHE], held), ((0, tail.shape[1] - CACHE), (0, 0)))
        tail = tail + jnp.concatenate([body, marks[None]], axis=0)
        step *= 2
    return tail


def silu(half):
    return half + half * jnp.tanh(half)


def lane_mask():
    return lax.broadcasted_iota(jnp.int32, (1, 1, 1, LANES), 3) < LANES // 2


def gains(gain_ref):
    low, high = 0.5 * gain_ref[:, :LANES], 0.5 * gain_ref[:, LANES:]
    return low.reshape(1, 1, 1, LANES), jnp.concatenate([high, high], axis=-1).reshape(1, 1, 1, LANES)


def rolled(values):
    shape = values.shape
    return pltpu.roll(values.reshape(-1, LANES), LANES // 2, 1).reshape(shape)


def first_rows(left, right, gain_ref, channels):
    raw = jnp.concatenate([left.astype(jnp.float32), right.astype(jnp.float32)], axis=2)
    front, back, high = raw[..., :LANES], raw[..., LANES:2 * LANES], raw[..., 2 * LANES:]
    lower = lane_mask()
    squared = high * high

    def inverse(low, mask):
        total = jnp.sum(low * low + jnp.where(mask, squared, 0.0), axis=-1, keepdims=True)
        return lax.rsqrt(total * (1.0 / channels) + epsilon)

    scale_front, scale_back = inverse(front, lower), inverse(back, jnp.logical_not(lower))
    gain_low, gain_high = gains(gain_ref)
    front = silu(front * scale_front * gain_low)
    back = silu(back * scale_back * gain_low)
    high = silu(high * jnp.where(lower, scale_front, scale_back) * gain_high)
    turned = rolled(high)
    one = [front, jnp.where(lower, high, 0.0), jnp.where(lower, 0.0, turned)]
    two = [back, jnp.where(lower, turned, 0.0), jnp.where(lower, 0.0, high)]
    return [[part.astype(jnp.bfloat16) for part in row] for row in (one, two)]


def second_rows(hidden, flag, gain_ref, channels):
    gain = 0.5 * gain_ref[...].reshape(1, 1, 1, channels)
    total = jnp.sum(hidden * hidden, axis=-1, keepdims=True)
    inverse = lax.rsqrt(total * (1.0 / channels) + epsilon) * flag
    values = silu(hidden * inverse * gain)
    rest = jnp.zeros(values.shape[:-1] + (LANES // 2,), jnp.float32)
    high = jnp.concatenate([values[..., LANES:], rest], axis=-1)
    parts = [values[..., :LANES], high, rolled(high)]
    return jnp.stack([part.astype(jnp.bfloat16) for part in parts])


def convolved(operand, weights_ref, bias_ref, frame, frames, rows, then):
    products = -(-frames * rows * operand.shape[3] // PRODUCT)
    step = -(-frames // products)
    for start in range(0, frames, step):
        count = min(step, frames - start)
        then(start, count, convolved_part(operand, weights_ref, bias_ref, frame + start, count, rows))


def convolved_part(operand, weights_ref, bias_ref, frame, frames, rows):
    width = operand.shape[3]
    channels = weights_ref.shape[-1]
    taps = [(a, i) for a in range(TAPS) for i in range(TAPS)]
    groups = [taps[start:start + 2] for start in range(0, len(taps), 2)]

    def window(tap, part):
        a, i = tap
        value = operand[part, frame + a:frame + a + frames, i:i + rows]
        return value.reshape(frames * rows * width, LANES)

    pieces = []
    for group in groups:
        pieces += [window(tap, 0) for tap in group]
        high = window(group[0], 1)
        pieces.append(high + window(group[1], 2) if len(group) > 1 else high)
    left = jnp.concatenate(pieces, axis=-1)
    products = []
    for j in range(TAPS):
        rights = []
        for group in groups:
            held = [weights_ref[a, i, j] for a, i in group]
            rights += [weight[:LANES] for weight in held] + [weight[LANES:] for weight in held]
        rights.append(jnp.zeros((left.shape[1] - sum(r.shape[0] for r in rights), channels), jnp.bfloat16))
        product = jnp.dot(left, jnp.concatenate(rights, axis=0), preferred_element_type=jnp.float32)
        products.append(product.reshape(frames * rows, width, channels))
    column = lax.broadcasted_iota(jnp.int32, (1, width, 1), 1)
    before = jnp.where(column == 0, 0.0, pltpu.roll(products[0], 1, 1))
    after = jnp.where(column == width - 1, 0.0, pltpu.roll(products[2], width - 1, 1))
    result = products[1] + before + after + bias_ref[...].reshape(1, 1, channels)
    return result.reshape(frames, rows, width, channels)


def halves(core, mine, other):
    return jnp.where(core == 0, mine, other), jnp.where(core == 0, other, mine)


def frame_flags(marks, frames):
    values = marks.astype(jnp.float32)
    return [values[k:k + 1, 0:1].reshape(1, 1, 1, 1) for k in frames]


def fill_rows(operand, frame, row, mine, other, gain_ref):
    left, right = halves(lax.axis_index("wa"), mine, other)
    frames, pairs = mine.shape[:2]
    upper, lower = first_rows(left, right, gain_ref, gain_ref.shape[-1])
    for part in range(len(upper)):
        for pair in range(pairs):
            operand[part, frame:frame + frames, pl.ds(row + 2 * pair, 1)] = upper[part][:, pair:pair + 1]
            operand[part, frame:frame + frames, pl.ds(row + 2 * pair + 1, 1)] = lower[part][:, pair:pair + 1]


def border_kernel(tail_ref, mine_ref, other_ref, tail_edge_ref, own_edge_ref):
    frames, held = mine_ref.shape[:2]
    pairs = tail_ref.shape[0] // CACHE
    core = lax.axis_index("wa")
    pair = core * (held - 1)
    for slot in range(CACHE):
        tail_edge_ref[0, slot] = tail_ref[slot * pairs + core * (pairs - 1)]
        tail_edge_ref[1, slot] = other_ref[slot * held + pair]
    for frame in range(frames):
        own_edge_ref[0, frame] = mine_ref[frame, pair]
        own_edge_ref[1, frame] = other_ref[(CACHE + frame) * held + pair]


def finish(mine_ref, other_ref, live, first, pairs, value, targets):
    _, held, side, _ = mine_ref.shape
    frames, channels = value.shape[0], value.shape[-1]
    start, count = pairs
    near, far = halves(lax.axis_index("wa"), value[:, :, :side], value[:, :, side:])
    for mine, value, target in ((True, near, targets[0]), (False, far, targets[1])):
        for frame in range(frames):
            for k in range(count):
                if mine:
                    raw = mine_ref[first + frame, start + k]
                else:
                    raw = other_ref[(CACHE + first + frame) * held + start + k]
                raw = raw.astype(jnp.float32)
                high = raw[:, 2 * LANES:]
                for row, tail in ((0, high), (1, pltpu.roll(high, LANES // 2, 1))):
                    low = raw[:, row * LANES:(row + 1) * LANES]
                    features = jnp.concatenate([low, tail[:, :channels - LANES]], axis=-1)
                    summed = features + value[frame, 2 * k + row]
                    kept = jnp.where(live[first + frame].reshape(1, 1) > 0.5, summed, 0.0)
                    target(first + frame, 2 * k + row, kept.astype(jnp.bfloat16))


def hide(operand, weights_ref, bias_ref, gain_ref, first, count, rows, flags, store):
    channels = weights_ref.shape[-1]

    def then(begin, part, hidden):
        flag = jnp.concatenate(flags[begin:begin + part], axis=0)
        store(begin, begin + part, second_rows(hidden, flag, gain_ref, channels))

    convolved(operand, weights_ref, bias_ref, first, count, rows, then)


def inside_flags(rows):
    core, place = lax.axis_index("wa"), lax.axis_index("ha")
    inside = jnp.where(core == 0, place > 0, place < lax.axis_size("ha") - 1)
    row = lax.broadcasted_iota(jnp.int32, (1, rows, 1, 1), 1)
    return jnp.where((row == (rows - 1) * core) & jnp.logical_not(inside), 0.0, 1.0)


def own_kernel(
    marks_ref, mine_ref, other_ref, gain1_ref, w1_ref, bias1_ref, gain2_ref, first_ref, late_ref
):
    frames, pairs, side, packed = mine_ref.shape
    other = other_ref[CACHE * pairs:].reshape(frames, pairs, side, packed)
    fill_rows(first_ref, 0, 0, mine_ref[...], other, gain1_ref)
    live = frame_flags(marks_ref[...], range(2, frames))

    def store(begin, end, rows):
        late_ref[:, begin:end] = rows

    hide(first_ref, w1_ref, bias1_ref, gain2_ref, 0, frames - 2, 2 * pairs - 2, live, store)


def tail_edge_kernel(edge_ref, gain_ref, rows_ref):
    fill_rows(rows_ref, 0, 0, edge_ref[1][:, None], edge_ref[0][:, None], gain_ref)


def edge_kernel(
    marks_ref, mine_ref, other_ref, edge_ref, tail_rows_ref, first_ref, late_ref,
    gain1_ref, w1_ref, bias1_ref, gain2_ref, w2_ref, bias2_ref,
    strip_ref, hidden_ref, keep_ref, send_ref, strip, operand,
):
    core = lax.axis_index("wa")
    frames, pairs = mine_ref.shape[:2]
    rows = 2 * pairs
    fill_rows(strip, 0, 2 * core, edge_ref[1][:, None], edge_ref[0][:, None], gain1_ref)
    strip[:, :, pl.ds(2 * (1 - core), 2)] = first_ref[:, :, pl.ds((rows - 2) * core, 2)]
    live = frame_flags(marks_ref[...], range(frames))
    inside = inside_flags(2)

    def store(begin, end, values):
        operand[:, begin:end, pl.ds((rows - 2) * core, 2)] = values

    hide(strip, w1_ref, bias1_ref, gain2_ref, 0, frames - 2, 2, [flag * inside for flag in live[2:]], store)
    operand[:, :, pl.ds(2 * (1 - core), rows - 2)] = late_ref[...]
    strip_ref[:, 0:CACHE] = tail_rows_ref[...]
    strip_ref[:, CACHE:] = strip[:, 0:2, pl.ds(2 * core, 2)]
    hidden_ref[...] = operand[:, 0:2]

    def put(ref):
        def store(frame, row, value):
            ref[frame - CACHE, row] = value
        return store

    def then(start, part, result):
        finish(
            mine_ref, other_ref, live, CACHE + start, (core, pairs - 1), result, (put(keep_ref), put(send_ref))
        )

    convolved(operand, w2_ref, bias2_ref, 0, frames - CACHE, rows - 2, then)


def early_kernel(
    marks_ref, tail_mine_ref, tail_other_ref, mine_ref, other_ref, first_ref, strip_ref, hidden_ref,
    late_keep_ref, late_send_ref, gain1_ref, w1_ref, bias1_ref, gain2_ref, w2_ref, bias2_ref,
    keep_ref, send_ref, plane, operand,
):
    core = lax.axis_index("wa")
    held = mine_ref.shape[1]
    rows = 2 * held
    pairs = tail_mine_ref.shape[0] // CACHE
    live = frame_flags(marks_ref[...], range(CACHE))
    inside = inside_flags(rows)
    earlier = lax.axis_index("tchunk") > 0
    middle, border = 2 * (1 - core), rows * core

    def unpacked(ref):
        return jnp.stack([ref[pl.ds(slot * pairs + core * (pairs - held), held)] for slot in range(CACHE)])

    plane[:, CACHE:, pl.ds(middle, rows)] = first_ref[:, 0:2]
    plane[:, :, pl.ds(border, 2)] = strip_ref[...]
    operand[:, CACHE:] = hidden_ref[...]

    def fill(first, flags):
        def store(begin, end, values):
            operand[:, first + begin:first + end] = values

        flags = [flag * inside for flag in flags]
        hide(plane, w1_ref, bias1_ref, gain2_ref, first, CACHE - first, rows, flags, store)

    @pl.when(earlier)
    def _():
        fill_rows(plane, 0, middle, unpacked(tail_mine_ref), unpacked(tail_other_ref), gain1_ref)
        fill(0, frame_flags(tail_mine_ref[CACHE * pairs], range(CACHE - 2, CACHE)) + live[0:2])

    @pl.when(jnp.logical_not(earlier))
    def _():
        plane[:, 0:CACHE, pl.ds(middle, rows)] = jnp.zeros(
            plane.shape[:1] + (CACHE, rows) + plane.shape[3:], plane.dtype
        )
        operand[:, 0:2] = jnp.zeros(operand.shape[:1] + (2,) + operand.shape[2:], operand.dtype)
        fill(2, live[0:2])

    def put(ref):
        def store(frame, row, value):
            ref[frame, row] = value
        return store

    def then(start, part, result):
        finish(mine_ref, other_ref, live, start, (core, held - 1), result, (put(keep_ref), put(send_ref)))

    convolved(operand, w2_ref, bias2_ref, 0, CACHE, rows - 2, then)
    keep_ref[CACHE:] = late_keep_ref[...]
    send_ref[CACHE:] = late_send_ref[...]


def place_kernel(keep_ref, got_ref, result_ref, arrived):
    core, half = lax.axis_index("wa"), keep_ref.shape[1]
    copies = [
        pltpu.make_async_copy(keep_ref, result_ref.at[:, pl.ds(half * core, half)], arrived.at[0]),
        pltpu.make_async_copy(got_ref, result_ref.at[:, pl.ds(half * (1 - core), half)], arrived.at[1]),
    ]
    for copy in copies:
        copy.start()
    for copy in copies:
        copy.wait()


def shards(features, frame_counts, gain_first, conv_first, bias_first, gain_second, conv_second, bias_second):
    frames, rows, side, channels = features.shape
    pairs, half = rows // 2, rows // 2
    held = half // 2 + 1
    tall, cores, blocks = lax.axis_size("ha"), lax.axis_size("wa"), lax.axis_size("tchunk")
    packed, width, tiles = 3 * LANES, 2 * side, CACHE * held
    bf16 = jnp.bfloat16
    vmem = pl.BlockSpec(memory_space=pltpu.VMEM)
    limit = pltpu.CompilerParams(vmem_limit_bytes=20 * 2**20)
    work = 2 * TAPS**3 * channels * channels * width

    def shape(*extent):
        return jax.ShapeDtypeStruct(extent, bf16)

    def cost(flops, fetched):
        return pl.CostEstimate(flops=flops, bytes_accessed=fetched, transcendentals=0)

    slots = pl.pallas_call(
        slots_kernel,
        out_shape=jax.ShapeDtypeStruct((side, packed), jnp.int32),
        out_specs=vmem,
        compiler_params=limit,
        cost_estimate=cost(2**34, 2**20),
    )()
    slots, frame_counts = lax.optimization_barrier((slots, frame_counts))
    tail, mine, theirs, marks = pl.pallas_call(
        prepare_kernel,
        out_shape=(
            shape(CACHE * pairs + 1, side, packed), shape(frames, held, side, packed),
            shape((CACHE + frames) * held, side, packed), shape(side, packed),
        ),
        in_specs=[pl.BlockSpec(memory_space=pltpu.SMEM), vmem, vmem],
        out_specs=(vmem,) * 4,
        scratch_shapes=[pltpu.VMEM((frames, pairs, side, packed), bf16)],
        compiler_params=limit,
    )(frame_counts, slots, features)

    if blocks > 2:
        tail = joined_tail(tail)
        rest = lax.dynamic_slice_in_dim(
            tail[:-1].reshape(CACHE, pairs, side, packed), (1 - lax.axis_index("wa")) * (pairs - held), held, 1
        )
        theirs = jnp.concatenate([rest.reshape(tiles, side, packed), theirs[tiles:]], axis=0)
    straight, diagonal, across = [], [], []

    def index(block, h, core):
        return (block * tall + h) * cores + core

    for k in range(blocks - 1):
        for h in range(tall):
            for core in range(cores):
                straight.append((index(k, h, core), index(k + 1, h, core)))
    for h in range(tall - 1):
        for k in range(blocks):
            lower, upper = index(k, h, 1), index(k, h + 1, 0)
            across += [(lower, upper), (upper, lower)]
            if k + 1 < blocks:
                lower_next, upper_next = index(k + 1, h, 1), index(k + 1, h + 1, 0)
                diagonal += [(lower, upper_next), (upper, lower_next)]
    axes = ("tchunk", "ha", "wa")
    swap = [(0, 1), (1, 0)]
    tail_mine = lax.ppermute(tail, axes, straight)
    other = lax.ppermute(theirs, "wa", swap)
    tail_edge, own_edge = pl.pallas_call(
        border_kernel,
        out_shape=(shape(2, CACHE, side, packed), shape(2, frames, side, packed)),
        in_specs=[vmem] * 3,
        out_specs=(vmem, vmem),
        compiler_params=limit,
        cost_estimate=cost(2**34, 2**20),
    )(tail, mine, other)
    own_edge = lax.ppermute(own_edge, axes, across)
    tail_edge = lax.ppermute(tail_edge, axes, diagonal)

    weights = (
        gain_first.reshape(1, channels), conv_first, bias_first.reshape(1, channels),
        gain_second.reshape(1, channels), conv_second, bias_second.reshape(1, channels),
    )
    first, late = pl.pallas_call(
        own_kernel,
        out_shape=(shape(3, frames, half + 2, width, LANES), shape(3, frames - 2, half, width, LANES)),
        in_specs=[vmem] * 7,
        out_specs=(vmem,) * 2,
        compiler_params=limit,
        cost_estimate=cost(work * (frames - 2) * half, 4 * 2**20),
    )(marks, mine, other, *weights[:4])
    late, tail_mine, tail_edge = lax.optimization_barrier((late, tail_mine, tail_edge))
    tail_other = lax.ppermute(tail_mine, "wa", swap)
    tail_rows = pl.pallas_call(
        tail_edge_kernel,
        out_shape=shape(3, CACHE, 2, width, LANES),
        in_specs=[vmem] * 2,
        out_specs=vmem,
        compiler_params=limit,
        cost_estimate=cost(2**31, 2**18),
    )(tail_edge, weights[0])
    strip, hidden, keep, send = pl.pallas_call(
        edge_kernel,
        out_shape=(
            shape(3, CACHE + 2, 2, width, LANES), shape(3, 2, half + 2, width, LANES),
            shape(frames - CACHE, half, side, channels), shape(frames - CACHE, half, side, channels),
        ),
        in_specs=[vmem] * 13,
        out_specs=(vmem,) * 4,
        scratch_shapes=[
            pltpu.VMEM((3, frames, 4, width, LANES), bf16),
            pltpu.VMEM((3, frames - 2, half + 2, width, LANES), bf16),
        ],
        compiler_params=limit,
        cost_estimate=cost(work * ((frames - 2) * 2 + (frames - CACHE) * half), 8 * 2**20),
    )(marks, mine, other, own_edge, tail_rows, first, late, *weights)
    keep, send = pl.pallas_call(
        early_kernel,
        out_shape=(shape(frames, half, side, channels), shape(frames, half, side, channels)),
        in_specs=[vmem] * 16,
        out_specs=(vmem, vmem),
        scratch_shapes=[
            pltpu.VMEM((3, CACHE + 2, half + 4, width, LANES), bf16),
            pltpu.VMEM((3, CACHE + 2, half + 2, width, LANES), bf16),
        ],
        compiler_params=limit,
        cost_estimate=cost(work * CACHE * (2 * half + 2), 8 * 2**20),
    )(marks, tail_mine, tail_other, mine, other, first, strip, hidden, keep, send, *weights)
    got = lax.ppermute(send, "wa", swap)
    return pl.pallas_call(
        place_kernel,
        out_shape=shape(*features.shape),
        in_specs=[vmem, vmem],
        out_specs=pl.BlockSpec(memory_space=pltpu.HBM),
        scratch_shapes=[pltpu.SemaphoreType.DMA((2,))],
        compiler_params=limit,
    )(keep, got)


def solution(mesh):
    return jax.shard_map(
        shards,
        mesh=mesh,
        in_specs=(
            P(("grp", "tchunk"), "ha", "wa", None),
            P(("grp", "tchunk")),
            P(), P(), P(), P(), P(), P(),
        ),
        out_specs=P(("grp", "tchunk"), "ha", "wa", None),
        check_vma=False,
    )
```

```python
import jax
import jax.numpy as jnp
from jax import lax
from jax.experimental import pallas as pl
from jax.experimental.pallas import tpu as pltpu
from jax.sharding import PartitionSpec as P

epsilon = 1e-06
CACHE = 4
TAPS = 3
LANES = 128
PRODUCT = 192


def slots_kernel(slots_ref):
    slots_ref[...] = lax.broadcasted_iota(jnp.int32, slots_ref.shape, 0)


def prepare_kernel(total_ref, slots_ref, raw, tail_ref, mine_ref, theirs_ref, marks_ref, pack):
    frames, rows = raw.shape[:2]
    pairs, held = rows // 2, mine_ref.shape[1]
    core = lax.axis_index("wa")
    total = total_ref[0]
    for frame in range(frames):
        for pair in range(pairs):
            first, second = raw[frame, 2 * pair], raw[frame, 2 * pair + 1]
            packed = jnp.concatenate(
                [first[:, :LANES], second[:, :LANES], first[:, LANES:], second[:, LANES:]], axis=-1
            )
            pack[frame, pair] = packed
    for slot in range(CACHE):
        frame = total - CACHE + slot
        value = pack[jnp.maximum(frame, 0)]
        tail_ref[slot * pairs:(slot + 1) * pairs] = jnp.where(frame >= 0, value, jnp.zeros_like(value))
        value = pack[jnp.maximum(frame, 0), pl.ds((1 - core) * (pairs - held), held)]
        theirs_ref[slot * held:(slot + 1) * held] = jnp.where(frame >= 0, value, jnp.zeros_like(value))
    for frame in range(frames):
        start = (CACHE + frame) * held
        value = pack[frame, pl.ds(core * (pairs - held), held)]
        mine_ref[frame] = jnp.where(frame < total, value, jnp.zeros_like(value))
        value = pack[frame, pl.ds((1 - core) * (pairs - held), held)]
        theirs_ref[start:start + held] = jnp.where(frame < total, value, jnp.zeros_like(value))
    slot = slots_ref[...]
    tail_ref[CACHE * pairs] = jnp.where(
        (slot < CACHE) & (total - CACHE + slot >= 0), 1.0, 0.0
    ).astype(tail_ref.dtype)
    marks_ref[...] = jnp.where(slot < total, 1.0, 0.0).astype(marks_ref.dtype)


def joined_tail(tail):
    count = lax.axis_size("tchunk")

    def pushed(value, held):
        return lax.dynamic_slice_in_dim(jnp.concatenate([value, jnp.zeros_like(value)], axis=0), held, CACHE, 0)

    step = 1
    while step < count - 1:
        early = lax.ppermute(tail, "tchunk", [(k, k + step) for k in range(count - step)])
        held = jnp.sum(tail[-1, :CACHE, 0].astype(jnp.int32))
        body = pushed(early[:-1].reshape((CACHE, -1) + tail.shape[1:]), held).reshape(tail[:-1].shape)
        marks = jnp.pad(pushed(early[-1, :CACHE], held), ((0, tail.shape[1] - CACHE), (0, 0)))
        tail = tail + jnp.concatenate([body, marks[None]], axis=0)
        step *= 2
    return tail


def silu(half):
    return half + half * jnp.tanh(half)


def lane_mask():
    return lax.broadcasted_iota(jnp.int32, (1, 1, 1, LANES), 3) < LANES // 2


def gains(gain_ref):
    low, high = 0.5 * gain_ref[:, :LANES], 0.5 * gain_ref[:, LANES:]
    return low.reshape(1, 1, 1, LANES), jnp.concatenate([high, high], axis=-1).reshape(1, 1, 1, LANES)


def rolled(values):
    shape = values.shape
    return pltpu.roll(values.reshape(-1, LANES), LANES // 2, 1).reshape(shape)


def first_rows(left, right, gain_ref, channels):
    raw = jnp.concatenate([left.astype(jnp.float32), right.astype(jnp.float32)], axis=2)
    front, back, high = raw[..., :LANES], raw[..., LANES:2 * LANES], raw[..., 2 * LANES:]
    lower = lane_mask()
    squared = high * high

    def inverse(low, mask):
        total = jnp.sum(low * low + jnp.where(mask, squared, 0.0), axis=-1, keepdims=True)
        return lax.rsqrt(total * (1.0 / channels) + epsilon)

    scale_front, scale_back = inverse(front, lower), inverse(back, jnp.logical_not(lower))
    gain_low, gain_high = gains(gain_ref)
    front = silu(front * scale_front * gain_low)
    back = silu(back * scale_back * gain_low)
    high = silu(high * jnp.where(lower, scale_front, scale_back) * gain_high)
    turned = rolled(high)
    one = [front, jnp.where(lower, high, 0.0), jnp.where(lower, 0.0, turned)]
    two = [back, jnp.where(lower, turned, 0.0), jnp.where(lower, 0.0, high)]
    return [[part.astype(jnp.bfloat16) for part in row] for row in (one, two)]


def second_rows(hidden, flag, gain_ref, channels):
    gain = 0.5 * gain_ref[...].reshape(1, 1, 1, channels)
    total = jnp.sum(hidden * hidden, axis=-1, keepdims=True)
    inverse = lax.rsqrt(total * (1.0 / channels) + epsilon) * flag
    values = silu(hidden * inverse * gain)
    rest = jnp.zeros(values.shape[:-1] + (LANES // 2,), jnp.float32)
    high = jnp.concatenate([values[..., LANES:], rest], axis=-1)
    parts = [values[..., :LANES], high, rolled(high)]
    return jnp.stack([part.astype(jnp.bfloat16) for part in parts])


def convolved(operand, weights_ref, bias_ref, frame, frames, rows, then):
    products = -(-frames * rows * operand.shape[3] // PRODUCT)
    step = -(-frames // products)
    for start in range(0, frames, step):
        count = min(step, frames - start)
        then(start, count, convolved_part(operand, weights_ref, bias_ref, frame + start, count, rows))


def convolved_part(operand, weights_ref, bias_ref, frame, frames, rows):
    width = operand.shape[3]
    channels = weights_ref.shape[-1]
    taps = [(a, i) for a in range(TAPS) for i in range(TAPS)]
    groups = [taps[start:start + 2] for start in range(0, len(taps), 2)]

    def window(tap, part):
        a, i = tap
        value = operand[part, frame + a:frame + a + frames, i:i + rows]
        return value.reshape(frames * rows * width, LANES)

    pieces = []
    for group in groups:
        pieces += [window(tap, 0) for tap in group]
        high = window(group[0], 1)
        pieces.append(high + window(group[1], 2) if len(group) > 1 else high)
    left = jnp.concatenate(pieces, axis=-1)
    products = []
    for j in range(TAPS):
        rights = []
        for group in groups:
            held = [weights_ref[a, i, j] for a, i in group]
            rights += [weight[:LANES] for weight in held] + [weight[LANES:] for weight in held]
        rights.append(jnp.zeros((left.shape[1] - sum(r.shape[0] for r in rights), channels), jnp.bfloat16))
        product = jnp.dot(left, jnp.concatenate(rights, axis=0), preferred_element_type=jnp.float32)
        products.append(product.reshape(frames * rows, width, channels))
    column = lax.broadcasted_iota(jnp.int32, (1, width, 1), 1)
    before = jnp.where(column == 0, 0.0, pltpu.roll(products[0], 1, 1))
    after = jnp.where(column == width - 1, 0.0, pltpu.roll(products[2], width - 1, 1))
    result = products[1] + before + after + bias_ref[...].reshape(1, 1, channels)
    return result.reshape(frames, rows, width, channels)


def halves(core, mine, other):
    return jnp.where(core == 0, mine, other), jnp.where(core == 0, other, mine)


def frame_flags(marks, frames):
    values = marks.astype(jnp.float32)
    return [values[k:k + 1, 0:1].reshape(1, 1, 1, 1) for k in frames]


def fill_rows(operand, frame, row, mine, other, gain_ref):
    left, right = halves(lax.axis_index("wa"), mine, other)
    frames, pairs = mine.shape[:2]
    upper, lower = first_rows(left, right, gain_ref, gain_ref.shape[-1])
    for part in range(len(upper)):
        for pair in range(pairs):
            operand[part, frame:frame + frames, pl.ds(row + 2 * pair, 1)] = upper[part][:, pair:pair + 1]
            operand[part, frame:frame + frames, pl.ds(row + 2 * pair + 1, 1)] = lower[part][:, pair:pair + 1]


def border_kernel(tail_ref, mine_ref, other_ref, tail_edge_ref, own_edge_ref):
    frames, held = mine_ref.shape[:2]
    pairs = tail_ref.shape[0] // CACHE
    core = lax.axis_index("wa")
    pair = core * (held - 1)
    for slot in range(CACHE):
        tail_edge_ref[slot] = tail_ref[slot * pairs + core * (pairs - 1)]
        tail_edge_ref[CACHE + slot] = other_ref[slot * held + pair]
    spare = tail_edge_ref.shape[0] - 2 * CACHE
    tail_edge_ref[2 * CACHE:] = jnp.zeros((spare,) + tail_edge_ref.shape[1:], tail_edge_ref.dtype)
    for frame in range(frames):
        own_edge_ref[0, frame] = mine_ref[frame, pair]
        own_edge_ref[1, frame] = other_ref[(CACHE + frame) * held + pair]


def finish(mine_ref, other_ref, live, first, pairs, value, targets):
    _, held, side, _ = mine_ref.shape
    frames, channels = value.shape[0], value.shape[-1]
    start, count = pairs
    near, far = halves(lax.axis_index("wa"), value[:, :, :side], value[:, :, side:])
    for mine, value, target in ((True, near, targets[0]), (False, far, targets[1])):
        for frame in range(frames):
            for k in range(count):
                if mine:
                    raw = mine_ref[first + frame, start + k]
                else:
                    raw = other_ref[(CACHE + first + frame) * held + start + k]
                raw = raw.astype(jnp.float32)
                high = raw[:, 2 * LANES:]
                for row, tail in ((0, high), (1, pltpu.roll(high, LANES // 2, 1))):
                    low = raw[:, row * LANES:(row + 1) * LANES]
                    features = jnp.concatenate([low, tail[:, :channels - LANES]], axis=-1)
                    summed = features + value[frame, 2 * k + row]
                    kept = jnp.where(live[first + frame].reshape(1, 1) > 0.5, summed, 0.0)
                    target(first + frame, 2 * k + row, kept.astype(jnp.bfloat16))


def hide(operand, weights_ref, bias_ref, gain_ref, first, count, rows, flags, store):
    channels = weights_ref.shape[-1]

    def then(begin, part, hidden):
        flag = jnp.concatenate(flags[begin:begin + part], axis=0)
        store(begin, begin + part, second_rows(hidden, flag, gain_ref, channels))

    convolved(operand, weights_ref, bias_ref, first, count, rows, then)


def inside_flags(rows):
    core, place = lax.axis_index("wa"), lax.axis_index("ha")
    inside = jnp.where(core == 0, place > 0, place < lax.axis_size("ha") - 1)
    row = lax.broadcasted_iota(jnp.int32, (1, rows, 1, 1), 1)
    return jnp.where((row == (rows - 1) * core) & jnp.logical_not(inside), 0.0, 1.0)


def other_rows_kernel(tail_ref, late_ref, rest_ref):
    pairs, held = tail_ref.shape[0] // CACHE, rest_ref.shape[0] // CACHE
    first = (1 - lax.axis_index("wa")) * (pairs - held)
    for slot in range(CACHE):
        rest_ref[slot * held:(slot + 1) * held] = tail_ref[pl.ds(slot * pairs + first, held)]


def own_kernel(
    marks_ref, mine_ref, other_ref, gain1_ref, w1_ref, bias1_ref, gain2_ref, first_ref, late_ref
):
    frames, pairs, side, packed = mine_ref.shape
    other = other_ref[CACHE * pairs:].reshape(frames, pairs, side, packed)
    fill_rows(first_ref, 0, 0, mine_ref[...], other, gain1_ref)
    live = frame_flags(marks_ref[...], range(2, frames))

    def store(begin, end, rows):
        late_ref[:, begin:end] = rows

    hide(first_ref, w1_ref, bias1_ref, gain2_ref, 0, frames - 2, 2 * pairs - 2, live, store)


def edge_kernel(
    marks_ref, mine_ref, other_ref, edge_ref, first_ref, late_ref,
    gain1_ref, w1_ref, bias1_ref, gain2_ref, w2_ref, bias2_ref,
    strip_ref, hidden_ref, keep_ref, send_ref, strip, operand,
):
    core = lax.axis_index("wa")
    frames, pairs = mine_ref.shape[:2]
    rows = 2 * pairs
    fill_rows(strip, 0, 2 * core, edge_ref[1][:, None], edge_ref[0][:, None], gain1_ref)
    strip[:, :, pl.ds(2 * (1 - core), 2)] = first_ref[:, :, pl.ds((rows - 2) * core, 2)]
    live = frame_flags(marks_ref[...], range(frames))
    inside = inside_flags(2)

    def store(begin, end, values):
        operand[:, begin:end, pl.ds((rows - 2) * core, 2)] = values

    hide(strip, w1_ref, bias1_ref, gain2_ref, 0, frames - 2, 2, [flag * inside for flag in live[2:]], store)
    operand[:, :, pl.ds(2 * (1 - core), rows - 2)] = late_ref[...]
    strip_ref[...] = strip[:, 0:2, pl.ds(2 * core, 2)]
    hidden_ref[...] = operand[:, 0:2]

    def put(ref):
        def store(frame, row, value):
            ref[frame - CACHE, row] = value
        return store

    def then(start, part, result):
        finish(
            mine_ref, other_ref, live, CACHE + start, (core, pairs - 1), result, (put(keep_ref), put(send_ref))
        )

    convolved(operand, w2_ref, bias2_ref, 0, frames - CACHE, rows - 2, then)


def early_kernel(
    marks_ref, tail_mine_ref, tail_other_ref, mine_ref, other_ref, edge_ref, first_ref, strip_ref, hidden_ref,
    late_keep_ref, late_send_ref, gain1_ref, w1_ref, bias1_ref, gain2_ref, w2_ref, bias2_ref,
    keep_ref, send_ref, plane, operand,
):
    core = lax.axis_index("wa")
    held = mine_ref.shape[1]
    rows = 2 * held
    pairs = tail_mine_ref.shape[0] // CACHE
    live = frame_flags(marks_ref[...], range(CACHE))
    inside = inside_flags(rows)
    earlier = lax.axis_index("tchunk") > 0
    middle, border = 2 * (1 - core), rows * core

    def unpacked(ref, stride, first):
        return jnp.stack([ref[pl.ds(slot * stride + first, held)] for slot in range(CACHE)])

    plane[:, CACHE:, pl.ds(middle, rows)] = first_ref[:, 0:2]
    plane[:, CACHE:, pl.ds(border, 2)] = strip_ref[...]
    operand[:, CACHE:] = hidden_ref[...]

    def fill(first, flags):
        def store(begin, end, values):
            operand[:, first + begin:first + end] = values

        flags = [flag * inside for flag in flags]
        hide(plane, w1_ref, bias1_ref, gain2_ref, first, CACHE - first, rows, flags, store)

    @pl.when(earlier)
    def _():
        mine = unpacked(tail_mine_ref, pairs, core * (pairs - held))
        fill_rows(plane, 0, middle, mine, unpacked(tail_other_ref, held, 0), gain1_ref)
        mine, other = edge_ref[CACHE:2 * CACHE], edge_ref[0:CACHE]
        fill_rows(plane, 0, border, mine[:, None], other[:, None], gain1_ref)
        fill(0, frame_flags(tail_mine_ref[CACHE * pairs], range(CACHE - 2, CACHE)) + live[0:2])

    @pl.when(jnp.logical_not(earlier))
    def _():
        plane[:, 0:CACHE] = jnp.zeros(plane.shape[:1] + (CACHE,) + plane.shape[2:], plane.dtype)
        operand[:, 0:2] = jnp.zeros(operand.shape[:1] + (2,) + operand.shape[2:], operand.dtype)
        fill(2, live[0:2])

    def put(ref):
        def store(frame, row, value):
            ref[frame, row] = value
        return store

    def then(start, part, result):
        finish(mine_ref, other_ref, live, start, (core, held - 1), result, (put(keep_ref), put(send_ref)))

    convolved(operand, w2_ref, bias2_ref, 0, CACHE, rows - 2, then)
    keep_ref[CACHE:] = late_keep_ref[...]
    send_ref[CACHE:] = late_send_ref[...]


def place_kernel(keep_ref, got_ref, result_ref, arrived):
    core, half = lax.axis_index("wa"), keep_ref.shape[1]
    copies = [
        pltpu.make_async_copy(keep_ref, result_ref.at[:, pl.ds(half * core, half)], arrived.at[0]),
        pltpu.make_async_copy(got_ref, result_ref.at[:, pl.ds(half * (1 - core), half)], arrived.at[1]),
    ]
    for copy in copies:
        copy.start()
    for copy in copies:
        copy.wait()


def shards(features, frame_counts, gain_first, conv_first, bias_first, gain_second, conv_second, bias_second):
    frames, rows, side, channels = features.shape
    pairs, half = rows // 2, rows // 2
    held = half // 2 + 1
    tall, cores, blocks = lax.axis_size("ha"), lax.axis_size("wa"), lax.axis_size("tchunk")
    packed, width, tiles = 3 * LANES, 2 * side, CACHE * held
    bf16 = jnp.bfloat16
    vmem = pl.BlockSpec(memory_space=pltpu.VMEM)
    limit = pltpu.CompilerParams(vmem_limit_bytes=20 * 2**20)
    work = 2 * TAPS**3 * channels * channels * width

    def shape(*extent):
        return jax.ShapeDtypeStruct(extent, bf16)

    def cost(flops, fetched):
        return pl.CostEstimate(flops=flops, bytes_accessed=fetched, transcendentals=0)

    slots = pl.pallas_call(
        slots_kernel,
        out_shape=jax.ShapeDtypeStruct((side, packed), jnp.int32),
        out_specs=vmem,
        compiler_params=limit,
        cost_estimate=cost(2**34, 2**20),
    )()
    slots, frame_counts = lax.optimization_barrier((slots, frame_counts))
    tail, mine, theirs, marks = pl.pallas_call(
        prepare_kernel,
        out_shape=(
            shape(CACHE * pairs + 1, side, packed), shape(frames, held, side, packed),
            shape((CACHE + frames) * held, side, packed), shape(side, packed),
        ),
        in_specs=[pl.BlockSpec(memory_space=pltpu.SMEM), vmem, vmem],
        out_specs=(vmem,) * 4,
        scratch_shapes=[pltpu.VMEM((frames, pairs, side, packed), bf16)],
        compiler_params=limit,
    )(frame_counts, slots, features)

    if blocks > 2:
        tail = joined_tail(tail)
        rest = lax.dynamic_slice_in_dim(
            tail[:-1].reshape(CACHE, pairs, side, packed), (1 - lax.axis_index("wa")) * (pairs - held), held, 1
        )
        theirs = jnp.concatenate([rest.reshape(tiles, side, packed), theirs[tiles:]], axis=0)
    straight, diagonal, across = [], [], []

    def index(block, h, core):
        return (block * tall + h) * cores + core

    for k in range(blocks - 1):
        for h in range(tall):
            for core in range(cores):
                straight.append((index(k, h, core), index(k + 1, h, core)))
    for h in range(tall - 1):
        for k in range(blocks):
            lower, upper = index(k, h, 1), index(k, h + 1, 0)
            across += [(lower, upper), (upper, lower)]
            if k + 1 < blocks:
                lower_next, upper_next = index(k + 1, h, 1), index(k + 1, h + 1, 0)
                diagonal += [(lower, upper_next), (upper, lower_next)]
    axes = ("tchunk", "ha", "wa")
    swap = [(0, 1), (1, 0)]
    tail_mine = lax.ppermute(tail, axes, straight)
    other = lax.ppermute(theirs, "wa", swap)
    tail_edge, own_edge = pl.pallas_call(
        border_kernel,
        out_shape=(shape(tiles + 1, side, packed), shape(2, frames, side, packed)),
        in_specs=[vmem] * 3,
        out_specs=(vmem, vmem),
        compiler_params=limit,
        cost_estimate=cost(2**34, 2**20),
    )(tail, mine, other)
    own_edge = lax.ppermute(own_edge, axes, across)
    tail_edge = lax.ppermute(tail_edge, axes, diagonal)

    weights = (
        gain_first.reshape(1, channels), conv_first, bias_first.reshape(1, channels),
        gain_second.reshape(1, channels), conv_second, bias_second.reshape(1, channels),
    )
    first, late = pl.pallas_call(
        own_kernel,
        out_shape=(shape(3, frames, half + 2, width, LANES), shape(3, frames - 2, half, width, LANES)),
        in_specs=[vmem] * 7,
        out_specs=(vmem,) * 2,
        compiler_params=limit,
        cost_estimate=cost(work * (frames - 2) * half, 4 * 2**20),
    )(marks, mine, other, *weights[:4])
    rest = pl.pallas_call(
        other_rows_kernel,
        out_shape=shape(tiles, side, packed),
        in_specs=[vmem, pl.BlockSpec(memory_space=pl.ANY)],
        out_specs=vmem,
        compiler_params=limit,
        cost_estimate=cost(1, 1),
    )(tail_mine, late)
    tail_other = lax.ppermute(rest, "wa", swap)
    strip, hidden, keep, send = pl.pallas_call(
        edge_kernel,
        out_shape=(
            shape(3, 2, 2, width, LANES), shape(3, 2, half + 2, width, LANES),
            shape(frames - CACHE, half, side, channels), shape(frames - CACHE, half, side, channels),
        ),
        in_specs=[vmem] * 12,
        out_specs=(vmem,) * 4,
        scratch_shapes=[
            pltpu.VMEM((3, frames, 4, width, LANES), bf16),
            pltpu.VMEM((3, frames - 2, half + 2, width, LANES), bf16),
        ],
        compiler_params=limit,
        cost_estimate=cost(2**20, 2**20),
    )(marks, mine, other, own_edge, first, late, *weights)
    keep, send = pl.pallas_call(
        early_kernel,
        out_shape=(shape(frames, half, side, channels), shape(frames, half, side, channels)),
        in_specs=[vmem] * 17,
        out_specs=(vmem, vmem),
        scratch_shapes=[
            pltpu.VMEM((3, CACHE + 2, half + 4, width, LANES), bf16),
            pltpu.VMEM((3, CACHE + 2, half + 2, width, LANES), bf16),
        ],
        compiler_params=limit,
        cost_estimate=cost(work * CACHE * (2 * half + 2), 8 * 2**20),
    )(marks, tail_mine, tail_other, mine, other, tail_edge, first, strip, hidden, keep, send, *weights)
    got = lax.ppermute(send, "wa", swap)
    return pl.pallas_call(
        place_kernel,
        out_shape=shape(*features.shape),
        in_specs=[vmem, vmem],
        out_specs=pl.BlockSpec(memory_space=pltpu.HBM),
        scratch_shapes=[pltpu.SemaphoreType.DMA((2,))],
        compiler_params=limit,
    )(keep, got)


def solution(mesh):
    return jax.shard_map(
        shards,
        mesh=mesh,
        in_specs=(
            P(("grp", "tchunk"), "ha", "wa", None),
            P(("grp", "tchunk")),
            P(), P(), P(), P(), P(), P(),
        ),
        out_specs=P(("grp", "tchunk"), "ha", "wa", None),
        check_vma=False,
    )
```

```python
import jax
import jax.numpy as jnp
from jax import lax
from jax.experimental import pallas as pl
from jax.experimental.pallas import tpu as pltpu
from jax.sharding import PartitionSpec as P

epsilon = 1e-06
CACHE = 4
TAPS = 3
LANES = 128
PRODUCT = 192


def slots_kernel(slots_ref):
    slots_ref[...] = lax.broadcasted_iota(jnp.int32, slots_ref.shape, 0)


def prepare_kernel(total_ref, slots_ref, raw, tail_ref, mine_ref, theirs_ref, marks_ref, pack):
    frames, rows = raw.shape[:2]
    pairs, held = rows // 2, mine_ref.shape[1]
    core = lax.axis_index("wa")
    total = total_ref[0]
    for frame in range(frames):
        for pair in range(pairs):
            first, second = raw[frame, 2 * pair], raw[frame, 2 * pair + 1]
            packed = jnp.concatenate(
                [first[:, :LANES], second[:, :LANES], first[:, LANES:], second[:, LANES:]], axis=-1
            )
            pack[frame, pair] = packed
    for slot in range(CACHE):
        frame = total - CACHE + slot
        value = pack[jnp.maximum(frame, 0)]
        tail_ref[slot * pairs:(slot + 1) * pairs] = jnp.where(frame >= 0, value, jnp.zeros_like(value))
        value = pack[jnp.maximum(frame, 0), pl.ds((1 - core) * (pairs - held), held)]
        theirs_ref[slot * held:(slot + 1) * held] = jnp.where(frame >= 0, value, jnp.zeros_like(value))
    for frame in range(frames):
        start = (CACHE + frame) * held
        value = pack[frame, pl.ds(core * (pairs - held), held)]
        mine_ref[frame] = jnp.where(frame < total, value, jnp.zeros_like(value))
        value = pack[frame, pl.ds((1 - core) * (pairs - held), held)]
        theirs_ref[start:start + held] = jnp.where(frame < total, value, jnp.zeros_like(value))
    slot = slots_ref[...]
    tail_ref[CACHE * pairs] = jnp.where(
        (slot < CACHE) & (total - CACHE + slot >= 0), 1.0, 0.0
    ).astype(tail_ref.dtype)
    marks_ref[...] = jnp.where(slot < total, 1.0, 0.0).astype(marks_ref.dtype)


def joined_tail(tail):
    count = lax.axis_size("tchunk")

    def pushed(value, held):
        return lax.dynamic_slice_in_dim(jnp.concatenate([value, jnp.zeros_like(value)], axis=0), held, CACHE, 0)

    step = 1
    while step < count - 1:
        early = lax.ppermute(tail, "tchunk", [(k, k + step) for k in range(count - step)])
        held = jnp.sum(tail[-1, :CACHE, 0].astype(jnp.int32))
        body = pushed(early[:-1].reshape((CACHE, -1) + tail.shape[1:]), held).reshape(tail[:-1].shape)
        marks = jnp.pad(pushed(early[-1, :CACHE], held), ((0, tail.shape[1] - CACHE), (0, 0)))
        tail = tail + jnp.concatenate([body, marks[None]], axis=0)
        step *= 2
    return tail


def silu(half):
    return half + half * jnp.tanh(half)


def lane_mask():
    return lax.broadcasted_iota(jnp.int32, (1, 1, 1, LANES), 3) < LANES // 2


def gains(gain_ref):
    low, high = 0.5 * gain_ref[:, :LANES], 0.5 * gain_ref[:, LANES:]
    return low.reshape(1, 1, 1, LANES), jnp.concatenate([high, high], axis=-1).reshape(1, 1, 1, LANES)


def rolled(values):
    shape = values.shape
    return pltpu.roll(values.reshape(-1, LANES), LANES // 2, 1).reshape(shape)


def first_rows(left, right, gain_ref, channels):
    raw = jnp.concatenate([left.astype(jnp.float32), right.astype(jnp.float32)], axis=2)
    front, back, high = raw[..., :LANES], raw[..., LANES:2 * LANES], raw[..., 2 * LANES:]
    lower = lane_mask()
    squared = high * high

    def inverse(low, mask):
        total = jnp.sum(low * low + jnp.where(mask, squared, 0.0), axis=-1, keepdims=True)
        return lax.rsqrt(total * (1.0 / channels) + epsilon)

    scale_front, scale_back = inverse(front, lower), inverse(back, jnp.logical_not(lower))
    gain_low, gain_high = gains(gain_ref)
    front = silu(front * scale_front * gain_low)
    back = silu(back * scale_back * gain_low)
    high = silu(high * jnp.where(lower, scale_front, scale_back) * gain_high)
    turned = rolled(high)
    one = [front, jnp.where(lower, high, 0.0), jnp.where(lower, 0.0, turned)]
    two = [back, jnp.where(lower, turned, 0.0), jnp.where(lower, 0.0, high)]
    return [[part.astype(jnp.bfloat16) for part in row] for row in (one, two)]


def second_rows(hidden, flag, gain_ref, channels):
    gain = 0.5 * gain_ref[...].reshape(1, 1, 1, channels)
    total = jnp.sum(hidden * hidden, axis=-1, keepdims=True)
    inverse = lax.rsqrt(total * (1.0 / channels) + epsilon) * flag
    values = silu(hidden * inverse * gain)
    rest = jnp.zeros(values.shape[:-1] + (LANES // 2,), jnp.float32)
    high = jnp.concatenate([values[..., LANES:], rest], axis=-1)
    parts = [values[..., :LANES], high, rolled(high)]
    return jnp.stack([part.astype(jnp.bfloat16) for part in parts])


def convolved(operand, weights_ref, bias_ref, frame, frames, rows, then):
    products = -(-frames * rows * operand.shape[3] // PRODUCT)
    step = -(-frames // products)
    for start in range(0, frames, step):
        count = min(step, frames - start)
        then(start, count, convolved_part(operand, weights_ref, bias_ref, frame + start, count, rows))


def convolved_part(operand, weights_ref, bias_ref, frame, frames, rows):
    width = operand.shape[3]
    channels = weights_ref.shape[-1]
    taps = [(a, i) for a in range(TAPS) for i in range(TAPS)]
    groups = [taps[start:start + 2] for start in range(0, len(taps), 2)]

    def window(tap, part):
        a, i = tap
        value = operand[part, frame + a:frame + a + frames, i:i + rows]
        return value.reshape(frames * rows * width, LANES)

    def operands(groups):
        pieces = []
        for group in groups:
            pieces += [window(tap, 0) for tap in group]
            high = window(group[0], 1)
            pieces.append(high + window(group[1], 2) if len(group) > 1 else high)
        return jnp.concatenate(pieces, axis=-1)

    def weights(groups, j, depth):
        rights = []
        for group in groups:
            held = [weights_ref[a, i, j] for a, i in group]
            rights += [weight[:LANES] for weight in held] + [weight[LANES:] for weight in held]
        rest = depth - sum(right.shape[0] for right in rights)
        if rest:
            rights.append(jnp.zeros((rest, channels), jnp.bfloat16))
        return jnp.concatenate(rights, axis=0)

    half = len(groups) // 2
    parts = [(part, operands(part)) for part in (groups[:half], groups[half:])]
    products = []
    for j in range(TAPS):
        total = None
        for part, left in parts if j % 2 == 0 else parts[::-1]:
            product = jnp.dot(left, weights(part, j, left.shape[1]), preferred_element_type=jnp.float32)
            total = product if total is None else total + product
        products.append(total.reshape(frames * rows, width, channels))
    column = lax.broadcasted_iota(jnp.int32, (1, width, 1), 1)
    before = jnp.where(column == 0, 0.0, pltpu.roll(products[0], 1, 1))
    after = jnp.where(column == width - 1, 0.0, pltpu.roll(products[2], width - 1, 1))
    result = products[1] + before + after + bias_ref[...].reshape(1, 1, channels)
    return result.reshape(frames, rows, width, channels)


def halves(core, mine, other):
    return jnp.where(core == 0, mine, other), jnp.where(core == 0, other, mine)


def frame_flags(marks, frames):
    values = marks.astype(jnp.float32)
    return [values[k:k + 1, 0:1].reshape(1, 1, 1, 1) for k in frames]


def fill_rows(operand, frame, row, mine, other, gain_ref):
    left, right = halves(lax.axis_index("wa"), mine, other)
    frames, pairs = mine.shape[:2]
    upper, lower = first_rows(left, right, gain_ref, gain_ref.shape[-1])
    for part in range(len(upper)):
        for pair in range(pairs):
            operand[part, frame:frame + frames, pl.ds(row + 2 * pair, 1)] = upper[part][:, pair:pair + 1]
            operand[part, frame:frame + frames, pl.ds(row + 2 * pair + 1, 1)] = lower[part][:, pair:pair + 1]


def border_kernel(tail_ref, mine_ref, other_ref, tail_edge_ref, own_edge_ref):
    frames, held = mine_ref.shape[:2]
    pairs = tail_ref.shape[0] // CACHE
    core = lax.axis_index("wa")
    pair = core * (held - 1)
    for slot in range(CACHE):
        tail_edge_ref[slot] = tail_ref[slot * pairs + core * (pairs - 1)]
        tail_edge_ref[CACHE + slot] = other_ref[slot * held + pair]
    spare = tail_edge_ref.shape[0] - 2 * CACHE
    tail_edge_ref[2 * CACHE:] = jnp.zeros((spare,) + tail_edge_ref.shape[1:], tail_edge_ref.dtype)
    for frame in range(frames):
        own_edge_ref[0, frame] = mine_ref[frame, pair]
        own_edge_ref[1, frame] = other_ref[(CACHE + frame) * held + pair]


def finish(mine_ref, other_ref, live, first, pairs, value, targets):
    _, held, side, _ = mine_ref.shape
    frames, channels = value.shape[0], value.shape[-1]
    start, count = pairs
    near, far = halves(lax.axis_index("wa"), value[:, :, :side], value[:, :, side:])
    for mine, value, target in ((True, near, targets[0]), (False, far, targets[1])):
        for frame in range(frames):
            for k in range(count):
                if mine:
                    raw = mine_ref[first + frame, start + k]
                else:
                    raw = other_ref[(CACHE + first + frame) * held + start + k]
                raw = raw.astype(jnp.float32)
                high = raw[:, 2 * LANES:]
                for row, tail in ((0, high), (1, pltpu.roll(high, LANES // 2, 1))):
                    low = raw[:, row * LANES:(row + 1) * LANES]
                    features = jnp.concatenate([low, tail[:, :channels - LANES]], axis=-1)
                    summed = features + value[frame, 2 * k + row]
                    kept = jnp.where(live[first + frame].reshape(1, 1) > 0.5, summed, 0.0)
                    target(first + frame, 2 * k + row, kept.astype(jnp.bfloat16))


def hide(operand, weights_ref, bias_ref, gain_ref, first, count, rows, flags, store):
    channels = weights_ref.shape[-1]

    def then(begin, part, hidden):
        flag = jnp.concatenate(flags[begin:begin + part], axis=0)
        store(begin, begin + part, second_rows(hidden, flag, gain_ref, channels))

    convolved(operand, weights_ref, bias_ref, first, count, rows, then)


def inside_flags(rows):
    core, place = lax.axis_index("wa"), lax.axis_index("ha")
    inside = jnp.where(core == 0, place > 0, place < lax.axis_size("ha") - 1)
    row = lax.broadcasted_iota(jnp.int32, (1, rows, 1, 1), 1)
    return jnp.where((row == (rows - 1) * core) & jnp.logical_not(inside), 0.0, 1.0)


def other_rows_kernel(tail_ref, late_ref, rest_ref):
    pairs, held = tail_ref.shape[0] // CACHE, rest_ref.shape[0] // CACHE
    first = (1 - lax.axis_index("wa")) * (pairs - held)
    for slot in range(CACHE):
        rest_ref[slot * held:(slot + 1) * held] = tail_ref[pl.ds(slot * pairs + first, held)]


def own_kernel(
    marks_ref, mine_ref, other_ref, gain1_ref, w1_ref, bias1_ref, gain2_ref, first_ref, late_ref
):
    frames, pairs, side, packed = mine_ref.shape
    other = other_ref[CACHE * pairs:].reshape(frames, pairs, side, packed)
    fill_rows(first_ref, 0, 0, mine_ref[...], other, gain1_ref)
    live = frame_flags(marks_ref[...], range(2, frames))

    def store(begin, end, rows):
        late_ref[:, begin:end] = rows

    hide(first_ref, w1_ref, bias1_ref, gain2_ref, 0, frames - 2, 2 * pairs - 2, live, store)


def edge_kernel(
    marks_ref, mine_ref, other_ref, edge_ref, first_ref, late_ref,
    gain1_ref, w1_ref, bias1_ref, gain2_ref, w2_ref, bias2_ref,
    strip_ref, hidden_ref, keep_ref, send_ref, strip, operand,
):
    core = lax.axis_index("wa")
    frames, pairs = mine_ref.shape[:2]
    rows = 2 * pairs
    fill_rows(strip, 0, 2 * core, edge_ref[1][:, None], edge_ref[0][:, None], gain1_ref)
    strip[:, :, pl.ds(2 * (1 - core), 2)] = first_ref[:, :, pl.ds((rows - 2) * core, 2)]
    live = frame_flags(marks_ref[...], range(frames))
    inside = inside_flags(2)

    def store(begin, end, values):
        operand[:, begin:end, pl.ds((rows - 2) * core, 2)] = values

    hide(strip, w1_ref, bias1_ref, gain2_ref, 0, frames - 2, 2, [flag * inside for flag in live[2:]], store)
    operand[:, :, pl.ds(2 * (1 - core), rows - 2)] = late_ref[...]
    strip_ref[...] = strip[:, 0:2, pl.ds(2 * core, 2)]
    hidden_ref[...] = operand[:, 0:2]

    def put(ref):
        def store(frame, row, value):
            ref[frame - CACHE, row] = value
        return store

    def then(start, part, result):
        finish(
            mine_ref, other_ref, live, CACHE + start, (core, pairs - 1), result, (put(keep_ref), put(send_ref))
        )

    convolved(operand, w2_ref, bias2_ref, 0, frames - CACHE, rows - 2, then)


def early_kernel(
    marks_ref, tail_mine_ref, tail_other_ref, mine_ref, other_ref, edge_ref, first_ref, strip_ref, hidden_ref,
    late_keep_ref, late_send_ref, gain1_ref, w1_ref, bias1_ref, gain2_ref, w2_ref, bias2_ref,
    keep_ref, send_ref, plane, operand,
):
    core = lax.axis_index("wa")
    held = mine_ref.shape[1]
    rows = 2 * held
    pairs = tail_mine_ref.shape[0] // CACHE
    live = frame_flags(marks_ref[...], range(CACHE))
    inside = inside_flags(rows)
    earlier = lax.axis_index("tchunk") > 0
    middle, border = 2 * (1 - core), rows * core

    def unpacked(ref, stride, first):
        return jnp.stack([ref[pl.ds(slot * stride + first, held)] for slot in range(CACHE)])

    plane[:, CACHE:, pl.ds(middle, rows)] = first_ref[:, 0:2]
    plane[:, CACHE:, pl.ds(border, 2)] = strip_ref[...]
    operand[:, CACHE:] = hidden_ref[...]

    def fill(first, flags):
        def store(begin, end, values):
            operand[:, first + begin:first + end] = values

        flags = [flag * inside for flag in flags]
        hide(plane, w1_ref, bias1_ref, gain2_ref, first, CACHE - first, rows, flags, store)

    @pl.when(earlier)
    def _():
        mine = unpacked(tail_mine_ref, pairs, core * (pairs - held))
        fill_rows(plane, 0, middle, mine, unpacked(tail_other_ref, held, 0), gain1_ref)
        mine, other = edge_ref[CACHE:2 * CACHE], edge_ref[0:CACHE]
        fill_rows(plane, 0, border, mine[:, None], other[:, None], gain1_ref)
        fill(0, frame_flags(tail_mine_ref[CACHE * pairs], range(CACHE - 2, CACHE)) + live[0:2])

    @pl.when(jnp.logical_not(earlier))
    def _():
        plane[:, 0:CACHE] = jnp.zeros(plane.shape[:1] + (CACHE,) + plane.shape[2:], plane.dtype)
        operand[:, 0:2] = jnp.zeros(operand.shape[:1] + (2,) + operand.shape[2:], operand.dtype)
        fill(2, live[0:2])

    def put(ref):
        def store(frame, row, value):
            ref[frame, row] = value
        return store

    def then(start, part, result):
        finish(mine_ref, other_ref, live, start, (core, held - 1), result, (put(keep_ref), put(send_ref)))

    convolved(operand, w2_ref, bias2_ref, 0, CACHE, rows - 2, then)
    keep_ref[CACHE:] = late_keep_ref[...]
    send_ref[CACHE:] = late_send_ref[...]


def place_kernel(keep_ref, got_ref, result_ref, arrived):
    core, half = lax.axis_index("wa"), keep_ref.shape[1]
    copies = [
        pltpu.make_async_copy(keep_ref, result_ref.at[:, pl.ds(half * core, half)], arrived.at[0]),
        pltpu.make_async_copy(got_ref, result_ref.at[:, pl.ds(half * (1 - core), half)], arrived.at[1]),
    ]
    for copy in copies:
        copy.start()
    for copy in copies:
        copy.wait()


def shards(features, frame_counts, gain_first, conv_first, bias_first, gain_second, conv_second, bias_second):
    frames, rows, side, channels = features.shape
    pairs, half = rows // 2, rows // 2
    held = half // 2 + 1
    tall, cores, blocks = lax.axis_size("ha"), lax.axis_size("wa"), lax.axis_size("tchunk")
    packed, width, tiles = 3 * LANES, 2 * side, CACHE * held
    bf16 = jnp.bfloat16
    vmem = pl.BlockSpec(memory_space=pltpu.VMEM)
    limit = pltpu.CompilerParams(vmem_limit_bytes=20 * 2**20)
    work = 2 * TAPS**3 * channels * channels * width

    def shape(*extent):
        return jax.ShapeDtypeStruct(extent, bf16)

    def cost(flops, fetched):
        return pl.CostEstimate(flops=flops, bytes_accessed=fetched, transcendentals=0)

    slots = pl.pallas_call(
        slots_kernel,
        out_shape=jax.ShapeDtypeStruct((side, packed), jnp.int32),
        out_specs=vmem,
        compiler_params=limit,
        cost_estimate=cost(2**34, 2**20),
    )()
    slots, frame_counts = lax.optimization_barrier((slots, frame_counts))
    tail, mine, theirs, marks = pl.pallas_call(
        prepare_kernel,
        out_shape=(
            shape(CACHE * pairs + 1, side, packed), shape(frames, held, side, packed),
            shape((CACHE + frames) * held, side, packed), shape(side, packed),
        ),
        in_specs=[pl.BlockSpec(memory_space=pltpu.SMEM), vmem, vmem],
        out_specs=(vmem,) * 4,
        scratch_shapes=[pltpu.VMEM((frames, pairs, side, packed), bf16)],
        compiler_params=limit,
    )(frame_counts, slots, features)

    if blocks > 2:
        tail = joined_tail(tail)
        rest = lax.dynamic_slice_in_dim(
            tail[:-1].reshape(CACHE, pairs, side, packed), (1 - lax.axis_index("wa")) * (pairs - held), held, 1
        )
        theirs = jnp.concatenate([rest.reshape(tiles, side, packed), theirs[tiles:]], axis=0)
    straight, diagonal, across = [], [], []

    def index(block, h, core):
        return (block * tall + h) * cores + core

    for k in range(blocks - 1):
        for h in range(tall):
            for core in range(cores):
                straight.append((index(k, h, core), index(k + 1, h, core)))
    for h in range(tall - 1):
        for k in range(blocks):
            lower, upper = index(k, h, 1), index(k, h + 1, 0)
            across += [(lower, upper), (upper, lower)]
            if k + 1 < blocks:
                lower_next, upper_next = index(k + 1, h, 1), index(k + 1, h + 1, 0)
                diagonal += [(lower, upper_next), (upper, lower_next)]
    axes = ("tchunk", "ha", "wa")
    swap = [(0, 1), (1, 0)]
    tail_mine = lax.ppermute(tail, axes, straight)
    other = lax.ppermute(theirs, "wa", swap)
    tail_edge, own_edge = pl.pallas_call(
        border_kernel,
        out_shape=(shape(tiles + 1, side, packed), shape(2, frames, side, packed)),
        in_specs=[vmem] * 3,
        out_specs=(vmem, vmem),
        compiler_params=limit,
        cost_estimate=cost(2**34, 2**20),
    )(tail, mine, other)
    own_edge = lax.ppermute(own_edge, axes, across)
    tail_edge = lax.ppermute(tail_edge, axes, diagonal)

    weights = (
        gain_first.reshape(1, channels), conv_first, bias_first.reshape(1, channels),
        gain_second.reshape(1, channels), conv_second, bias_second.reshape(1, channels),
    )
    first, late = pl.pallas_call(
        own_kernel,
        out_shape=(shape(3, frames, half + 2, width, LANES), shape(3, frames - 2, half, width, LANES)),
        in_specs=[vmem] * 7,
        out_specs=(vmem,) * 2,
        compiler_params=limit,
        cost_estimate=cost(work * (frames - 2) * half, 4 * 2**20),
    )(marks, mine, other, *weights[:4])
    rest = pl.pallas_call(
        other_rows_kernel,
        out_shape=shape(tiles, side, packed),
        in_specs=[vmem, pl.BlockSpec(memory_space=pl.ANY)],
        out_specs=vmem,
        compiler_params=limit,
        cost_estimate=cost(1, 1),
    )(tail_mine, late)
    tail_other = lax.ppermute(rest, "wa", swap)
    strip, hidden, keep, send = pl.pallas_call(
        edge_kernel,
        out_shape=(
            shape(3, 2, 2, width, LANES), shape(3, 2, half + 2, width, LANES),
            shape(frames - CACHE, half, side, channels), shape(frames - CACHE, half, side, channels),
        ),
        in_specs=[vmem] * 12,
        out_specs=(vmem,) * 4,
        scratch_shapes=[
            pltpu.VMEM((3, frames, 4, width, LANES), bf16),
            pltpu.VMEM((3, frames - 2, half + 2, width, LANES), bf16),
        ],
        compiler_params=limit,
        cost_estimate=cost(2**20, 2**20),
    )(marks, mine, other, own_edge, first, late, *weights)
    keep, send = pl.pallas_call(
        early_kernel,
        out_shape=(shape(frames, half, side, channels), shape(frames, half, side, channels)),
        in_specs=[vmem] * 17,
        out_specs=(vmem, vmem),
        scratch_shapes=[
            pltpu.VMEM((3, CACHE + 2, half + 4, width, LANES), bf16),
            pltpu.VMEM((3, CACHE + 2, half + 2, width, LANES), bf16),
        ],
        compiler_params=limit,
        cost_estimate=cost(work * CACHE * (2 * half + 2), 8 * 2**20),
    )(marks, tail_mine, tail_other, mine, other, tail_edge, first, strip, hidden, keep, send, *weights)
    got = lax.ppermute(send, "wa", swap)
    return pl.pallas_call(
        place_kernel,
        out_shape=shape(*features.shape),
        in_specs=[vmem, vmem],
        out_specs=pl.BlockSpec(memory_space=pltpu.HBM),
        scratch_shapes=[pltpu.SemaphoreType.DMA((2,))],
        compiler_params=limit,
    )(keep, got)


def solution(mesh):
    return jax.shard_map(
        shards,
        mesh=mesh,
        in_specs=(
            P(("grp", "tchunk"), "ha", "wa", None),
            P(("grp", "tchunk")),
            P(), P(), P(), P(), P(), P(),
        ),
        out_specs=P(("grp", "tchunk"), "ha", "wa", None),
        check_vma=False,
    )
```

```python
import jax
import jax.numpy as jnp
from jax import lax
from jax.experimental import pallas as pl
from jax.experimental.pallas import tpu as pltpu
from jax.sharding import PartitionSpec as P

epsilon = 1e-06
CACHE = 4
TAPS = 3
LANES = 128
PRODUCT = 192


def slots_kernel(slots_ref):
    slots_ref[...] = lax.broadcasted_iota(jnp.int32, slots_ref.shape, 0)


def prepare_kernel(total_ref, slots_ref, raw, tail_ref, mine_ref, theirs_ref, marks_ref, pack):
    frames, rows = raw.shape[:2]
    pairs, held = rows // 2, mine_ref.shape[1]
    core = lax.axis_index("wa")
    total = total_ref[0]
    for frame in range(frames):
        for pair in range(pairs):
            first, second = raw[frame, 2 * pair], raw[frame, 2 * pair + 1]
            packed = jnp.concatenate(
                [first[:, :LANES], second[:, :LANES], first[:, LANES:], second[:, LANES:]], axis=-1
            )
            pack[frame, pair] = packed
    for slot in range(CACHE):
        frame = total - CACHE + slot
        value = pack[jnp.maximum(frame, 0)]
        tail_ref[slot * pairs:(slot + 1) * pairs] = jnp.where(frame >= 0, value, jnp.zeros_like(value))
        value = pack[jnp.maximum(frame, 0), pl.ds((1 - core) * (pairs - held), held)]
        theirs_ref[slot * held:(slot + 1) * held] = jnp.where(frame >= 0, value, jnp.zeros_like(value))
    for frame in range(frames):
        start = (CACHE + frame) * held
        value = pack[frame, pl.ds(core * (pairs - held), held)]
        mine_ref[frame] = jnp.where(frame < total, value, jnp.zeros_like(value))
        value = pack[frame, pl.ds((1 - core) * (pairs - held), held)]
        theirs_ref[start:start + held] = jnp.where(frame < total, value, jnp.zeros_like(value))
    slot = slots_ref[...]
    tail_ref[CACHE * pairs] = jnp.where(
        (slot < CACHE) & (total - CACHE + slot >= 0), 1.0, 0.0
    ).astype(tail_ref.dtype)
    marks_ref[...] = jnp.where(slot < total, 1.0, 0.0).astype(marks_ref.dtype)


def joined_tail(tail):
    count = lax.axis_size("tchunk")

    def pushed(value, held):
        return lax.dynamic_slice_in_dim(jnp.concatenate([value, jnp.zeros_like(value)], axis=0), held, CACHE, 0)

    step = 1
    while step < count - 1:
        early = lax.ppermute(tail, "tchunk", [(k, k + step) for k in range(count - step)])
        held = jnp.sum(tail[-1, :CACHE, 0].astype(jnp.int32))
        body = pushed(early[:-1].reshape((CACHE, -1) + tail.shape[1:]), held).reshape(tail[:-1].shape)
        marks = jnp.pad(pushed(early[-1, :CACHE], held), ((0, tail.shape[1] - CACHE), (0, 0)))
        tail = tail + jnp.concatenate([body, marks[None]], axis=0)
        step *= 2
    return tail


def silu(half):
    return half + half * jnp.tanh(half)


def lane_mask():
    return lax.broadcasted_iota(jnp.int32, (1, 1, 1, LANES), 3) < LANES // 2


def gains(gain_ref):
    low, high = 0.5 * gain_ref[:, :LANES], 0.5 * gain_ref[:, LANES:]
    return low.reshape(1, 1, 1, LANES), jnp.concatenate([high, high], axis=-1).reshape(1, 1, 1, LANES)


def rolled(values):
    shape = values.shape
    return pltpu.roll(values.reshape(-1, LANES), LANES // 2, 1).reshape(shape)


def first_rows(left, right, gain_ref, channels):
    raw = jnp.concatenate([left.astype(jnp.float32), right.astype(jnp.float32)], axis=2)
    front, back, high = raw[..., :LANES], raw[..., LANES:2 * LANES], raw[..., 2 * LANES:]
    lower = lane_mask()
    squared = high * high

    def inverse(low, mask):
        total = jnp.sum(low * low + jnp.where(mask, squared, 0.0), axis=-1, keepdims=True)
        return lax.rsqrt(total * (1.0 / channels) + epsilon)

    scale_front, scale_back = inverse(front, lower), inverse(back, jnp.logical_not(lower))
    gain_low, gain_high = gains(gain_ref)
    front = silu(front * scale_front * gain_low)
    back = silu(back * scale_back * gain_low)
    high = silu(high * jnp.where(lower, scale_front, scale_back) * gain_high)
    turned = rolled(high)
    one = [front, jnp.where(lower, high, 0.0), jnp.where(lower, 0.0, turned)]
    two = [back, jnp.where(lower, turned, 0.0), jnp.where(lower, 0.0, high)]
    return [[part.astype(jnp.bfloat16) for part in row] for row in (one, two)]


def second_rows(hidden, flag, gain_ref, channels):
    gain = 0.5 * gain_ref[...].reshape(1, 1, 1, channels)
    total = jnp.sum(hidden * hidden, axis=-1, keepdims=True)
    inverse = lax.rsqrt(total * (1.0 / channels) + epsilon) * flag
    values = silu(hidden * inverse * gain)
    rest = jnp.zeros(values.shape[:-1] + (LANES // 2,), jnp.float32)
    high = jnp.concatenate([values[..., LANES:], rest], axis=-1)
    parts = [values[..., :LANES], high, rolled(high)]
    return jnp.stack([part.astype(jnp.bfloat16) for part in parts])


def convolved(operand, refs, bias_ref, frame, frames, rows, then):
    products = -(-frames * rows * operand.shape[3] // PRODUCT)
    step = -(-frames // products)
    for start in range(0, frames, step):
        count = min(step, frames - start)
        then(start, count, convolved_part(operand, refs, bias_ref, frame + start, count, rows))


def convolved_part(operand, refs, bias_ref, frame, frames, rows):
    width = operand.shape[3]
    channels = bias_ref.shape[-1]
    taps = [(a, i) for a in range(TAPS) for i in range(TAPS)]
    groups = [taps[start:start + 2] for start in range(0, len(taps), 2)]

    def window(tap, part):
        a, i = tap
        value = operand[part, frame + a:frame + a + frames, i:i + rows]
        return value.reshape(frames * rows * width, LANES)

    def operands(groups):
        pieces = []
        for group in groups:
            pieces += [window(tap, 0) for tap in group]
            high = window(group[0], 1)
            pieces.append(high + window(group[1], 2) if len(group) > 1 else high)
        return jnp.concatenate(pieces, axis=-1)

    def weights(groups, j, depth):
        sides = []
        for ref in refs:
            rights = []
            for group in groups:
                held = [ref[a, i, j] for a, i in group]
                rights += [weight[:LANES] for weight in held] + [weight[LANES:] for weight in held]
            rest = depth - sum(right.shape[0] for right in rights)
            if rest:
                rights.append(jnp.zeros((rest, ref.shape[-1]), jnp.bfloat16))
            sides.append(jnp.concatenate(rights, axis=0))
        return sides[0] if len(sides) == 1 else jnp.concatenate(sides, axis=1)

    half = len(groups) // 2
    parts = [(part, operands(part)) for part in (groups[:half], groups[half:])]
    products = []
    for j in range(TAPS):
        total = None
        for part, left in parts if j % 2 == 0 else parts[::-1]:
            product = jnp.dot(left, weights(part, j, left.shape[1]), preferred_element_type=jnp.float32)
            total = product if total is None else total + product
        products.append(total.reshape(frames * rows, width, channels))
    column = lax.broadcasted_iota(jnp.int32, (1, width, 1), 1)
    before = jnp.where(column == 0, 0.0, pltpu.roll(products[0], 1, 1))
    after = jnp.where(column == width - 1, 0.0, pltpu.roll(products[2], width - 1, 1))
    result = products[1] + before + after + bias_ref[...].reshape(1, 1, channels)
    return result.reshape(frames, rows, width, channels)


def halves(core, mine, other):
    return jnp.where(core == 0, mine, other), jnp.where(core == 0, other, mine)


def frame_flags(marks, frames):
    values = marks.astype(jnp.float32)
    return [values[k:k + 1, 0:1].reshape(1, 1, 1, 1) for k in frames]


def fill_rows(operand, frame, row, mine, other, gain_ref):
    left, right = halves(lax.axis_index("wa"), mine, other)
    frames, pairs = mine.shape[:2]
    upper, lower = first_rows(left, right, gain_ref, gain_ref.shape[-1])
    for part in range(len(upper)):
        for pair in range(pairs):
            operand[part, frame:frame + frames, pl.ds(row + 2 * pair, 1)] = upper[part][:, pair:pair + 1]
            operand[part, frame:frame + frames, pl.ds(row + 2 * pair + 1, 1)] = lower[part][:, pair:pair + 1]


def border_kernel(tail_ref, mine_ref, other_ref, tail_edge_ref, own_edge_ref):
    frames, held = mine_ref.shape[:2]
    pairs = tail_ref.shape[0] // CACHE
    core = lax.axis_index("wa")
    pair = core * (held - 1)
    for slot in range(CACHE):
        tail_edge_ref[slot] = tail_ref[slot * pairs + core * (pairs - 1)]
        tail_edge_ref[CACHE + slot] = other_ref[slot * held + pair]
    spare = tail_edge_ref.shape[0] - 2 * CACHE
    tail_edge_ref[2 * CACHE:] = jnp.zeros((spare,) + tail_edge_ref.shape[1:], tail_edge_ref.dtype)
    for frame in range(frames):
        own_edge_ref[0, frame] = mine_ref[frame, pair]
        own_edge_ref[1, frame] = other_ref[(CACHE + frame) * held + pair]


def finish(mine_ref, other_ref, live, first, pairs, value, targets):
    _, held, side, _ = mine_ref.shape
    frames, channels = value.shape[0], value.shape[-1]
    start, count = pairs
    near, far = halves(lax.axis_index("wa"), value[:, :, :side], value[:, :, side:])
    for mine, value, target in ((True, near, targets[0]), (False, far, targets[1])):
        for frame in range(frames):
            for k in range(count):
                if mine:
                    raw = mine_ref[first + frame, start + k]
                else:
                    raw = other_ref[(CACHE + first + frame) * held + start + k]
                raw = raw.astype(jnp.float32)
                high = raw[:, 2 * LANES:]
                for row, tail in ((0, high), (1, pltpu.roll(high, LANES // 2, 1))):
                    low = raw[:, row * LANES:(row + 1) * LANES]
                    features = jnp.concatenate([low, tail[:, :channels - LANES]], axis=-1)
                    summed = features + value[frame, 2 * k + row]
                    kept = jnp.where(live[first + frame].reshape(1, 1) > 0.5, summed, 0.0)
                    target(first + frame, 2 * k + row, kept.astype(jnp.bfloat16))


def hide(operand, refs, bias_ref, gain_ref, first, count, rows, flags, store):
    channels = bias_ref.shape[-1]

    def then(begin, part, hidden):
        flag = jnp.concatenate(flags[begin:begin + part], axis=0)
        store(begin, begin + part, second_rows(hidden, flag, gain_ref, channels))

    convolved(operand, refs, bias_ref, first, count, rows, then)


def inside_flags(rows):
    core, place = lax.axis_index("wa"), lax.axis_index("ha")
    inside = jnp.where(core == 0, place > 0, place < lax.axis_size("ha") - 1)
    row = lax.broadcasted_iota(jnp.int32, (1, rows, 1, 1), 1)
    return jnp.where((row == (rows - 1) * core) & jnp.logical_not(inside), 0.0, 1.0)


def other_rows_kernel(tail_ref, late_ref, rest_ref):
    pairs, held = tail_ref.shape[0] // CACHE, rest_ref.shape[0] // CACHE
    first = (1 - lax.axis_index("wa")) * (pairs - held)
    for slot in range(CACHE):
        rest_ref[slot * held:(slot + 1) * held] = tail_ref[pl.ds(slot * pairs + first, held)]


def own_kernel(
    marks_ref, mine_ref, other_ref, gain1_ref, w1_ref, bias1_ref, gain2_ref, w2_hbm,
    first_ref, late_ref, low1_ref, high1_ref, low2_ref, high2_ref, arrived,
):
    fetches = []
    for source, low, high in ((w2_hbm, low2_ref, high2_ref), (w1_ref, low1_ref, high1_ref)):
        for target, lanes in ((low, pl.ds(0, LANES)), (high, pl.ds(LANES, source.shape[-1] - LANES))):
            fetches.append(
                pltpu.make_async_copy(source.at[:, :, :, :, lanes], target, arrived.at[len(fetches)])
            )
    for fetch in fetches:
        fetch.start()
    frames, pairs, side, packed = mine_ref.shape
    other = other_ref[CACHE * pairs:].reshape(frames, pairs, side, packed)
    fill_rows(first_ref, 0, 0, mine_ref[...], other, gain1_ref)
    live = frame_flags(marks_ref[...], range(2, frames))

    def store(begin, end, rows):
        late_ref[:, begin:end] = rows

    hide(first_ref, [w1_ref], bias1_ref, gain2_ref, 0, frames - 2, 2 * pairs - 2, live, store)
    for fetch in fetches:
        fetch.wait()


def edge_kernel(
    marks_ref, mine_ref, other_ref, edge_ref, first_ref, late_ref,
    low1_ref, high1_ref, low2_ref, high2_ref, gain1_ref, bias1_ref, gain2_ref, bias2_ref,
    strip_ref, hidden_ref, keep_ref, send_ref, strip, operand,
):
    core = lax.axis_index("wa")
    frames, pairs = mine_ref.shape[:2]
    rows = 2 * pairs
    fill_rows(strip, 0, 2 * core, edge_ref[1][:, None], edge_ref[0][:, None], gain1_ref)
    strip[:, :, pl.ds(2 * (1 - core), 2)] = first_ref[:, :, pl.ds((rows - 2) * core, 2)]
    live = frame_flags(marks_ref[...], range(frames))
    inside = inside_flags(2)

    def store(begin, end, values):
        operand[:, begin:end, pl.ds((rows - 2) * core, 2)] = values

    hide(strip, [low1_ref, high1_ref], bias1_ref, gain2_ref, 0, frames - 2, 2, [flag * inside for flag in live[2:]], store)
    operand[:, :, pl.ds(2 * (1 - core), rows - 2)] = late_ref[...]
    strip_ref[...] = strip[:, 0:2, pl.ds(2 * core, 2)]
    hidden_ref[...] = operand[:, 0:2]

    def put(ref):
        def store(frame, row, value):
            ref[frame - CACHE, row] = value
        return store

    def then(start, part, result):
        finish(
            mine_ref, other_ref, live, CACHE + start, (core, pairs - 1), result, (put(keep_ref), put(send_ref))
        )

    convolved(operand, [low2_ref, high2_ref], bias2_ref, 0, frames - CACHE, rows - 2, then)


def early_kernel(
    marks_ref, tail_mine_ref, tail_other_ref, mine_ref, other_ref, edge_ref, first_ref, strip_ref, hidden_ref,
    late_keep_ref, late_send_ref,
    low1_ref, high1_ref, low2_ref, high2_ref, gain1_ref, bias1_ref, gain2_ref, bias2_ref,
    keep_ref, send_ref, plane, operand,
):
    core = lax.axis_index("wa")
    held = mine_ref.shape[1]
    rows = 2 * held
    pairs = tail_mine_ref.shape[0] // CACHE
    live = frame_flags(marks_ref[...], range(CACHE))
    inside = inside_flags(rows)
    earlier = lax.axis_index("tchunk") > 0
    middle, border = 2 * (1 - core), rows * core

    def unpacked(ref, stride, first):
        return jnp.stack([ref[pl.ds(slot * stride + first, held)] for slot in range(CACHE)])

    plane[:, CACHE:, pl.ds(middle, rows)] = first_ref[:, 0:2]
    plane[:, CACHE:, pl.ds(border, 2)] = strip_ref[...]
    operand[:, CACHE:] = hidden_ref[...]

    def fill(first, flags):
        def store(begin, end, values):
            operand[:, first + begin:first + end] = values

        flags = [flag * inside for flag in flags]
        hide(plane, [low1_ref, high1_ref], bias1_ref, gain2_ref, first, CACHE - first, rows, flags, store)

    @pl.when(earlier)
    def _():
        mine = unpacked(tail_mine_ref, pairs, core * (pairs - held))
        fill_rows(plane, 0, middle, mine, unpacked(tail_other_ref, held, 0), gain1_ref)
        mine, other = edge_ref[CACHE:2 * CACHE], edge_ref[0:CACHE]
        fill_rows(plane, 0, border, mine[:, None], other[:, None], gain1_ref)
        fill(0, frame_flags(tail_mine_ref[CACHE * pairs], range(CACHE - 2, CACHE)) + live[0:2])

    @pl.when(jnp.logical_not(earlier))
    def _():
        plane[:, 0:CACHE] = jnp.zeros(plane.shape[:1] + (CACHE,) + plane.shape[2:], plane.dtype)
        operand[:, 0:2] = jnp.zeros(operand.shape[:1] + (2,) + operand.shape[2:], operand.dtype)
        fill(2, live[0:2])

    def put(ref):
        def store(frame, row, value):
            ref[frame, row] = value
        return store

    def then(start, part, result):
        finish(mine_ref, other_ref, live, start, (core, held - 1), result, (put(keep_ref), put(send_ref)))

    convolved(operand, [low2_ref, high2_ref], bias2_ref, 0, CACHE, rows - 2, then)
    keep_ref[CACHE:] = late_keep_ref[...]
    send_ref[CACHE:] = late_send_ref[...]


def place_kernel(keep_ref, got_ref, result_ref, arrived):
    core, half = lax.axis_index("wa"), keep_ref.shape[1]
    copies = [
        pltpu.make_async_copy(keep_ref, result_ref.at[:, pl.ds(half * core, half)], arrived.at[0]),
        pltpu.make_async_copy(got_ref, result_ref.at[:, pl.ds(half * (1 - core), half)], arrived.at[1]),
    ]
    for copy in copies:
        copy.start()
    for copy in copies:
        copy.wait()


def shards(features, frame_counts, gain_first, conv_first, bias_first, gain_second, conv_second, bias_second):
    frames, rows, side, channels = features.shape
    pairs, half = rows // 2, rows // 2
    held = half // 2 + 1
    tall, cores, blocks = lax.axis_size("ha"), lax.axis_size("wa"), lax.axis_size("tchunk")
    packed, width, tiles = 3 * LANES, 2 * side, CACHE * held
    bf16 = jnp.bfloat16
    vmem = pl.BlockSpec(memory_space=pltpu.VMEM)
    limit = pltpu.CompilerParams(vmem_limit_bytes=20 * 2**20)
    work = 2 * TAPS**3 * channels * channels * width

    def shape(*extent):
        return jax.ShapeDtypeStruct(extent, bf16)

    def cost(flops, fetched):
        return pl.CostEstimate(flops=flops, bytes_accessed=fetched, transcendentals=0)

    slots = pl.pallas_call(
        slots_kernel,
        out_shape=jax.ShapeDtypeStruct((side, packed), jnp.int32),
        out_specs=vmem,
        compiler_params=limit,
        cost_estimate=cost(2**34, 2**20),
    )()
    slots, frame_counts = lax.optimization_barrier((slots, frame_counts))
    tail, mine, theirs, marks = pl.pallas_call(
        prepare_kernel,
        out_shape=(
            shape(CACHE * pairs + 1, side, packed), shape(frames, held, side, packed),
            shape((CACHE + frames) * held, side, packed), shape(side, packed),
        ),
        in_specs=[pl.BlockSpec(memory_space=pltpu.SMEM), vmem, vmem],
        out_specs=(vmem,) * 4,
        scratch_shapes=[pltpu.VMEM((frames, pairs, side, packed), bf16)],
        compiler_params=limit,
    )(frame_counts, slots, features)

    if blocks > 2:
        tail = joined_tail(tail)
        rest = lax.dynamic_slice_in_dim(
            tail[:-1].reshape(CACHE, pairs, side, packed), (1 - lax.axis_index("wa")) * (pairs - held), held, 1
        )
        theirs = jnp.concatenate([rest.reshape(tiles, side, packed), theirs[tiles:]], axis=0)
    straight, diagonal, across = [], [], []

    def index(block, h, core):
        return (block * tall + h) * cores + core

    for k in range(blocks - 1):
        for h in range(tall):
            for core in range(cores):
                straight.append((index(k, h, core), index(k + 1, h, core)))
    for h in range(tall - 1):
        for k in range(blocks):
            lower, upper = index(k, h, 1), index(k, h + 1, 0)
            across += [(lower, upper), (upper, lower)]
            if k + 1 < blocks:
                lower_next, upper_next = index(k + 1, h, 1), index(k + 1, h + 1, 0)
                diagonal += [(lower, upper_next), (upper, lower_next)]
    axes = ("tchunk", "ha", "wa")
    swap = [(0, 1), (1, 0)]
    tail_mine = lax.ppermute(tail, axes, straight)
    other = lax.ppermute(theirs, "wa", swap)
    tail_edge, own_edge = pl.pallas_call(
        border_kernel,
        out_shape=(shape(tiles + 1, side, packed), shape(2, frames, side, packed)),
        in_specs=[vmem] * 3,
        out_specs=(vmem, vmem),
        compiler_params=limit,
        cost_estimate=cost(2**34, 2**20),
    )(tail, mine, other)
    own_edge = lax.ppermute(own_edge, axes, across)
    tail_edge = lax.ppermute(tail_edge, axes, diagonal)

    gain1, gain2 = gain_first.reshape(1, channels), gain_second.reshape(1, channels)
    bias1, bias2 = bias_first.reshape(1, channels), bias_second.reshape(1, channels)
    low, high = shape(*conv_first.shape[:-1], LANES), shape(*conv_first.shape[:-1], channels - LANES)
    first, late, *cut = pl.pallas_call(
        own_kernel,
        out_shape=(
            shape(3, frames, half + 2, width, LANES), shape(3, frames - 2, half, width, LANES), low, high, low, high
        ),
        in_specs=[vmem] * 7 + [pl.BlockSpec(memory_space=pltpu.HBM)],
        out_specs=(vmem,) * 6,
        scratch_shapes=[pltpu.SemaphoreType.DMA((4,))],
        compiler_params=limit,
        cost_estimate=cost(work * (frames - 2) * half, 4 * 2**20),
    )(
        marks, mine, other, gain1, conv_first, bias1, gain2,
        pltpu.with_memory_space_constraint(conv_second, pltpu.HBM),
    )
    weights = (*cut, gain1, bias1, gain2, bias2)
    rest = pl.pallas_call(
        other_rows_kernel,
        out_shape=shape(tiles, side, packed),
        in_specs=[vmem, pl.BlockSpec(memory_space=pl.ANY)],
        out_specs=vmem,
        compiler_params=limit,
        cost_estimate=cost(1, 1),
    )(tail_mine, late)
    tail_other = lax.ppermute(rest, "wa", swap)
    strip, hidden, keep, send = pl.pallas_call(
        edge_kernel,
        out_shape=(
            shape(3, 2, 2, width, LANES), shape(3, 2, half + 2, width, LANES),
            shape(frames - CACHE, half, side, channels), shape(frames - CACHE, half, side, channels),
        ),
        in_specs=[vmem] * 14,
        out_specs=(vmem,) * 4,
        scratch_shapes=[
            pltpu.VMEM((3, frames, 4, width, LANES), bf16),
            pltpu.VMEM((3, frames - 2, half + 2, width, LANES), bf16),
        ],
        compiler_params=limit,
        cost_estimate=cost(2**20, 2**20),
    )(marks, mine, other, own_edge, first, late, *weights)
    keep, send = pl.pallas_call(
        early_kernel,
        out_shape=(shape(frames, half, side, channels), shape(frames, half, side, channels)),
        in_specs=[vmem] * 19,
        out_specs=(vmem, vmem),
        scratch_shapes=[
            pltpu.VMEM((3, CACHE + 2, half + 4, width, LANES), bf16),
            pltpu.VMEM((3, CACHE + 2, half + 2, width, LANES), bf16),
        ],
        compiler_params=limit,
        cost_estimate=cost(work * CACHE * (2 * half + 2), 8 * 2**20),
    )(marks, tail_mine, tail_other, mine, other, tail_edge, first, strip, hidden, keep, send, *weights)
    got = lax.ppermute(send, "wa", swap)
    return pl.pallas_call(
        place_kernel,
        out_shape=shape(*features.shape),
        in_specs=[vmem, vmem],
        out_specs=pl.BlockSpec(memory_space=pltpu.HBM),
        scratch_shapes=[pltpu.SemaphoreType.DMA((2,))],
        compiler_params=limit,
    )(keep, got)


def solution(mesh):
    return jax.shard_map(
        shards,
        mesh=mesh,
        in_specs=(
            P(("grp", "tchunk"), "ha", "wa", None),
            P(("grp", "tchunk")),
            P(), P(), P(), P(), P(), P(),
        ),
        out_specs=P(("grp", "tchunk"), "ha", "wa", None),
        check_vma=False,
    )
```

```python
import jax
import jax.numpy as jnp
from jax import lax
from jax.experimental import pallas as pl
from jax.experimental.pallas import tpu as pltpu
from jax.sharding import PartitionSpec as P

epsilon = 1e-06
CACHE = 4
TAPS = 3
LANES = 128
PRODUCT = 192


def slots_kernel(slots_ref):
    slots_ref[...] = lax.broadcasted_iota(jnp.int32, slots_ref.shape, 0)


def prepare_kernel(total_ref, slots_ref, raw, tail_ref, mine_ref, theirs_ref, marks_ref, pack):
    frames, rows = raw.shape[:2]
    pairs, held = rows // 2, mine_ref.shape[1]
    core = lax.axis_index("wa")
    total = total_ref[0]
    for frame in range(frames):
        for pair in range(pairs):
            first, second = raw[frame, 2 * pair], raw[frame, 2 * pair + 1]
            packed = jnp.concatenate(
                [first[:, :LANES], second[:, :LANES], first[:, LANES:], second[:, LANES:]], axis=-1
            )
            pack[frame, pair] = packed
    for slot in range(CACHE):
        frame = total - CACHE + slot
        value = pack[jnp.maximum(frame, 0)]
        tail_ref[slot * pairs:(slot + 1) * pairs] = jnp.where(frame >= 0, value, jnp.zeros_like(value))
        value = pack[jnp.maximum(frame, 0), pl.ds((1 - core) * (pairs - held), held)]
        theirs_ref[slot * held:(slot + 1) * held] = jnp.where(frame >= 0, value, jnp.zeros_like(value))
    for frame in range(frames):
        start = (CACHE + frame) * held
        value = pack[frame, pl.ds(core * (pairs - held), held)]
        mine_ref[frame] = jnp.where(frame < total, value, jnp.zeros_like(value))
        value = pack[frame, pl.ds((1 - core) * (pairs - held), held)]
        theirs_ref[start:start + held] = jnp.where(frame < total, value, jnp.zeros_like(value))
    slot = slots_ref[...]
    tail_ref[CACHE * pairs] = jnp.where(
        (slot < CACHE) & (total - CACHE + slot >= 0), 1.0, 0.0
    ).astype(tail_ref.dtype)
    marks_ref[...] = jnp.where(slot < total, 1.0, 0.0).astype(marks_ref.dtype)


def joined_tail(tail):
    count = lax.axis_size("tchunk")

    def pushed(value, held):
        return lax.dynamic_slice_in_dim(jnp.concatenate([value, jnp.zeros_like(value)], axis=0), held, CACHE, 0)

    step = 1
    while step < count - 1:
        early = lax.ppermute(tail, "tchunk", [(k, k + step) for k in range(count - step)])
        held = jnp.sum(tail[-1, :CACHE, 0].astype(jnp.int32))
        body = pushed(early[:-1].reshape((CACHE, -1) + tail.shape[1:]), held).reshape(tail[:-1].shape)
        marks = jnp.pad(pushed(early[-1, :CACHE], held), ((0, tail.shape[1] - CACHE), (0, 0)))
        tail = tail + jnp.concatenate([body, marks[None]], axis=0)
        step *= 2
    return tail


def silu(half):
    return half + half * jnp.tanh(half)


def lane_mask():
    return lax.broadcasted_iota(jnp.int32, (1, 1, 1, LANES), 3) < LANES // 2


def gains(gain_ref):
    low, high = 0.5 * gain_ref[:, :LANES], 0.5 * gain_ref[:, LANES:]
    return low.reshape(1, 1, 1, LANES), jnp.concatenate([high, high], axis=-1).reshape(1, 1, 1, LANES)


def rolled(values):
    shape = values.shape
    return pltpu.roll(values.reshape(-1, LANES), LANES // 2, 1).reshape(shape)


def first_rows(left, right, gain_ref, channels):
    raw = jnp.concatenate([left.astype(jnp.float32), right.astype(jnp.float32)], axis=2)
    front, back, high = raw[..., :LANES], raw[..., LANES:2 * LANES], raw[..., 2 * LANES:]
    lower = lane_mask()
    squared = high * high

    def inverse(low, mask):
        total = jnp.sum(low * low + jnp.where(mask, squared, 0.0), axis=-1, keepdims=True)
        return lax.rsqrt(total * (1.0 / channels) + epsilon)

    scale_front, scale_back = inverse(front, lower), inverse(back, jnp.logical_not(lower))
    gain_low, gain_high = gains(gain_ref)
    front = silu(front * scale_front * gain_low)
    back = silu(back * scale_back * gain_low)
    high = silu(high * jnp.where(lower, scale_front, scale_back) * gain_high)
    turned = rolled(high)
    one = [front, jnp.where(lower, high, 0.0), jnp.where(lower, 0.0, turned)]
    two = [back, jnp.where(lower, turned, 0.0), jnp.where(lower, 0.0, high)]
    return [[part.astype(jnp.bfloat16) for part in row] for row in (one, two)]


def second_rows(hidden, flag, gain_ref, channels):
    gain = 0.5 * gain_ref[...].reshape(1, 1, 1, channels)
    total = jnp.sum(hidden * hidden, axis=-1, keepdims=True)
    inverse = lax.rsqrt(total * (1.0 / channels) + epsilon) * flag
    values = silu(hidden * inverse * gain)
    rest = jnp.zeros(values.shape[:-1] + (LANES // 2,), jnp.float32)
    high = jnp.concatenate([values[..., LANES:], rest], axis=-1)
    parts = [values[..., :LANES], high, rolled(high)]
    return jnp.stack([part.astype(jnp.bfloat16) for part in parts])


def in_turn(steps):
    waiting = None
    for product, then in steps:
        result = product()
        if waiting:
            waiting[1](waiting[0])
        waiting = (result, then)
    waiting[1](waiting[0])


def convolved(operand, weights_ref, bias_ref, frame, frames, rows, then):
    products = -(-frames * rows * operand.shape[3] // PRODUCT)
    step = -(-frames // products)

    def part(start):
        count = min(step, frames - start)
        return (
            lambda: convolved_part(operand, weights_ref, bias_ref, frame + start, count, rows),
            lambda result: then(start, count, result),
        )

    return [part(start) for start in range(0, frames, step)]


def convolved_part(operand, weights_ref, bias_ref, frame, frames, rows):
    width = operand.shape[3]
    channels = weights_ref.shape[-1]
    taps = [(a, i) for a in range(TAPS) for i in range(TAPS)]
    groups = [taps[start:start + 2] for start in range(0, len(taps), 2)]

    def window(tap, part):
        a, i = tap
        value = operand[part, frame + a:frame + a + frames, i:i + rows]
        return value.reshape(frames * rows * width, LANES)

    def operands(groups):
        pieces = []
        for group in groups:
            pieces += [window(tap, 0) for tap in group]
            high = window(group[0], 1)
            pieces.append(high + window(group[1], 2) if len(group) > 1 else high)
        return jnp.concatenate(pieces, axis=-1)

    def weights(groups, j, depth):
        rights = []
        for group in groups:
            held = [weights_ref[a, i, j] for a, i in group]
            rights += [weight[:LANES] for weight in held] + [weight[LANES:] for weight in held]
        rest = depth - sum(right.shape[0] for right in rights)
        if rest:
            rights.append(jnp.zeros((rest, channels), jnp.bfloat16))
        return jnp.concatenate(rights, axis=0)

    half = len(groups) // 2
    parts = [(part, operands(part)) for part in (groups[:half], groups[half:])]
    products = []
    for j in range(TAPS):
        total = None
        for part, left in parts if j % 2 == 0 else parts[::-1]:
            product = jnp.dot(left, weights(part, j, left.shape[1]), preferred_element_type=jnp.float32)
            total = product if total is None else total + product
        products.append(total.reshape(frames * rows, width, channels))
    column = lax.broadcasted_iota(jnp.int32, (1, width, 1), 1)
    before = jnp.where(column == 0, 0.0, pltpu.roll(products[0], 1, 1))
    after = jnp.where(column == width - 1, 0.0, pltpu.roll(products[2], width - 1, 1))
    result = products[1] + before + after + bias_ref[...].reshape(1, 1, channels)
    return result.reshape(frames, rows, width, channels)


def halves(core, mine, other):
    return jnp.where(core == 0, mine, other), jnp.where(core == 0, other, mine)


def frame_flags(marks, frames):
    values = marks.astype(jnp.float32)
    return [values[k:k + 1, 0:1].reshape(1, 1, 1, 1) for k in frames]


def fill_rows(operand, frame, row, mine, other, gain_ref):
    left, right = halves(lax.axis_index("wa"), mine, other)
    frames, pairs = mine.shape[:2]
    upper, lower = first_rows(left, right, gain_ref, gain_ref.shape[-1])
    for part in range(len(upper)):
        for pair in range(pairs):
            operand[part, frame:frame + frames, pl.ds(row + 2 * pair, 1)] = upper[part][:, pair:pair + 1]
            operand[part, frame:frame + frames, pl.ds(row + 2 * pair + 1, 1)] = lower[part][:, pair:pair + 1]


def border_kernel(tail_ref, mine_ref, other_ref, tail_edge_ref, own_edge_ref):
    frames, held = mine_ref.shape[:2]
    pairs = tail_ref.shape[0] // CACHE
    core = lax.axis_index("wa")
    pair = core * (held - 1)
    for slot in range(CACHE):
        tail_edge_ref[slot] = tail_ref[slot * pairs + core * (pairs - 1)]
        tail_edge_ref[CACHE + slot] = other_ref[slot * held + pair]
    spare = tail_edge_ref.shape[0] - 2 * CACHE
    tail_edge_ref[2 * CACHE:] = jnp.zeros((spare,) + tail_edge_ref.shape[1:], tail_edge_ref.dtype)
    for frame in range(frames):
        own_edge_ref[0, frame] = mine_ref[frame, pair]
        own_edge_ref[1, frame] = other_ref[(CACHE + frame) * held + pair]


def finish(mine_ref, other_ref, live, first, pairs, value, targets):
    _, held, side, _ = mine_ref.shape
    frames, channels = value.shape[0], value.shape[-1]
    start, count = pairs
    near, far = halves(lax.axis_index("wa"), value[:, :, :side], value[:, :, side:])
    for mine, value, target in ((True, near, targets[0]), (False, far, targets[1])):
        for frame in range(frames):
            for k in range(count):
                if mine:
                    raw = mine_ref[first + frame, start + k]
                else:
                    raw = other_ref[(CACHE + first + frame) * held + start + k]
                raw = raw.astype(jnp.float32)
                high = raw[:, 2 * LANES:]
                for row, tail in ((0, high), (1, pltpu.roll(high, LANES // 2, 1))):
                    low = raw[:, row * LANES:(row + 1) * LANES]
                    features = jnp.concatenate([low, tail[:, :channels - LANES]], axis=-1)
                    summed = features + value[frame, 2 * k + row]
                    kept = jnp.where(live[first + frame].reshape(1, 1) > 0.5, summed, 0.0)
                    target(first + frame, 2 * k + row, kept.astype(jnp.bfloat16))


def hide(operand, weights_ref, bias_ref, gain_ref, first, count, rows, flags, store):
    channels = weights_ref.shape[-1]

    def then(begin, part, hidden):
        flag = jnp.concatenate(flags[begin:begin + part], axis=0)
        store(begin, begin + part, second_rows(hidden, flag, gain_ref, channels))

    return convolved(operand, weights_ref, bias_ref, first, count, rows, then)


def inside_flags(rows):
    core, place = lax.axis_index("wa"), lax.axis_index("ha")
    inside = jnp.where(core == 0, place > 0, place < lax.axis_size("ha") - 1)
    row = lax.broadcasted_iota(jnp.int32, (1, rows, 1, 1), 1)
    return jnp.where((row == (rows - 1) * core) & jnp.logical_not(inside), 0.0, 1.0)


def other_rows_kernel(tail_ref, late_ref, rest_ref):
    pairs, held = tail_ref.shape[0] // CACHE, rest_ref.shape[0] // CACHE
    first = (1 - lax.axis_index("wa")) * (pairs - held)
    for slot in range(CACHE):
        rest_ref[slot * held:(slot + 1) * held] = tail_ref[pl.ds(slot * pairs + first, held)]


def own_kernel(
    marks_ref, mine_ref, other_ref, gain1_ref, w1_ref, bias1_ref, gain2_ref, first_ref, late_ref
):
    frames, pairs, side, packed = mine_ref.shape
    live = frame_flags(marks_ref[...], range(2, frames))

    def fill(start, end):
        other = other_ref[(CACHE + start) * pairs:(CACHE + end) * pairs].reshape(end - start, pairs, side, packed)
        fill_rows(first_ref, start, 0, mine_ref[start:end], other, gain1_ref)

    def store(begin, end, rows):
        late_ref[:, begin:end] = rows

    steps = hide(first_ref, w1_ref, bias1_ref, gain2_ref, 0, frames - 2, 2 * pairs - 2, live, store)
    half = -(-(frames - 2) // len(steps)) + 2
    fill(0, half)
    product, then = steps[0]
    held = product()
    fill(half, frames)
    in_turn([(lambda: held, then)] + steps[1:])


def edge_kernel(
    marks_ref, mine_ref, other_ref, edge_ref, first_ref, late_ref,
    gain1_ref, w1_ref, bias1_ref, gain2_ref, w2_ref, bias2_ref,
    strip_ref, hidden_ref, keep_ref, send_ref, strip, operand,
):
    core = lax.axis_index("wa")
    frames, pairs = mine_ref.shape[:2]
    rows = 2 * pairs
    late = frames - CACHE
    outward, inward = pl.ds(2 * core, 2), pl.ds(2 * (1 - core), 2)
    fill_rows(strip, 0, 2 * core, edge_ref[1][:, None], edge_ref[0][:, None], gain1_ref)
    strip[:, :, inward] = first_ref[:, :, pl.ds((rows - 2) * core, 2)]
    operand[:, :, inward] = late_ref[:, :, pl.ds((rows - 4) * core, 2)]
    live = frame_flags(marks_ref[...], range(frames))
    inside = inside_flags(2)

    def store(begin, end, values):
        operand[:, begin:end, outward] = values

    def finished(start_row, pair, count):
        def put(ref):
            def store(frame, row, value):
                ref[frame - CACHE, start_row + row] = value
            return store

        def then(start, part, result):
            targets = (put(keep_ref), put(send_ref))
            finish(mine_ref, other_ref, live, CACHE + start, (pair, count), result, targets)

        return then

    flags = [flag * inside for flag in live[2:]]
    middle, border = finished(2 * (1 - core), 1, pairs - 2), finished((rows - 4) * core, (pairs - 1) * core, 1)
    in_turn(
        hide(strip, w1_ref, bias1_ref, gain2_ref, 0, frames - 2, 2, flags, store)
        + convolved(late_ref, w2_ref, bias2_ref, 0, late, rows - 4, middle)
        + convolved(operand, w2_ref, bias2_ref, 0, late, 2, border)
    )
    strip_ref[...] = strip[:, 0:2, outward]
    hidden_ref[:, :, pl.ds(2 * (1 - core), rows - 2)] = late_ref[:, 0:2]
    hidden_ref[:, :, pl.ds((rows - 2) * core, 2)] = operand[:, 0:2, outward]


def early_kernel(
    marks_ref, tail_mine_ref, tail_other_ref, mine_ref, other_ref, edge_ref, first_ref, strip_ref, hidden_ref,
    late_keep_ref, late_send_ref, gain1_ref, w1_ref, bias1_ref, gain2_ref, w2_ref, bias2_ref,
    keep_ref, send_ref, plane, operand,
):
    core = lax.axis_index("wa")
    held = mine_ref.shape[1]
    rows = 2 * held
    pairs = tail_mine_ref.shape[0] // CACHE
    live = frame_flags(marks_ref[...], range(CACHE))
    inside = inside_flags(rows)
    earlier = lax.axis_index("tchunk") > 0
    middle, border = 2 * (1 - core), rows * core

    def unpacked(ref, stride, first):
        return jnp.stack([ref[pl.ds(slot * stride + first, held)] for slot in range(CACHE)])

    plane[:, CACHE:, pl.ds(middle, rows)] = first_ref[:, 0:2]
    plane[:, CACHE:, pl.ds(border, 2)] = strip_ref[...]
    operand[:, CACHE:] = hidden_ref[...]

    def fill(first, flags):
        def store(begin, end, values):
            operand[:, first + begin:first + end] = values

        flags = [flag * inside for flag in flags]
        in_turn(hide(plane, w1_ref, bias1_ref, gain2_ref, first, CACHE - first, rows, flags, store))

    @pl.when(earlier)
    def _():
        mine = unpacked(tail_mine_ref, pairs, core * (pairs - held))
        fill_rows(plane, 0, middle, mine, unpacked(tail_other_ref, held, 0), gain1_ref)
        mine, other = edge_ref[CACHE:2 * CACHE], edge_ref[0:CACHE]
        fill_rows(plane, 0, border, mine[:, None], other[:, None], gain1_ref)
        fill(0, frame_flags(tail_mine_ref[CACHE * pairs], range(CACHE - 2, CACHE)) + live[0:2])

    @pl.when(jnp.logical_not(earlier))
    def _():
        plane[:, 0:CACHE] = jnp.zeros(plane.shape[:1] + (CACHE,) + plane.shape[2:], plane.dtype)
        operand[:, 0:2] = jnp.zeros(operand.shape[:1] + (2,) + operand.shape[2:], operand.dtype)
        fill(2, live[0:2])

    def put(ref):
        def store(frame, row, value):
            ref[frame, row] = value
        return store

    def then(start, part, result):
        finish(mine_ref, other_ref, live, start, (core, held - 1), result, (put(keep_ref), put(send_ref)))

    in_turn(convolved(operand, w2_ref, bias2_ref, 0, CACHE, rows - 2, then))
    keep_ref[CACHE:] = late_keep_ref[...]
    send_ref[CACHE:] = late_send_ref[...]


def place_kernel(keep_ref, got_ref, result_ref, arrived):
    core, half = lax.axis_index("wa"), keep_ref.shape[1]
    copies = [
        pltpu.make_async_copy(keep_ref, result_ref.at[:, pl.ds(half * core, half)], arrived.at[0]),
        pltpu.make_async_copy(got_ref, result_ref.at[:, pl.ds(half * (1 - core), half)], arrived.at[1]),
    ]
    for copy in copies:
        copy.start()
    for copy in copies:
        copy.wait()


def shards(features, frame_counts, gain_first, conv_first, bias_first, gain_second, conv_second, bias_second):
    frames, rows, side, channels = features.shape
    pairs, half = rows // 2, rows // 2
    held = half // 2 + 1
    tall, cores, blocks = lax.axis_size("ha"), lax.axis_size("wa"), lax.axis_size("tchunk")
    packed, width, tiles = 3 * LANES, 2 * side, CACHE * held
    bf16 = jnp.bfloat16
    vmem = pl.BlockSpec(memory_space=pltpu.VMEM)
    limit = pltpu.CompilerParams(vmem_limit_bytes=20 * 2**20)
    work = 2 * TAPS**3 * channels * channels * width

    def shape(*extent):
        return jax.ShapeDtypeStruct(extent, bf16)

    def cost(flops, fetched):
        return pl.CostEstimate(flops=flops, bytes_accessed=fetched, transcendentals=0)

    slots = pl.pallas_call(
        slots_kernel,
        out_shape=jax.ShapeDtypeStruct((side, packed), jnp.int32),
        out_specs=vmem,
        compiler_params=limit,
        cost_estimate=cost(2**34, 2**20),
    )()
    slots, frame_counts = lax.optimization_barrier((slots, frame_counts))
    tail, mine, theirs, marks = pl.pallas_call(
        prepare_kernel,
        out_shape=(
            shape(CACHE * pairs + 1, side, packed), shape(frames, held, side, packed),
            shape((CACHE + frames) * held, side, packed), shape(side, packed),
        ),
        in_specs=[pl.BlockSpec(memory_space=pltpu.SMEM), vmem, vmem],
        out_specs=(vmem,) * 4,
        scratch_shapes=[pltpu.VMEM((frames, pairs, side, packed), bf16)],
        compiler_params=limit,
    )(frame_counts, slots, features)

    if blocks > 2:
        tail = joined_tail(tail)
        rest = lax.dynamic_slice_in_dim(
            tail[:-1].reshape(CACHE, pairs, side, packed), (1 - lax.axis_index("wa")) * (pairs - held), held, 1
        )
        theirs = jnp.concatenate([rest.reshape(tiles, side, packed), theirs[tiles:]], axis=0)
    straight, diagonal, across = [], [], []

    def index(block, h, core):
        return (block * tall + h) * cores + core

    for k in range(blocks - 1):
        for h in range(tall):
            for core in range(cores):
                straight.append((index(k, h, core), index(k + 1, h, core)))
    for h in range(tall - 1):
        for k in range(blocks):
            lower, upper = index(k, h, 1), index(k, h + 1, 0)
            across += [(lower, upper), (upper, lower)]
            if k + 1 < blocks:
                lower_next, upper_next = index(k + 1, h, 1), index(k + 1, h + 1, 0)
                diagonal += [(lower, upper_next), (upper, lower_next)]
    axes = ("tchunk", "ha", "wa")
    swap = [(0, 1), (1, 0)]
    tail_mine = lax.ppermute(tail, axes, straight)
    other = lax.ppermute(theirs, "wa", swap)
    tail_edge, own_edge = pl.pallas_call(
        border_kernel,
        out_shape=(shape(tiles + 1, side, packed), shape(2, frames, side, packed)),
        in_specs=[vmem] * 3,
        out_specs=(vmem, vmem),
        compiler_params=limit,
        cost_estimate=cost(2**34, 2**20),
    )(tail, mine, other)
    own_edge = lax.ppermute(own_edge, axes, across)
    tail_edge = lax.ppermute(tail_edge, axes, diagonal)

    weights = (
        gain_first.reshape(1, channels), conv_first, bias_first.reshape(1, channels),
        gain_second.reshape(1, channels), conv_second, bias_second.reshape(1, channels),
    )
    first, late = pl.pallas_call(
        own_kernel,
        out_shape=(shape(3, frames, half + 2, width, LANES), shape(3, frames - 2, half, width, LANES)),
        in_specs=[vmem] * 7,
        out_specs=(vmem,) * 2,
        compiler_params=limit,
        cost_estimate=cost(work * (frames - 2) * half, 4 * 2**20),
    )(marks, mine, other, *weights[:4])
    rest = pl.pallas_call(
        other_rows_kernel,
        out_shape=shape(tiles, side, packed),
        in_specs=[vmem, pl.BlockSpec(memory_space=pl.ANY)],
        out_specs=vmem,
        compiler_params=limit,
        cost_estimate=cost(1, 1),
    )(tail_mine, late)
    tail_other = lax.ppermute(rest, "wa", swap)
    strip, hidden, keep, send = pl.pallas_call(
        edge_kernel,
        out_shape=(
            shape(3, 2, 2, width, LANES), shape(3, 2, half + 2, width, LANES),
            shape(frames - CACHE, half, side, channels), shape(frames - CACHE, half, side, channels),
        ),
        in_specs=[vmem] * 12,
        out_specs=(vmem,) * 4,
        scratch_shapes=[
            pltpu.VMEM((3, frames, 4, width, LANES), bf16),
            pltpu.VMEM((3, frames - 2, 4, width, LANES), bf16),
        ],
        compiler_params=limit,
        cost_estimate=cost(2**20, 2**20),
    )(marks, mine, other, own_edge, first, late, *weights)
    keep, send = pl.pallas_call(
        early_kernel,
        out_shape=(shape(frames, half, side, channels), shape(frames, half, side, channels)),
        in_specs=[vmem] * 17,
        out_specs=(vmem, vmem),
        scratch_shapes=[
            pltpu.VMEM((3, CACHE + 2, half + 4, width, LANES), bf16),
            pltpu.VMEM((3, CACHE + 2, half + 2, width, LANES), bf16),
        ],
        compiler_params=limit,
        cost_estimate=cost(work * CACHE * (2 * half + 2), 8 * 2**20),
    )(marks, tail_mine, tail_other, mine, other, tail_edge, first, strip, hidden, keep, send, *weights)
    got = lax.ppermute(send, "wa", swap)
    return pl.pallas_call(
        place_kernel,
        out_shape=shape(*features.shape),
        in_specs=[vmem, vmem],
        out_specs=pl.BlockSpec(memory_space=pltpu.HBM),
        scratch_shapes=[pltpu.SemaphoreType.DMA((2,))],
        compiler_params=limit,
    )(keep, got)


def solution(mesh):
    return jax.shard_map(
        shards,
        mesh=mesh,
        in_specs=(
            P(("grp", "tchunk"), "ha", "wa", None),
            P(("grp", "tchunk")),
            P(), P(), P(), P(), P(), P(),
        ),
        out_specs=P(("grp", "tchunk"), "ha", "wa", None),
        check_vma=False,
    )
```

```python
import jax
import jax.numpy as jnp
from jax import lax
from jax.experimental import pallas as pl
from jax.experimental.pallas import tpu as pltpu
from jax.sharding import PartitionSpec as P

epsilon = 1e-06
CACHE = 4
TAPS = 3
LANES = 128
PRODUCT = 192


def slots_kernel(slots_ref):
    slots_ref[...] = lax.broadcasted_iota(jnp.int32, slots_ref.shape, 0)


def lower_part():
    return 1 - lax.axis_index("wa")


def prepare_kernel(total_ref, slots_ref, raw, tail_ref, mine_ref, theirs_ref, marks_ref, pack):
    frames, rows = raw.shape[:2]
    pairs, held = rows // 2, mine_ref.shape[1]
    core = lower_part()
    total = total_ref[0]
    for frame in range(frames):
        for pair in range(pairs):
            first, second = raw[frame, 2 * pair], raw[frame, 2 * pair + 1]
            packed = jnp.concatenate(
                [first[:, :LANES], second[:, :LANES], first[:, LANES:], second[:, LANES:]], axis=-1
            )
            pack[frame, pair] = packed
    for slot in range(CACHE):
        frame = total - CACHE + slot
        value = pack[jnp.maximum(frame, 0)]
        tail_ref[slot * pairs:(slot + 1) * pairs] = jnp.where(frame >= 0, value, jnp.zeros_like(value))
        value = pack[jnp.maximum(frame, 0), pl.ds((1 - core) * (pairs - held), held)]
        theirs_ref[slot * held:(slot + 1) * held] = jnp.where(frame >= 0, value, jnp.zeros_like(value))
    for frame in range(frames):
        start = (CACHE + frame) * held
        value = pack[frame, pl.ds(core * (pairs - held), held)]
        mine_ref[frame] = jnp.where(frame < total, value, jnp.zeros_like(value))
        value = pack[frame, pl.ds((1 - core) * (pairs - held), held)]
        theirs_ref[start:start + held] = jnp.where(frame < total, value, jnp.zeros_like(value))
    slot = slots_ref[...]
    tail_ref[CACHE * pairs] = jnp.where(
        (slot < CACHE) & (total - CACHE + slot >= 0), 1.0, 0.0
    ).astype(tail_ref.dtype)
    marks_ref[...] = jnp.where(slot < total, 1.0, 0.0).astype(marks_ref.dtype)


def joined_tail(tail):
    count = lax.axis_size("tchunk")

    def pushed(value, held):
        return lax.dynamic_slice_in_dim(jnp.concatenate([value, jnp.zeros_like(value)], axis=0), held, CACHE, 0)

    step = 1
    while step < count - 1:
        early = lax.ppermute(tail, "tchunk", [(k, k + step) for k in range(count - step)])
        held = jnp.sum(tail[-1, :CACHE, 0].astype(jnp.int32))
        body = pushed(early[:-1].reshape((CACHE, -1) + tail.shape[1:]), held).reshape(tail[:-1].shape)
        marks = jnp.pad(pushed(early[-1, :CACHE], held), ((0, tail.shape[1] - CACHE), (0, 0)))
        tail = tail + jnp.concatenate([body, marks[None]], axis=0)
        step *= 2
    return tail


def silu(half):
    return half + half * jnp.tanh(half)


def lane_mask():
    return lax.broadcasted_iota(jnp.int32, (1, 1, 1, LANES), 3) < LANES // 2


def gains(gain_ref):
    low, high = 0.5 * gain_ref[:, :LANES], 0.5 * gain_ref[:, LANES:]
    return low.reshape(1, 1, 1, LANES), jnp.concatenate([high, high], axis=-1).reshape(1, 1, 1, LANES)


def rolled(values):
    shape = values.shape
    return pltpu.roll(values.reshape(-1, LANES), LANES // 2, 1).reshape(shape)


def first_rows(left, right, gain_ref, channels):
    raw = jnp.concatenate([left.astype(jnp.float32), right.astype(jnp.float32)], axis=2)
    front, back, high = raw[..., :LANES], raw[..., LANES:2 * LANES], raw[..., 2 * LANES:]
    lower = lane_mask()
    squared = high * high

    def inverse(low, mask):
        total = jnp.sum(low * low + jnp.where(mask, squared, 0.0), axis=-1, keepdims=True)
        return lax.rsqrt(total * (1.0 / channels) + epsilon)

    scale_front, scale_back = inverse(front, lower), inverse(back, jnp.logical_not(lower))
    gain_low, gain_high = gains(gain_ref)
    front = silu(front * scale_front * gain_low)
    back = silu(back * scale_back * gain_low)
    high = silu(high * jnp.where(lower, scale_front, scale_back) * gain_high)
    turned = rolled(high)
    one = [front, jnp.where(lower, high, 0.0), jnp.where(lower, 0.0, turned)]
    two = [back, jnp.where(lower, turned, 0.0), jnp.where(lower, 0.0, high)]
    return [[part.astype(jnp.bfloat16) for part in row] for row in (one, two)]


def second_rows(hidden, flag, gain_ref, channels):
    gain = 0.5 * gain_ref[...].reshape(1, 1, 1, channels)
    total = jnp.sum(hidden * hidden, axis=-1, keepdims=True)
    inverse = lax.rsqrt(total * (1.0 / channels) + epsilon) * flag
    values = silu(hidden * inverse * gain)
    rest = jnp.zeros(values.shape[:-1] + (LANES // 2,), jnp.float32)
    high = jnp.concatenate([values[..., LANES:], rest], axis=-1)
    parts = [values[..., :LANES], high, rolled(high)]
    return jnp.stack([part.astype(jnp.bfloat16) for part in parts])


def in_turn(steps):
    waiting = None
    for product, then in steps:
        result = product()
        if waiting:
            waiting[1](waiting[0])
        waiting = (result, then)
    waiting[1](waiting[0])


def convolved(operand, weights_ref, bias_ref, frame, frames, rows, then, most=PRODUCT):
    products = -(-frames * rows * operand.shape[3] // most)
    step = -(-frames // products)

    def part(start):
        count = min(step, frames - start)
        return (
            lambda: convolved_part(operand, weights_ref, bias_ref, frame + start, count, rows),
            lambda result: then(start, count, result),
        )

    return [part(start) for start in range(0, frames, step)]


def convolved_part(operand, weights_ref, bias_ref, frame, frames, rows):
    width = operand.shape[3]
    channels = weights_ref.shape[-1]
    taps = [(a, i) for a in range(TAPS) for i in range(TAPS)]
    groups = [taps[start:start + 2] for start in range(0, len(taps), 2)]

    def window(tap, part):
        a, i = tap
        value = operand[part, frame + a:frame + a + frames, i:i + rows]
        return value.reshape(frames * rows * width, LANES)

    def operands(groups):
        pieces = []
        for group in groups:
            pieces += [window(tap, 0) for tap in group]
            high = window(group[0], 1)
            pieces.append(high + window(group[1], 2) if len(group) > 1 else high)
        return jnp.concatenate(pieces, axis=-1)

    def weights(groups, j, depth):
        rights = []
        for group in groups:
            held = [weights_ref[a, i, j] for a, i in group]
            rights += [weight[:LANES] for weight in held] + [weight[LANES:] for weight in held]
        rest = depth - sum(right.shape[0] for right in rights)
        if rest:
            rights.append(jnp.zeros((rest, channels), jnp.bfloat16))
        return jnp.concatenate(rights, axis=0)

    half = len(groups) // 2
    parts = [(part, operands(part)) for part in (groups[:half], groups[half:])]
    products = []
    for j in range(TAPS):
        total = None
        for part, left in parts if j % 2 == 0 else parts[::-1]:
            product = jnp.dot(left, weights(part, j, left.shape[1]), preferred_element_type=jnp.float32)
            total = product if total is None else total + product
        products.append(total.reshape(frames * rows, width, channels))
    column = lax.broadcasted_iota(jnp.int32, (1, width, 1), 1)
    before = jnp.where(column == 0, 0.0, pltpu.roll(products[0], 1, 1))
    after = jnp.where(column == width - 1, 0.0, pltpu.roll(products[2], width - 1, 1))
    result = products[1] + before + after + bias_ref[...].reshape(1, 1, channels)
    return result.reshape(frames, rows, width, channels)


def halves(core, mine, other):
    return jnp.where(core == 0, mine, other), jnp.where(core == 0, other, mine)


def frame_flags(marks, frames):
    values = marks.astype(jnp.float32)
    return [values[k:k + 1, 0:1].reshape(1, 1, 1, 1) for k in frames]


def fill_rows(operand, frame, row, mine, other, gain_ref):
    left, right = halves(lax.axis_index("wa"), mine, other)
    frames, pairs = mine.shape[:2]
    upper, lower = first_rows(left, right, gain_ref, gain_ref.shape[-1])
    for part in range(len(upper)):
        for pair in range(pairs):
            operand[part, frame:frame + frames, pl.ds(row + 2 * pair, 1)] = upper[part][:, pair:pair + 1]
            operand[part, frame:frame + frames, pl.ds(row + 2 * pair + 1, 1)] = lower[part][:, pair:pair + 1]


def border_kernel(tail_ref, mine_ref, other_ref, tail_edge_ref, own_edge_ref):
    frames, held = mine_ref.shape[:2]
    pairs = tail_ref.shape[0] // CACHE
    core = lower_part()
    pair = core * (held - 1)
    for slot in range(CACHE):
        tail_edge_ref[slot] = tail_ref[slot * pairs + core * (pairs - 1)]
        tail_edge_ref[CACHE + slot] = other_ref[slot * held + pair]
    spare = tail_edge_ref.shape[0] - 2 * CACHE
    tail_edge_ref[2 * CACHE:] = jnp.zeros((spare,) + tail_edge_ref.shape[1:], tail_edge_ref.dtype)
    for frame in range(frames):
        own_edge_ref[0, frame] = mine_ref[frame, pair]
        own_edge_ref[1, frame] = other_ref[(CACHE + frame) * held + pair]


def finish(mine_ref, other_ref, live, first, pairs, value, targets):
    _, held, side, _ = mine_ref.shape
    frames, channels = value.shape[0], value.shape[-1]
    start, count = pairs
    near, far = halves(lax.axis_index("wa"), value[:, :, :side], value[:, :, side:])
    for mine, value, target in ((True, near, targets[0]), (False, far, targets[1])):
        for frame in range(frames):
            for k in range(count):
                if mine:
                    raw = mine_ref[first + frame, start + k]
                else:
                    raw = other_ref[(CACHE + first + frame) * held + start + k]
                raw = raw.astype(jnp.float32)
                high = raw[:, 2 * LANES:]
                for row, tail in ((0, high), (1, pltpu.roll(high, LANES // 2, 1))):
                    low = raw[:, row * LANES:(row + 1) * LANES]
                    features = jnp.concatenate([low, tail[:, :channels - LANES]], axis=-1)
                    summed = features + value[frame, 2 * k + row]
                    kept = jnp.where(live[first + frame].reshape(1, 1) > 0.5, summed, 0.0)
                    target(first + frame, 2 * k + row, kept.astype(jnp.bfloat16))


def hide(operand, weights_ref, bias_ref, gain_ref, first, count, rows, flags, store, most=PRODUCT):
    channels = weights_ref.shape[-1]

    def then(begin, part, hidden):
        flag = jnp.concatenate(flags[begin:begin + part], axis=0)
        store(begin, begin + part, second_rows(hidden, flag, gain_ref, channels))

    return convolved(operand, weights_ref, bias_ref, first, count, rows, then, most)


def inside_flags(rows):
    core, place = lower_part(), lax.axis_index("ha")
    inside = jnp.where(core == 0, place > 0, place < lax.axis_size("ha") - 1)
    row = lax.broadcasted_iota(jnp.int32, (1, rows, 1, 1), 1)
    return jnp.where((row == (rows - 1) * core) & jnp.logical_not(inside), 0.0, 1.0)


def other_rows_kernel(tail_ref, late_ref, rest_ref):
    pairs, held = tail_ref.shape[0] // CACHE, rest_ref.shape[0] // CACHE
    first = (1 - lower_part()) * (pairs - held)
    for slot in range(CACHE):
        rest_ref[slot * held:(slot + 1) * held] = tail_ref[pl.ds(slot * pairs + first, held)]


def own_kernel(
    marks_ref, mine_ref, other_ref, gain1_ref, w1_ref, bias1_ref, gain2_ref, first_ref, late_ref
):
    frames, pairs, side, packed = mine_ref.shape
    live = frame_flags(marks_ref[...], range(2, frames))

    def fill(start, end):
        other = other_ref[(CACHE + start) * pairs:(CACHE + end) * pairs].reshape(end - start, pairs, side, packed)
        fill_rows(first_ref, start, 0, mine_ref[start:end], other, gain1_ref)

    def store(begin, end, rows):
        late_ref[:, begin:end] = rows

    steps = hide(first_ref, w1_ref, bias1_ref, gain2_ref, 0, frames - 2, 2 * pairs - 2, live, store, 2 * PRODUCT // 3)
    each = -(-(frames - 2) // len(steps))

    def filled(k, product):
        def run():
            fill(min(frames, each * k + (2 if k else 0)), min(frames, each * (k + 1) + 2))
            return product()
        return run

    in_turn([(filled(k, product), then) for k, (product, then) in enumerate(steps)])


def edge_kernel(
    marks_ref, mine_ref, other_ref, edge_ref, first_ref, late_ref,
    gain1_ref, w1_ref, bias1_ref, gain2_ref, w2_ref, bias2_ref,
    strip_ref, hidden_ref, keep_ref, send_ref, strip, operand,
):
    core = lower_part()
    frames, pairs = mine_ref.shape[:2]
    rows = 2 * pairs
    late = frames - CACHE
    outward, inward = pl.ds(2 * core, 2), pl.ds(2 * (1 - core), 2)
    fill_rows(strip, 0, 2 * core, edge_ref[1][:, None], edge_ref[0][:, None], gain1_ref)
    strip[:, :, inward] = first_ref[:, :, pl.ds((rows - 2) * core, 2)]
    operand[:, :, inward] = late_ref[:, :, pl.ds((rows - 4) * core, 2)]
    live = frame_flags(marks_ref[...], range(frames))
    inside = inside_flags(2)

    def store(begin, end, values):
        operand[:, begin:end, outward] = values

    def finished(start_row, pair, count):
        def put(ref):
            def store(frame, row, value):
                ref[frame - CACHE, start_row + row] = value
            return store

        def then(start, part, result):
            targets = (put(keep_ref), put(send_ref))
            finish(mine_ref, other_ref, live, CACHE + start, (pair, count), result, targets)

        return then

    flags = [flag * inside for flag in live[2:]]
    middle, border = finished(2 * (1 - core), 1, pairs - 2), finished((rows - 4) * core, (pairs - 1) * core, 1)
    in_turn(
        hide(strip, w1_ref, bias1_ref, gain2_ref, 0, frames - 2, 2, flags, store)
        + convolved(late_ref, w2_ref, bias2_ref, 0, late, rows - 4, middle)
        + convolved(operand, w2_ref, bias2_ref, 0, late, 2, border)
    )
    strip_ref[...] = strip[:, 0:2, outward]
    hidden_ref[:, :, pl.ds(2 * (1 - core), rows - 2)] = late_ref[:, 0:2]
    hidden_ref[:, :, pl.ds((rows - 2) * core, 2)] = operand[:, 0:2, outward]


def early_kernel(
    marks_ref, tail_mine_ref, tail_other_ref, mine_ref, other_ref, edge_ref, first_ref, strip_ref, hidden_ref,
    late_keep_ref, late_send_ref, gain1_ref, w1_ref, bias1_ref, gain2_ref, w2_ref, bias2_ref,
    keep_ref, send_ref, plane, operand,
):
    core = lower_part()
    held = mine_ref.shape[1]
    rows = 2 * held
    pairs = tail_mine_ref.shape[0] // CACHE
    live = frame_flags(marks_ref[...], range(CACHE))
    inside = inside_flags(rows)
    earlier = lax.axis_index("tchunk") > 0
    middle, border = 2 * (1 - core), rows * core

    def unpacked(ref, stride, first):
        return jnp.stack([ref[pl.ds(slot * stride + first, held)] for slot in range(CACHE)])

    plane[:, CACHE:, pl.ds(middle, rows)] = first_ref[:, 0:2]
    plane[:, CACHE:, pl.ds(border, 2)] = strip_ref[...]
    operand[:, CACHE:] = hidden_ref[...]

    def fill(first, flags):
        def store(begin, end, values):
            operand[:, first + begin:first + end] = values

        flags = [flag * inside for flag in flags]
        in_turn(hide(plane, w1_ref, bias1_ref, gain2_ref, first, CACHE - first, rows, flags, store))

    @pl.when(earlier)
    def _():
        mine = unpacked(tail_mine_ref, pairs, core * (pairs - held))
        fill_rows(plane, 0, middle, mine, unpacked(tail_other_ref, held, 0), gain1_ref)
        mine, other = edge_ref[CACHE:2 * CACHE], edge_ref[0:CACHE]
        fill_rows(plane, 0, border, mine[:, None], other[:, None], gain1_ref)
        fill(0, frame_flags(tail_mine_ref[CACHE * pairs], range(CACHE - 2, CACHE)) + live[0:2])

    @pl.when(jnp.logical_not(earlier))
    def _():
        plane[:, 0:CACHE] = jnp.zeros(plane.shape[:1] + (CACHE,) + plane.shape[2:], plane.dtype)
        operand[:, 0:2] = jnp.zeros(operand.shape[:1] + (2,) + operand.shape[2:], operand.dtype)
        fill(2, live[0:2])

    def put(ref):
        def store(frame, row, value):
            ref[frame, row] = value
        return store

    def then(start, part, result):
        finish(mine_ref, other_ref, live, start, (core, held - 1), result, (put(keep_ref), put(send_ref)))

    in_turn(convolved(operand, w2_ref, bias2_ref, 0, CACHE, rows - 2, then))
    keep_ref[CACHE:] = late_keep_ref[...]
    send_ref[CACHE:] = late_send_ref[...]


def place_kernel(keep_ref, got_ref, result_ref, arrived):
    core, half = lower_part(), keep_ref.shape[1]
    copies = [
        pltpu.make_async_copy(keep_ref, result_ref.at[:, pl.ds(half * core, half)], arrived.at[0]),
        pltpu.make_async_copy(got_ref, result_ref.at[:, pl.ds(half * (1 - core), half)], arrived.at[1]),
    ]
    for copy in copies:
        copy.start()
    for copy in copies:
        copy.wait()


def shards(features, frame_counts, gain_first, conv_first, bias_first, gain_second, conv_second, bias_second):
    frames, rows, side, channels = features.shape
    pairs, half = rows // 2, rows // 2
    held = half // 2 + 1
    tall, cores, blocks = lax.axis_size("ha"), lax.axis_size("wa"), lax.axis_size("tchunk")
    packed, width, tiles = 3 * LANES, 2 * side, CACHE * held
    bf16 = jnp.bfloat16
    vmem = pl.BlockSpec(memory_space=pltpu.VMEM)
    limit = pltpu.CompilerParams(vmem_limit_bytes=20 * 2**20)
    work = 2 * TAPS**3 * channels * channels * width

    def shape(*extent):
        return jax.ShapeDtypeStruct(extent, bf16)

    def cost(flops, fetched):
        return pl.CostEstimate(flops=flops, bytes_accessed=fetched, transcendentals=0)

    slots = pl.pallas_call(
        slots_kernel,
        out_shape=jax.ShapeDtypeStruct((side, packed), jnp.int32),
        out_specs=vmem,
        compiler_params=limit,
        cost_estimate=cost(2**34, 2**20),
    )()
    slots, frame_counts = lax.optimization_barrier((slots, frame_counts))
    tail, mine, theirs, marks = pl.pallas_call(
        prepare_kernel,
        out_shape=(
            shape(CACHE * pairs + 1, side, packed), shape(frames, held, side, packed),
            shape((CACHE + frames) * held, side, packed), shape(side, packed),
        ),
        in_specs=[pl.BlockSpec(memory_space=pltpu.SMEM), vmem, vmem],
        out_specs=(vmem,) * 4,
        scratch_shapes=[pltpu.VMEM((frames, pairs, side, packed), bf16)],
        compiler_params=limit,
    )(frame_counts, slots, features)

    if blocks > 2:
        tail = joined_tail(tail)
        rest = lax.dynamic_slice_in_dim(
            tail[:-1].reshape(CACHE, pairs, side, packed), (1 - lower_part()) * (pairs - held), held, 1
        )
        theirs = jnp.concatenate([rest.reshape(tiles, side, packed), theirs[tiles:]], axis=0)
    straight, diagonal, across = [], [], []

    def index(block, h, core):
        return (block * tall + h) * cores + core

    for k in range(blocks - 1):
        for h in range(tall):
            for core in range(cores):
                straight.append((index(k, h, core), index(k + 1, h, core)))
    for h in range(tall - 1):
        for k in range(blocks):
            lower, upper = index(k, h, 0), index(k, h + 1, 1)
            across += [(lower, upper), (upper, lower)]
            if k + 1 < blocks:
                lower_next, upper_next = index(k + 1, h, 0), index(k + 1, h + 1, 1)
                diagonal += [(lower, upper_next), (upper, lower_next)]
    axes = ("tchunk", "ha", "wa")
    swap = [(0, 1), (1, 0)]
    tail_mine = lax.ppermute(tail, axes, straight)
    other = lax.ppermute(theirs, "wa", swap)
    tail_edge, own_edge = pl.pallas_call(
        border_kernel,
        out_shape=(shape(tiles + 1, side, packed), shape(2, frames, side, packed)),
        in_specs=[vmem] * 3,
        out_specs=(vmem, vmem),
        compiler_params=limit,
        cost_estimate=cost(2**34, 2**20),
    )(tail, mine, other)
    own_edge = lax.ppermute(own_edge, axes, across)
    tail_edge = lax.ppermute(tail_edge, axes, diagonal)

    weights = (
        gain_first.reshape(1, channels), conv_first, bias_first.reshape(1, channels),
        gain_second.reshape(1, channels), conv_second, bias_second.reshape(1, channels),
    )
    first, late = pl.pallas_call(
        own_kernel,
        out_shape=(shape(3, frames, half + 2, width, LANES), shape(3, frames - 2, half, width, LANES)),
        in_specs=[vmem] * 7,
        out_specs=(vmem,) * 2,
        compiler_params=limit,
        cost_estimate=cost(work * (frames - 2) * half, 4 * 2**20),
    )(marks, mine, other, *weights[:4])
    rest = pl.pallas_call(
        other_rows_kernel,
        out_shape=shape(tiles, side, packed),
        in_specs=[vmem, pl.BlockSpec(memory_space=pl.ANY)],
        out_specs=vmem,
        compiler_params=limit,
        cost_estimate=cost(1, 1),
    )(tail_mine, late)
    tail_other = lax.ppermute(rest, "wa", swap)
    strip, hidden, keep, send = pl.pallas_call(
        edge_kernel,
        out_shape=(
            shape(3, 2, 2, width, LANES), shape(3, 2, half + 2, width, LANES),
            shape(frames - CACHE, half, side, channels), shape(frames - CACHE, half, side, channels),
        ),
        in_specs=[vmem] * 12,
        out_specs=(vmem,) * 4,
        scratch_shapes=[
            pltpu.VMEM((3, frames, 4, width, LANES), bf16),
            pltpu.VMEM((3, frames - 2, 4, width, LANES), bf16),
        ],
        compiler_params=limit,
        cost_estimate=cost(2**20, 2**20),
    )(marks, mine, other, own_edge, first, late, *weights)
    keep, send = pl.pallas_call(
        early_kernel,
        out_shape=(shape(frames, half, side, channels), shape(frames, half, side, channels)),
        in_specs=[vmem] * 17,
        out_specs=(vmem, vmem),
        scratch_shapes=[
            pltpu.VMEM((3, CACHE + 2, half + 4, width, LANES), bf16),
            pltpu.VMEM((3, CACHE + 2, half + 2, width, LANES), bf16),
        ],
        compiler_params=limit,
        cost_estimate=cost(work * CACHE * (2 * half + 2), 8 * 2**20),
    )(marks, tail_mine, tail_other, mine, other, tail_edge, first, strip, hidden, keep, send, *weights)
    got = lax.ppermute(send, "wa", swap)
    return pl.pallas_call(
        place_kernel,
        out_shape=shape(*features.shape),
        in_specs=[vmem, vmem],
        out_specs=pl.BlockSpec(memory_space=pltpu.HBM),
        scratch_shapes=[pltpu.SemaphoreType.DMA((2,))],
        compiler_params=limit,
    )(keep, got)


def solution(mesh):
    return jax.shard_map(
        shards,
        mesh=mesh,
        in_specs=(
            P(("grp", "tchunk"), "ha", "wa", None),
            P(("grp", "tchunk")),
            P(), P(), P(), P(), P(), P(),
        ),
        out_specs=P(("grp", "tchunk"), "ha", "wa", None),
        check_vma=False,
    )
```

```python
import jax
import jax.numpy as jnp
from jax import lax
from jax.experimental import pallas as pl
from jax.experimental.pallas import tpu as pltpu
from jax.sharding import PartitionSpec as P

epsilon = 1e-06
CACHE = 4
TAPS = 3
LANES = 128
PRODUCT = 192


def slots_kernel(slots_ref):
    slots_ref[...] = lax.broadcasted_iota(jnp.int32, slots_ref.shape, 0)


def lower_part():
    return 1 - lax.axis_index("wa")


def prepare_kernel(total_ref, slots_ref, raw, tail_ref, mine_ref, theirs_ref, marks_ref, pack):
    frames, rows = raw.shape[:2]
    pairs, held = rows // 2, mine_ref.shape[1]
    core = lower_part()
    total = total_ref[0]
    for frame in range(frames):
        for pair in range(pairs):
            first, second = raw[frame, 2 * pair], raw[frame, 2 * pair + 1]
            packed = jnp.concatenate(
                [first[:, :LANES], second[:, :LANES], first[:, LANES:], second[:, LANES:]], axis=-1
            )
            pack[frame, pair] = packed
    for slot in range(CACHE):
        frame = total - CACHE + slot
        value = pack[jnp.maximum(frame, 0)]
        tail_ref[slot * pairs:(slot + 1) * pairs] = jnp.where(frame >= 0, value, jnp.zeros_like(value))
        value = pack[jnp.maximum(frame, 0), pl.ds((1 - core) * (pairs - held), held)]
        theirs_ref[slot * held:(slot + 1) * held] = jnp.where(frame >= 0, value, jnp.zeros_like(value))
    for frame in range(frames):
        start = (CACHE + frame) * held
        value = pack[frame, pl.ds(core * (pairs - held), held)]
        mine_ref[frame] = jnp.where(frame < total, value, jnp.zeros_like(value))
        value = pack[frame, pl.ds((1 - core) * (pairs - held), held)]
        theirs_ref[start:start + held] = jnp.where(frame < total, value, jnp.zeros_like(value))
    slot = slots_ref[...]
    tail_ref[CACHE * pairs] = jnp.where(
        (slot < CACHE) & (total - CACHE + slot >= 0), 1.0, 0.0
    ).astype(tail_ref.dtype)
    marks_ref[...] = jnp.where(slot < total, 1.0, 0.0).astype(marks_ref.dtype)


def joined_tail(tail):
    count = lax.axis_size("tchunk")

    def pushed(value, held):
        return lax.dynamic_slice_in_dim(jnp.concatenate([value, jnp.zeros_like(value)], axis=0), held, CACHE, 0)

    step = 1
    while step < count - 1:
        early = lax.ppermute(tail, "tchunk", [(k, k + step) for k in range(count - step)])
        held = jnp.sum(tail[-1, :CACHE, 0].astype(jnp.int32))
        body = pushed(early[:-1].reshape((CACHE, -1) + tail.shape[1:]), held).reshape(tail[:-1].shape)
        marks = jnp.pad(pushed(early[-1, :CACHE], held), ((0, tail.shape[1] - CACHE), (0, 0)))
        tail = tail + jnp.concatenate([body, marks[None]], axis=0)
        step *= 2
    return tail


def silu(half):
    return half + half * jnp.tanh(half)


def lane_mask():
    return lax.broadcasted_iota(jnp.int32, (1, 1, 1, LANES), 3) < LANES // 2


def gains(gain_ref):
    low, high = 0.5 * gain_ref[:, :LANES], 0.5 * gain_ref[:, LANES:]
    return low.reshape(1, 1, 1, LANES), jnp.concatenate([high, high], axis=-1).reshape(1, 1, 1, LANES)


def rolled(values):
    shape = values.shape
    return pltpu.roll(values.reshape(-1, LANES), LANES // 2, 1).reshape(shape)


def first_active(raw, gain_ref, channels):
    front, back, high = raw[..., :LANES], raw[..., LANES:2 * LANES], raw[..., 2 * LANES:]
    lower = lane_mask()
    squared = high * high

    def inverse(low, mask):
        total = jnp.sum(low * low + jnp.where(mask, squared, 0.0), axis=-1, keepdims=True)
        return lax.rsqrt(total * (1.0 / channels) + epsilon)

    scale_front, scale_back = inverse(front, lower), inverse(back, jnp.logical_not(lower))
    gain_low, gain_high = gains(gain_ref)
    front = silu(front * scale_front * gain_low)
    back = silu(back * scale_back * gain_low)
    high = silu(high * jnp.where(lower, scale_front, scale_back) * gain_high)
    return front, back, high


def first_rows(front, back, high):
    lower = lane_mask()
    turned = rolled(high)
    one = [front, jnp.where(lower, high, 0.0), jnp.where(lower, 0.0, turned)]
    two = [back, jnp.where(lower, turned, 0.0), jnp.where(lower, 0.0, high)]
    return [[part.astype(jnp.bfloat16) for part in row] for row in (one, two)]


def second_rows(hidden, flag, gain_ref, channels):
    gain = 0.5 * gain_ref[...].reshape(1, 1, 1, channels)
    total = jnp.sum(hidden * hidden, axis=-1, keepdims=True)
    inverse = lax.rsqrt(total * (1.0 / channels) + epsilon) * flag
    values = silu(hidden * inverse * gain)
    rest = jnp.zeros(values.shape[:-1] + (LANES // 2,), jnp.float32)
    high = jnp.concatenate([values[..., LANES:], rest], axis=-1)
    parts = [values[..., :LANES], high, rolled(high)]
    return jnp.stack([part.astype(jnp.bfloat16) for part in parts])


def in_turn(steps):
    waiting = None
    for product, then in steps:
        result = product()
        if waiting:
            waiting[1](waiting[0])
        waiting = (result, then)
    waiting[1](waiting[0])


def convolved(operand, weights_ref, bias_ref, frame, frames, rows, then, most=PRODUCT):
    products = -(-frames * rows * operand.shape[3] // most)
    step = -(-frames // products)

    def part(start):
        count = min(step, frames - start)
        return (
            lambda: convolved_part(operand, weights_ref, bias_ref, frame + start, count, rows),
            lambda result: then(start, count, result),
        )

    return [part(start) for start in range(0, frames, step)]


def convolved_part(operand, weights_ref, bias_ref, frame, frames, rows):
    width = operand.shape[3]
    channels = weights_ref.shape[-1]
    taps = [(a, i) for a in range(TAPS) for i in range(TAPS)]
    groups = [taps[start:start + 2] for start in range(0, len(taps), 2)]

    def window(tap, part):
        a, i = tap
        value = operand[part, frame + a:frame + a + frames, i:i + rows]
        return value.reshape(frames * rows * width, LANES)

    def operands(groups):
        pieces = []
        for group in groups:
            pieces += [window(tap, 0) for tap in group]
            high = window(group[0], 1)
            pieces.append(high + window(group[1], 2) if len(group) > 1 else high)
        return jnp.concatenate(pieces, axis=-1)

    def weights(groups, j, depth):
        rights = []
        for group in groups:
            held = [weights_ref[a, i, j] for a, i in group]
            rights += [weight[:LANES] for weight in held] + [weight[LANES:] for weight in held]
        rest = depth - sum(right.shape[0] for right in rights)
        if rest:
            rights.append(jnp.zeros((rest, channels), jnp.bfloat16))
        return jnp.concatenate(rights, axis=0)

    half = len(groups) // 2
    parts = [(part, operands(part)) for part in (groups[:half], groups[half:])]
    products = []
    for j in range(TAPS):
        total = None
        for part, left in parts if j % 2 == 0 else parts[::-1]:
            product = jnp.dot(left, weights(part, j, left.shape[1]), preferred_element_type=jnp.float32)
            total = product if total is None else total + product
        products.append(total.reshape(frames * rows, width, channels))
    column = lax.broadcasted_iota(jnp.int32, (1, width, 1), 1)
    before = jnp.where(column == 0, 0.0, pltpu.roll(products[0], 1, 1))
    after = jnp.where(column == width - 1, 0.0, pltpu.roll(products[2], width - 1, 1))
    result = products[1] + before + after + bias_ref[...].reshape(1, 1, channels)
    return result.reshape(frames, rows, width, channels)


def halves(core, mine, other):
    return jnp.where(core == 0, mine, other), jnp.where(core == 0, other, mine)


def frame_flags(marks, frames):
    values = marks.astype(jnp.float32)
    return [values[k:k + 1, 0:1].reshape(1, 1, 1, 1) for k in frames]


def fill_rows(operand, frame, row, mine, other, gain_ref):
    left, right = halves(lax.axis_index("wa"), mine, other)
    raw = jnp.concatenate([left.astype(jnp.float32), right.astype(jnp.float32)], axis=2)
    frames, pairs = mine.shape[:2]
    if gain_ref is None:
        active = raw[..., :LANES], raw[..., LANES:2 * LANES], raw[..., 2 * LANES:]
    else:
        active = first_active(raw, gain_ref, gain_ref.shape[-1])
    upper, lower = first_rows(*active)
    for part in range(len(upper)):
        for pair in range(pairs):
            operand[part, frame:frame + frames, pl.ds(row + 2 * pair, 1)] = upper[part][:, pair:pair + 1]
            operand[part, frame:frame + frames, pl.ds(row + 2 * pair + 1, 1)] = lower[part][:, pair:pair + 1]


def border_kernel(tail_ref, mine_ref, other_ref, tail_edge_ref, own_edge_ref):
    frames, held = mine_ref.shape[:2]
    pairs = tail_ref.shape[0] // CACHE
    core = lower_part()
    pair = core * (held - 1)
    for slot in range(CACHE):
        tail_edge_ref[slot] = tail_ref[slot * pairs + core * (pairs - 1)]
        tail_edge_ref[CACHE + slot] = other_ref[slot * held + pair]
    spare = tail_edge_ref.shape[0] - 2 * CACHE
    tail_edge_ref[2 * CACHE:] = jnp.zeros((spare,) + tail_edge_ref.shape[1:], tail_edge_ref.dtype)
    for frame in range(frames):
        own_edge_ref[0, frame] = mine_ref[frame, pair]
        own_edge_ref[1, frame] = other_ref[(CACHE + frame) * held + pair]


def finish(mine_ref, other_ref, live, first, pairs, value, targets):
    _, held, side, _ = mine_ref.shape
    frames, channels = value.shape[0], value.shape[-1]
    start, count = pairs
    near, far = halves(lax.axis_index("wa"), value[:, :, :side], value[:, :, side:])
    for mine, value, target in ((True, near, targets[0]), (False, far, targets[1])):
        for frame in range(frames):
            for k in range(count):
                if mine:
                    raw = mine_ref[first + frame, start + k]
                else:
                    raw = other_ref[(CACHE + first + frame) * held + start + k]
                raw = raw.astype(jnp.float32)
                high = raw[:, 2 * LANES:]
                for row, tail in ((0, high), (1, pltpu.roll(high, LANES // 2, 1))):
                    low = raw[:, row * LANES:(row + 1) * LANES]
                    features = jnp.concatenate([low, tail[:, :channels - LANES]], axis=-1)
                    summed = features + value[frame, 2 * k + row]
                    kept = jnp.where(live[first + frame].reshape(1, 1) > 0.5, summed, 0.0)
                    target(first + frame, 2 * k + row, kept.astype(jnp.bfloat16))


def hide(operand, weights_ref, bias_ref, gain_ref, first, count, rows, flags, store, most=PRODUCT):
    channels = weights_ref.shape[-1]

    def then(begin, part, hidden):
        flag = jnp.concatenate(flags[begin:begin + part], axis=0)
        store(begin, begin + part, second_rows(hidden, flag, gain_ref, channels))

    return convolved(operand, weights_ref, bias_ref, first, count, rows, then, most)


def inside_flags(rows):
    core, place = lower_part(), lax.axis_index("ha")
    inside = jnp.where(core == 0, place > 0, place < lax.axis_size("ha") - 1)
    row = lax.broadcasted_iota(jnp.int32, (1, rows, 1, 1), 1)
    return jnp.where((row == (rows - 1) * core) & jnp.logical_not(inside), 0.0, 1.0)


def tail_kernel(tail_ref, gain_ref, late_ref, mine_ref, rest_ref, active):
    pairs, held = tail_ref.shape[0] // CACHE, rest_ref.shape[0] // CACHE
    place = lower_part() * (pairs - held)
    earlier = lax.axis_index("tchunk") > 0

    @pl.when(earlier)
    def _():
        raw = tail_ref[0:CACHE * pairs].astype(jnp.float32)[None]
        parts = first_active(raw, gain_ref, gain_ref.shape[-1])
        active[...] = jnp.concatenate([part[0].astype(jnp.bfloat16) for part in parts], axis=-1)
        for slot in range(CACHE):
            for ref, first in ((mine_ref, place), (rest_ref, pairs - held - place)):
                ref[slot * held:(slot + 1) * held] = active[pl.ds(slot * pairs + first, held)]

    @pl.when(jnp.logical_not(earlier))
    def _():
        for ref in (mine_ref, rest_ref):
            ref[...] = jnp.zeros(ref.shape, ref.dtype)


def own_kernel(
    marks_ref, mine_ref, other_ref, gain1_ref, w1_ref, bias1_ref, gain2_ref, first_ref, late_ref
):
    frames, pairs, side, packed = mine_ref.shape
    live = frame_flags(marks_ref[...], range(2, frames))

    def fill(start, end):
        other = other_ref[(CACHE + start) * pairs:(CACHE + end) * pairs].reshape(end - start, pairs, side, packed)
        fill_rows(first_ref, start, 0, mine_ref[start:end], other, gain1_ref)

    def store(begin, end, rows):
        late_ref[:, begin:end] = rows

    steps = hide(first_ref, w1_ref, bias1_ref, gain2_ref, 0, frames - 2, 2 * pairs - 2, live, store, 2 * PRODUCT // 3)
    each = -(-(frames - 2) // len(steps))

    def filled(k, product):
        def run():
            fill(min(frames, each * k + (2 if k else 0)), min(frames, each * (k + 1) + 2))
            return product()
        return run

    in_turn([(filled(k, product), then) for k, (product, then) in enumerate(steps)])


def edge_kernel(
    marks_ref, mine_ref, other_ref, edge_ref, first_ref, late_ref,
    gain1_ref, w1_ref, bias1_ref, gain2_ref, w2_ref, bias2_ref,
    strip_ref, hidden_ref, keep_ref, send_ref, strip, operand,
):
    core = lower_part()
    frames, pairs = mine_ref.shape[:2]
    rows = 2 * pairs
    late = frames - CACHE
    outward, inward = pl.ds(2 * core, 2), pl.ds(2 * (1 - core), 2)
    fill_rows(strip, 0, 2 * core, edge_ref[1][:, None], edge_ref[0][:, None], gain1_ref)
    strip[:, :, inward] = first_ref[:, :, pl.ds((rows - 2) * core, 2)]
    operand[:, :, inward] = late_ref[:, :, pl.ds((rows - 4) * core, 2)]
    live = frame_flags(marks_ref[...], range(frames))
    inside = inside_flags(2)

    def store(begin, end, values):
        operand[:, begin:end, outward] = values

    def finished(start_row, pair, count):
        def put(ref):
            def store(frame, row, value):
                ref[frame - CACHE, start_row + row] = value
            return store

        def then(start, part, result):
            targets = (put(keep_ref), put(send_ref))
            finish(mine_ref, other_ref, live, CACHE + start, (pair, count), result, targets)

        return then

    flags = [flag * inside for flag in live[2:]]
    middle, border = finished(2 * (1 - core), 1, pairs - 2), finished((rows - 4) * core, (pairs - 1) * core, 1)
    in_turn(
        hide(strip, w1_ref, bias1_ref, gain2_ref, 0, frames - 2, 2, flags, store)
        + convolved(late_ref, w2_ref, bias2_ref, 0, late, rows - 4, middle)
        + convolved(operand, w2_ref, bias2_ref, 0, late, 2, border)
    )
    strip_ref[...] = strip[:, 0:2, outward]
    hidden_ref[:, :, pl.ds(2 * (1 - core), rows - 2)] = late_ref[:, 0:2]
    hidden_ref[:, :, pl.ds((rows - 2) * core, 2)] = operand[:, 0:2, outward]


def early_kernel(
    marks_ref, tail_mine_ref, tail_rows_ref, tail_other_ref, mine_ref, other_ref, edge_ref, first_ref, strip_ref, hidden_ref,
    late_keep_ref, late_send_ref, gain1_ref, w1_ref, bias1_ref, gain2_ref, w2_ref, bias2_ref,
    keep_ref, send_ref, plane, operand,
):
    core = lower_part()
    held = mine_ref.shape[1]
    rows = 2 * held
    pairs = tail_mine_ref.shape[0] // CACHE
    live = frame_flags(marks_ref[...], range(CACHE))
    inside = inside_flags(rows)
    earlier = lax.axis_index("tchunk") > 0
    middle, border = 2 * (1 - core), rows * core

    def unpacked(ref):
        return ref[...].reshape((CACHE, held) + ref.shape[1:])

    plane[:, CACHE:, pl.ds(middle, rows)] = first_ref[:, 0:2]
    plane[:, CACHE:, pl.ds(border, 2)] = strip_ref[...]
    operand[:, CACHE:] = hidden_ref[...]

    def fill(first, flags):
        def store(begin, end, values):
            operand[:, first + begin:first + end] = values

        flags = [flag * inside for flag in flags]
        in_turn(hide(plane, w1_ref, bias1_ref, gain2_ref, first, CACHE - first, rows, flags, store))

    @pl.when(earlier)
    def _():
        fill_rows(plane, 0, middle, unpacked(tail_rows_ref), unpacked(tail_other_ref), None)
        mine, other = edge_ref[CACHE:2 * CACHE], edge_ref[0:CACHE]
        fill_rows(plane, 0, border, mine[:, None], other[:, None], gain1_ref)
        fill(0, frame_flags(tail_mine_ref[CACHE * pairs], range(CACHE - 2, CACHE)) + live[0:2])

    @pl.when(jnp.logical_not(earlier))
    def _():
        plane[:, 0:CACHE] = jnp.zeros(plane.shape[:1] + (CACHE,) + plane.shape[2:], plane.dtype)
        operand[:, 0:2] = jnp.zeros(operand.shape[:1] + (2,) + operand.shape[2:], operand.dtype)
        fill(2, live[0:2])

    def put(ref):
        def store(frame, row, value):
            ref[frame, row] = value
        return store

    def then(start, part, result):
        finish(mine_ref, other_ref, live, start, (core, held - 1), result, (put(keep_ref), put(send_ref)))

    in_turn(convolved(operand, w2_ref, bias2_ref, 0, CACHE, rows - 2, then))
    keep_ref[CACHE:] = late_keep_ref[...]
    send_ref[CACHE:] = late_send_ref[...]


def place_kernel(keep_ref, got_ref, result_ref, arrived):
    core = lower_part()
    frames, half = keep_ref.shape[:2]
    step = max(1, frames // 4)
    copies = []
    for source, place in ((keep_ref, core), (got_ref, 1 - core)):
        for frame in range(0, frames, step):
            chosen = pl.ds(frame, min(step, frames - frame))
            copies.append(pltpu.make_async_copy(
                source.at[chosen], result_ref.at[chosen, pl.ds(half * place, half)], arrived.at[len(copies)]
            ))
    for copy in copies:
        copy.start()
    for copy in copies:
        copy.wait()


def shards(features, frame_counts, gain_first, conv_first, bias_first, gain_second, conv_second, bias_second):
    frames, rows, side, channels = features.shape
    pairs, half = rows // 2, rows // 2
    held = half // 2 + 1
    tall, cores, blocks = lax.axis_size("ha"), lax.axis_size("wa"), lax.axis_size("tchunk")
    packed, width, tiles = 3 * LANES, 2 * side, CACHE * held
    bf16 = jnp.bfloat16
    vmem = pl.BlockSpec(memory_space=pltpu.VMEM)
    limit = pltpu.CompilerParams(vmem_limit_bytes=20 * 2**20)
    work = 2 * TAPS**3 * channels * channels * width

    def shape(*extent):
        return jax.ShapeDtypeStruct(extent, bf16)

    def cost(flops, fetched):
        return pl.CostEstimate(flops=flops, bytes_accessed=fetched, transcendentals=0)

    slots = pl.pallas_call(
        slots_kernel,
        out_shape=jax.ShapeDtypeStruct((side, packed), jnp.int32),
        out_specs=vmem,
        compiler_params=limit,
        cost_estimate=cost(2**34, 2**20),
    )()
    slots, frame_counts = lax.optimization_barrier((slots, frame_counts))
    tail, mine, theirs, marks = pl.pallas_call(
        prepare_kernel,
        out_shape=(
            shape(CACHE * pairs + 1, side, packed), shape(frames, held, side, packed),
            shape((CACHE + frames) * held, side, packed), shape(side, packed),
        ),
        in_specs=[pl.BlockSpec(memory_space=pltpu.SMEM), vmem, vmem],
        out_specs=(vmem,) * 4,
        scratch_shapes=[pltpu.VMEM((frames, pairs, side, packed), bf16)],
        compiler_params=limit,
    )(frame_counts, slots, features)

    if blocks > 2:
        tail = joined_tail(tail)
        rest = lax.dynamic_slice_in_dim(
            tail[:-1].reshape(CACHE, pairs, side, packed), (1 - lower_part()) * (pairs - held), held, 1
        )
        theirs = jnp.concatenate([rest.reshape(tiles, side, packed), theirs[tiles:]], axis=0)
    straight, diagonal, across = [], [], []

    def index(block, h, core):
        return (block * tall + h) * cores + core

    for k in range(blocks - 1):
        for h in range(tall):
            for core in range(cores):
                straight.append((index(k, h, core), index(k + 1, h, core)))
    for h in range(tall - 1):
        for k in range(blocks):
            lower, upper = index(k, h, 0), index(k, h + 1, 1)
            across += [(lower, upper), (upper, lower)]
            if k + 1 < blocks:
                lower_next, upper_next = index(k + 1, h, 0), index(k + 1, h + 1, 1)
                diagonal += [(lower, upper_next), (upper, lower_next)]
    axes = ("tchunk", "ha", "wa")
    swap = [(0, 1), (1, 0)]
    tail_mine = lax.ppermute(tail, axes, straight)
    other = lax.ppermute(theirs, "wa", swap)
    tail_edge, own_edge = pl.pallas_call(
        border_kernel,
        out_shape=(shape(tiles + 1, side, packed), shape(2, frames, side, packed)),
        in_specs=[vmem] * 3,
        out_specs=(vmem, vmem),
        compiler_params=limit,
        cost_estimate=cost(2**34, 2**20),
    )(tail, mine, other)
    own_edge = lax.ppermute(own_edge, axes, across)
    tail_edge = lax.ppermute(tail_edge, axes, diagonal)

    weights = (
        gain_first.reshape(1, channels), conv_first, bias_first.reshape(1, channels),
        gain_second.reshape(1, channels), conv_second, bias_second.reshape(1, channels),
    )
    first, late = pl.pallas_call(
        own_kernel,
        out_shape=(shape(3, frames, half + 2, width, LANES), shape(3, frames - 2, half, width, LANES)),
        in_specs=[vmem] * 7,
        out_specs=(vmem,) * 2,
        compiler_params=limit,
        cost_estimate=cost(work * (frames - 2) * half, 4 * 2**20),
    )(marks, mine, other, *weights[:4])
    tail_rows, rest = pl.pallas_call(
        tail_kernel,
        out_shape=(shape(tiles, side, packed), shape(tiles, side, packed)),
        in_specs=[vmem, vmem, pl.BlockSpec(memory_space=pl.ANY)],
        out_specs=(vmem, vmem),
        scratch_shapes=[pltpu.VMEM((CACHE * pairs, side, packed), bf16)],
        compiler_params=limit,
        cost_estimate=cost(1, 1),
    )(tail_mine, weights[0], late)
    tail_other = lax.ppermute(rest, "wa", swap)
    strip, hidden, keep, send = pl.pallas_call(
        edge_kernel,
        out_shape=(
            shape(3, 2, 2, width, LANES), shape(3, 2, half + 2, width, LANES),
            shape(frames - CACHE, half, side, channels), shape(frames - CACHE, half, side, channels),
        ),
        in_specs=[vmem] * 12,
        out_specs=(vmem,) * 4,
        scratch_shapes=[
            pltpu.VMEM((3, frames, 4, width, LANES), bf16),
            pltpu.VMEM((3, frames - 2, 4, width, LANES), bf16),
        ],
        compiler_params=limit,
        cost_estimate=cost(2**20, 2**20),
    )(marks, mine, other, own_edge, first, late, *weights)
    keep, send = pl.pallas_call(
        early_kernel,
        out_shape=(shape(frames, half, side, channels), shape(frames, half, side, channels)),
        in_specs=[vmem] * 18,
        out_specs=(vmem, vmem),
        scratch_shapes=[
            pltpu.VMEM((3, CACHE + 2, half + 4, width, LANES), bf16),
            pltpu.VMEM((3, CACHE + 2, half + 2, width, LANES), bf16),
        ],
        compiler_params=limit,
        cost_estimate=cost(work * CACHE * (2 * half + 2), 8 * 2**20),
    )(marks, tail_mine, tail_rows, tail_other, mine, other, tail_edge, first, strip, hidden, keep, send, *weights)
    got = lax.ppermute(send, "wa", swap)
    return pl.pallas_call(
        place_kernel,
        out_shape=shape(*features.shape),
        in_specs=[vmem, vmem],
        out_specs=pl.BlockSpec(memory_space=pltpu.HBM),
        scratch_shapes=[pltpu.SemaphoreType.DMA((2 * frames,))],
        compiler_params=limit,
    )(keep, got)


def solution(mesh):
    return jax.shard_map(
        shards,
        mesh=mesh,
        in_specs=(
            P(("grp", "tchunk"), "ha", "wa", None),
            P(("grp", "tchunk")),
            P(), P(), P(), P(), P(), P(),
        ),
        out_specs=P(("grp", "tchunk"), "ha", "wa", None),
        check_vma=False,
    )
```

```python
import jax
import jax.numpy as jnp
from jax import lax
from jax.experimental import pallas as pl
from jax.experimental.pallas import tpu as pltpu
from jax.sharding import PartitionSpec as P

epsilon = 1e-06
CACHE = 4
TAPS = 3
LANES = 128
PRODUCT = 192


def slots_kernel(slots_ref):
    slots_ref[...] = lax.broadcasted_iota(jnp.int32, slots_ref.shape, 0)


def lower_part():
    return 1 - lax.axis_index("wa")


def prepare_kernel(total_ref, slots_ref, raw, tail_ref, mine_ref, theirs_ref, marks_ref, pack):
    frames, rows = raw.shape[:2]
    pairs, held = rows // 2, mine_ref.shape[1]
    core = lower_part()
    total = total_ref[0]
    for frame in range(frames):
        for pair in range(pairs):
            first, second = raw[frame, 2 * pair], raw[frame, 2 * pair + 1]
            packed = jnp.concatenate(
                [first[:, :LANES], second[:, :LANES], first[:, LANES:], second[:, LANES:]], axis=-1
            )
            pack[frame, pair] = packed
    for slot in range(CACHE):
        frame = total - CACHE + slot
        value = pack[jnp.maximum(frame, 0)]
        tail_ref[slot * pairs:(slot + 1) * pairs] = jnp.where(frame >= 0, value, jnp.zeros_like(value))
        value = pack[jnp.maximum(frame, 0), pl.ds((1 - core) * (pairs - held), held)]
        theirs_ref[slot * held:(slot + 1) * held] = jnp.where(frame >= 0, value, jnp.zeros_like(value))
    for frame in range(frames):
        start = (CACHE + frame) * held
        value = pack[frame, pl.ds(core * (pairs - held), held)]
        mine_ref[frame] = jnp.where(frame < total, value, jnp.zeros_like(value))
        value = pack[frame, pl.ds((1 - core) * (pairs - held), held)]
        theirs_ref[start:start + held] = jnp.where(frame < total, value, jnp.zeros_like(value))
    slot = slots_ref[...]
    tail_ref[CACHE * pairs] = jnp.where(
        (slot < CACHE) & (total - CACHE + slot >= 0), 1.0, 0.0
    ).astype(tail_ref.dtype)
    marks_ref[...] = jnp.where(slot < total, 1.0, 0.0).astype(marks_ref.dtype)


def joined_tail(tail):
    count = lax.axis_size("tchunk")

    def pushed(value, held):
        return lax.dynamic_slice_in_dim(jnp.concatenate([value, jnp.zeros_like(value)], axis=0), held, CACHE, 0)

    step = 1
    while step < count - 1:
        early = lax.ppermute(tail, "tchunk", [(k, k + step) for k in range(count - step)])
        held = jnp.sum(tail[-1, :CACHE, 0].astype(jnp.int32))
        body = pushed(early[:-1].reshape((CACHE, -1) + tail.shape[1:]), held).reshape(tail[:-1].shape)
        marks = jnp.pad(pushed(early[-1, :CACHE], held), ((0, tail.shape[1] - CACHE), (0, 0)))
        tail = tail + jnp.concatenate([body, marks[None]], axis=0)
        step *= 2
    return tail


def silu(half):
    return half + half * jnp.tanh(half)


def lane_mask():
    return lax.broadcasted_iota(jnp.int32, (1, 1, 1, LANES), 3) < LANES // 2


def gains(gain_ref):
    low, high = 0.5 * gain_ref[:, :LANES], 0.5 * gain_ref[:, LANES:]
    return low.reshape(1, 1, 1, LANES), jnp.concatenate([high, high], axis=-1).reshape(1, 1, 1, LANES)


def rolled(values):
    shape = values.shape
    return pltpu.roll(values.reshape(-1, LANES), LANES // 2, 1).reshape(shape)


def first_rows(left, right, gain_ref, channels):
    raw = jnp.concatenate([left.astype(jnp.float32), right.astype(jnp.float32)], axis=2)
    front, back, high = raw[..., :LANES], raw[..., LANES:2 * LANES], raw[..., 2 * LANES:]
    lower = lane_mask()
    squared = high * high

    def inverse(low, mask):
        total = jnp.sum(low * low + jnp.where(mask, squared, 0.0), axis=-1, keepdims=True)
        return lax.rsqrt(total * (1.0 / channels) + epsilon)

    scale_front, scale_back = inverse(front, lower), inverse(back, jnp.logical_not(lower))
    gain_low, gain_high = gains(gain_ref)
    front = silu(front * scale_front * gain_low)
    back = silu(back * scale_back * gain_low)
    high = silu(high * jnp.where(lower, scale_front, scale_back) * gain_high)
    turned = rolled(high)
    one = [front, jnp.where(lower, high, 0.0), jnp.where(lower, 0.0, turned)]
    two = [back, jnp.where(lower, turned, 0.0), jnp.where(lower, 0.0, high)]
    return [[part.astype(jnp.bfloat16) for part in row] for row in (one, two)]


def second_rows(hidden, flag, gain_ref, channels):
    gain = 0.5 * gain_ref[...].reshape(1, 1, 1, channels)
    total = jnp.sum(hidden * hidden, axis=-1, keepdims=True)
    inverse = lax.rsqrt(total * (1.0 / channels) + epsilon) * flag
    values = silu(hidden * inverse * gain)
    rest = jnp.zeros(values.shape[:-1] + (LANES // 2,), jnp.float32)
    high = jnp.concatenate([values[..., LANES:], rest], axis=-1)
    parts = [values[..., :LANES], high, rolled(high)]
    return jnp.stack([part.astype(jnp.bfloat16) for part in parts])


def in_turn(steps):
    waiting = None
    for product, then in steps:
        result = product()
        if waiting:
            waiting[1](waiting[0])
        waiting = (result, then)
    waiting[1](waiting[0])


def convolved(operand, weights, bias_ref, frame, frames, rows, then, most=PRODUCT):
    products = -(-frames * rows * operand.shape[3] // most)
    step = -(-frames // products)

    def part(start):
        count = min(step, frames - start)
        return (
            lambda: convolved_part(operand, weights, bias_ref, frame + start, count, rows),
            lambda result: then(start, count, result),
        )

    return [part(start) for start in range(0, frames, step)]


def operand_of(weights_ref):
    made = {}

    def weights(groups, j, depth):
        key = (groups[0][0], j)
        if key not in made:
            rights = []
            for group in groups:
                held = [weights_ref[a, i, j] for a, i in group]
                rights += [weight[:LANES] for weight in held] + [weight[LANES:] for weight in held]
            rest = depth - sum(right.shape[0] for right in rights)
            if rest:
                rights.append(jnp.zeros((rest, weights_ref.shape[-1]), jnp.bfloat16))
            made[key] = jnp.concatenate(rights, axis=0)
        return made[key]

    return weights


def convolved_part(operand, weights, bias_ref, frame, frames, rows):
    width = operand.shape[3]
    channels = bias_ref.shape[-1]
    taps = [(a, i) for a in range(TAPS) for i in range(TAPS)]
    groups = [taps[start:start + 2] for start in range(0, len(taps), 2)]

    def window(tap, part):
        a, i = tap
        value = operand[part, frame + a:frame + a + frames, i:i + rows]
        return value.reshape(frames * rows * width, LANES)

    def operands(groups):
        pieces = []
        for group in groups:
            pieces += [window(tap, 0) for tap in group]
            high = window(group[0], 1)
            pieces.append(high + window(group[1], 2) if len(group) > 1 else high)
        return jnp.concatenate(pieces, axis=-1)

    half = len(groups) // 2
    parts = [(part, operands(part)) for part in (groups[:half], groups[half:])]
    products = []
    for j in range(TAPS):
        total = None
        for part, left in parts if j % 2 == 0 else parts[::-1]:
            product = jnp.dot(left, weights(part, j, left.shape[1]), preferred_element_type=jnp.float32)
            total = product if total is None else total + product
        products.append(total.reshape(frames * rows, width, channels))
    column = lax.broadcasted_iota(jnp.int32, (1, width, 1), 1)
    before = jnp.where(column == 0, 0.0, pltpu.roll(products[0], 1, 1))
    after = jnp.where(column == width - 1, 0.0, pltpu.roll(products[2], width - 1, 1))
    result = products[1] + before + after + bias_ref[...].reshape(1, 1, channels)
    return result.reshape(frames, rows, width, channels)


def halves(core, mine, other):
    return jnp.where(core == 0, mine, other), jnp.where(core == 0, other, mine)


def frame_flags(marks, frames):
    values = marks.astype(jnp.float32)
    return [values[k:k + 1, 0:1].reshape(1, 1, 1, 1) for k in frames]


def fill_rows(operand, frame, row, mine, other, gain_ref):
    left, right = halves(lax.axis_index("wa"), mine, other)
    frames, pairs = mine.shape[:2]
    upper, lower = first_rows(left, right, gain_ref, gain_ref.shape[-1])
    for part in range(len(upper)):
        for pair in range(pairs):
            operand[part, frame:frame + frames, pl.ds(row + 2 * pair, 1)] = upper[part][:, pair:pair + 1]
            operand[part, frame:frame + frames, pl.ds(row + 2 * pair + 1, 1)] = lower[part][:, pair:pair + 1]


def border_kernel(tail_ref, mine_ref, other_ref, tail_edge_ref, own_edge_ref):
    frames, held = mine_ref.shape[:2]
    pairs = tail_ref.shape[0] // CACHE
    core = lower_part()
    pair = core * (held - 1)
    for slot in range(CACHE):
        tail_edge_ref[slot] = tail_ref[slot * pairs + core * (pairs - 1)]
        tail_edge_ref[CACHE + slot] = other_ref[slot * held + pair]
    spare = tail_edge_ref.shape[0] - 2 * CACHE
    tail_edge_ref[2 * CACHE:] = jnp.zeros((spare,) + tail_edge_ref.shape[1:], tail_edge_ref.dtype)
    for frame in range(frames):
        own_edge_ref[0, frame] = mine_ref[frame, pair]
        own_edge_ref[1, frame] = other_ref[(CACHE + frame) * held + pair]


def finish(mine_ref, other_ref, live, first, pairs, value, targets):
    _, held, side, _ = mine_ref.shape
    frames, channels = value.shape[0], value.shape[-1]
    start, count = pairs
    near, far = halves(lax.axis_index("wa"), value[:, :, :side], value[:, :, side:])
    for mine, value, target in ((True, near, targets[0]), (False, far, targets[1])):
        for frame in range(frames):
            for k in range(count):
                if mine:
                    raw = mine_ref[first + frame, start + k]
                else:
                    raw = other_ref[(CACHE + first + frame) * held + start + k]
                raw = raw.astype(jnp.float32)
                high = raw[:, 2 * LANES:]
                for row, tail in ((0, high), (1, pltpu.roll(high, LANES // 2, 1))):
                    low = raw[:, row * LANES:(row + 1) * LANES]
                    features = jnp.concatenate([low, tail[:, :channels - LANES]], axis=-1)
                    summed = features + value[frame, 2 * k + row]
                    kept = jnp.where(live[first + frame].reshape(1, 1) > 0.5, summed, 0.0)
                    target(first + frame, 2 * k + row, kept.astype(jnp.bfloat16))


def hide(operand, weights, bias_ref, gain_ref, first, count, rows, flags, store, most=PRODUCT):
    channels = bias_ref.shape[-1]

    def then(begin, part, hidden):
        flag = jnp.concatenate(flags[begin:begin + part], axis=0)
        store(begin, begin + part, second_rows(hidden, flag, gain_ref, channels))

    return convolved(operand, weights, bias_ref, first, count, rows, then, most)


def inside_flags(rows):
    core, place = lower_part(), lax.axis_index("ha")
    inside = jnp.where(core == 0, place > 0, place < lax.axis_size("ha") - 1)
    row = lax.broadcasted_iota(jnp.int32, (1, rows, 1, 1), 1)
    return jnp.where((row == (rows - 1) * core) & jnp.logical_not(inside), 0.0, 1.0)


def other_rows_kernel(tail_ref, late_ref, rest_ref):
    pairs, held = tail_ref.shape[0] // CACHE, rest_ref.shape[0] // CACHE
    first = (1 - lower_part()) * (pairs - held)
    for slot in range(CACHE):
        rest_ref[slot * held:(slot + 1) * held] = tail_ref[pl.ds(slot * pairs + first, held)]


def own_kernel(
    marks_ref, mine_ref, other_ref, gain1_ref, w1_ref, bias1_ref, gain2_ref, first_ref, late_ref
):
    frames, pairs, side, packed = mine_ref.shape
    live = frame_flags(marks_ref[...], range(2, frames))

    def fill(start, end):
        other = other_ref[(CACHE + start) * pairs:(CACHE + end) * pairs].reshape(end - start, pairs, side, packed)
        fill_rows(first_ref, start, 0, mine_ref[start:end], other, gain1_ref)

    def store(begin, end, rows):
        late_ref[:, begin:end] = rows

    steps = hide(first_ref, operand_of(w1_ref), bias1_ref, gain2_ref, 0, frames - 2, 2 * pairs - 2, live, store, 2 * PRODUCT // 3)
    each = -(-(frames - 2) // len(steps))

    def filled(k, product):
        def run():
            fill(min(frames, each * k + (2 if k else 0)), min(frames, each * (k + 1) + 2))
            return product()
        return run

    in_turn([(filled(k, product), then) for k, (product, then) in enumerate(steps)])


def edge_kernel(
    marks_ref, mine_ref, other_ref, edge_ref, first_ref, late_ref,
    gain1_ref, w1_ref, bias1_ref, gain2_ref, w2_ref, bias2_ref,
    strip_ref, hidden_ref, keep_ref, send_ref, strip, operand,
):
    core = lower_part()
    frames, pairs = mine_ref.shape[:2]
    rows = 2 * pairs
    late = frames - CACHE
    outward, inward = pl.ds(2 * core, 2), pl.ds(2 * (1 - core), 2)
    fill_rows(strip, 0, 2 * core, edge_ref[1][:, None], edge_ref[0][:, None], gain1_ref)
    strip[:, :, inward] = first_ref[:, :, pl.ds((rows - 2) * core, 2)]
    operand[:, :, inward] = late_ref[:, :, pl.ds((rows - 4) * core, 2)]
    live = frame_flags(marks_ref[...], range(frames))
    inside = inside_flags(2)

    def store(begin, end, values):
        operand[:, begin:end, outward] = values

    def finished(start_row, pair, count):
        def put(ref):
            def store(frame, row, value):
                ref[frame - CACHE, start_row + row] = value
            return store

        def then(start, part, result):
            targets = (put(keep_ref), put(send_ref))
            finish(mine_ref, other_ref, live, CACHE + start, (pair, count), result, targets)

        return then

    flags = [flag * inside for flag in live[2:]]
    middle, border = finished(2 * (1 - core), 1, pairs - 2), finished((rows - 4) * core, (pairs - 1) * core, 1)
    second = operand_of(w2_ref)
    in_turn(
        hide(strip, operand_of(w1_ref), bias1_ref, gain2_ref, 0, frames - 2, 2, flags, store)
        + convolved(late_ref, second, bias2_ref, 0, late, rows - 4, middle)
        + convolved(operand, second, bias2_ref, 0, late, 2, border)
    )
    strip_ref[...] = strip[:, 0:2, outward]
    hidden_ref[:, :, pl.ds(2 * (1 - core), rows - 2)] = late_ref[:, 0:2]
    hidden_ref[:, :, pl.ds((rows - 2) * core, 2)] = operand[:, 0:2, outward]


def early_kernel(
    marks_ref, tail_mine_ref, tail_other_ref, mine_ref, other_ref, edge_ref, first_ref, strip_ref, hidden_ref,
    late_keep_ref, late_send_ref, gain1_ref, w1_ref, bias1_ref, gain2_ref, w2_ref, bias2_ref,
    keep_ref, send_ref, plane, operand,
):
    core = lower_part()
    held = mine_ref.shape[1]
    rows = 2 * held
    pairs = tail_mine_ref.shape[0] // CACHE
    live = frame_flags(marks_ref[...], range(CACHE))
    inside = inside_flags(rows)
    earlier = lax.axis_index("tchunk") > 0
    middle, border = 2 * (1 - core), rows * core

    def unpacked(ref, stride, first):
        return jnp.stack([ref[pl.ds(slot * stride + first, held)] for slot in range(CACHE)])

    plane[:, CACHE:, pl.ds(middle, rows)] = first_ref[:, 0:2]
    plane[:, CACHE:, pl.ds(border, 2)] = strip_ref[...]
    operand[:, CACHE:] = hidden_ref[...]

    def fill(first, flags):
        def store(begin, end, values):
            operand[:, first + begin:first + end] = values

        flags = [flag * inside for flag in flags]
        in_turn(hide(plane, operand_of(w1_ref), bias1_ref, gain2_ref, first, CACHE - first, rows, flags, store))

    @pl.when(earlier)
    def _():
        mine = unpacked(tail_mine_ref, pairs, core * (pairs - held))
        fill_rows(plane, 0, middle, mine, unpacked(tail_other_ref, held, 0), gain1_ref)
        mine, other = edge_ref[CACHE:2 * CACHE], edge_ref[0:CACHE]
        fill_rows(plane, 0, border, mine[:, None], other[:, None], gain1_ref)
        fill(0, frame_flags(tail_mine_ref[CACHE * pairs], range(CACHE - 2, CACHE)) + live[0:2])

    @pl.when(jnp.logical_not(earlier))
    def _():
        plane[:, 0:CACHE] = jnp.zeros(plane.shape[:1] + (CACHE,) + plane.shape[2:], plane.dtype)
        operand[:, 0:2] = jnp.zeros(operand.shape[:1] + (2,) + operand.shape[2:], operand.dtype)
        fill(2, live[0:2])

    def put(ref):
        def store(frame, row, value):
            ref[frame, row] = value
        return store

    def then(start, part, result):
        finish(mine_ref, other_ref, live, start, (core, held - 1), result, (put(keep_ref), put(send_ref)))

    in_turn(convolved(operand, operand_of(w2_ref), bias2_ref, 0, CACHE, rows - 2, then))
    keep_ref[CACHE:] = late_keep_ref[...]
    send_ref[CACHE:] = late_send_ref[...]


def place_kernel(keep_ref, got_ref, result_ref, arrived):
    core, half = lower_part(), keep_ref.shape[1]
    copies = [
        pltpu.make_async_copy(keep_ref, result_ref.at[:, pl.ds(half * core, half)], arrived.at[0]),
        pltpu.make_async_copy(got_ref, result_ref.at[:, pl.ds(half * (1 - core), half)], arrived.at[1]),
    ]
    for copy in copies:
        copy.start()
    for copy in copies:
        copy.wait()


def shards(features, frame_counts, gain_first, conv_first, bias_first, gain_second, conv_second, bias_second):
    frames, rows, side, channels = features.shape
    pairs, half = rows // 2, rows // 2
    held = half // 2 + 1
    tall, cores, blocks = lax.axis_size("ha"), lax.axis_size("wa"), lax.axis_size("tchunk")
    packed, width, tiles = 3 * LANES, 2 * side, CACHE * held
    bf16 = jnp.bfloat16
    vmem = pl.BlockSpec(memory_space=pltpu.VMEM)
    limit = pltpu.CompilerParams(vmem_limit_bytes=20 * 2**20)
    work = 2 * TAPS**3 * channels * channels * width

    def shape(*extent):
        return jax.ShapeDtypeStruct(extent, bf16)

    def cost(flops, fetched):
        return pl.CostEstimate(flops=flops, bytes_accessed=fetched, transcendentals=0)

    slots = pl.pallas_call(
        slots_kernel,
        out_shape=jax.ShapeDtypeStruct((side, packed), jnp.int32),
        out_specs=vmem,
        compiler_params=limit,
        cost_estimate=cost(2**34, 2**20),
    )()
    slots, frame_counts = lax.optimization_barrier((slots, frame_counts))
    tail, mine, theirs, marks = pl.pallas_call(
        prepare_kernel,
        out_shape=(
            shape(CACHE * pairs + 1, side, packed), shape(frames, held, side, packed),
            shape((CACHE + frames) * held, side, packed), shape(side, packed),
        ),
        in_specs=[pl.BlockSpec(memory_space=pltpu.SMEM), vmem, vmem],
        out_specs=(vmem,) * 4,
        scratch_shapes=[pltpu.VMEM((frames, pairs, side, packed), bf16)],
        compiler_params=limit,
    )(frame_counts, slots, features)

    if blocks > 2:
        tail = joined_tail(tail)
        rest = lax.dynamic_slice_in_dim(
            tail[:-1].reshape(CACHE, pairs, side, packed), (1 - lower_part()) * (pairs - held), held, 1
        )
        theirs = jnp.concatenate([rest.reshape(tiles, side, packed), theirs[tiles:]], axis=0)
    straight, diagonal, across = [], [], []

    def index(block, h, core):
        return (block * tall + h) * cores + core

    for k in range(blocks - 1):
        for h in range(tall):
            for core in range(cores):
                straight.append((index(k, h, core), index(k + 1, h, core)))
    for h in range(tall - 1):
        for k in range(blocks):
            lower, upper = index(k, h, 0), index(k, h + 1, 1)
            across += [(lower, upper), (upper, lower)]
            if k + 1 < blocks:
                lower_next, upper_next = index(k + 1, h, 0), index(k + 1, h + 1, 1)
                diagonal += [(lower, upper_next), (upper, lower_next)]
    axes = ("tchunk", "ha", "wa")
    swap = [(0, 1), (1, 0)]
    tail_mine = lax.ppermute(tail, axes, straight)
    other = lax.ppermute(theirs, "wa", swap)
    tail_edge, own_edge = pl.pallas_call(
        border_kernel,
        out_shape=(shape(tiles + 1, side, packed), shape(2, frames, side, packed)),
        in_specs=[vmem] * 3,
        out_specs=(vmem, vmem),
        compiler_params=limit,
        cost_estimate=cost(2**34, 2**20),
    )(tail, mine, other)
    own_edge = lax.ppermute(own_edge, axes, across)
    tail_edge = lax.ppermute(tail_edge, axes, diagonal)

    weights = (
        gain_first.reshape(1, channels), conv_first, bias_first.reshape(1, channels),
        gain_second.reshape(1, channels), conv_second, bias_second.reshape(1, channels),
    )
    first, late = pl.pallas_call(
        own_kernel,
        out_shape=(shape(3, frames, half + 2, width, LANES), shape(3, frames - 2, half, width, LANES)),
        in_specs=[vmem] * 7,
        out_specs=(vmem,) * 2,
        compiler_params=limit,
        cost_estimate=cost(work * (frames - 2) * half, 4 * 2**20),
    )(marks, mine, other, *weights[:4])
    rest = pl.pallas_call(
        other_rows_kernel,
        out_shape=shape(tiles, side, packed),
        in_specs=[vmem, pl.BlockSpec(memory_space=pl.ANY)],
        out_specs=vmem,
        compiler_params=limit,
        cost_estimate=cost(1, 1),
    )(tail_mine, late)
    tail_other = lax.ppermute(rest, "wa", swap)
    strip, hidden, keep, send = pl.pallas_call(
        edge_kernel,
        out_shape=(
            shape(3, 2, 2, width, LANES), shape(3, 2, half + 2, width, LANES),
            shape(frames - CACHE, half, side, channels), shape(frames - CACHE, half, side, channels),
        ),
        in_specs=[vmem] * 12,
        out_specs=(vmem,) * 4,
        scratch_shapes=[
            pltpu.VMEM((3, frames, 4, width, LANES), bf16),
            pltpu.VMEM((3, frames - 2, 4, width, LANES), bf16),
        ],
        compiler_params=limit,
        cost_estimate=cost(2**20, 2**20),
    )(marks, mine, other, own_edge, first, late, *weights)
    keep, send = pl.pallas_call(
        early_kernel,
        out_shape=(shape(frames, half, side, channels), shape(frames, half, side, channels)),
        in_specs=[vmem] * 17,
        out_specs=(vmem, vmem),
        scratch_shapes=[
            pltpu.VMEM((3, CACHE + 2, half + 4, width, LANES), bf16),
            pltpu.VMEM((3, CACHE + 2, half + 2, width, LANES), bf16),
        ],
        compiler_params=limit,
        cost_estimate=cost(work * CACHE * (2 * half + 2), 8 * 2**20),
    )(marks, tail_mine, tail_other, mine, other, tail_edge, first, strip, hidden, keep, send, *weights)
    got = lax.ppermute(send, "wa", swap)
    return pl.pallas_call(
        place_kernel,
        out_shape=shape(*features.shape),
        in_specs=[vmem, vmem],
        out_specs=pl.BlockSpec(memory_space=pltpu.HBM),
        scratch_shapes=[pltpu.SemaphoreType.DMA((2,))],
        compiler_params=limit,
    )(keep, got)


def solution(mesh):
    return jax.shard_map(
        shards,
        mesh=mesh,
        in_specs=(
            P(("grp", "tchunk"), "ha", "wa", None),
            P(("grp", "tchunk")),
            P(), P(), P(), P(), P(), P(),
        ),
        out_specs=P(("grp", "tchunk"), "ha", "wa", None),
        check_vma=False,
    )
```

```python
import jax
import jax.numpy as jnp
from jax import lax
from jax.experimental import pallas as pl
from jax.experimental.pallas import tpu as pltpu
from jax.sharding import PartitionSpec as P

epsilon = 1e-06
CACHE = 4
TAPS = 3
LANES = 128
PRODUCT = 192


def slots_kernel(slots_ref):
    slots_ref[...] = lax.broadcasted_iota(jnp.int32, slots_ref.shape, 0)


def lower_part():
    return 1 - lax.axis_index("wa")


def prepare_kernel(total_ref, slots_ref, raw, tail_ref, mine_ref, theirs_ref, marks_ref, pack):
    frames, rows = raw.shape[:2]
    pairs, held = rows // 2, mine_ref.shape[1]
    core = lower_part()
    total = total_ref[0]
    for frame in range(frames):
        for pair in range(pairs):
            first, second = raw[frame, 2 * pair], raw[frame, 2 * pair + 1]
            packed = jnp.concatenate(
                [first[:, :LANES], second[:, :LANES], first[:, LANES:], second[:, LANES:]], axis=-1
            )
            pack[frame, pair] = packed
    for slot in range(CACHE):
        frame = total - CACHE + slot
        value = pack[jnp.maximum(frame, 0)]
        tail_ref[slot * pairs:(slot + 1) * pairs] = jnp.where(frame >= 0, value, jnp.zeros_like(value))
        value = pack[jnp.maximum(frame, 0), pl.ds((1 - core) * (pairs - held), held)]
        theirs_ref[slot * held:(slot + 1) * held] = jnp.where(frame >= 0, value, jnp.zeros_like(value))
    for frame in range(frames):
        start = (CACHE + frame) * held
        value = pack[frame, pl.ds(core * (pairs - held), held)]
        mine_ref[frame] = jnp.where(frame < total, value, jnp.zeros_like(value))
        value = pack[frame, pl.ds((1 - core) * (pairs - held), held)]
        theirs_ref[start:start + held] = jnp.where(frame < total, value, jnp.zeros_like(value))
    slot = slots_ref[...]
    tail_ref[CACHE * pairs] = jnp.where(
        (slot < CACHE) & (total - CACHE + slot >= 0), 1.0, 0.0
    ).astype(tail_ref.dtype)
    marks_ref[...] = jnp.where(slot < total, 1.0, 0.0).astype(marks_ref.dtype)


def joined_tail(tail):
    count = lax.axis_size("tchunk")

    def pushed(value, held):
        return lax.dynamic_slice_in_dim(jnp.concatenate([value, jnp.zeros_like(value)], axis=0), held, CACHE, 0)

    step = 1
    while step < count - 1:
        early = lax.ppermute(tail, "tchunk", [(k, k + step) for k in range(count - step)])
        held = jnp.sum(tail[-1, :CACHE, 0].astype(jnp.int32))
        body = pushed(early[:-1].reshape((CACHE, -1) + tail.shape[1:]), held).reshape(tail[:-1].shape)
        marks = jnp.pad(pushed(early[-1, :CACHE], held), ((0, tail.shape[1] - CACHE), (0, 0)))
        tail = tail + jnp.concatenate([body, marks[None]], axis=0)
        step *= 2
    return tail


def silu(half):
    return half + half * jnp.tanh(half)


def lane_mask():
    return lax.broadcasted_iota(jnp.int32, (1, 1, 1, LANES), 3) < LANES // 2


def gains(gain_ref):
    low, high = 0.5 * gain_ref[:, :LANES], 0.5 * gain_ref[:, LANES:]
    return low.reshape(1, 1, 1, LANES), jnp.concatenate([high, high], axis=-1).reshape(1, 1, 1, LANES)


def rolled(values):
    shape = values.shape
    return pltpu.roll(values.reshape(-1, LANES), LANES // 2, 1).reshape(shape)


def first_rows(left, right, gain_ref, channels):
    raw = jnp.concatenate([left.astype(jnp.float32), right.astype(jnp.float32)], axis=2)
    front, back, high = raw[..., :LANES], raw[..., LANES:2 * LANES], raw[..., 2 * LANES:]
    lower = lane_mask()
    squared = high * high

    def inverse(low, mask):
        total = jnp.sum(low * low + jnp.where(mask, squared, 0.0), axis=-1, keepdims=True)
        return lax.rsqrt(total * (1.0 / channels) + epsilon)

    scale_front, scale_back = inverse(front, lower), inverse(back, jnp.logical_not(lower))
    gain_low, gain_high = gains(gain_ref)
    front = silu(front * scale_front * gain_low)
    back = silu(back * scale_back * gain_low)
    high = silu(high * jnp.where(lower, scale_front, scale_back) * gain_high)
    turned = rolled(high)
    one = [front, jnp.where(lower, high, 0.0), jnp.where(lower, 0.0, turned)]
    two = [back, jnp.where(lower, turned, 0.0), jnp.where(lower, 0.0, high)]
    return [[part.astype(jnp.bfloat16) for part in row] for row in (one, two)]


def second_rows(hidden, flag, gain_ref, channels):
    gain = 0.5 * gain_ref[...].reshape(1, 1, 1, channels)
    total = jnp.sum(hidden * hidden, axis=-1, keepdims=True)
    inverse = lax.rsqrt(total * (1.0 / channels) + epsilon) * flag
    values = silu(hidden * inverse * gain)
    rest = jnp.zeros(values.shape[:-1] + (LANES // 2,), jnp.float32)
    high = jnp.concatenate([values[..., LANES:], rest], axis=-1)
    parts = [values[..., :LANES], high, rolled(high)]
    return jnp.stack([part.astype(jnp.bfloat16) for part in parts])


def in_turn(steps):
    waiting = None
    for product, then in steps:
        result = product()
        if waiting:
            waiting[1](waiting[0])
        waiting = (result, then)
    waiting[1](waiting[0])


def convolved(operand, weights_ref, bias_ref, frame, frames, rows, then, most=PRODUCT):
    products = -(-frames * rows * operand.shape[3] // most)
    step = -(-frames // products)

    def part(start):
        count = min(step, frames - start)
        return (
            lambda: convolved_part(operand, weights_ref, bias_ref, frame + start, count, rows),
            lambda result: then(start, count, result),
        )

    return [part(start) for start in range(0, frames, step)]


def convolved_part(operand, weights_ref, bias_ref, frame, frames, rows):
    width = operand.shape[3]
    channels = weights_ref.shape[-1]
    taps = [(a, i) for a in range(TAPS) for i in range(TAPS)]
    groups = [taps[start:start + 2] for start in range(0, len(taps), 2)]

    def window(tap, part):
        a, i = tap
        value = operand[part, frame + a:frame + a + frames, i:i + rows]
        return value.reshape(frames * rows * width, LANES)

    def operands(groups):
        pieces = []
        for group in groups:
            pieces += [window(tap, 0) for tap in group]
            high = window(group[0], 1)
            pieces.append(high + window(group[1], 2) if len(group) > 1 else high)
        return jnp.concatenate(pieces, axis=-1)

    def weights(groups, j, depth):
        rights = []
        for group in groups:
            held = [weights_ref[a, i, j] for a, i in group]
            rights += [weight[:LANES] for weight in held] + [weight[LANES:] for weight in held]
        rest = depth - sum(right.shape[0] for right in rights)
        if rest:
            rights.append(jnp.zeros((rest, channels), jnp.bfloat16))
        return jnp.concatenate(rights, axis=0)

    half = len(groups) // 2
    parts = [(part, operands(part)) for part in (groups[:half], groups[half:])]
    products = []
    for j in range(TAPS):
        total = None
        for part, left in parts if j % 2 == 0 else parts[::-1]:
            product = jnp.dot(left, weights(part, j, left.shape[1]), preferred_element_type=jnp.float32)
            total = product if total is None else total + product
        products.append(total.reshape(frames * rows, width, channels))
    column = lax.broadcasted_iota(jnp.int32, (1, width, 1), 1)
    before = jnp.where(column == 0, 0.0, pltpu.roll(products[0], 1, 1))
    after = jnp.where(column == width - 1, 0.0, pltpu.roll(products[2], width - 1, 1))
    result = products[1] + before + after + bias_ref[...].reshape(1, 1, channels)
    return result.reshape(frames, rows, width, channels)


def halves(core, mine, other):
    return jnp.where(core == 0, mine, other), jnp.where(core == 0, other, mine)


def frame_flags(marks, frames):
    values = marks.astype(jnp.float32)
    return [values[k:k + 1, 0:1].reshape(1, 1, 1, 1) for k in frames]


def fill_rows(operand, frame, row, mine, other, gain_ref):
    left, right = halves(lax.axis_index("wa"), mine, other)
    frames, pairs = mine.shape[:2]
    upper, lower = first_rows(left, right, gain_ref, gain_ref.shape[-1])
    for part in range(len(upper)):
        for pair in range(pairs):
            operand[part, frame:frame + frames, pl.ds(row + 2 * pair, 1)] = upper[part][:, pair:pair + 1]
            operand[part, frame:frame + frames, pl.ds(row + 2 * pair + 1, 1)] = lower[part][:, pair:pair + 1]


def border_kernel(tail_ref, mine_ref, other_ref, tail_edge_ref, own_edge_ref):
    frames, held = mine_ref.shape[:2]
    pairs = tail_ref.shape[0] // CACHE
    core = lower_part()
    pair = core * (held - 1)
    for slot in range(CACHE):
        tail_edge_ref[slot] = tail_ref[slot * pairs + core * (pairs - 1)]
        tail_edge_ref[CACHE + slot] = other_ref[slot * held + pair]
    for frame in range(frames):
        own_edge_ref[0, frame] = mine_ref[frame, pair]
        own_edge_ref[1, frame] = other_ref[(CACHE + frame) * held + pair]


def finish(mine_ref, other_ref, live, first, pairs, value, targets):
    _, held, side, _ = mine_ref.shape
    frames, channels = value.shape[0], value.shape[-1]
    start, count = pairs
    near, far = halves(lax.axis_index("wa"), value[:, :, :side], value[:, :, side:])
    for mine, value, target in ((True, near, targets[0]), (False, far, targets[1])):
        for frame in range(frames):
            for k in range(count):
                if mine:
                    raw = mine_ref[first + frame, start + k]
                else:
                    raw = other_ref[(CACHE + first + frame) * held + start + k]
                raw = raw.astype(jnp.float32)
                high = raw[:, 2 * LANES:]
                for row, tail in ((0, high), (1, pltpu.roll(high, LANES // 2, 1))):
                    low = raw[:, row * LANES:(row + 1) * LANES]
                    features = jnp.concatenate([low, tail[:, :channels - LANES]], axis=-1)
                    summed = features + value[frame, 2 * k + row]
                    kept = jnp.where(live[first + frame].reshape(1, 1) > 0.5, summed, 0.0)
                    target(first + frame, 2 * k + row, kept.astype(jnp.bfloat16))


def hide(operand, weights_ref, bias_ref, gain_ref, first, count, rows, flags, store, most=PRODUCT):
    channels = weights_ref.shape[-1]

    def then(begin, part, hidden):
        flag = jnp.concatenate(flags[begin:begin + part], axis=0)
        store(begin, begin + part, second_rows(hidden, flag, gain_ref, channels))

    return convolved(operand, weights_ref, bias_ref, first, count, rows, then, most)


def inside_flags(rows):
    core, place = lower_part(), lax.axis_index("ha")
    inside = jnp.where(core == 0, place > 0, place < lax.axis_size("ha") - 1)
    row = lax.broadcasted_iota(jnp.int32, (1, rows, 1, 1), 1)
    return jnp.where((row == (rows - 1) * core) & jnp.logical_not(inside), 0.0, 1.0)


def other_rows_kernel(tail_ref, late_ref, rest_ref):
    pairs, held = tail_ref.shape[0] // CACHE, rest_ref.shape[0] // CACHE
    first = (1 - lower_part()) * (pairs - held)
    for slot in range(CACHE):
        rest_ref[slot * held:(slot + 1) * held] = tail_ref[pl.ds(slot * pairs + first, held)]


def own_kernel(
    marks_ref, mine_ref, other_ref, gain1_ref, w1_ref, bias1_ref, gain2_ref, first_ref, late_ref
):
    frames, pairs, side, packed = mine_ref.shape
    live = frame_flags(marks_ref[...], range(2, frames))

    def fill(start, end):
        other = other_ref[(CACHE + start) * pairs:(CACHE + end) * pairs].reshape(end - start, pairs, side, packed)
        fill_rows(first_ref, start, 0, mine_ref[start:end], other, gain1_ref)

    def store(begin, end, rows):
        late_ref[:, begin:end] = rows

    steps = hide(first_ref, w1_ref, bias1_ref, gain2_ref, 0, frames - 2, 2 * pairs - 2, live, store, 2 * PRODUCT // 3)
    each = -(-(frames - 2) // len(steps))

    def filled(k, product):
        def run():
            fill(min(frames, each * k + (2 if k else 0)), min(frames, each * (k + 1) + 2))
            return product()
        return run

    in_turn([(filled(k, product), then) for k, (product, then) in enumerate(steps)])


def edge_kernel(
    marks_ref, mine_ref, other_ref, edge_ref, first_ref, late_ref,
    gain1_ref, w1_ref, bias1_ref, gain2_ref, w2_ref, bias2_ref,
    strip_ref, hidden_ref, keep_ref, send_ref, strip, operand,
):
    core = lower_part()
    frames, pairs = mine_ref.shape[:2]
    rows = 2 * pairs
    late = frames - CACHE
    outward, inward = pl.ds(2 * core, 2), pl.ds(2 * (1 - core), 2)
    fill_rows(strip, 0, 2 * core, edge_ref[1][:, None], edge_ref[0][:, None], gain1_ref)
    strip[:, :, inward] = first_ref[:, :, pl.ds((rows - 2) * core, 2)]
    operand[:, :, inward] = late_ref[:, :, pl.ds((rows - 4) * core, 2)]
    live = frame_flags(marks_ref[...], range(frames))
    inside = inside_flags(2)

    def store(begin, end, values):
        operand[:, begin:end, outward] = values

    def finished(start_row, pair, count):
        def put(ref):
            def store(frame, row, value):
                ref[frame - CACHE, start_row + row] = value
            return store

        def then(start, part, result):
            targets = (put(keep_ref), put(send_ref))
            finish(mine_ref, other_ref, live, CACHE + start, (pair, count), result, targets)

        return then

    flags = [flag * inside for flag in live[2:]]
    middle, border = finished(2 * (1 - core), 1, pairs - 2), finished((rows - 4) * core, (pairs - 1) * core, 1)
    in_turn(
        hide(strip, w1_ref, bias1_ref, gain2_ref, 0, frames - 2, 2, flags, store)
        + convolved(late_ref, w2_ref, bias2_ref, 0, late, rows - 4, middle)
        + convolved(operand, w2_ref, bias2_ref, 0, late, 2, border)
    )
    strip_ref[...] = strip[:, 0:2, outward]
    hidden_ref[:, :, pl.ds(2 * (1 - core), rows - 2)] = late_ref[:, 0:2]
    hidden_ref[:, :, pl.ds((rows - 2) * core, 2)] = operand[:, 0:2, outward]


def tail_edge_kernel(edge_ref, strip_ref, gain_ref, rows_ref):
    rows_ref[:, CACHE:] = strip_ref[...]

    @pl.when(lax.axis_index("tchunk") > 0)
    def _():
        fill_rows(rows_ref, 0, 0, edge_ref[CACHE:2 * CACHE][:, None], edge_ref[0:CACHE][:, None], gain_ref)

    @pl.when(lax.axis_index("tchunk") == 0)
    def _():
        rows_ref[:, 0:CACHE] = jnp.zeros((rows_ref.shape[0], CACHE) + rows_ref.shape[2:], rows_ref.dtype)


def early_kernel(
    marks_ref, tail_mine_ref, tail_other_ref, mine_ref, other_ref, edge_ref, first_ref, hidden_ref,
    late_keep_ref, late_send_ref, gain1_ref, w1_ref, bias1_ref, gain2_ref, w2_ref, bias2_ref,
    keep_ref, send_ref, plane, operand,
):
    core = lower_part()
    held = mine_ref.shape[1]
    rows = 2 * held
    pairs = tail_mine_ref.shape[0] // CACHE
    live = frame_flags(marks_ref[...], range(CACHE))
    inside = inside_flags(rows)
    earlier = lax.axis_index("tchunk") > 0
    middle, border = 2 * (1 - core), rows * core

    def unpacked(ref, stride, first):
        return jnp.stack([ref[pl.ds(slot * stride + first, held)] for slot in range(CACHE)])

    plane[:, CACHE:, pl.ds(middle, rows)] = first_ref[:, 0:2]
    plane[:, :, pl.ds(border, 2)] = edge_ref[...]
    operand[:, CACHE:] = hidden_ref[...]

    def fill(first, flags):
        def store(begin, end, values):
            operand[:, first + begin:first + end] = values

        flags = [flag * inside for flag in flags]
        in_turn(hide(plane, w1_ref, bias1_ref, gain2_ref, first, CACHE - first, rows, flags, store))

    @pl.when(earlier)
    def _():
        mine = unpacked(tail_mine_ref, pairs, core * (pairs - held))
        fill_rows(plane, 0, middle, mine, unpacked(tail_other_ref, held, 0), gain1_ref)
        fill(0, frame_flags(tail_mine_ref[CACHE * pairs], range(CACHE - 2, CACHE)) + live[0:2])

    @pl.when(jnp.logical_not(earlier))
    def _():
        plane[:, 0:CACHE, pl.ds(middle, rows)] = jnp.zeros(
            plane.shape[:1] + (CACHE, rows) + plane.shape[3:], plane.dtype
        )
        operand[:, 0:2] = jnp.zeros(operand.shape[:1] + (2,) + operand.shape[2:], operand.dtype)
        fill(2, live[0:2])

    def put(ref):
        def store(frame, row, value):
            ref[frame, row] = value
        return store

    def then(start, part, result):
        finish(mine_ref, other_ref, live, start, (core, held - 1), result, (put(keep_ref), put(send_ref)))

    in_turn(convolved(operand, w2_ref, bias2_ref, 0, CACHE, rows - 2, then))
    keep_ref[CACHE:] = late_keep_ref[...]
    send_ref[CACHE:] = late_send_ref[...]


def place_kernel(keep_ref, got_ref, result_ref, arrived):
    core, half = lower_part(), keep_ref.shape[1]
    copies = [
        pltpu.make_async_copy(keep_ref, result_ref.at[:, pl.ds(half * core, half)], arrived.at[0]),
        pltpu.make_async_copy(got_ref, result_ref.at[:, pl.ds(half * (1 - core), half)], arrived.at[1]),
    ]
    for copy in copies:
        copy.start()
    for copy in copies:
        copy.wait()


def shards(features, frame_counts, gain_first, conv_first, bias_first, gain_second, conv_second, bias_second):
    frames, rows, side, channels = features.shape
    pairs, half = rows // 2, rows // 2
    held = half // 2 + 1
    tall, cores, blocks = lax.axis_size("ha"), lax.axis_size("wa"), lax.axis_size("tchunk")
    packed, width, tiles = 3 * LANES, 2 * side, CACHE * held
    bf16 = jnp.bfloat16
    vmem = pl.BlockSpec(memory_space=pltpu.VMEM)
    limit = pltpu.CompilerParams(vmem_limit_bytes=20 * 2**20)
    work = 2 * TAPS**3 * channels * channels * width

    def shape(*extent):
        return jax.ShapeDtypeStruct(extent, bf16)

    def cost(flops, fetched):
        return pl.CostEstimate(flops=flops, bytes_accessed=fetched, transcendentals=0)

    slots = pl.pallas_call(
        slots_kernel,
        out_shape=jax.ShapeDtypeStruct((side, packed), jnp.int32),
        out_specs=vmem,
        compiler_params=limit,
        cost_estimate=cost(2**34, 2**20),
    )()
    slots, frame_counts = lax.optimization_barrier((slots, frame_counts))
    tail, mine, theirs, marks = pl.pallas_call(
        prepare_kernel,
        out_shape=(
            shape(CACHE * pairs + 1, side, packed), shape(frames, held, side, packed),
            shape((CACHE + frames) * held, side, packed), shape(side, packed),
        ),
        in_specs=[pl.BlockSpec(memory_space=pltpu.SMEM), vmem, vmem],
        out_specs=(vmem,) * 4,
        scratch_shapes=[pltpu.VMEM((frames, pairs, side, packed), bf16)],
        compiler_params=limit,
    )(frame_counts, slots, features)

    if blocks > 2:
        tail = joined_tail(tail)
        rest = lax.dynamic_slice_in_dim(
            tail[:-1].reshape(CACHE, pairs, side, packed), (1 - lower_part()) * (pairs - held), held, 1
        )
        theirs = jnp.concatenate([rest.reshape(tiles, side, packed), theirs[tiles:]], axis=0)
    straight, diagonal, across = [], [], []

    def index(block, h, core):
        return (block * tall + h) * cores + core

    for k in range(blocks - 1):
        for h in range(tall):
            for core in range(cores):
                straight.append((index(k, h, core), index(k + 1, h, core)))
    for h in range(tall - 1):
        for k in range(blocks):
            lower, upper = index(k, h, 0), index(k, h + 1, 1)
            across += [(lower, upper), (upper, lower)]
            if k + 1 < blocks:
                lower_next, upper_next = index(k + 1, h, 0), index(k + 1, h + 1, 1)
                diagonal += [(lower, upper_next), (upper, lower_next)]
    axes = ("tchunk", "ha", "wa")
    swap = [(0, 1), (1, 0)]
    tail_mine = lax.ppermute(tail, axes, straight)
    other = lax.ppermute(theirs, "wa", swap)
    tail_edge, own_edge = pl.pallas_call(
        border_kernel,
        out_shape=(shape(2 * CACHE, side, packed), shape(2, frames, side, packed)),
        in_specs=[vmem] * 3,
        out_specs=(vmem, vmem),
        compiler_params=limit,
        cost_estimate=cost(2**34, 2**20),
    )(tail, mine, other)
    own_edge = lax.ppermute(own_edge, axes, across)
    tail_edge = lax.ppermute(tail_edge, axes, diagonal)

    weights = (
        gain_first.reshape(1, channels), conv_first, bias_first.reshape(1, channels),
        gain_second.reshape(1, channels), conv_second, bias_second.reshape(1, channels),
    )
    first, late = pl.pallas_call(
        own_kernel,
        out_shape=(shape(3, frames, half + 2, width, LANES), shape(3, frames - 2, half, width, LANES)),
        in_specs=[vmem] * 7,
        out_specs=(vmem,) * 2,
        compiler_params=limit,
        cost_estimate=cost(work * (frames - 2) * half, 4 * 2**20),
    )(marks, mine, other, *weights[:4])
    rest = pl.pallas_call(
        other_rows_kernel,
        out_shape=shape(tiles, side, packed),
        in_specs=[vmem, pl.BlockSpec(memory_space=pl.ANY)],
        out_specs=vmem,
        compiler_params=limit,
        cost_estimate=cost(1, 1),
    )(tail_mine, late)
    tail_other = lax.ppermute(rest, "wa", swap)
    strip, hidden, keep, send = pl.pallas_call(
        edge_kernel,
        out_shape=(
            shape(3, 2, 2, width, LANES), shape(3, 2, half + 2, width, LANES),
            shape(frames - CACHE, half, side, channels), shape(frames - CACHE, half, side, channels),
        ),
        in_specs=[vmem] * 12,
        out_specs=(vmem,) * 4,
        scratch_shapes=[
            pltpu.VMEM((3, frames, 4, width, LANES), bf16),
            pltpu.VMEM((3, frames - 2, 4, width, LANES), bf16),
        ],
        compiler_params=limit,
        cost_estimate=cost(2**20, 2**20),
    )(marks, mine, other, own_edge, first, late, *weights)
    tail_edge = pl.pallas_call(
        tail_edge_kernel,
        out_shape=shape(3, CACHE + 2, 2, width, LANES),
        in_specs=[vmem] * 3,
        out_specs=vmem,
        compiler_params=limit,
        cost_estimate=cost(2**30, 2**18),
    )(tail_edge, strip, weights[0])
    keep, send = pl.pallas_call(
        early_kernel,
        out_shape=(shape(frames, half, side, channels), shape(frames, half, side, channels)),
        in_specs=[vmem] * 16,
        out_specs=(vmem, vmem),
        scratch_shapes=[
            pltpu.VMEM((3, CACHE + 2, half + 4, width, LANES), bf16),
            pltpu.VMEM((3, CACHE + 2, half + 2, width, LANES), bf16),
        ],
        compiler_params=limit,
        cost_estimate=cost(work * CACHE * (2 * half + 2), 8 * 2**20),
    )(marks, tail_mine, tail_other, mine, other, tail_edge, first, hidden, keep, send, *weights)
    got = lax.ppermute(send, "wa", swap)
    return pl.pallas_call(
        place_kernel,
        out_shape=shape(*features.shape),
        in_specs=[vmem, vmem],
        out_specs=pl.BlockSpec(memory_space=pltpu.HBM),
        scratch_shapes=[pltpu.SemaphoreType.DMA((2,))],
        compiler_params=limit,
    )(keep, got)


def solution(mesh):
    return jax.shard_map(
        shards,
        mesh=mesh,
        in_specs=(
            P(("grp", "tchunk"), "ha", "wa", None),
            P(("grp", "tchunk")),
            P(), P(), P(), P(), P(), P(),
        ),
        out_specs=P(("grp", "tchunk"), "ha", "wa", None),
        check_vma=False,
    )
```

```python
import jax
import jax.numpy as jnp
from jax import lax
from jax.experimental import pallas as pl
from jax.experimental.pallas import tpu as pltpu
from jax.sharding import PartitionSpec as P

epsilon = 1e-06
CACHE = 4
TAPS = 3
LANES = 128
PRODUCT = 192
OWN = 128


def slots_kernel(slots_ref):
    slots_ref[...] = lax.broadcasted_iota(jnp.int32, slots_ref.shape, 0)


def lower_part():
    return 1 - lax.axis_index("wa")


def prepare_kernel(total_ref, slots_ref, raw, tail_ref, mine_ref, theirs_ref, marks_ref, pack):
    frames, rows = raw.shape[:2]
    pairs, held = rows // 2, mine_ref.shape[1]
    core = lower_part()
    total = total_ref[0]
    for frame in range(frames):
        for pair in range(pairs):
            first, second = raw[frame, 2 * pair], raw[frame, 2 * pair + 1]
            packed = jnp.concatenate(
                [first[:, :LANES], second[:, :LANES], first[:, LANES:], second[:, LANES:]], axis=-1
            )
            pack[frame, pair] = packed
    for slot in range(CACHE):
        frame = total - CACHE + slot
        value = pack[jnp.maximum(frame, 0)]
        tail_ref[slot * pairs:(slot + 1) * pairs] = jnp.where(frame >= 0, value, jnp.zeros_like(value))
        value = pack[jnp.maximum(frame, 0), pl.ds((1 - core) * (pairs - held), held)]
        theirs_ref[slot * held:(slot + 1) * held] = jnp.where(frame >= 0, value, jnp.zeros_like(value))
    for frame in range(frames):
        start = (CACHE + frame) * held
        value = pack[frame, pl.ds(core * (pairs - held), held)]
        mine_ref[frame] = jnp.where(frame < total, value, jnp.zeros_like(value))
        value = pack[frame, pl.ds((1 - core) * (pairs - held), held)]
        theirs_ref[start:start + held] = jnp.where(frame < total, value, jnp.zeros_like(value))
    slot = slots_ref[...]
    tail_ref[CACHE * pairs] = jnp.where(
        (slot < CACHE) & (total - CACHE + slot >= 0), 1.0, 0.0
    ).astype(tail_ref.dtype)
    marks_ref[...] = jnp.where(slot < total, 1.0, 0.0).astype(marks_ref.dtype)


def joined_tail(tail):
    count = lax.axis_size("tchunk")

    def pushed(value, held):
        return lax.dynamic_slice_in_dim(jnp.concatenate([value, jnp.zeros_like(value)], axis=0), held, CACHE, 0)

    step = 1
    while step < count - 1:
        early = lax.ppermute(tail, "tchunk", [(k, k + step) for k in range(count - step)])
        held = jnp.sum(tail[-1, :CACHE, 0].astype(jnp.int32))
        body = pushed(early[:-1].reshape((CACHE, -1) + tail.shape[1:]), held).reshape(tail[:-1].shape)
        marks = jnp.pad(pushed(early[-1, :CACHE], held), ((0, tail.shape[1] - CACHE), (0, 0)))
        tail = tail + jnp.concatenate([body, marks[None]], axis=0)
        step *= 2
    return tail


def silu(half):
    return half + half * jnp.tanh(half)


def lane_mask():
    return lax.broadcasted_iota(jnp.int32, (1, 1, 1, LANES), 3) < LANES // 2


def gains(gain_ref):
    low, high = 0.5 * gain_ref[:, :LANES], 0.5 * gain_ref[:, LANES:]
    return low.reshape(1, 1, 1, LANES), jnp.concatenate([high, high], axis=-1).reshape(1, 1, 1, LANES)


def rolled(values):
    shape = values.shape
    return pltpu.roll(values.reshape(-1, LANES), LANES // 2, 1).reshape(shape)


def first_rows(left, right, gain_ref, channels):
    raw = jnp.concatenate([left.astype(jnp.float32), right.astype(jnp.float32)], axis=2)
    front, back, high = raw[..., :LANES], raw[..., LANES:2 * LANES], raw[..., 2 * LANES:]
    lower = lane_mask()
    squared = high * high

    def inverse(low, mask):
        total = jnp.sum(low * low + jnp.where(mask, squared, 0.0), axis=-1, keepdims=True)
        return lax.rsqrt(total * (1.0 / channels) + epsilon)

    scale_front, scale_back = inverse(front, lower), inverse(back, jnp.logical_not(lower))
    gain_low, gain_high = gains(gain_ref)
    front = silu(front * scale_front * gain_low)
    back = silu(back * scale_back * gain_low)
    high = silu(high * jnp.where(lower, scale_front, scale_back) * gain_high)
    turned = rolled(high)
    one = [front, jnp.where(lower, high, 0.0), jnp.where(lower, 0.0, turned)]
    two = [back, jnp.where(lower, turned, 0.0), jnp.where(lower, 0.0, high)]
    return [[part.astype(jnp.bfloat16) for part in row] for row in (one, two)]


def second_rows(hidden, flag, gain_ref, channels):
    gain = 0.5 * gain_ref[...].reshape(1, 1, 1, channels)
    total = jnp.sum(hidden * hidden, axis=-1, keepdims=True)
    inverse = lax.rsqrt(total * (1.0 / channels) + epsilon) * flag
    values = silu(hidden * inverse * gain)
    rest = jnp.zeros(values.shape[:-1] + (LANES // 2,), jnp.float32)
    high = jnp.concatenate([values[..., LANES:], rest], axis=-1)
    parts = [values[..., :LANES], high, rolled(high)]
    return jnp.stack([part.astype(jnp.bfloat16) for part in parts])


def in_turn(steps, beside=None):
    waiting = None
    for product, then in steps:
        result = product()
        if waiting:
            waiting[1](waiting[0])
        elif beside:
            beside()
        waiting = (result, then)
    waiting[1](waiting[0])


def convolved(operand, weights_ref, bias_ref, frame, frames, rows, then, most=PRODUCT):
    products = -(-frames * rows * operand.shape[3] // most)
    step = -(-frames // products)

    def part(start):
        count = min(step, frames - start)
        return (
            lambda: convolved_part(operand, weights_ref, bias_ref, frame + start, count, rows),
            lambda result: then(start, count, result),
        )

    return [part(start) for start in range(0, frames, step)]


def convolved_part(operand, weights_ref, bias_ref, frame, frames, rows):
    width = operand.shape[3]
    channels = weights_ref.shape[-1]
    taps = [(a, i) for a in range(TAPS) for i in range(TAPS)]
    groups = [taps[start:start + 2] for start in range(0, len(taps), 2)]

    def window(tap, part):
        a, i = tap
        value = operand[part, frame + a:frame + a + frames, i:i + rows]
        return value.reshape(frames * rows * width, LANES)

    def operands(groups):
        pieces = []
        for group in groups:
            pieces += [window(tap, 0) for tap in group]
            high = window(group[0], 1)
            pieces.append(high + window(group[1], 2) if len(group) > 1 else high)
        return jnp.concatenate(pieces, axis=-1)

    def weights(groups, j, depth):
        rights = []
        for group in groups:
            held = [weights_ref[a, i, j] for a, i in group]
            rights += [weight[:LANES] for weight in held] + [weight[LANES:] for weight in held]
        rest = depth - sum(right.shape[0] for right in rights)
        if rest:
            rights.append(jnp.zeros((rest, channels), jnp.bfloat16))
        return jnp.concatenate(rights, axis=0)

    half = len(groups) // 2
    parts = [(part, operands(part)) for part in (groups[:half], groups[half:])]
    products = []
    for j in range(TAPS):
        total = None
        for part, left in parts if j % 2 == 0 else parts[::-1]:
            product = jnp.dot(left, weights(part, j, left.shape[1]), preferred_element_type=jnp.float32)
            total = product if total is None else total + product
        products.append(total.reshape(frames * rows, width, channels))
    column = lax.broadcasted_iota(jnp.int32, (1, width, 1), 1)
    before = jnp.where(column == 0, 0.0, pltpu.roll(products[0], 1, 1))
    after = jnp.where(column == width - 1, 0.0, pltpu.roll(products[2], width - 1, 1))
    result = products[1] + before + after + bias_ref[...].reshape(1, 1, channels)
    return result.reshape(frames, rows, width, channels)


def halves(core, mine, other):
    return jnp.where(core == 0, mine, other), jnp.where(core == 0, other, mine)


def frame_flags(marks, frames):
    values = marks.astype(jnp.float32)
    return [values[k:k + 1, 0:1].reshape(1, 1, 1, 1) for k in frames]


def fill_rows(operand, frame, row, mine, other, gain_ref):
    left, right = halves(lax.axis_index("wa"), mine, other)
    frames, pairs = mine.shape[:2]
    upper, lower = first_rows(left, right, gain_ref, gain_ref.shape[-1])
    for part in range(len(upper)):
        for pair in range(pairs):
            operand[part, frame:frame + frames, pl.ds(row + 2 * pair, 1)] = upper[part][:, pair:pair + 1]
            operand[part, frame:frame + frames, pl.ds(row + 2 * pair + 1, 1)] = lower[part][:, pair:pair + 1]


def border_kernel(tail_ref, mine_ref, other_ref, tail_edge_ref, own_edge_ref):
    frames, held = mine_ref.shape[:2]
    pairs = tail_ref.shape[0] // CACHE
    core = lower_part()
    pair = core * (held - 1)
    for slot in range(CACHE):
        tail_edge_ref[slot] = tail_ref[slot * pairs + core * (pairs - 1)]
        tail_edge_ref[CACHE + slot] = other_ref[slot * held + pair]
    for frame in range(frames):
        own_edge_ref[0, frame] = mine_ref[frame, pair]
        own_edge_ref[1, frame] = other_ref[(CACHE + frame) * held + pair]


def finish(mine_ref, other_ref, live, first, pairs, value, targets):
    _, held, side, _ = mine_ref.shape
    frames, channels = value.shape[0], value.shape[-1]
    start, count = pairs
    near, far = halves(lax.axis_index("wa"), value[:, :, :side], value[:, :, side:])
    for mine, value, target in ((True, near, targets[0]), (False, far, targets[1])):
        for frame in range(frames):
            for k in range(count):
                if mine:
                    raw = mine_ref[first + frame, start + k]
                else:
                    raw = other_ref[(CACHE + first + frame) * held + start + k]
                raw = raw.astype(jnp.float32)
                high = raw[:, 2 * LANES:]
                for row, tail in ((0, high), (1, pltpu.roll(high, LANES // 2, 1))):
                    low = raw[:, row * LANES:(row + 1) * LANES]
                    features = jnp.concatenate([low, tail[:, :channels - LANES]], axis=-1)
                    summed = features + value[frame, 2 * k + row]
                    kept = jnp.where(live[first + frame].reshape(1, 1) > 0.5, summed, 0.0)
                    target(first + frame, 2 * k + row, kept.astype(jnp.bfloat16))


def hide(operand, weights_ref, bias_ref, gain_ref, first, count, rows, flags, store, most=PRODUCT):
    channels = weights_ref.shape[-1]

    def then(begin, part, hidden):
        flag = jnp.concatenate(flags[begin:begin + part], axis=0)
        store(begin, begin + part, second_rows(hidden, flag, gain_ref, channels))

    return convolved(operand, weights_ref, bias_ref, first, count, rows, then, most)


def inside_flags(rows):
    core, place = lower_part(), lax.axis_index("ha")
    inside = jnp.where(core == 0, place > 0, place < lax.axis_size("ha") - 1)
    row = lax.broadcasted_iota(jnp.int32, (1, rows, 1, 1), 1)
    return jnp.where((row == (rows - 1) * core) & jnp.logical_not(inside), 0.0, 1.0)


def other_rows_kernel(tail_ref, late_ref, rest_ref):
    pairs, held = tail_ref.shape[0] // CACHE, rest_ref.shape[0] // CACHE
    first = (1 - lower_part()) * (pairs - held)
    for slot in range(CACHE):
        rest_ref[slot * held:(slot + 1) * held] = tail_ref[pl.ds(slot * pairs + first, held)]


def own_kernel(
    marks_ref, mine_ref, other_ref, gain1_ref, w1_ref, bias1_ref, gain2_ref,
    first_ref, late_ref, raw_ref,
):
    frames, pairs, side, packed = mine_ref.shape
    live = frame_flags(marks_ref[...], range(2, frames))

    def fill(start, end):
        other = other_ref[(CACHE + start) * pairs:(CACHE + end) * pairs].reshape(end - start, pairs, side, packed)
        fill_rows(first_ref, start, 0, mine_ref[start:end], other, gain1_ref)

    def store(begin, end, rows):
        late_ref[:, begin:end] = rows

    steps = hide(first_ref, w1_ref, bias1_ref, gain2_ref, 0, frames - 2, 2 * pairs - 2, live, store, OWN)
    each = -(-(frames - 2) // len(steps))

    def filled(k, product):
        def run():
            fill(min(frames, each * k + (2 if k else 0)), min(frames, each * (k + 1) + 2))
            return product()
        return run

    def left(result):
        raw_ref[...] = result

    steps[-1] = (steps[-1][0], left)
    in_turn([(filled(k, product), then) for k, (product, then) in enumerate(steps)])


def edge_kernel(
    marks_ref, mine_ref, other_ref, edge_ref, first_ref, done_ref, raw_ref,
    gain1_ref, w1_ref, bias1_ref, gain2_ref, w2_ref, bias2_ref,
    strip_ref, hidden_ref, keep_ref, send_ref, border_ref, strip, operand, late_ref,
):
    core = lower_part()
    frames, pairs = mine_ref.shape[:2]
    rows = 2 * pairs
    late = frames - CACHE
    outward, inward = pl.ds(2 * core, 2), pl.ds(2 * (1 - core), 2)
    fill_rows(strip, 0, 2 * core, edge_ref[1][:, None], edge_ref[0][:, None], gain1_ref)
    strip[:, :, inward] = first_ref[:, :, pl.ds((rows - 2) * core, 2)]
    live = frame_flags(marks_ref[...], range(frames))
    inside = inside_flags(2)
    done = done_ref.shape[1]
    late_ref[:, 0:done] = done_ref[...]

    def activate():
        flag = jnp.concatenate(live[2 + done:], axis=0)
        late_ref[:, done:] = second_rows(raw_ref[...], flag, gain2_ref, gain2_ref.shape[-1])
        operand[:, :, inward] = late_ref[:, :, pl.ds((rows - 4) * core, 2)]

    def store(begin, end, values):
        operand[:, begin:end, outward] = values

    def put(ref):
        def store(frame, row, value):
            ref[frame - CACHE, row] = value
        return store

    def middle(start, part, result):
        targets = (put(keep_ref), put(send_ref))
        finish(mine_ref, other_ref, live, CACHE + start, (1, pairs - 2), result, targets)

    def border(start, part, result):
        border_ref[start:start + part] = result

    flags = [flag * inside for flag in live[2:]]
    in_turn(
        hide(strip, w1_ref, bias1_ref, gain2_ref, 0, frames - 2, 2, flags, store)
        + convolved(late_ref, w2_ref, bias2_ref, 0, late, rows - 4, middle)
        + convolved(operand, w2_ref, bias2_ref, 0, late, 2, border),
        activate,
    )
    strip_ref[...] = strip[:, 0:2, outward]
    hidden_ref[:, :, pl.ds(2 * (1 - core), rows - 2)] = late_ref[:, 0:2]
    hidden_ref[:, :, pl.ds((rows - 2) * core, 2)] = operand[:, 0:2, outward]


def tail_edge_kernel(edge_ref, strip_ref, gain_ref, rows_ref):
    rows_ref[:, CACHE:] = strip_ref[...]

    @pl.when(lax.axis_index("tchunk") > 0)
    def _():
        fill_rows(rows_ref, 0, 0, edge_ref[CACHE:2 * CACHE][:, None], edge_ref[0:CACHE][:, None], gain_ref)

    @pl.when(lax.axis_index("tchunk") == 0)
    def _():
        rows_ref[:, 0:CACHE] = jnp.zeros((rows_ref.shape[0], CACHE) + rows_ref.shape[2:], rows_ref.dtype)


def early_kernel(
    marks_ref, tail_mine_ref, tail_other_ref, mine_ref, other_ref, edge_ref, first_ref, hidden_ref,
    late_keep_ref, late_send_ref, late_border_ref, gain1_ref, w1_ref, bias1_ref, gain2_ref, w2_ref, bias2_ref,
    keep_ref, send_ref, plane, operand,
):
    core = lower_part()
    held = mine_ref.shape[1]
    rows = 2 * held
    pairs = tail_mine_ref.shape[0] // CACHE
    live = frame_flags(marks_ref[...], range(mine_ref.shape[0]))
    inside = inside_flags(rows)
    earlier = lax.axis_index("tchunk") > 0
    middle, border = 2 * (1 - core), rows * core

    def unpacked(ref, stride, first):
        return jnp.stack([ref[pl.ds(slot * stride + first, held)] for slot in range(CACHE)])

    plane[:, CACHE:, pl.ds(middle, rows)] = first_ref[:, 0:2]
    plane[:, :, pl.ds(border, 2)] = edge_ref[...]
    operand[:, CACHE:] = hidden_ref[...]

    def put(ref, offset=0):
        def store(frame, row, value):
            ref[frame, offset + row] = value
        return store

    def finish_late():
        offset = (rows - 4) * core
        targets = (put(keep_ref, offset), put(send_ref, offset))
        finish(mine_ref, other_ref, live, CACHE, ((held - 1) * core, 1), late_border_ref[...], targets)
        for source, target in ((late_keep_ref, keep_ref), (late_send_ref, send_ref)):
            target[CACHE:, pl.ds(2 * (1 - core), rows - 4)] = source[...]

    def fill(first, flags):
        def store(begin, end, values):
            operand[:, first + begin:first + end] = values

        flags = [flag * inside for flag in flags]
        in_turn(hide(plane, w1_ref, bias1_ref, gain2_ref, first, CACHE - first, rows, flags, store), finish_late)

    @pl.when(earlier)
    def _():
        mine = unpacked(tail_mine_ref, pairs, core * (pairs - held))
        fill_rows(plane, 0, middle, mine, unpacked(tail_other_ref, held, 0), gain1_ref)
        fill(0, frame_flags(tail_mine_ref[CACHE * pairs], range(CACHE - 2, CACHE)) + live[0:2])

    @pl.when(jnp.logical_not(earlier))
    def _():
        plane[:, 0:CACHE, pl.ds(middle, rows)] = jnp.zeros(
            plane.shape[:1] + (CACHE, rows) + plane.shape[3:], plane.dtype
        )
        operand[:, 0:2] = jnp.zeros(operand.shape[:1] + (2,) + operand.shape[2:], operand.dtype)
        fill(2, live[0:2])

    def then(start, part, result):
        finish(mine_ref, other_ref, live, start, (core, held - 1), result, (put(keep_ref), put(send_ref)))

    in_turn(convolved(operand, w2_ref, bias2_ref, 0, CACHE, rows - 2, then))


def place_kernel(keep_ref, got_ref, result_ref, arrived):
    core, half = lower_part(), keep_ref.shape[1]
    copies = [
        pltpu.make_async_copy(keep_ref, result_ref.at[:, pl.ds(half * core, half)], arrived.at[0]),
        pltpu.make_async_copy(got_ref, result_ref.at[:, pl.ds(half * (1 - core), half)], arrived.at[1]),
    ]
    for copy in copies:
        copy.start()
    for copy in copies:
        copy.wait()


def shards(features, frame_counts, gain_first, conv_first, bias_first, gain_second, conv_second, bias_second):
    frames, rows, side, channels = features.shape
    pairs, half = rows // 2, rows // 2
    held = half // 2 + 1
    tall, cores, blocks = lax.axis_size("ha"), lax.axis_size("wa"), lax.axis_size("tchunk")
    packed, width, tiles = 3 * LANES, 2 * side, CACHE * held
    bf16 = jnp.bfloat16
    vmem = pl.BlockSpec(memory_space=pltpu.VMEM)
    limit = pltpu.CompilerParams(vmem_limit_bytes=20 * 2**20)
    work = 2 * TAPS**3 * channels * channels * width

    def shape(*extent):
        return jax.ShapeDtypeStruct(extent, bf16)

    def cost(flops, fetched):
        return pl.CostEstimate(flops=flops, bytes_accessed=fetched, transcendentals=0)

    slots = pl.pallas_call(
        slots_kernel,
        out_shape=jax.ShapeDtypeStruct((side, packed), jnp.int32),
        out_specs=vmem,
        compiler_params=limit,
        cost_estimate=cost(2**34, 2**20),
    )()
    slots, frame_counts = lax.optimization_barrier((slots, frame_counts))
    tail, mine, theirs, marks = pl.pallas_call(
        prepare_kernel,
        out_shape=(
            shape(CACHE * pairs + 1, side, packed), shape(frames, held, side, packed),
            shape((CACHE + frames) * held, side, packed), shape(side, packed),
        ),
        in_specs=[pl.BlockSpec(memory_space=pltpu.SMEM), vmem, vmem],
        out_specs=(vmem,) * 4,
        scratch_shapes=[pltpu.VMEM((frames, pairs, side, packed), bf16)],
        compiler_params=limit,
    )(frame_counts, slots, features)

    if blocks > 2:
        tail = joined_tail(tail)
        rest = lax.dynamic_slice_in_dim(
            tail[:-1].reshape(CACHE, pairs, side, packed), (1 - lower_part()) * (pairs - held), held, 1
        )
        theirs = jnp.concatenate([rest.reshape(tiles, side, packed), theirs[tiles:]], axis=0)
    straight, diagonal, across = [], [], []

    def index(block, h, core):
        return (block * tall + h) * cores + core

    for k in range(blocks - 1):
        for h in range(tall):
            for core in range(cores):
                straight.append((index(k, h, core), index(k + 1, h, core)))
    for h in range(tall - 1):
        for k in range(blocks):
            lower, upper = index(k, h, 0), index(k, h + 1, 1)
            across += [(lower, upper), (upper, lower)]
            if k + 1 < blocks:
                lower_next, upper_next = index(k + 1, h, 0), index(k + 1, h + 1, 1)
                diagonal += [(lower, upper_next), (upper, lower_next)]
    axes = ("tchunk", "ha", "wa")
    swap = [(0, 1), (1, 0)]
    tail_mine = lax.ppermute(tail, axes, straight)
    other = lax.ppermute(theirs, "wa", swap)
    tail_edge, own_edge = pl.pallas_call(
        border_kernel,
        out_shape=(shape(2 * CACHE, side, packed), shape(2, frames, side, packed)),
        in_specs=[vmem] * 3,
        out_specs=(vmem, vmem),
        compiler_params=limit,
        cost_estimate=cost(2**34, 2**20),
    )(tail, mine, other)
    own_edge = lax.ppermute(own_edge, axes, across)
    tail_edge = lax.ppermute(tail_edge, axes, diagonal)

    weights = (
        gain_first.reshape(1, channels), conv_first, bias_first.reshape(1, channels),
        gain_second.reshape(1, channels), conv_second, bias_second.reshape(1, channels),
    )
    products = -(-(frames - 2) * half * width // OWN)
    done = -(-(frames - 2) // products) * (products - 1)
    first, late, raw = pl.pallas_call(
        own_kernel,
        out_shape=(
            shape(3, frames, half + 2, width, LANES), shape(3, done, half, width, LANES),
            jax.ShapeDtypeStruct((frames - 2 - done, half, width, channels), jnp.float32),
        ),
        in_specs=[vmem] * 7,
        out_specs=(vmem,) * 3,
        compiler_params=limit,
        cost_estimate=cost(work * (frames - 2) * half, 4 * 2**20),
    )(marks, mine, other, *weights[:4])
    rest = pl.pallas_call(
        other_rows_kernel,
        out_shape=shape(tiles, side, packed),
        in_specs=[vmem, pl.BlockSpec(memory_space=pl.ANY)],
        out_specs=vmem,
        compiler_params=limit,
        cost_estimate=cost(1, 1),
    )(tail_mine, late)
    tail_other = lax.ppermute(rest, "wa", swap)
    strip, hidden, keep, send, border = pl.pallas_call(
        edge_kernel,
        out_shape=(
            shape(3, 2, 2, width, LANES), shape(3, 2, half + 2, width, LANES),
            shape(frames - CACHE, half - 2, side, channels), shape(frames - CACHE, half - 2, side, channels),
            jax.ShapeDtypeStruct((frames - CACHE, 2, width, channels), jnp.float32),
        ),
        in_specs=[vmem] * 13,
        out_specs=(vmem,) * 5,
        scratch_shapes=[
            pltpu.VMEM((3, frames, 4, width, LANES), bf16),
            pltpu.VMEM((3, frames - 2, 4, width, LANES), bf16),
            pltpu.VMEM((3, frames - 2, half, width, LANES), bf16),
        ],
        compiler_params=limit,
        cost_estimate=cost(2**20, 2**20),
    )(marks, mine, other, own_edge, first, late, raw, *weights)
    tail_edge = pl.pallas_call(
        tail_edge_kernel,
        out_shape=shape(3, CACHE + 2, 2, width, LANES),
        in_specs=[vmem] * 3,
        out_specs=vmem,
        compiler_params=limit,
        cost_estimate=cost(2**30, 2**18),
    )(tail_edge, strip, weights[0])
    keep, send = pl.pallas_call(
        early_kernel,
        out_shape=(shape(frames, half, side, channels), shape(frames, half, side, channels)),
        in_specs=[vmem] * 17,
        out_specs=(vmem, vmem),
        scratch_shapes=[
            pltpu.VMEM((3, CACHE + 2, half + 4, width, LANES), bf16),
            pltpu.VMEM((3, CACHE + 2, half + 2, width, LANES), bf16),
        ],
        compiler_params=limit,
        cost_estimate=cost(work * CACHE * (2 * half + 2), 8 * 2**20),
    )(marks, tail_mine, tail_other, mine, other, tail_edge, first, hidden, keep, send, border, *weights)
    got = lax.ppermute(send, "wa", swap)
    return pl.pallas_call(
        place_kernel,
        out_shape=shape(*features.shape),
        in_specs=[vmem, vmem],
        out_specs=pl.BlockSpec(memory_space=pltpu.HBM),
        scratch_shapes=[pltpu.SemaphoreType.DMA((2,))],
        compiler_params=limit,
    )(keep, got)


def solution(mesh):
    return jax.shard_map(
        shards,
        mesh=mesh,
        in_specs=(
            P(("grp", "tchunk"), "ha", "wa", None),
            P(("grp", "tchunk")),
            P(), P(), P(), P(), P(), P(),
        ),
        out_specs=P(("grp", "tchunk"), "ha", "wa", None),
        check_vma=False,
    )
```

```python
import jax
import jax.numpy as jnp
from jax import lax
from jax.experimental import pallas as pl
from jax.experimental.pallas import tpu as pltpu
from jax.sharding import PartitionSpec as P

epsilon = 1e-06
CACHE = 4
TAPS = 3
LANES = 128
PRODUCT = 192
OWN = 128


def slots_kernel(slots_ref):
    slots_ref[...] = lax.broadcasted_iota(jnp.int32, slots_ref.shape, 0)


def lower_part():
    return 1 - lax.axis_index("wa")


def prepare_kernel(total_ref, slots_ref, raw, tail_ref, mine_ref, theirs_ref, marks_ref, pack):
    frames, rows = raw.shape[:2]
    pairs, held = rows // 2, mine_ref.shape[1]
    core = lower_part()
    total = total_ref[0]
    for frame in range(frames):
        for pair in range(pairs):
            first, second = raw[frame, 2 * pair], raw[frame, 2 * pair + 1]
            packed = jnp.concatenate(
                [first[:, :LANES], second[:, :LANES], first[:, LANES:], second[:, LANES:]], axis=-1
            )
            pack[frame, pair] = packed
    for slot in range(CACHE):
        frame = total - CACHE + slot
        value = pack[jnp.maximum(frame, 0)]
        tail_ref[slot * pairs:(slot + 1) * pairs] = jnp.where(frame >= 0, value, jnp.zeros_like(value))
        value = pack[jnp.maximum(frame, 0), pl.ds((1 - core) * (pairs - held), held)]
        theirs_ref[slot * held:(slot + 1) * held] = jnp.where(frame >= 0, value, jnp.zeros_like(value))
    for frame in range(frames):
        start = (CACHE + frame) * held
        value = pack[frame, pl.ds(core * (pairs - held), held)]
        mine_ref[frame] = jnp.where(frame < total, value, jnp.zeros_like(value))
        value = pack[frame, pl.ds((1 - core) * (pairs - held), held)]
        theirs_ref[start:start + held] = jnp.where(frame < total, value, jnp.zeros_like(value))
    slot = slots_ref[...]
    tail_ref[CACHE * pairs] = jnp.where(
        (slot < CACHE) & (total - CACHE + slot >= 0), 1.0, 0.0
    ).astype(tail_ref.dtype)
    marks_ref[...] = jnp.where(slot < total, 1.0, 0.0).astype(marks_ref.dtype)


def joined_tail(tail):
    count = lax.axis_size("tchunk")

    def pushed(value, held):
        return lax.dynamic_slice_in_dim(jnp.concatenate([value, jnp.zeros_like(value)], axis=0), held, CACHE, 0)

    step = 1
    while step < count - 1:
        early = lax.ppermute(tail, "tchunk", [(k, k + step) for k in range(count - step)])
        held = jnp.sum(tail[-1, :CACHE, 0].astype(jnp.int32))
        body = pushed(early[:-1].reshape((CACHE, -1) + tail.shape[1:]), held).reshape(tail[:-1].shape)
        marks = jnp.pad(pushed(early[-1, :CACHE], held), ((0, tail.shape[1] - CACHE), (0, 0)))
        tail = tail + jnp.concatenate([body, marks[None]], axis=0)
        step *= 2
    return tail


def silu(half):
    return half + half * jnp.tanh(half)


def lane_mask():
    return lax.broadcasted_iota(jnp.int32, (1, 1, 1, LANES), 3) < LANES // 2


def gains(gain_ref):
    low, high = 0.5 * gain_ref[:, :LANES], 0.5 * gain_ref[:, LANES:]
    return low.reshape(1, 1, 1, LANES), jnp.concatenate([high, high], axis=-1).reshape(1, 1, 1, LANES)


def rolled(values):
    shape = values.shape
    return pltpu.roll(values.reshape(-1, LANES), LANES // 2, 1).reshape(shape)


def first_rows(left, right, gain_ref, channels):
    raw = jnp.concatenate([left.astype(jnp.float32), right.astype(jnp.float32)], axis=2)
    front, back, high = raw[..., :LANES], raw[..., LANES:2 * LANES], raw[..., 2 * LANES:]
    lower = lane_mask()
    squared = high * high

    def inverse(low, mask):
        total = jnp.sum(low * low + jnp.where(mask, squared, 0.0), axis=-1, keepdims=True)
        return lax.rsqrt(total * (1.0 / channels) + epsilon)

    scale_front, scale_back = inverse(front, lower), inverse(back, jnp.logical_not(lower))
    gain_low, gain_high = gains(gain_ref)
    front = silu(front * scale_front * gain_low)
    back = silu(back * scale_back * gain_low)
    high = silu(high * jnp.where(lower, scale_front, scale_back) * gain_high)
    turned = rolled(high)
    one = [front, jnp.where(lower, high, 0.0), jnp.where(lower, 0.0, turned)]
    two = [back, jnp.where(lower, turned, 0.0), jnp.where(lower, 0.0, high)]
    return [[part.astype(jnp.bfloat16) for part in row] for row in (one, two)]


def second_rows(hidden, flag, gain_ref, channels):
    gain = 0.5 * gain_ref[...].reshape(1, 1, 1, channels)
    total = jnp.sum(hidden * hidden, axis=-1, keepdims=True)
    inverse = lax.rsqrt(total * (1.0 / channels) + epsilon) * flag
    values = silu(hidden * inverse * gain)
    rest = jnp.zeros(values.shape[:-1] + (LANES // 2,), jnp.float32)
    high = jnp.concatenate([values[..., LANES:], rest], axis=-1)
    parts = [values[..., :LANES], high, rolled(high)]
    return jnp.stack([part.astype(jnp.bfloat16) for part in parts])


def in_turn(steps, beside=None):
    waiting = None
    for product, then in steps:
        result = product()
        if waiting:
            waiting[1](waiting[0])
        elif beside:
            beside()
        waiting = (result, then)
    waiting[1](waiting[0])


def convolved(operand, weights_ref, bias_ref, frame, frames, rows, then, most=PRODUCT):
    products = -(-frames * rows * operand.shape[3] // most)
    step = -(-frames // products)

    def part(start):
        count = min(step, frames - start)
        return (
            lambda: convolved_part(operand, weights_ref, bias_ref, frame + start, count, rows),
            lambda result: then(start, count, result),
        )

    return [part(start) for start in range(0, frames, step)]


def convolved_part(operand, weights_ref, bias_ref, frame, frames, rows):
    width = operand.shape[3]
    channels = weights_ref.shape[-1]
    taps = [(a, i) for a in range(TAPS) for i in range(TAPS)]
    groups = [taps[start:start + 2] for start in range(0, len(taps), 2)]

    def window(tap, part):
        a, i = tap
        value = operand[part, frame + a:frame + a + frames, i:i + rows]
        return value.reshape(frames * rows * width, LANES)

    def operands(groups):
        pieces = []
        for group in groups:
            pieces += [window(tap, 0) for tap in group]
            high = window(group[0], 1)
            pieces.append(high + window(group[1], 2) if len(group) > 1 else high)
        return jnp.concatenate(pieces, axis=-1)

    def weights(groups, j, depth):
        rights = []
        for group in groups:
            held = [weights_ref[a, i, j] for a, i in group]
            rights += [weight[:LANES] for weight in held] + [weight[LANES:] for weight in held]
        rest = depth - sum(right.shape[0] for right in rights)
        if rest:
            rights.append(jnp.zeros((rest, channels), jnp.bfloat16))
        return jnp.concatenate(rights, axis=0)

    half = len(groups) // 2
    parts = [(part, operands(part)) for part in (groups[:half], groups[half:])]
    products = []
    for j in range(TAPS):
        total = None
        for part, left in parts if j % 2 == 0 else parts[::-1]:
            product = jnp.dot(left, weights(part, j, left.shape[1]), preferred_element_type=jnp.float32)
            total = product if total is None else total + product
        products.append(total.reshape(frames * rows, width, channels))
    column = lax.broadcasted_iota(jnp.int32, (1, width, 1), 1)
    before = jnp.where(column == 0, 0.0, pltpu.roll(products[0], 1, 1))
    after = jnp.where(column == width - 1, 0.0, pltpu.roll(products[2], width - 1, 1))
    result = products[1] + before + after + bias_ref[...].reshape(1, 1, channels)
    return result.reshape(frames, rows, width, channels)


def halves(core, mine, other):
    return jnp.where(core == 0, mine, other), jnp.where(core == 0, other, mine)


def frame_flags(marks, frames):
    values = marks.astype(jnp.float32)
    return [values[k:k + 1, 0:1].reshape(1, 1, 1, 1) for k in frames]


def fill_rows(operand, frame, row, mine, other, gain_ref):
    left, right = halves(lax.axis_index("wa"), mine, other)
    frames, pairs = mine.shape[:2]
    upper, lower = first_rows(left, right, gain_ref, gain_ref.shape[-1])
    for part in range(len(upper)):
        for pair in range(pairs):
            operand[part, frame:frame + frames, pl.ds(row + 2 * pair, 1)] = upper[part][:, pair:pair + 1]
            operand[part, frame:frame + frames, pl.ds(row + 2 * pair + 1, 1)] = lower[part][:, pair:pair + 1]


def border_kernel(tail_ref, mine_ref, other_ref, tail_edge_ref, own_edge_ref):
    frames, held = mine_ref.shape[:2]
    pairs = tail_ref.shape[0] // CACHE
    core = lower_part()
    pair = core * (held - 1)
    for slot in range(CACHE):
        tail_edge_ref[slot] = tail_ref[slot * pairs + core * (pairs - 1)]
        tail_edge_ref[CACHE + slot] = other_ref[slot * held + pair]
    for frame in range(frames):
        own_edge_ref[0, frame] = mine_ref[frame, pair]
        own_edge_ref[1, frame] = other_ref[(CACHE + frame) * held + pair]


def finish(mine_ref, other_ref, live, first, pairs, value, targets):
    _, held, side, _ = mine_ref.shape
    frames, channels = value.shape[0], value.shape[-1]
    start, count = pairs
    near, far = halves(lax.axis_index("wa"), value[:, :, :side], value[:, :, side:])
    for mine, value, target in ((True, near, targets[0]), (False, far, targets[1])):
        for frame in range(frames):
            for k in range(count):
                if mine:
                    raw = mine_ref[first + frame, start + k]
                else:
                    raw = other_ref[(CACHE + first + frame) * held + start + k]
                raw = raw.astype(jnp.float32)
                high = raw[:, 2 * LANES:]
                for row, tail in ((0, high), (1, pltpu.roll(high, LANES // 2, 1))):
                    low = raw[:, row * LANES:(row + 1) * LANES]
                    features = jnp.concatenate([low, tail[:, :channels - LANES]], axis=-1)
                    summed = features + value[frame, 2 * k + row]
                    kept = jnp.where(live[first + frame].reshape(1, 1) > 0.5, summed, 0.0)
                    target(first + frame, 2 * k + row, kept.astype(jnp.bfloat16))


def hide(operand, weights_ref, bias_ref, gain_ref, first, count, rows, flags, store, most=PRODUCT):
    channels = weights_ref.shape[-1]

    def then(begin, part, hidden):
        flag = jnp.concatenate(flags[begin:begin + part], axis=0)
        store(begin, begin + part, second_rows(hidden, flag, gain_ref, channels))

    return convolved(operand, weights_ref, bias_ref, first, count, rows, then, most)


def inside_flags(rows):
    core, place = lower_part(), lax.axis_index("ha")
    inside = jnp.where(core == 0, place > 0, place < lax.axis_size("ha") - 1)
    row = lax.broadcasted_iota(jnp.int32, (1, rows, 1, 1), 1)
    return jnp.where((row == (rows - 1) * core) & jnp.logical_not(inside), 0.0, 1.0)


def other_rows_kernel(tail_ref, late_ref, rest_ref):
    pairs, held = tail_ref.shape[0] // CACHE, rest_ref.shape[0] // CACHE
    first = (1 - lower_part()) * (pairs - held)
    for slot in range(CACHE):
        rest_ref[slot * held:(slot + 1) * held] = tail_ref[pl.ds(slot * pairs + first, held)]


def own_kernel(
    marks_ref, mine_ref, other_ref, gain1_ref, w1_ref, bias1_ref, gain2_ref,
    first_ref, late_ref, raw_ref,
):
    frames, pairs, side, packed = mine_ref.shape
    live = frame_flags(marks_ref[...], range(2, frames))

    def fill(start, end):
        other = other_ref[(CACHE + start) * pairs:(CACHE + end) * pairs].reshape(end - start, pairs, side, packed)
        fill_rows(first_ref, start, 0, mine_ref[start:end], other, gain1_ref)

    def store(begin, end, rows):
        late_ref[:, begin:end] = rows

    steps = hide(first_ref, w1_ref, bias1_ref, gain2_ref, 0, frames - 2, 2 * pairs - 2, live, store, OWN)
    each = -(-(frames - 2) // len(steps))

    def filled(k, product):
        def run():
            fill(min(frames, each * k + (2 if k else 0)), min(frames, each * (k + 1) + 2))
            return product()
        return run

    def left(result):
        raw_ref[...] = result

    steps[-1] = (steps[-1][0], left)
    in_turn([(filled(k, product), then) for k, (product, then) in enumerate(steps)])


def edge_kernel(
    marks_ref, mine_ref, other_ref, edge_ref, first_ref, done_ref, raw_ref,
    gain1_ref, w1_ref, bias1_ref, gain2_ref, w2_ref, bias2_ref,
    strip_ref, hidden_ref, keep_ref, send_ref, border_ref, operand, strip, late_ref,
):
    core = lower_part()
    frames, pairs = mine_ref.shape[:2]
    rows = 2 * pairs
    late = frames - CACHE
    outward, inward = pl.ds(2 * core, 2), pl.ds(2 * (1 - core), 2)
    fill_rows(strip, 0, 2 * core, edge_ref[1][:, None], edge_ref[0][:, None], gain1_ref)
    strip[:, :, inward] = first_ref[:, :, pl.ds((rows - 2) * core, 2)]
    live = frame_flags(marks_ref[...], range(frames))
    inside = inside_flags(2)
    done = done_ref.shape[1]
    late_ref[:, 0:done] = done_ref[...]

    def activate():
        flag = jnp.concatenate(live[2 + done:], axis=0)
        late_ref[:, done:] = second_rows(raw_ref[...], flag, gain2_ref, gain2_ref.shape[-1])
        operand[:, :, inward] = late_ref[:, :, pl.ds((rows - 4) * core, 2)]

    def store(begin, end, values):
        operand[:, begin:end, outward] = values

    def put(ref):
        def store(frame, row, value):
            ref[frame - CACHE, row] = value
        return store

    def middle(start, part, result):
        targets = (put(keep_ref), put(send_ref))
        finish(mine_ref, other_ref, live, CACHE + start, (1, pairs - 2), result, targets)

    def border(start, part, result):
        border_ref[start:start + part] = result

    flags = [flag * inside for flag in live[2:]]
    earlier = lax.axis_index("tchunk") > 0

    def steps():
        return hide(strip, w1_ref, bias1_ref, gain2_ref, 0, frames - 2, 2, flags, store) + convolved(
            late_ref, w2_ref, bias2_ref, 0, late, rows - 4, middle
        )

    @pl.when(earlier)
    def _():
        in_turn(steps() + convolved(operand, w2_ref, bias2_ref, 0, late, 2, border), activate)

    @pl.when(jnp.logical_not(earlier))
    def _():
        in_turn(steps(), activate)

    strip_ref[...] = strip[:, 0:2, outward]
    hidden_ref[:, :, pl.ds(2 * (1 - core), rows - 2)] = late_ref[:, 0:2]
    hidden_ref[:, :, pl.ds((rows - 2) * core, 2)] = operand[:, 0:2, outward]


def tail_edge_kernel(edge_ref, strip_ref, gain_ref, rows_ref):
    rows_ref[:, CACHE:] = strip_ref[...]

    @pl.when(lax.axis_index("tchunk") > 0)
    def _():
        fill_rows(rows_ref, 0, 0, edge_ref[CACHE:2 * CACHE][:, None], edge_ref[0:CACHE][:, None], gain_ref)

    @pl.when(lax.axis_index("tchunk") == 0)
    def _():
        rows_ref[:, 0:CACHE] = jnp.zeros((rows_ref.shape[0], CACHE) + rows_ref.shape[2:], rows_ref.dtype)


def early_kernel(
    marks_ref, tail_mine_ref, tail_other_ref, mine_ref, other_ref, edge_ref, first_ref, hidden_ref,
    late_keep_ref, late_send_ref, late_border_ref, late_operand_ref, gain1_ref, w1_ref, bias1_ref, gain2_ref, w2_ref, bias2_ref,
    keep_ref, send_ref, plane, operand,
):
    core = lower_part()
    held = mine_ref.shape[1]
    rows = 2 * held
    pairs = tail_mine_ref.shape[0] // CACHE
    live = frame_flags(marks_ref[...], range(mine_ref.shape[0]))
    inside = inside_flags(rows)
    earlier = lax.axis_index("tchunk") > 0
    middle, border = 2 * (1 - core), rows * core

    def unpacked(ref, stride, first):
        return jnp.stack([ref[pl.ds(slot * stride + first, held)] for slot in range(CACHE)])

    plane[:, CACHE:, pl.ds(middle, rows)] = first_ref[:, 0:2]
    plane[:, :, pl.ds(border, 2)] = edge_ref[...]
    operand[:, CACHE:] = hidden_ref[...]

    def put(ref, offset=0):
        def store(frame, row, value):
            ref[frame, offset + row] = value
        return store

    def late_border(start, part, result):
        offset = (rows - 4) * core
        targets = (put(keep_ref, offset), put(send_ref, offset))
        finish(mine_ref, other_ref, live, CACHE + start, ((held - 1) * core, 1), result, targets)

    def late_middle():
        for source, target in ((late_keep_ref, keep_ref), (late_send_ref, send_ref)):
            target[CACHE:, pl.ds(2 * (1 - core), rows - 4)] = source[...]

    def hidden_steps(first, flags):
        def store(begin, end, values):
            operand[:, first + begin:first + end] = values

        flags = [flag * inside for flag in flags]
        return hide(plane, w1_ref, bias1_ref, gain2_ref, first, CACHE - first, rows, flags, store)

    def then(start, part, result):
        finish(mine_ref, other_ref, live, start, (core, held - 1), result, (put(keep_ref), put(send_ref)))

    def result_steps():
        return convolved(operand, w2_ref, bias2_ref, 0, CACHE, rows - 2, then)

    @pl.when(earlier)
    def _():
        fill_rows(
            plane, 0, middle, unpacked(tail_mine_ref, pairs, core * (pairs - held)),
            unpacked(tail_other_ref, held, 0), gain1_ref,
        )
        flags = frame_flags(tail_mine_ref[CACHE * pairs], range(CACHE - 2, CACHE)) + live[0:2]

        def beside():
            late_middle()
            late_border(0, late_border_ref.shape[0], late_border_ref[...])

        hidden, results = hidden_steps(0, flags), result_steps()
        if len(hidden) == 2 and len(results) == 2:
            in_turn(hidden[::-1] + results[::-1], beside)
        else:
            in_turn(hidden, beside)
            in_turn(results)

    @pl.when(jnp.logical_not(earlier))
    def _():
        plane[:, 0:CACHE, pl.ds(middle, rows)] = jnp.zeros(
            plane.shape[:1] + (CACHE, rows) + plane.shape[3:], plane.dtype
        )
        operand[:, 0:2] = jnp.zeros(operand.shape[:1] + (2,) + operand.shape[2:], operand.dtype)
        border = convolved(late_operand_ref, w2_ref, bias2_ref, 0, late_border_ref.shape[0], 2, late_border)
        in_turn(hidden_steps(2, live[0:2]) + border + result_steps()[::-1], late_middle)


def place_kernel(keep_ref, got_ref, result_ref, arrived):
    core, half = lower_part(), keep_ref.shape[1]
    copies = [
        pltpu.make_async_copy(keep_ref, result_ref.at[:, pl.ds(half * core, half)], arrived.at[0]),
        pltpu.make_async_copy(got_ref, result_ref.at[:, pl.ds(half * (1 - core), half)], arrived.at[1]),
    ]
    for copy in copies:
        copy.start()
    for copy in copies:
        copy.wait()


def shards(features, frame_counts, gain_first, conv_first, bias_first, gain_second, conv_second, bias_second):
    frames, rows, side, channels = features.shape
    pairs, half = rows // 2, rows // 2
    held = half // 2 + 1
    tall, cores, blocks = lax.axis_size("ha"), lax.axis_size("wa"), lax.axis_size("tchunk")
    packed, width, tiles = 3 * LANES, 2 * side, CACHE * held
    bf16 = jnp.bfloat16
    vmem = pl.BlockSpec(memory_space=pltpu.VMEM)
    limit = pltpu.CompilerParams(vmem_limit_bytes=20 * 2**20)
    work = 2 * TAPS**3 * channels * channels * width

    def shape(*extent):
        return jax.ShapeDtypeStruct(extent, bf16)

    def cost(flops, fetched):
        return pl.CostEstimate(flops=flops, bytes_accessed=fetched, transcendentals=0)

    slots = pl.pallas_call(
        slots_kernel,
        out_shape=jax.ShapeDtypeStruct((side, packed), jnp.int32),
        out_specs=vmem,
        compiler_params=limit,
        cost_estimate=cost(2**34, 2**20),
    )()
    slots, frame_counts = lax.optimization_barrier((slots, frame_counts))
    tail, mine, theirs, marks = pl.pallas_call(
        prepare_kernel,
        out_shape=(
            shape(CACHE * pairs + 1, side, packed), shape(frames, held, side, packed),
            shape((CACHE + frames) * held, side, packed), shape(side, packed),
        ),
        in_specs=[pl.BlockSpec(memory_space=pltpu.SMEM), vmem, vmem],
        out_specs=(vmem,) * 4,
        scratch_shapes=[pltpu.VMEM((frames, pairs, side, packed), bf16)],
        compiler_params=limit,
    )(frame_counts, slots, features)

    if blocks > 2:
        tail = joined_tail(tail)
        rest = lax.dynamic_slice_in_dim(
            tail[:-1].reshape(CACHE, pairs, side, packed), (1 - lower_part()) * (pairs - held), held, 1
        )
        theirs = jnp.concatenate([rest.reshape(tiles, side, packed), theirs[tiles:]], axis=0)
    straight, diagonal, across = [], [], []

    def index(block, h, core):
        return (block * tall + h) * cores + core

    for k in range(blocks - 1):
        for h in range(tall):
            for core in range(cores):
                straight.append((index(k, h, core), index(k + 1, h, core)))
    for h in range(tall - 1):
        for k in range(blocks):
            lower, upper = index(k, h, 0), index(k, h + 1, 1)
            across += [(lower, upper), (upper, lower)]
            if k + 1 < blocks:
                lower_next, upper_next = index(k + 1, h, 0), index(k + 1, h + 1, 1)
                diagonal += [(lower, upper_next), (upper, lower_next)]
    axes = ("tchunk", "ha", "wa")
    swap = [(0, 1), (1, 0)]
    tail_mine = lax.ppermute(tail, axes, straight)
    other = lax.ppermute(theirs, "wa", swap)
    tail_edge, own_edge = pl.pallas_call(
        border_kernel,
        out_shape=(shape(2 * CACHE, side, packed), shape(2, frames, side, packed)),
        in_specs=[vmem] * 3,
        out_specs=(vmem, vmem),
        compiler_params=limit,
        cost_estimate=cost(2**34, 2**20),
    )(tail, mine, other)
    own_edge = lax.ppermute(own_edge, axes, across)
    tail_edge = lax.ppermute(tail_edge, axes, diagonal)

    weights = (
        gain_first.reshape(1, channels), conv_first, bias_first.reshape(1, channels),
        gain_second.reshape(1, channels), conv_second, bias_second.reshape(1, channels),
    )
    products = -(-(frames - 2) * half * width // OWN)
    done = -(-(frames - 2) // products) * (products - 1)
    first, late, raw = pl.pallas_call(
        own_kernel,
        out_shape=(
            shape(3, frames, half + 2, width, LANES), shape(3, done, half, width, LANES),
            jax.ShapeDtypeStruct((frames - 2 - done, half, width, channels), jnp.float32),
        ),
        in_specs=[vmem] * 7,
        out_specs=(vmem,) * 3,
        compiler_params=limit,
        cost_estimate=cost(work * (frames - 2) * half, 4 * 2**20),
    )(marks, mine, other, *weights[:4])
    rest = pl.pallas_call(
        other_rows_kernel,
        out_shape=shape(tiles, side, packed),
        in_specs=[vmem, pl.BlockSpec(memory_space=pl.ANY)],
        out_specs=vmem,
        compiler_params=limit,
        cost_estimate=cost(1, 1),
    )(tail_mine, late)
    tail_other = lax.ppermute(rest, "wa", swap)
    strip, hidden, keep, send, border, late = pl.pallas_call(
        edge_kernel,
        out_shape=(
            shape(3, 2, 2, width, LANES), shape(3, 2, half + 2, width, LANES),
            shape(frames - CACHE, half - 2, side, channels), shape(frames - CACHE, half - 2, side, channels),
            jax.ShapeDtypeStruct((frames - CACHE, 2, width, channels), jnp.float32),
            shape(3, frames - 2, 4, width, LANES),
        ),
        in_specs=[vmem] * 13,
        out_specs=(vmem,) * 6,
        scratch_shapes=[
            pltpu.VMEM((3, frames, 4, width, LANES), bf16),
            pltpu.VMEM((3, frames - 2, half, width, LANES), bf16),
        ],
        compiler_params=limit,
        cost_estimate=cost(2**20, 2**20),
    )(marks, mine, other, own_edge, first, late, raw, *weights)
    tail_edge = pl.pallas_call(
        tail_edge_kernel,
        out_shape=shape(3, CACHE + 2, 2, width, LANES),
        in_specs=[vmem] * 3,
        out_specs=vmem,
        compiler_params=limit,
        cost_estimate=cost(2**30, 2**18),
    )(tail_edge, strip, weights[0])
    keep, send = pl.pallas_call(
        early_kernel,
        out_shape=(shape(frames, half, side, channels), shape(frames, half, side, channels)),
        in_specs=[vmem] * 18,
        out_specs=(vmem, vmem),
        scratch_shapes=[
            pltpu.VMEM((3, CACHE + 2, half + 4, width, LANES), bf16),
            pltpu.VMEM((3, CACHE + 2, half + 2, width, LANES), bf16),
        ],
        compiler_params=limit,
        cost_estimate=cost(work * CACHE * (2 * half + 2), 8 * 2**20),
    )(marks, tail_mine, tail_other, mine, other, tail_edge, first, hidden, keep, send, border, late, *weights)
    got = lax.ppermute(send, "wa", swap)
    return pl.pallas_call(
        place_kernel,
        out_shape=shape(*features.shape),
        in_specs=[vmem, vmem],
        out_specs=pl.BlockSpec(memory_space=pltpu.HBM),
        scratch_shapes=[pltpu.SemaphoreType.DMA((2,))],
        compiler_params=limit,
    )(keep, got)


def solution(mesh):
    return jax.shard_map(
        shards,
        mesh=mesh,
        in_specs=(
            P(("grp", "tchunk"), "ha", "wa", None),
            P(("grp", "tchunk")),
            P(), P(), P(), P(), P(), P(),
        ),
        out_specs=P(("grp", "tchunk"), "ha", "wa", None),
        check_vma=False,
    )
```

```python
import jax
import jax.numpy as jnp
from jax import lax
from jax.experimental import pallas as pl
from jax.experimental.pallas import tpu as pltpu
from jax.sharding import PartitionSpec as P

epsilon = 1e-06
CACHE = 4
TAPS = 3
LANES = 128
PRODUCT = 192
OWN = 192


def slots_kernel(slots_ref):
    slots_ref[...] = lax.broadcasted_iota(jnp.int32, slots_ref.shape, 0)


def lower_part():
    return 1 - lax.axis_index("wa")


def prepare_kernel(total_ref, slots_ref, raw, tail_ref, mine_ref, theirs_ref, marks_ref, pack):
    frames, rows = raw.shape[:2]
    pairs, held = rows // 2, mine_ref.shape[1]
    core = lower_part()
    total = total_ref[0]
    for frame in range(frames):
        for pair in range(pairs):
            first, second = raw[frame, 2 * pair], raw[frame, 2 * pair + 1]
            packed = jnp.concatenate(
                [first[:, :LANES], second[:, :LANES], first[:, LANES:], second[:, LANES:]], axis=-1
            )
            pack[frame, pair] = packed
    for slot in range(CACHE):
        frame = total - CACHE + slot
        value = pack[jnp.maximum(frame, 0)]
        tail_ref[slot * pairs:(slot + 1) * pairs] = jnp.where(frame >= 0, value, jnp.zeros_like(value))
        value = pack[jnp.maximum(frame, 0), pl.ds((1 - core) * (pairs - held), held)]
        theirs_ref[slot * held:(slot + 1) * held] = jnp.where(frame >= 0, value, jnp.zeros_like(value))
    for frame in range(frames):
        start = (CACHE + frame) * held
        value = pack[frame, pl.ds(core * (pairs - held), held)]
        mine_ref[frame] = jnp.where(frame < total, value, jnp.zeros_like(value))
        value = pack[frame, pl.ds((1 - core) * (pairs - held), held)]
        theirs_ref[start:start + held] = jnp.where(frame < total, value, jnp.zeros_like(value))
    slot = slots_ref[...]
    tail_ref[CACHE * pairs] = jnp.where(
        (slot < CACHE) & (total - CACHE + slot >= 0), 1.0, 0.0
    ).astype(tail_ref.dtype)
    marks_ref[...] = jnp.where(slot < total, 1.0, 0.0).astype(marks_ref.dtype)


def joined_tail(tail):
    count = lax.axis_size("tchunk")

    def pushed(value, held):
        return lax.dynamic_slice_in_dim(jnp.concatenate([value, jnp.zeros_like(value)], axis=0), held, CACHE, 0)

    step = 1
    while step < count - 1:
        early = lax.ppermute(tail, "tchunk", [(k, k + step) for k in range(count - step)])
        held = jnp.sum(tail[-1, :CACHE, 0].astype(jnp.int32))
        body = pushed(early[:-1].reshape((CACHE, -1) + tail.shape[1:]), held).reshape(tail[:-1].shape)
        marks = jnp.pad(pushed(early[-1, :CACHE], held), ((0, tail.shape[1] - CACHE), (0, 0)))
        tail = tail + jnp.concatenate([body, marks[None]], axis=0)
        step *= 2
    return tail


def silu(half):
    return half + half * jnp.tanh(half)


def lane_mask():
    return lax.broadcasted_iota(jnp.int32, (1, 1, 1, LANES), 3) < LANES // 2


def gains(gain_ref):
    low, high = 0.5 * gain_ref[:, :LANES], 0.5 * gain_ref[:, LANES:]
    return low.reshape(1, 1, 1, LANES), jnp.concatenate([high, high], axis=-1).reshape(1, 1, 1, LANES)


def rolled(values):
    shape = values.shape
    return pltpu.roll(values.reshape(-1, LANES), LANES // 2, 1).reshape(shape)


def first_rows(left, right, gain_ref, channels):
    raw = jnp.concatenate([left.astype(jnp.float32), right.astype(jnp.float32)], axis=2)
    front, back, high = raw[..., :LANES], raw[..., LANES:2 * LANES], raw[..., 2 * LANES:]
    lower = lane_mask()
    squared = high * high

    def inverse(low, mask):
        total = jnp.sum(low * low + jnp.where(mask, squared, 0.0), axis=-1, keepdims=True)
        return lax.rsqrt(total * (1.0 / channels) + epsilon)

    scale_front, scale_back = inverse(front, lower), inverse(back, jnp.logical_not(lower))
    gain_low, gain_high = gains(gain_ref)
    front = silu(front * scale_front * gain_low)
    back = silu(back * scale_back * gain_low)
    high = silu(high * jnp.where(lower, scale_front, scale_back) * gain_high)
    turned = rolled(high)
    one = [front, jnp.where(lower, high, 0.0), jnp.where(lower, 0.0, turned)]
    two = [back, jnp.where(lower, turned, 0.0), jnp.where(lower, 0.0, high)]
    return [[part.astype(jnp.bfloat16) for part in row] for row in (one, two)]


def second_rows(hidden, flag, gain_ref, channels):
    gain = 0.5 * gain_ref[...].reshape(1, 1, 1, channels)
    total = jnp.sum(hidden * hidden, axis=-1, keepdims=True)
    inverse = lax.rsqrt(total * (1.0 / channels) + epsilon) * flag
    values = silu(hidden * inverse * gain)
    rest = jnp.zeros(values.shape[:-1] + (LANES // 2,), jnp.float32)
    high = jnp.concatenate([values[..., LANES:], rest], axis=-1)
    parts = [values[..., :LANES], high, rolled(high)]
    return jnp.stack([part.astype(jnp.bfloat16) for part in parts])


def in_turn(steps, beside=None):
    waiting = None
    for product, then in steps:
        result = product()
        if waiting:
            waiting[1](waiting[0])
        elif beside:
            beside()
        waiting = (result, then)
    waiting[1](waiting[0])


def convolved(operand, weights_ref, bias_ref, frame, frames, rows, then, most=PRODUCT):
    products = -(-frames * rows * operand.shape[3] // most)
    step = -(-frames // products)

    def part(start):
        count = min(step, frames - start)
        return (
            lambda: convolved_part(operand, weights_ref, bias_ref, frame + start, count, rows),
            lambda result: then(start, count, result),
        )

    return [part(start) for start in range(0, frames, step)]


def convolved_part(operand, weights_ref, bias_ref, frame, frames, rows):
    width = operand.shape[3]
    channels = weights_ref.shape[-1]
    taps = [(a, i) for a in range(TAPS) for i in range(TAPS)]
    groups = [taps[start:start + 2] for start in range(0, len(taps), 2)]

    def window(tap, part):
        a, i = tap
        value = operand[part, frame + a:frame + a + frames, i:i + rows]
        return value.reshape(frames * rows * width, LANES)

    def operands(groups):
        pieces = []
        for group in groups:
            pieces += [window(tap, 0) for tap in group]
            high = window(group[0], 1)
            pieces.append(high + window(group[1], 2) if len(group) > 1 else high)
        return jnp.concatenate(pieces, axis=-1)

    def weights(groups, j, depth):
        rights = []
        for group in groups:
            held = [weights_ref[a, i, j] for a, i in group]
            rights += [weight[:LANES] for weight in held] + [weight[LANES:] for weight in held]
        rest = depth - sum(right.shape[0] for right in rights)
        if rest:
            rights.append(jnp.zeros((rest, channels), jnp.bfloat16))
        return jnp.concatenate(rights, axis=0)

    left = operands(groups)
    products = []
    for j in range(TAPS):
        product = jnp.dot(left, weights(groups, j, left.shape[1]), preferred_element_type=jnp.float32)
        products.append(product.reshape(frames * rows, width, channels))
    column = lax.broadcasted_iota(jnp.int32, (1, width, 1), 1)
    before = jnp.where(column == 0, 0.0, pltpu.roll(products[0], 1, 1))
    after = jnp.where(column == width - 1, 0.0, pltpu.roll(products[2], width - 1, 1))
    result = products[1] + before + after + bias_ref[...].reshape(1, 1, channels)
    return result.reshape(frames, rows, width, channels)


def halves(core, mine, other):
    return jnp.where(core == 0, mine, other), jnp.where(core == 0, other, mine)


def frame_flags(marks, frames):
    values = marks.astype(jnp.float32)
    return [values[k:k + 1, 0:1].reshape(1, 1, 1, 1) for k in frames]


def fill_rows(operand, frame, row, mine, other, gain_ref):
    left, right = halves(lax.axis_index("wa"), mine, other)
    frames, pairs = mine.shape[:2]
    upper, lower = first_rows(left, right, gain_ref, gain_ref.shape[-1])
    for part in range(len(upper)):
        for pair in range(pairs):
            operand[part, frame:frame + frames, pl.ds(row + 2 * pair, 1)] = upper[part][:, pair:pair + 1]
            operand[part, frame:frame + frames, pl.ds(row + 2 * pair + 1, 1)] = lower[part][:, pair:pair + 1]


def border_kernel(tail_ref, mine_ref, other_ref, tail_edge_ref, own_edge_ref):
    frames, held = mine_ref.shape[:2]
    pairs = tail_ref.shape[0] // CACHE
    core = lower_part()
    pair = core * (held - 1)
    for slot in range(CACHE):
        tail_edge_ref[slot] = tail_ref[slot * pairs + core * (pairs - 1)]
        tail_edge_ref[CACHE + slot] = other_ref[slot * held + pair]
    for frame in range(frames):
        own_edge_ref[0, frame] = mine_ref[frame, pair]
        own_edge_ref[1, frame] = other_ref[(CACHE + frame) * held + pair]


def finish(mine_ref, other_ref, live, first, pairs, value, targets):
    _, held, side, _ = mine_ref.shape
    frames, channels = value.shape[0], value.shape[-1]
    start, count = pairs
    near, far = halves(lax.axis_index("wa"), value[:, :, :side], value[:, :, side:])
    for mine, value, target in ((True, near, targets[0]), (False, far, targets[1])):
        for frame in range(frames):
            for k in range(count):
                if mine:
                    raw = mine_ref[first + frame, start + k]
                else:
                    raw = other_ref[(CACHE + first + frame) * held + start + k]
                raw = raw.astype(jnp.float32)
                high = raw[:, 2 * LANES:]
                for row, tail in ((0, high), (1, pltpu.roll(high, LANES // 2, 1))):
                    low = raw[:, row * LANES:(row + 1) * LANES]
                    features = jnp.concatenate([low, tail[:, :channels - LANES]], axis=-1)
                    summed = features + value[frame, 2 * k + row]
                    kept = jnp.where(live[first + frame].reshape(1, 1) > 0.5, summed, 0.0)
                    target(first + frame, 2 * k + row, kept.astype(jnp.bfloat16))


def hide(operand, weights_ref, bias_ref, gain_ref, first, count, rows, flags, store, most=PRODUCT):
    channels = weights_ref.shape[-1]

    def then(begin, part, hidden):
        flag = jnp.concatenate(flags[begin:begin + part], axis=0)
        store(begin, begin + part, second_rows(hidden, flag, gain_ref, channels))

    return convolved(operand, weights_ref, bias_ref, first, count, rows, then, most)


def inside_flags(rows):
    core, place = lower_part(), lax.axis_index("ha")
    inside = jnp.where(core == 0, place > 0, place < lax.axis_size("ha") - 1)
    row = lax.broadcasted_iota(jnp.int32, (1, rows, 1, 1), 1)
    return jnp.where((row == (rows - 1) * core) & jnp.logical_not(inside), 0.0, 1.0)


def other_rows_kernel(tail_ref, late_ref, rest_ref):
    pairs, held = tail_ref.shape[0] // CACHE, rest_ref.shape[0] // CACHE
    first = (1 - lower_part()) * (pairs - held)
    for slot in range(CACHE):
        rest_ref[slot * held:(slot + 1) * held] = tail_ref[pl.ds(slot * pairs + first, held)]


def own_kernel(
    marks_ref, mine_ref, other_ref, gain1_ref, w1_ref, bias1_ref, gain2_ref,
    first_ref, late_ref, raw_ref,
):
    frames, pairs, side, packed = mine_ref.shape
    live = frame_flags(marks_ref[...], range(2, frames))

    def fill(start, end):
        other = other_ref[(CACHE + start) * pairs:(CACHE + end) * pairs].reshape(end - start, pairs, side, packed)
        fill_rows(first_ref, start, 0, mine_ref[start:end], other, gain1_ref)

    def store(begin, end, rows):
        late_ref[:, begin:end] = rows

    steps = hide(first_ref, w1_ref, bias1_ref, gain2_ref, 0, frames - 2, 2 * pairs - 2, live, store, OWN)
    each = -(-(frames - 2) // len(steps))

    def filled(k, product):
        def run():
            fill(min(frames, each * k + (2 if k else 0)), min(frames, each * (k + 1) + 2))
            return product()
        return run

    def left(result):
        raw_ref[...] = result

    steps[-1] = (steps[-1][0], left)
    in_turn([(filled(k, product), then) for k, (product, then) in enumerate(steps)])


def edge_kernel(
    marks_ref, mine_ref, other_ref, edge_ref, first_ref, done_ref, raw_ref,
    gain1_ref, w1_ref, bias1_ref, gain2_ref, w2_ref, bias2_ref,
    strip_ref, hidden_ref, keep_ref, send_ref, border_ref, operand, strip, late_ref,
):
    core = lower_part()
    frames, pairs = mine_ref.shape[:2]
    rows = 2 * pairs
    late = frames - CACHE
    outward, inward = pl.ds(2 * core, 2), pl.ds(2 * (1 - core), 2)
    fill_rows(strip, 0, 2 * core, edge_ref[1][:, None], edge_ref[0][:, None], gain1_ref)
    strip[:, :, inward] = first_ref[:, :, pl.ds((rows - 2) * core, 2)]
    live = frame_flags(marks_ref[...], range(frames))
    inside = inside_flags(2)
    done = done_ref.shape[1]
    late_ref[:, 0:done] = done_ref[...]

    def activate():
        flag = jnp.concatenate(live[2 + done:], axis=0)
        late_ref[:, done:] = second_rows(raw_ref[...], flag, gain2_ref, gain2_ref.shape[-1])
        operand[:, :, inward] = late_ref[:, :, pl.ds((rows - 4) * core, 2)]

    def store(begin, end, values):
        operand[:, begin:end, outward] = values

    def put(ref):
        def store(frame, row, value):
            ref[frame - CACHE, row] = value
        return store

    def middle(start, part, result):
        targets = (put(keep_ref), put(send_ref))
        finish(mine_ref, other_ref, live, CACHE + start, (1, pairs - 2), result, targets)

    def border(start, part, result):
        border_ref[start:start + part] = result

    flags = [flag * inside for flag in live[2:]]
    earlier = lax.axis_index("tchunk") > 0

    def steps():
        return hide(strip, w1_ref, bias1_ref, gain2_ref, 0, frames - 2, 2, flags, store) + convolved(
            late_ref, w2_ref, bias2_ref, 0, late, rows - 4, middle
        )

    @pl.when(earlier)
    def _():
        in_turn(steps() + convolved(operand, w2_ref, bias2_ref, 0, late, 2, border), activate)

    @pl.when(jnp.logical_not(earlier))
    def _():
        in_turn(steps(), activate)

    strip_ref[...] = strip[:, 0:2, outward]
    hidden_ref[:, :, pl.ds(2 * (1 - core), rows - 2)] = late_ref[:, 0:2]
    hidden_ref[:, :, pl.ds((rows - 2) * core, 2)] = operand[:, 0:2, outward]


def tail_edge_kernel(edge_ref, strip_ref, gain_ref, rows_ref):
    rows_ref[:, CACHE:] = strip_ref[...]

    @pl.when(lax.axis_index("tchunk") > 0)
    def _():
        fill_rows(rows_ref, 0, 0, edge_ref[CACHE:2 * CACHE][:, None], edge_ref[0:CACHE][:, None], gain_ref)

    @pl.when(lax.axis_index("tchunk") == 0)
    def _():
        rows_ref[:, 0:CACHE] = jnp.zeros((rows_ref.shape[0], CACHE) + rows_ref.shape[2:], rows_ref.dtype)


def early_kernel(
    marks_ref, tail_mine_ref, tail_other_ref, mine_ref, other_ref, edge_ref, first_ref, hidden_ref,
    late_keep_ref, late_send_ref, late_border_ref, late_operand_ref, gain1_ref, w1_ref, bias1_ref, gain2_ref, w2_ref, bias2_ref,
    keep_ref, send_ref, plane, operand,
):
    core = lower_part()
    held = mine_ref.shape[1]
    rows = 2 * held
    pairs = tail_mine_ref.shape[0] // CACHE
    live = frame_flags(marks_ref[...], range(mine_ref.shape[0]))
    inside = inside_flags(rows)
    earlier = lax.axis_index("tchunk") > 0
    middle, border = 2 * (1 - core), rows * core

    def unpacked(ref, stride, first):
        return jnp.stack([ref[pl.ds(slot * stride + first, held)] for slot in range(CACHE)])

    plane[:, CACHE:, pl.ds(middle, rows)] = first_ref[:, 0:2]
    plane[:, :, pl.ds(border, 2)] = edge_ref[...]
    operand[:, CACHE:] = hidden_ref[...]

    def put(ref, offset=0):
        def store(frame, row, value):
            ref[frame, offset + row] = value
        return store

    def late_border(start, part, result):
        offset = (rows - 4) * core
        targets = (put(keep_ref, offset), put(send_ref, offset))
        finish(mine_ref, other_ref, live, CACHE + start, ((held - 1) * core, 1), result, targets)

    def late_middle():
        for source, target in ((late_keep_ref, keep_ref), (late_send_ref, send_ref)):
            target[CACHE:, pl.ds(2 * (1 - core), rows - 4)] = source[...]

    def hidden_steps(first, flags):
        def store(begin, end, values):
            operand[:, first + begin:first + end] = values

        flags = [flag * inside for flag in flags]
        return hide(plane, w1_ref, bias1_ref, gain2_ref, first, CACHE - first, rows, flags, store)

    def then(start, part, result):
        finish(mine_ref, other_ref, live, start, (core, held - 1), result, (put(keep_ref), put(send_ref)))

    def result_steps():
        return convolved(operand, w2_ref, bias2_ref, 0, CACHE, rows - 2, then)

    @pl.when(earlier)
    def _():
        fill_rows(
            plane, 0, middle, unpacked(tail_mine_ref, pairs, core * (pairs - held)),
            unpacked(tail_other_ref, held, 0), gain1_ref,
        )
        flags = frame_flags(tail_mine_ref[CACHE * pairs], range(CACHE - 2, CACHE)) + live[0:2]

        def beside():
            late_middle()
            late_border(0, late_border_ref.shape[0], late_border_ref[...])

        hidden, results = hidden_steps(0, flags), result_steps()
        if len(hidden) == 2 and len(results) == 2:
            in_turn(hidden[::-1] + results[::-1], beside)
        else:
            in_turn(hidden, beside)
            in_turn(results)

    @pl.when(jnp.logical_not(earlier))
    def _():
        plane[:, 0:CACHE, pl.ds(middle, rows)] = jnp.zeros(
            plane.shape[:1] + (CACHE, rows) + plane.shape[3:], plane.dtype
        )
        operand[:, 0:2] = jnp.zeros(operand.shape[:1] + (2,) + operand.shape[2:], operand.dtype)
        border = convolved(late_operand_ref, w2_ref, bias2_ref, 0, late_border_ref.shape[0], 2, late_border)
        in_turn(hidden_steps(2, live[0:2]) + border + result_steps()[::-1], late_middle)


def place_kernel(keep_ref, got_ref, result_ref, arrived):
    core, half = lower_part(), keep_ref.shape[1]
    copies = [
        pltpu.make_async_copy(keep_ref, result_ref.at[:, pl.ds(half * core, half)], arrived.at[0]),
        pltpu.make_async_copy(got_ref, result_ref.at[:, pl.ds(half * (1 - core), half)], arrived.at[1]),
    ]
    for copy in copies:
        copy.start()
    for copy in copies:
        copy.wait()


def shards(features, frame_counts, gain_first, conv_first, bias_first, gain_second, conv_second, bias_second):
    frames, rows, side, channels = features.shape
    pairs, half = rows // 2, rows // 2
    held = half // 2 + 1
    tall, cores, blocks = lax.axis_size("ha"), lax.axis_size("wa"), lax.axis_size("tchunk")
    packed, width, tiles = 3 * LANES, 2 * side, CACHE * held
    bf16 = jnp.bfloat16
    vmem = pl.BlockSpec(memory_space=pltpu.VMEM)
    limit = pltpu.CompilerParams(vmem_limit_bytes=20 * 2**20)
    work = 2 * TAPS**3 * channels * channels * width

    def shape(*extent):
        return jax.ShapeDtypeStruct(extent, bf16)

    def cost(flops, fetched):
        return pl.CostEstimate(flops=flops, bytes_accessed=fetched, transcendentals=0)

    slots = pl.pallas_call(
        slots_kernel,
        out_shape=jax.ShapeDtypeStruct((side, packed), jnp.int32),
        out_specs=vmem,
        compiler_params=limit,
        cost_estimate=cost(2**34, 2**20),
    )()
    slots, frame_counts = lax.optimization_barrier((slots, frame_counts))
    tail, mine, theirs, marks = pl.pallas_call(
        prepare_kernel,
        out_shape=(
            shape(CACHE * pairs + 1, side, packed), shape(frames, held, side, packed),
            shape((CACHE + frames) * held, side, packed), shape(side, packed),
        ),
        in_specs=[pl.BlockSpec(memory_space=pltpu.SMEM), vmem, vmem],
        out_specs=(vmem,) * 4,
        scratch_shapes=[pltpu.VMEM((frames, pairs, side, packed), bf16)],
        compiler_params=limit,
    )(frame_counts, slots, features)

    if blocks > 2:
        tail = joined_tail(tail)
        rest = lax.dynamic_slice_in_dim(
            tail[:-1].reshape(CACHE, pairs, side, packed), (1 - lower_part()) * (pairs - held), held, 1
        )
        theirs = jnp.concatenate([rest.reshape(tiles, side, packed), theirs[tiles:]], axis=0)
    straight, diagonal, across = [], [], []

    def index(block, h, core):
        return (block * tall + h) * cores + core

    for k in range(blocks - 1):
        for h in range(tall):
            for core in range(cores):
                straight.append((index(k, h, core), index(k + 1, h, core)))
    for h in range(tall - 1):
        for k in range(blocks):
            lower, upper = index(k, h, 0), index(k, h + 1, 1)
            across += [(lower, upper), (upper, lower)]
            if k + 1 < blocks:
                lower_next, upper_next = index(k + 1, h, 0), index(k + 1, h + 1, 1)
                diagonal += [(lower, upper_next), (upper, lower_next)]
    axes = ("tchunk", "ha", "wa")
    swap = [(0, 1), (1, 0)]
    tail_mine = lax.ppermute(tail, axes, straight)
    other = lax.ppermute(theirs, "wa", swap)
    tail_edge, own_edge = pl.pallas_call(
        border_kernel,
        out_shape=(shape(2 * CACHE, side, packed), shape(2, frames, side, packed)),
        in_specs=[vmem] * 3,
        out_specs=(vmem, vmem),
        compiler_params=limit,
        cost_estimate=cost(2**34, 2**20),
    )(tail, mine, other)
    own_edge = lax.ppermute(own_edge, axes, across)
    tail_edge = lax.ppermute(tail_edge, axes, diagonal)

    weights = (
        gain_first.reshape(1, channels), conv_first, bias_first.reshape(1, channels),
        gain_second.reshape(1, channels), conv_second, bias_second.reshape(1, channels),
    )
    products = -(-(frames - 2) * half * width // OWN)
    done = -(-(frames - 2) // products) * (products - 1)
    first, late, raw = pl.pallas_call(
        own_kernel,
        out_shape=(
            shape(3, frames, half + 2, width, LANES), shape(3, done, half, width, LANES),
            jax.ShapeDtypeStruct((frames - 2 - done, half, width, channels), jnp.float32),
        ),
        in_specs=[vmem] * 7,
        out_specs=(vmem,) * 3,
        compiler_params=limit,
        cost_estimate=cost(work * (frames - 2) * half, 4 * 2**20),
    )(marks, mine, other, *weights[:4])
    rest = pl.pallas_call(
        other_rows_kernel,
        out_shape=shape(tiles, side, packed),
        in_specs=[vmem, pl.BlockSpec(memory_space=pl.ANY)],
        out_specs=vmem,
        compiler_params=limit,
        cost_estimate=cost(1, 1),
    )(tail_mine, late)
    tail_other = lax.ppermute(rest, "wa", swap)
    strip, hidden, keep, send, border, late = pl.pallas_call(
        edge_kernel,
        out_shape=(
            shape(3, 2, 2, width, LANES), shape(3, 2, half + 2, width, LANES),
            shape(frames - CACHE, half - 2, side, channels), shape(frames - CACHE, half - 2, side, channels),
            jax.ShapeDtypeStruct((frames - CACHE, 2, width, channels), jnp.float32),
            shape(3, frames - 2, 4, width, LANES),
        ),
        in_specs=[vmem] * 13,
        out_specs=(vmem,) * 6,
        scratch_shapes=[
            pltpu.VMEM((3, frames, 4, width, LANES), bf16),
            pltpu.VMEM((3, frames - 2, half, width, LANES), bf16),
        ],
        compiler_params=limit,
        cost_estimate=cost(2**20, 2**20),
    )(marks, mine, other, own_edge, first, late, raw, *weights)
    tail_edge = pl.pallas_call(
        tail_edge_kernel,
        out_shape=shape(3, CACHE + 2, 2, width, LANES),
        in_specs=[vmem] * 3,
        out_specs=vmem,
        compiler_params=limit,
        cost_estimate=cost(2**30, 2**18),
    )(tail_edge, strip, weights[0])
    keep, send = pl.pallas_call(
        early_kernel,
        out_shape=(shape(frames, half, side, channels), shape(frames, half, side, channels)),
        in_specs=[vmem] * 18,
        out_specs=(vmem, vmem),
        scratch_shapes=[
            pltpu.VMEM((3, CACHE + 2, half + 4, width, LANES), bf16),
            pltpu.VMEM((3, CACHE + 2, half + 2, width, LANES), bf16),
        ],
        compiler_params=limit,
        cost_estimate=cost(work * CACHE * (2 * half + 2), 8 * 2**20),
    )(marks, tail_mine, tail_other, mine, other, tail_edge, first, hidden, keep, send, border, late, *weights)
    got = lax.ppermute(send, "wa", swap)
    return pl.pallas_call(
        place_kernel,
        out_shape=shape(*features.shape),
        in_specs=[vmem, vmem],
        out_specs=pl.BlockSpec(memory_space=pltpu.HBM),
        scratch_shapes=[pltpu.SemaphoreType.DMA((2,))],
        compiler_params=limit,
    )(keep, got)


def solution(mesh):
    return jax.shard_map(
        shards,
        mesh=mesh,
        in_specs=(
            P(("grp", "tchunk"), "ha", "wa", None),
            P(("grp", "tchunk")),
            P(), P(), P(), P(), P(), P(),
        ),
        out_specs=P(("grp", "tchunk"), "ha", "wa", None),
        check_vma=False,
    )
```

```python
import jax
import jax.numpy as jnp
from jax import lax
from jax.experimental import pallas as pl
from jax.experimental.pallas import tpu as pltpu
from jax.sharding import PartitionSpec as P

epsilon = 1e-06
CACHE = 4
TAPS = 3
LANES = 128
PRODUCT = 192
OWN = 128


def slots_kernel(slots_ref):
    slots_ref[...] = lax.broadcasted_iota(jnp.int32, slots_ref.shape, 0)


def lower_part():
    return 1 - lax.axis_index("wa")


def prepare_kernel(total_ref, slots_ref, raw, tail_ref, mine_ref, theirs_ref, marks_ref, pack):
    frames, rows = raw.shape[:2]
    pairs, held = rows // 2, mine_ref.shape[1]
    core = lower_part()
    total = total_ref[0]
    for frame in range(frames):
        for pair in range(pairs):
            first, second = raw[frame, 2 * pair], raw[frame, 2 * pair + 1]
            packed = jnp.concatenate(
                [first[:, :LANES], second[:, :LANES], first[:, LANES:], second[:, LANES:]], axis=-1
            )
            pack[frame, pair] = packed
    for slot in range(CACHE):
        frame = total - CACHE + slot
        value = pack[jnp.maximum(frame, 0)]
        tail_ref[slot * pairs:(slot + 1) * pairs] = jnp.where(frame >= 0, value, jnp.zeros_like(value))
        value = pack[jnp.maximum(frame, 0), pl.ds((1 - core) * (pairs - held), held)]
        theirs_ref[slot * held:(slot + 1) * held] = jnp.where(frame >= 0, value, jnp.zeros_like(value))
    for frame in range(frames):
        start = (CACHE + frame) * held
        value = pack[frame, pl.ds(core * (pairs - held), held)]
        mine_ref[frame] = jnp.where(frame < total, value, jnp.zeros_like(value))
        value = pack[frame, pl.ds((1 - core) * (pairs - held), held)]
        theirs_ref[start:start + held] = jnp.where(frame < total, value, jnp.zeros_like(value))
    slot = slots_ref[...]
    tail_ref[CACHE * pairs] = jnp.where(
        (slot < CACHE) & (total - CACHE + slot >= 0), 1.0, 0.0
    ).astype(tail_ref.dtype)
    marks_ref[...] = jnp.where(slot < total, 1.0, 0.0).astype(marks_ref.dtype)


def joined_tail(tail):
    count = lax.axis_size("tchunk")

    def pushed(value, held):
        return lax.dynamic_slice_in_dim(jnp.concatenate([value, jnp.zeros_like(value)], axis=0), held, CACHE, 0)

    step = 1
    while step < count - 1:
        early = lax.ppermute(tail, "tchunk", [(k, k + step) for k in range(count - step)])
        held = jnp.sum(tail[-1, :CACHE, 0].astype(jnp.int32))
        body = pushed(early[:-1].reshape((CACHE, -1) + tail.shape[1:]), held).reshape(tail[:-1].shape)
        marks = jnp.pad(pushed(early[-1, :CACHE], held), ((0, tail.shape[1] - CACHE), (0, 0)))
        tail = tail + jnp.concatenate([body, marks[None]], axis=0)
        step *= 2
    return tail


def silu(half):
    return half + half * jnp.tanh(half)


def lane_mask():
    return lax.broadcasted_iota(jnp.int32, (1, 1, 1, LANES), 3) < LANES // 2


def gains(gain_ref):
    low, high = 0.5 * gain_ref[:, :LANES], 0.5 * gain_ref[:, LANES:]
    return low.reshape(1, 1, 1, LANES), jnp.concatenate([high, high], axis=-1).reshape(1, 1, 1, LANES)


def rolled(values):
    shape = values.shape
    return pltpu.roll(values.reshape(-1, LANES), LANES // 2, 1).reshape(shape)


def first_rows(left, right, gain_ref, channels):
    raw = jnp.concatenate([left.astype(jnp.float32), right.astype(jnp.float32)], axis=2)
    front, back, high = raw[..., :LANES], raw[..., LANES:2 * LANES], raw[..., 2 * LANES:]
    lower = lane_mask()
    squared = high * high

    def inverse(low, mask):
        total = jnp.sum(low * low + jnp.where(mask, squared, 0.0), axis=-1, keepdims=True)
        return lax.rsqrt(total * (1.0 / channels) + epsilon)

    scale_front, scale_back = inverse(front, lower), inverse(back, jnp.logical_not(lower))
    gain_low, gain_high = gains(gain_ref)
    front = silu(front * scale_front * gain_low)
    back = silu(back * scale_back * gain_low)
    high = silu(high * jnp.where(lower, scale_front, scale_back) * gain_high)
    turned = rolled(high)
    one = [front, jnp.where(lower, high, 0.0), jnp.where(lower, 0.0, turned)]
    two = [back, jnp.where(lower, turned, 0.0), jnp.where(lower, 0.0, high)]
    return [[part.astype(jnp.bfloat16) for part in row] for row in (one, two)]


def second_rows(hidden, flag, gain_ref, channels):
    gain = 0.5 * gain_ref[...].reshape(1, 1, 1, channels)
    total = jnp.sum(hidden * hidden, axis=-1, keepdims=True)
    inverse = lax.rsqrt(total * (1.0 / channels) + epsilon) * flag
    values = silu(hidden * inverse * gain)
    rest = jnp.zeros(values.shape[:-1] + (LANES // 2,), jnp.float32)
    high = jnp.concatenate([values[..., LANES:], rest], axis=-1)
    parts = [values[..., :LANES], high, rolled(high)]
    return jnp.stack([part.astype(jnp.bfloat16) for part in parts])


def in_turn(steps, beside=None):
    waiting = None
    for product, then in steps:
        result = product()
        if waiting:
            waiting[1](waiting[0])
        elif beside:
            beside()
        waiting = (result, then)
    waiting[1](waiting[0])


def convolved(operand, weights_ref, bias_ref, frame, frames, rows, then, most=PRODUCT):
    products = -(-frames * rows * operand.shape[3] // most)
    step = -(-frames // products)

    def part(start):
        count = min(step, frames - start)
        return (
            lambda: convolved_part(operand, weights_ref, bias_ref, frame + start, count, rows),
            lambda result: then(start, count, result),
        )

    return [part(start) for start in range(0, frames, step)]


def convolved_part(operand, weights_ref, bias_ref, frame, frames, rows):
    width = operand.shape[3]
    channels = weights_ref.shape[-1]
    taps = [(a, i) for a in range(TAPS) for i in range(TAPS)]
    groups = [taps[start:start + 2] for start in range(0, len(taps), 2)]

    def window(tap, part):
        a, i = tap
        value = operand[part, frame + a:frame + a + frames, i:i + rows]
        return value.reshape(frames * rows * width, LANES)

    def operands(groups):
        pieces = []
        for group in groups:
            pieces += [window(tap, 0) for tap in group]
            high = window(group[0], 1)
            pieces.append(high + window(group[1], 2) if len(group) > 1 else high)
        return jnp.concatenate(pieces, axis=-1)

    def weights(groups, j, depth):
        rights = []
        for group in groups:
            held = [weights_ref[a, i, j] for a, i in group]
            rights += [weight[:LANES] for weight in held] + [weight[LANES:] for weight in held]
        rest = depth - sum(right.shape[0] for right in rights)
        if rest:
            rights.append(jnp.zeros((rest, channels), jnp.bfloat16))
        return jnp.concatenate(rights, axis=0)

    half = len(groups) // 2
    parts = [(part, operands(part)) for part in (groups[:half], groups[half:])]
    products = []
    for j in range(TAPS):
        total = None
        for part, left in parts if j % 2 == 0 else parts[::-1]:
            product = jnp.dot(left, weights(part, j, left.shape[1]), preferred_element_type=jnp.float32)
            total = product if total is None else total + product
        products.append(total.reshape(frames * rows, width, channels))
    column = lax.broadcasted_iota(jnp.int32, (1, width, 1), 1)
    before = jnp.where(column == 0, 0.0, pltpu.roll(products[0], 1, 1))
    after = jnp.where(column == width - 1, 0.0, pltpu.roll(products[2], width - 1, 1))
    result = products[1] + before + after + bias_ref[...].reshape(1, 1, channels)
    return result.reshape(frames, rows, width, channels)


def halves(core, mine, other):
    return jnp.where(core == 0, mine, other), jnp.where(core == 0, other, mine)


def frame_flags(marks, frames):
    values = marks.astype(jnp.float32)
    return [values[k:k + 1, 0:1].reshape(1, 1, 1, 1) for k in frames]


def fill_rows(operand, frame, row, mine, other, gain_ref):
    left, right = halves(lax.axis_index("wa"), mine, other)
    frames, pairs = mine.shape[:2]
    upper, lower = first_rows(left, right, gain_ref, gain_ref.shape[-1])
    for part in range(len(upper)):
        for pair in range(pairs):
            operand[part, frame:frame + frames, pl.ds(row + 2 * pair, 1)] = upper[part][:, pair:pair + 1]
            operand[part, frame:frame + frames, pl.ds(row + 2 * pair + 1, 1)] = lower[part][:, pair:pair + 1]


def border_kernel(tail_ref, mine_ref, other_ref, tail_edge_ref, own_edge_ref):
    frames, held = mine_ref.shape[:2]
    pairs = tail_ref.shape[0] // CACHE
    core = lower_part()
    pair = core * (held - 1)
    for slot in range(CACHE):
        tail_edge_ref[slot] = tail_ref[slot * pairs + core * (pairs - 1)]
        tail_edge_ref[CACHE + slot] = other_ref[slot * held + pair]
    for frame in range(frames):
        own_edge_ref[0, frame] = mine_ref[frame, pair]
        own_edge_ref[1, frame] = other_ref[(CACHE + frame) * held + pair]


def finish(mine_ref, other_ref, live, first, pairs, value, targets):
    _, held, side, _ = mine_ref.shape
    frames, channels = value.shape[0], value.shape[-1]
    start, count = pairs
    near, far = halves(lax.axis_index("wa"), value[:, :, :side], value[:, :, side:])
    for mine, value, target in ((True, near, targets[0]), (False, far, targets[1])):
        for frame in range(frames):
            for k in range(count):
                if mine:
                    raw = mine_ref[first + frame, start + k]
                else:
                    raw = other_ref[(CACHE + first + frame) * held + start + k]
                raw = raw.astype(jnp.float32)
                high = raw[:, 2 * LANES:]
                for row, tail in ((0, high), (1, pltpu.roll(high, LANES // 2, 1))):
                    low = raw[:, row * LANES:(row + 1) * LANES]
                    features = jnp.concatenate([low, tail[:, :channels - LANES]], axis=-1)
                    summed = features + value[frame, 2 * k + row]
                    kept = jnp.where(live[first + frame].reshape(1, 1) > 0.5, summed, 0.0)
                    target(first + frame, 2 * k + row, kept.astype(jnp.bfloat16))


def hide(operand, weights_ref, bias_ref, gain_ref, first, count, rows, flags, store, most=PRODUCT):
    channels = weights_ref.shape[-1]

    def then(begin, part, hidden):
        flag = jnp.concatenate(flags[begin:begin + part], axis=0)
        store(begin, begin + part, second_rows(hidden, flag, gain_ref, channels))

    return convolved(operand, weights_ref, bias_ref, first, count, rows, then, most)


def inside_flags(rows):
    core, place = lower_part(), lax.axis_index("ha")
    inside = jnp.where(core == 0, place > 0, place < lax.axis_size("ha") - 1)
    row = lax.broadcasted_iota(jnp.int32, (1, rows, 1, 1), 1)
    return jnp.where((row == (rows - 1) * core) & jnp.logical_not(inside), 0.0, 1.0)


def other_rows_kernel(tail_ref, late_ref, rest_ref):
    pairs, held = tail_ref.shape[0] // CACHE, rest_ref.shape[0] // CACHE
    first = (1 - lower_part()) * (pairs - held)
    for slot in range(CACHE):
        rest_ref[slot * held:(slot + 1) * held] = tail_ref[pl.ds(slot * pairs + first, held)]


def own_kernel(
    marks_ref, mine_ref, other_ref, gain1_ref, w1_ref, bias1_ref, gain2_ref,
    first_ref, late_ref, raw_ref,
):
    frames, pairs, side, packed = mine_ref.shape
    live = frame_flags(marks_ref[...], range(2, frames))

    def fill(start, end):
        other = other_ref[(CACHE + start) * pairs:(CACHE + end) * pairs].reshape(end - start, pairs, side, packed)
        fill_rows(first_ref, start, 0, mine_ref[start:end], other, gain1_ref)

    def store(begin, end, rows):
        late_ref[:, begin:end] = rows

    steps = hide(first_ref, w1_ref, bias1_ref, gain2_ref, 0, frames - 2, 2 * pairs - 2, live, store, OWN)
    each = -(-(frames - 2) // len(steps))

    def filled(k, product):
        def run():
            fill(min(frames, each * k + (2 if k else 0)), min(frames, each * (k + 1) + 2))
            return product()
        return run

    def left(result):
        raw_ref[...] = result

    steps[-1] = (steps[-1][0], left)
    in_turn([(filled(k, product), then) for k, (product, then) in enumerate(steps)])


def edge_kernel(
    marks_ref, mine_ref, other_ref, edge_ref, first_ref, done_ref, raw_ref,
    gain1_ref, w1_ref, bias1_ref, gain2_ref, w2_ref, bias2_ref,
    strip_ref, hidden_ref, keep_ref, send_ref, border_ref, operand, strip, late_ref,
):
    core = lower_part()
    frames, pairs = mine_ref.shape[:2]
    rows = 2 * pairs
    late = frames - CACHE
    outward, inward = pl.ds(2 * core, 2), pl.ds(2 * (1 - core), 2)
    fill_rows(strip, 0, 2 * core, edge_ref[1][:, None], edge_ref[0][:, None], gain1_ref)
    strip[:, :, inward] = first_ref[:, :, pl.ds((rows - 2) * core, 2)]
    live = frame_flags(marks_ref[...], range(frames))
    inside = inside_flags(2)
    done = done_ref.shape[1]
    late_ref[:, 0:done] = done_ref[...]

    def activate():
        flag = jnp.concatenate(live[2 + done:], axis=0)
        late_ref[:, done:] = second_rows(raw_ref[...], flag, gain2_ref, gain2_ref.shape[-1])
        operand[:, :, inward] = late_ref[:, :, pl.ds((rows - 4) * core, 2)]

    def store(begin, end, values):
        operand[:, begin:end, outward] = values

    def put(ref):
        def store(frame, row, value):
            ref[frame - CACHE, row] = value
        return store

    def middle(start, part, result):
        targets = (put(keep_ref), put(send_ref))
        finish(mine_ref, other_ref, live, CACHE + start, (1, pairs - 2), result, targets)

    def border(start, part, result):
        border_ref[start:start + part] = result

    flags = [flag * inside for flag in live[2:]]
    earlier = lax.axis_index("tchunk") > 0

    def steps():
        return hide(strip, w1_ref, bias1_ref, gain2_ref, 0, frames - 2, 2, flags, store) + convolved(
            late_ref, w2_ref, bias2_ref, 0, late, rows - 4, middle
        )

    @pl.when(earlier)
    def _():
        in_turn(steps() + convolved(operand, w2_ref, bias2_ref, 0, late, 2, border), activate)

    @pl.when(jnp.logical_not(earlier))
    def _():
        in_turn(steps(), activate)

    strip_ref[...] = strip[:, 0:2, outward]
    hidden_ref[:, :, pl.ds(2 * (1 - core), rows - 2)] = late_ref[:, 0:2]
    hidden_ref[:, :, pl.ds((rows - 2) * core, 2)] = operand[:, 0:2, outward]


def tail_edge_kernel(edge_ref, strip_ref, gain_ref, rows_ref):
    rows_ref[:, CACHE:] = strip_ref[...]

    @pl.when(lax.axis_index("tchunk") > 0)
    def _():
        fill_rows(rows_ref, 0, 0, edge_ref[CACHE:2 * CACHE][:, None], edge_ref[0:CACHE][:, None], gain_ref)

    @pl.when(lax.axis_index("tchunk") == 0)
    def _():
        rows_ref[:, 0:CACHE] = jnp.zeros((rows_ref.shape[0], CACHE) + rows_ref.shape[2:], rows_ref.dtype)


def early_kernel(
    marks_ref, tail_mine_ref, tail_other_ref, mine_ref, other_ref, edge_ref, first_ref, hidden_ref,
    late_keep_ref, late_send_ref, late_border_ref, late_operand_ref, gain1_ref, w1_ref, bias1_ref, gain2_ref, w2_ref, bias2_ref,
    keep_ref, send_ref, plane, operand,
):
    core = lower_part()
    held = mine_ref.shape[1]
    rows = 2 * held
    pairs = tail_mine_ref.shape[0] // CACHE
    live = frame_flags(marks_ref[...], range(mine_ref.shape[0]))
    inside = inside_flags(rows)
    earlier = lax.axis_index("tchunk") > 0
    middle, border = 2 * (1 - core), rows * core

    def unpacked(ref, stride, first):
        return jnp.stack([ref[pl.ds(slot * stride + first, held)] for slot in range(CACHE)])

    plane[:, CACHE:, pl.ds(middle, rows)] = first_ref[:, 0:2]
    plane[:, :, pl.ds(border, 2)] = edge_ref[...]
    operand[:, CACHE:] = hidden_ref[...]

    def put(ref, offset=0):
        def store(frame, row, value):
            ref[frame, offset + row] = value
        return store

    def late_border(start, part, result):
        offset = (rows - 4) * core
        targets = (put(keep_ref, offset), put(send_ref, offset))
        finish(mine_ref, other_ref, live, CACHE + start, ((held - 1) * core, 1), result, targets)

    def late_middle():
        for source, target in ((late_keep_ref, keep_ref), (late_send_ref, send_ref)):
            target[CACHE:, pl.ds(2 * (1 - core), rows - 4)] = source[...]

    def hidden_steps(first, flags):
        def store(begin, end, values):
            operand[:, first + begin:first + end] = values

        flags = [flag * inside for flag in flags]
        return hide(plane, w1_ref, bias1_ref, gain2_ref, first, CACHE - first, rows, flags, store)

    def then(start, part, result):
        finish(mine_ref, other_ref, live, start, (core, held - 1), result, (put(keep_ref), put(send_ref)))

    def result_steps():
        return convolved(operand, w2_ref, bias2_ref, 0, CACHE, rows - 2, then)

    @pl.when(earlier)
    def _():
        fill_rows(
            plane, 0, middle, unpacked(tail_mine_ref, pairs, core * (pairs - held)),
            unpacked(tail_other_ref, held, 0), gain1_ref,
        )
        flags = frame_flags(tail_mine_ref[CACHE * pairs], range(CACHE - 2, CACHE)) + live[0:2]

        def beside():
            late_middle()
            late_border(0, late_border_ref.shape[0], late_border_ref[...])

        hidden, results = hidden_steps(0, flags), result_steps()
        if len(hidden) == 2 and len(results) == 2:
            in_turn(hidden[::-1] + results[::-1], beside)
        else:
            in_turn(hidden, beside)
            in_turn(results)

    @pl.when(jnp.logical_not(earlier))
    def _():
        plane[:, 0:CACHE, pl.ds(middle, rows)] = jnp.zeros(
            plane.shape[:1] + (CACHE, rows) + plane.shape[3:], plane.dtype
        )
        operand[:, 0:2] = jnp.zeros(operand.shape[:1] + (2,) + operand.shape[2:], operand.dtype)
        border = convolved(late_operand_ref, w2_ref, bias2_ref, 0, late_border_ref.shape[0], 2, late_border)
        in_turn(hidden_steps(2, live[0:2]) + border + result_steps()[::-1], late_middle)


def keep_kernel(keep_ref, result_ref, arrived):
    half = keep_ref.shape[1]
    copy = pltpu.make_async_copy(keep_ref, result_ref.at[:, pl.ds(half * lower_part(), half)], arrived)
    copy.start()
    copy.wait()


def got_kernel(got_ref, kept_ref, result_ref, arrived):
    half = got_ref.shape[1]
    copy = pltpu.make_async_copy(got_ref, result_ref.at[:, pl.ds(half * (1 - lower_part()), half)], arrived)
    copy.start()
    copy.wait()


def shards(features, frame_counts, gain_first, conv_first, bias_first, gain_second, conv_second, bias_second):
    frames, rows, side, channels = features.shape
    pairs, half = rows // 2, rows // 2
    held = half // 2 + 1
    tall, cores, blocks = lax.axis_size("ha"), lax.axis_size("wa"), lax.axis_size("tchunk")
    packed, width, tiles = 3 * LANES, 2 * side, CACHE * held
    bf16 = jnp.bfloat16
    vmem = pl.BlockSpec(memory_space=pltpu.VMEM)
    limit = pltpu.CompilerParams(vmem_limit_bytes=20 * 2**20)
    work = 2 * TAPS**3 * channels * channels * width

    def shape(*extent):
        return jax.ShapeDtypeStruct(extent, bf16)

    def cost(flops, fetched):
        return pl.CostEstimate(flops=flops, bytes_accessed=fetched, transcendentals=0)

    slots = pl.pallas_call(
        slots_kernel,
        out_shape=jax.ShapeDtypeStruct((side, packed), jnp.int32),
        out_specs=vmem,
        compiler_params=limit,
        cost_estimate=cost(2**34, 2**20),
    )()
    slots, frame_counts = lax.optimization_barrier((slots, frame_counts))
    tail, mine, theirs, marks = pl.pallas_call(
        prepare_kernel,
        out_shape=(
            shape(CACHE * pairs + 1, side, packed), shape(frames, held, side, packed),
            shape((CACHE + frames) * held, side, packed), shape(side, packed),
        ),
        in_specs=[pl.BlockSpec(memory_space=pltpu.SMEM), vmem, vmem],
        out_specs=(vmem,) * 4,
        scratch_shapes=[pltpu.VMEM((frames, pairs, side, packed), bf16)],
        compiler_params=limit,
    )(frame_counts, slots, features)

    if blocks > 2:
        tail = joined_tail(tail)
        rest = lax.dynamic_slice_in_dim(
            tail[:-1].reshape(CACHE, pairs, side, packed), (1 - lower_part()) * (pairs - held), held, 1
        )
        theirs = jnp.concatenate([rest.reshape(tiles, side, packed), theirs[tiles:]], axis=0)
    straight, diagonal, across = [], [], []

    def index(block, h, core):
        return (block * tall + h) * cores + core

    for k in range(blocks - 1):
        for h in range(tall):
            for core in range(cores):
                straight.append((index(k, h, core), index(k + 1, h, core)))
    for h in range(tall - 1):
        for k in range(blocks):
            lower, upper = index(k, h, 0), index(k, h + 1, 1)
            across += [(lower, upper), (upper, lower)]
            if k + 1 < blocks:
                lower_next, upper_next = index(k + 1, h, 0), index(k + 1, h + 1, 1)
                diagonal += [(lower, upper_next), (upper, lower_next)]
    axes = ("tchunk", "ha", "wa")
    swap = [(0, 1), (1, 0)]
    tail_mine = lax.ppermute(tail, axes, straight)
    other = lax.ppermute(theirs, "wa", swap)
    tail_edge, own_edge = pl.pallas_call(
        border_kernel,
        out_shape=(shape(2 * CACHE, side, packed), shape(2, frames, side, packed)),
        in_specs=[vmem] * 3,
        out_specs=(vmem, vmem),
        compiler_params=limit,
        cost_estimate=cost(2**34, 2**20),
    )(tail, mine, other)
    own_edge = lax.ppermute(own_edge, axes, across)
    tail_edge = lax.ppermute(tail_edge, axes, diagonal)

    weights = (
        gain_first.reshape(1, channels), conv_first, bias_first.reshape(1, channels),
        gain_second.reshape(1, channels), conv_second, bias_second.reshape(1, channels),
    )
    products = -(-(frames - 2) * half * width // OWN)
    done = -(-(frames - 2) // products) * (products - 1)
    first, late, raw = pl.pallas_call(
        own_kernel,
        out_shape=(
            shape(3, frames, half + 2, width, LANES), shape(3, done, half, width, LANES),
            jax.ShapeDtypeStruct((frames - 2 - done, half, width, channels), jnp.float32),
        ),
        in_specs=[vmem] * 7,
        out_specs=(vmem,) * 3,
        compiler_params=limit,
        cost_estimate=cost(work * (frames - 2) * half, 4 * 2**20),
    )(marks, mine, other, *weights[:4])
    rest = pl.pallas_call(
        other_rows_kernel,
        out_shape=shape(tiles, side, packed),
        in_specs=[vmem, pl.BlockSpec(memory_space=pl.ANY)],
        out_specs=vmem,
        compiler_params=limit,
        cost_estimate=cost(1, 1),
    )(tail_mine, late)
    tail_other = lax.ppermute(rest, "wa", swap)
    strip, hidden, keep, send, border, late = pl.pallas_call(
        edge_kernel,
        out_shape=(
            shape(3, 2, 2, width, LANES), shape(3, 2, half + 2, width, LANES),
            shape(frames - CACHE, half - 2, side, channels), shape(frames - CACHE, half - 2, side, channels),
            jax.ShapeDtypeStruct((frames - CACHE, 2, width, channels), jnp.float32),
            shape(3, frames - 2, 4, width, LANES),
        ),
        in_specs=[vmem] * 13,
        out_specs=(vmem,) * 6,
        scratch_shapes=[
            pltpu.VMEM((3, frames, 4, width, LANES), bf16),
            pltpu.VMEM((3, frames - 2, half, width, LANES), bf16),
        ],
        compiler_params=limit,
        cost_estimate=cost(2**20, 2**20),
    )(marks, mine, other, own_edge, first, late, raw, *weights)
    tail_edge = pl.pallas_call(
        tail_edge_kernel,
        out_shape=shape(3, CACHE + 2, 2, width, LANES),
        in_specs=[vmem] * 3,
        out_specs=vmem,
        compiler_params=limit,
        cost_estimate=cost(2**30, 2**18),
    )(tail_edge, strip, weights[0])
    keep, send = pl.pallas_call(
        early_kernel,
        out_shape=(shape(frames, half, side, channels), shape(frames, half, side, channels)),
        in_specs=[vmem] * 18,
        out_specs=(vmem, vmem),
        scratch_shapes=[
            pltpu.VMEM((3, CACHE + 2, half + 4, width, LANES), bf16),
            pltpu.VMEM((3, CACHE + 2, half + 2, width, LANES), bf16),
        ],
        compiler_params=limit,
        cost_estimate=cost(work * CACHE * (2 * half + 2), 8 * 2**20),
    )(marks, tail_mine, tail_other, mine, other, tail_edge, first, hidden, keep, send, border, late, *weights)
    got = lax.ppermute(send, "wa", swap)
    hbm = pl.BlockSpec(memory_space=pltpu.HBM)
    kept = pl.pallas_call(
        keep_kernel,
        out_shape=shape(*features.shape),
        in_specs=[vmem],
        out_specs=hbm,
        scratch_shapes=[pltpu.SemaphoreType.DMA],
        compiler_params=limit,
        cost_estimate=cost(2**28, 2**20),
    )(keep)
    return pl.pallas_call(
        got_kernel,
        out_shape=shape(*features.shape),
        in_specs=[vmem, hbm],
        out_specs=hbm,
        input_output_aliases={1: 0},
        scratch_shapes=[pltpu.SemaphoreType.DMA],
        compiler_params=limit,
    )(got, kept)


def solution(mesh):
    return jax.shard_map(
        shards,
        mesh=mesh,
        in_specs=(
            P(("grp", "tchunk"), "ha", "wa", None),
            P(("grp", "tchunk")),
            P(), P(), P(), P(), P(), P(),
        ),
        out_specs=P(("grp", "tchunk"), "ha", "wa", None),
        check_vma=False,
    )
```

```python
import jax
import jax.numpy as jnp
from jax import lax
from jax.experimental import pallas as pl
from jax.experimental.pallas import tpu as pltpu
from jax.sharding import PartitionSpec as P

epsilon = 1e-06
CACHE = 4
TAPS = 3
LANES = 128
PRODUCT = 192
OWN = 128


def slots_kernel(slots_ref):
    slots_ref[...] = lax.broadcasted_iota(jnp.int32, slots_ref.shape, 0)


def lower_part():
    return 1 - lax.axis_index("wa")


def prepare_kernel(total_ref, slots_ref, raw, tail_ref, mine_ref, theirs_ref, marks_ref, pack):
    frames, rows = raw.shape[:2]
    pairs, held = rows // 2, mine_ref.shape[1]
    core = lower_part()
    total = total_ref[0]
    for frame in range(frames):
        for pair in range(pairs):
            first, second = raw[frame, 2 * pair], raw[frame, 2 * pair + 1]
            packed = jnp.concatenate(
                [first[:, :LANES], second[:, :LANES], first[:, LANES:], second[:, LANES:]], axis=-1
            )
            pack[frame, pair] = packed
    for slot in range(CACHE):
        frame = total - CACHE + slot
        value = pack[jnp.maximum(frame, 0)]
        tail_ref[slot * pairs:(slot + 1) * pairs] = jnp.where(frame >= 0, value, jnp.zeros_like(value))
        value = pack[jnp.maximum(frame, 0), pl.ds((1 - core) * (pairs - held), held)]
        theirs_ref[slot * held:(slot + 1) * held] = jnp.where(frame >= 0, value, jnp.zeros_like(value))
    for frame in range(frames):
        start = (CACHE + frame) * held
        value = pack[frame, pl.ds(core * (pairs - held), held)]
        mine_ref[frame] = jnp.where(frame < total, value, jnp.zeros_like(value))
        value = pack[frame, pl.ds((1 - core) * (pairs - held), held)]
        theirs_ref[start:start + held] = jnp.where(frame < total, value, jnp.zeros_like(value))
    slot = slots_ref[...]
    tail_ref[CACHE * pairs] = jnp.where(
        (slot < CACHE) & (total - CACHE + slot >= 0), 1.0, 0.0
    ).astype(tail_ref.dtype)
    marks_ref[...] = jnp.where(slot < total, 1.0, 0.0).astype(marks_ref.dtype)


def joined_tail(tail):
    count = lax.axis_size("tchunk")

    def pushed(value, held):
        return lax.dynamic_slice_in_dim(jnp.concatenate([value, jnp.zeros_like(value)], axis=0), held, CACHE, 0)

    step = 1
    while step < count - 1:
        early = lax.ppermute(tail, "tchunk", [(k, k + step) for k in range(count - step)])
        held = jnp.sum(tail[-1, :CACHE, 0].astype(jnp.int32))
        body = pushed(early[:-1].reshape((CACHE, -1) + tail.shape[1:]), held).reshape(tail[:-1].shape)
        marks = jnp.pad(pushed(early[-1, :CACHE], held), ((0, tail.shape[1] - CACHE), (0, 0)))
        tail = tail + jnp.concatenate([body, marks[None]], axis=0)
        step *= 2
    return tail


def silu(half):
    return half + half * jnp.tanh(half)


def lane_mask():
    return lax.broadcasted_iota(jnp.int32, (1, 1, 1, LANES), 3) < LANES // 2


def gains(gain_ref):
    low, high = 0.5 * gain_ref[:, :LANES], 0.5 * gain_ref[:, LANES:]
    return low.reshape(1, 1, 1, LANES), jnp.concatenate([high, high], axis=-1).reshape(1, 1, 1, LANES)


def rolled(values):
    shape = values.shape
    return pltpu.roll(values.reshape(-1, LANES), LANES // 2, 1).reshape(shape)


def first_rows(left, right, gain_ref, channels):
    raw = jnp.concatenate([left.astype(jnp.float32), right.astype(jnp.float32)], axis=2)
    front, back, high = raw[..., :LANES], raw[..., LANES:2 * LANES], raw[..., 2 * LANES:]
    lower = lane_mask()
    squared = high * high

    def inverse(low, mask):
        total = jnp.sum(low * low + jnp.where(mask, squared, 0.0), axis=-1, keepdims=True)
        return lax.rsqrt(total * (1.0 / channels) + epsilon)

    scale_front, scale_back = inverse(front, lower), inverse(back, jnp.logical_not(lower))
    gain_low, gain_high = gains(gain_ref)
    front = silu(front * scale_front * gain_low)
    back = silu(back * scale_back * gain_low)
    high = silu(high * jnp.where(lower, scale_front, scale_back) * gain_high)
    turned = rolled(high)
    one = [front, jnp.where(lower, high, 0.0), jnp.where(lower, 0.0, turned)]
    two = [back, jnp.where(lower, turned, 0.0), jnp.where(lower, 0.0, high)]
    return [[part.astype(jnp.bfloat16) for part in row] for row in (one, two)]


def second_rows(hidden, flag, gain_ref, channels):
    gain = 0.5 * gain_ref[...].reshape(1, 1, 1, channels)
    total = jnp.sum(hidden * hidden, axis=-1, keepdims=True)
    inverse = lax.rsqrt(total * (1.0 / channels) + epsilon) * flag
    values = silu(hidden * inverse * gain)
    rest = jnp.zeros(values.shape[:-1] + (LANES // 2,), jnp.float32)
    high = jnp.concatenate([values[..., LANES:], rest], axis=-1)
    parts = [values[..., :LANES], high, rolled(high)]
    return jnp.stack([part.astype(jnp.bfloat16) for part in parts])


def in_turn(steps, beside=None):
    waiting = None
    for product, then in steps:
        result = product()
        if waiting:
            waiting[1](waiting[0])
        elif beside:
            beside()
        waiting = (result, then)
    waiting[1](waiting[0])


def convolved(operand, weights_ref, bias_ref, frame, frames, rows, then, most=PRODUCT):
    products = -(-frames * rows * operand.shape[3] // most)
    step = -(-frames // products)

    def part(start):
        count = min(step, frames - start)
        return (
            lambda: convolved_part(operand, weights_ref, bias_ref, frame + start, count, rows),
            lambda result: then(start, count, result),
        )

    return [part(start) for start in range(0, frames, step)]


def convolved_part(operand, weights_ref, bias_ref, frame, frames, rows):
    width = operand.shape[3]
    channels = weights_ref.shape[-1]
    taps = [(a, i) for a in range(TAPS) for i in range(TAPS)]
    groups = [taps[start:start + 2] for start in range(0, len(taps), 2)]

    def window(tap, part):
        a, i = tap
        value = operand[part, frame + a:frame + a + frames, i:i + rows]
        return value.reshape(frames * rows * width, LANES)

    def operands(groups):
        pieces = []
        for group in groups:
            pieces += [window(tap, 0) for tap in group]
            high = window(group[0], 1)
            pieces.append(high + window(group[1], 2) if len(group) > 1 else high)
        return jnp.concatenate(pieces, axis=-1)

    def weights(groups, j, depth):
        rights = []
        for group in groups:
            held = [weights_ref[a, i, j] for a, i in group]
            rights += [weight[:LANES] for weight in held] + [weight[LANES:] for weight in held]
        rest = depth - sum(right.shape[0] for right in rights)
        if rest:
            rights.append(jnp.zeros((rest, channels), jnp.bfloat16))
        return jnp.concatenate(rights, axis=0)

    half = len(groups) // 2
    parts = [(part, operands(part)) for part in (groups[:half], groups[half:])]
    products = []
    for j in range(TAPS):
        total = None
        for part, left in parts if j % 2 == 0 else parts[::-1]:
            product = jnp.dot(left, weights(part, j, left.shape[1]), preferred_element_type=jnp.float32)
            total = product if total is None else total + product
        products.append(total.reshape(frames * rows, width, channels))
    column = lax.broadcasted_iota(jnp.int32, (1, width, 1), 1)
    before = jnp.where(column == 0, 0.0, pltpu.roll(products[0], 1, 1))
    after = jnp.where(column == width - 1, 0.0, pltpu.roll(products[2], width - 1, 1))
    result = products[1] + before + after + bias_ref[...].reshape(1, 1, channels)
    return result.reshape(frames, rows, width, channels)


def halves(core, mine, other):
    return jnp.where(core == 0, mine, other), jnp.where(core == 0, other, mine)


def frame_flags(marks, frames):
    values = marks.astype(jnp.float32)
    return [values[k:k + 1, 0:1].reshape(1, 1, 1, 1) for k in frames]


def fill_rows(operand, frame, row, mine, other, gain_ref):
    left, right = halves(lax.axis_index("wa"), mine, other)
    frames, pairs = mine.shape[:2]
    upper, lower = first_rows(left, right, gain_ref, gain_ref.shape[-1])
    for part in range(len(upper)):
        for pair in range(pairs):
            operand[part, frame:frame + frames, pl.ds(row + 2 * pair, 1)] = upper[part][:, pair:pair + 1]
            operand[part, frame:frame + frames, pl.ds(row + 2 * pair + 1, 1)] = lower[part][:, pair:pair + 1]


def border_kernel(tail_ref, mine_ref, other_ref, tail_edge_ref, own_edge_ref):
    frames, held = mine_ref.shape[:2]
    pairs = tail_ref.shape[0] // CACHE
    core = lower_part()
    pair = core * (held - 1)
    for slot in range(CACHE):
        tail_edge_ref[slot] = tail_ref[slot * pairs + core * (pairs - 1)]
        tail_edge_ref[CACHE + slot] = other_ref[slot * held + pair]
    for frame in range(frames):
        own_edge_ref[0, frame] = mine_ref[frame, pair]
        own_edge_ref[1, frame] = other_ref[(CACHE + frame) * held + pair]


def finish(mine_ref, other_ref, live, first, pairs, value, targets):
    _, held, side, _ = mine_ref.shape
    frames, channels = value.shape[0], value.shape[-1]
    start, count = pairs
    near, far = halves(lax.axis_index("wa"), value[:, :, :side], value[:, :, side:])
    for mine, value, target in ((True, near, targets[0]), (False, far, targets[1])):
        for frame in range(frames):
            for k in range(count):
                if mine:
                    raw = mine_ref[first + frame, start + k]
                else:
                    raw = other_ref[(CACHE + first + frame) * held + start + k]
                raw = raw.astype(jnp.float32)
                high = raw[:, 2 * LANES:]
                for row, tail in ((0, high), (1, pltpu.roll(high, LANES // 2, 1))):
                    low = raw[:, row * LANES:(row + 1) * LANES]
                    features = jnp.concatenate([low, tail[:, :channels - LANES]], axis=-1)
                    summed = features + value[frame, 2 * k + row]
                    kept = jnp.where(live[first + frame].reshape(1, 1) > 0.5, summed, 0.0)
                    target(first + frame, 2 * k + row, kept.astype(jnp.bfloat16))


def hide(operand, weights_ref, bias_ref, gain_ref, first, count, rows, flags, store, most=PRODUCT):
    channels = weights_ref.shape[-1]

    def then(begin, part, hidden):
        flag = jnp.concatenate(flags[begin:begin + part], axis=0)
        store(begin, begin + part, second_rows(hidden, flag, gain_ref, channels))

    return convolved(operand, weights_ref, bias_ref, first, count, rows, then, most)


def inside_flags(rows):
    core, place = lower_part(), lax.axis_index("ha")
    inside = jnp.where(core == 0, place > 0, place < lax.axis_size("ha") - 1)
    row = lax.broadcasted_iota(jnp.int32, (1, rows, 1, 1), 1)
    return jnp.where((row == (rows - 1) * core) & jnp.logical_not(inside), 0.0, 1.0)


def other_rows_kernel(tail_ref, late_ref, rest_ref):
    pairs, held = tail_ref.shape[0] // CACHE, rest_ref.shape[0] // CACHE
    first = (1 - lower_part()) * (pairs - held)
    for slot in range(CACHE):
        rest_ref[slot * held:(slot + 1) * held] = tail_ref[pl.ds(slot * pairs + first, held)]


def own_kernel(
    marks_ref, mine_ref, other_ref, gain1_ref, w1_ref, bias1_ref, gain2_ref,
    first_ref, late_ref, raw_ref,
):
    frames, pairs, side, packed = mine_ref.shape
    live = frame_flags(marks_ref[...], range(2, frames))

    def fill(start, end):
        other = other_ref[(CACHE + start) * pairs:(CACHE + end) * pairs].reshape(end - start, pairs, side, packed)
        fill_rows(first_ref, start, 0, mine_ref[start:end], other, gain1_ref)

    def store(begin, end, rows):
        late_ref[:, begin:end] = rows

    steps = hide(first_ref, w1_ref, bias1_ref, gain2_ref, 0, frames - 2, 2 * pairs - 2, live, store, OWN)
    each = -(-(frames - 2) // len(steps))

    position, result = 0, None
    for k, (product, _) in enumerate(steps[:-1]):
        fill(position, each * (k + 1) + 2)
        position = each * (k + 1) + 2
        before, result = result, product()
        if k:
            steps[k - 1][1](before)
    fill(position, frames)
    raw_ref[...] = result


def edge_kernel(
    marks_ref, mine_ref, other_ref, edge_ref, first_ref, done_ref, raw_ref,
    gain1_ref, w1_ref, bias1_ref, gain2_ref, w2_ref, bias2_ref,
    strip_ref, hidden_ref, keep_ref, send_ref, border_ref, operand, strip, late_ref,
):
    core = lower_part()
    frames, pairs = mine_ref.shape[:2]
    rows = 2 * pairs
    late = frames - CACHE
    outward, inward = pl.ds(2 * core, 2), pl.ds(2 * (1 - core), 2)
    live = frame_flags(marks_ref[...], range(frames))
    inside = inside_flags(2)
    done, made = done_ref.shape[1], done_ref.shape[1] + raw_ref.shape[0]

    def activate():
        fill_rows(strip, 0, 2 * core, edge_ref[1][:, None], edge_ref[0][:, None], gain1_ref)
        strip[:, :, inward] = first_ref[:, :, pl.ds((rows - 2) * core, 2)]
        late_ref[:, 0:done] = done_ref[...]
        flag = jnp.concatenate(live[2 + done:2 + made], axis=0)
        late_ref[:, done:made] = second_rows(raw_ref[...], flag, gain2_ref, gain2_ref.shape[-1])

    def store_last(begin, end, values):
        late_ref[:, made + begin:made + end] = values
        if made + end == frames - 2:
            operand[:, :, inward] = late_ref[:, :, pl.ds((rows - 4) * core, 2)]

    def store(begin, end, values):
        operand[:, begin:end, outward] = values

    def put(ref):
        def store(frame, row, value):
            ref[frame - CACHE, row] = value
        return store

    def middle(start, part, result):
        targets = (put(keep_ref), put(send_ref))
        finish(mine_ref, other_ref, live, CACHE + start, (1, pairs - 2), result, targets)

    def border(start, part, result):
        border_ref[start:start + part] = result

    flags = [flag * inside for flag in live[2:]]
    earlier = lax.axis_index("tchunk") > 0

    def steps():
        left = frames - 2 - made
        return (
            hide(first_ref, w1_ref, bias1_ref, gain2_ref, made, left, rows - 2, live[2 + made:], store_last, OWN)
            + hide(strip, w1_ref, bias1_ref, gain2_ref, 0, frames - 2, 2, flags, store)
            + convolved(late_ref, w2_ref, bias2_ref, 0, late, rows - 4, middle)
        )

    @pl.when(earlier)
    def _():
        in_turn(steps() + convolved(operand, w2_ref, bias2_ref, 0, late, 2, border), activate)

    @pl.when(jnp.logical_not(earlier))
    def _():
        in_turn(steps(), activate)

    strip_ref[...] = strip[:, 0:2, outward]
    hidden_ref[:, :, pl.ds(2 * (1 - core), rows - 2)] = late_ref[:, 0:2]
    hidden_ref[:, :, pl.ds((rows - 2) * core, 2)] = operand[:, 0:2, outward]


def tail_edge_kernel(edge_ref, strip_ref, gain_ref, rows_ref):
    rows_ref[:, CACHE:] = strip_ref[...]

    @pl.when(lax.axis_index("tchunk") > 0)
    def _():
        fill_rows(rows_ref, 0, 0, edge_ref[CACHE:2 * CACHE][:, None], edge_ref[0:CACHE][:, None], gain_ref)

    @pl.when(lax.axis_index("tchunk") == 0)
    def _():
        rows_ref[:, 0:CACHE] = jnp.zeros((rows_ref.shape[0], CACHE) + rows_ref.shape[2:], rows_ref.dtype)


def early_kernel(
    marks_ref, tail_mine_ref, tail_other_ref, mine_ref, other_ref, edge_ref, first_ref, hidden_ref,
    late_keep_ref, late_send_ref, late_border_ref, late_operand_ref, gain1_ref, w1_ref, bias1_ref, gain2_ref, w2_ref, bias2_ref,
    keep_ref, send_ref, plane, operand,
):
    core = lower_part()
    held = mine_ref.shape[1]
    rows = 2 * held
    pairs = tail_mine_ref.shape[0] // CACHE
    live = frame_flags(marks_ref[...], range(mine_ref.shape[0]))
    inside = inside_flags(rows)
    earlier = lax.axis_index("tchunk") > 0
    middle, border = 2 * (1 - core), rows * core

    def unpacked(ref, stride, first):
        return jnp.stack([ref[pl.ds(slot * stride + first, held)] for slot in range(CACHE)])

    plane[:, CACHE:, pl.ds(middle, rows)] = first_ref[:, 0:2]
    plane[:, :, pl.ds(border, 2)] = edge_ref[...]
    operand[:, CACHE:] = hidden_ref[...]

    def put(ref, offset=0):
        def store(frame, row, value):
            ref[frame, offset + row] = value
        return store

    def late_border(start, part, result):
        offset = (rows - 4) * core
        targets = (put(keep_ref, offset), put(send_ref, offset))
        finish(mine_ref, other_ref, live, CACHE + start, ((held - 1) * core, 1), result, targets)

    def late_middle():
        for source, target in ((late_keep_ref, keep_ref), (late_send_ref, send_ref)):
            target[CACHE:, pl.ds(2 * (1 - core), rows - 4)] = source[...]

    def hidden_steps(first, flags):
        def store(begin, end, values):
            operand[:, first + begin:first + end] = values

        flags = [flag * inside for flag in flags]
        return hide(plane, w1_ref, bias1_ref, gain2_ref, first, CACHE - first, rows, flags, store)

    def then(start, part, result):
        finish(mine_ref, other_ref, live, start, (core, held - 1), result, (put(keep_ref), put(send_ref)))

    def result_steps():
        return convolved(operand, w2_ref, bias2_ref, 0, CACHE, rows - 2, then)

    @pl.when(earlier)
    def _():
        fill_rows(
            plane, 0, middle, unpacked(tail_mine_ref, pairs, core * (pairs - held)),
            unpacked(tail_other_ref, held, 0), gain1_ref,
        )
        flags = frame_flags(tail_mine_ref[CACHE * pairs], range(CACHE - 2, CACHE)) + live[0:2]

        def beside():
            late_middle()
            late_border(0, late_border_ref.shape[0], late_border_ref[...])

        hidden, results = hidden_steps(0, flags), result_steps()
        if len(hidden) == 2 and len(results) == 2:
            in_turn(hidden[::-1] + results[::-1], beside)
        else:
            in_turn(hidden, beside)
            in_turn(results)

    @pl.when(jnp.logical_not(earlier))
    def _():
        plane[:, 0:CACHE, pl.ds(middle, rows)] = jnp.zeros(
            plane.shape[:1] + (CACHE, rows) + plane.shape[3:], plane.dtype
        )
        operand[:, 0:2] = jnp.zeros(operand.shape[:1] + (2,) + operand.shape[2:], operand.dtype)
        border = convolved(late_operand_ref, w2_ref, bias2_ref, 0, late_border_ref.shape[0], 2, late_border)
        in_turn(hidden_steps(2, live[0:2]) + border + result_steps()[::-1], late_middle)


def keep_kernel(keep_ref, result_ref, arrived):
    half = keep_ref.shape[1]
    copy = pltpu.make_async_copy(keep_ref, result_ref.at[:, pl.ds(half * lower_part(), half)], arrived)
    copy.start()
    copy.wait()


def got_kernel(got_ref, kept_ref, result_ref, arrived):
    half = got_ref.shape[1]
    copy = pltpu.make_async_copy(got_ref, result_ref.at[:, pl.ds(half * (1 - lower_part()), half)], arrived)
    copy.start()
    copy.wait()


def shards(features, frame_counts, gain_first, conv_first, bias_first, gain_second, conv_second, bias_second):
    frames, rows, side, channels = features.shape
    pairs, half = rows // 2, rows // 2
    held = half // 2 + 1
    tall, cores, blocks = lax.axis_size("ha"), lax.axis_size("wa"), lax.axis_size("tchunk")
    packed, width, tiles = 3 * LANES, 2 * side, CACHE * held
    bf16 = jnp.bfloat16
    vmem = pl.BlockSpec(memory_space=pltpu.VMEM)
    limit = pltpu.CompilerParams(vmem_limit_bytes=20 * 2**20)
    work = 2 * TAPS**3 * channels * channels * width

    def shape(*extent):
        return jax.ShapeDtypeStruct(extent, bf16)

    def cost(flops, fetched):
        return pl.CostEstimate(flops=flops, bytes_accessed=fetched, transcendentals=0)

    slots = pl.pallas_call(
        slots_kernel,
        out_shape=jax.ShapeDtypeStruct((side, packed), jnp.int32),
        out_specs=vmem,
        compiler_params=limit,
        cost_estimate=cost(2**34, 2**20),
    )()
    slots, frame_counts = lax.optimization_barrier((slots, frame_counts))
    tail, mine, theirs, marks = pl.pallas_call(
        prepare_kernel,
        out_shape=(
            shape(CACHE * pairs + 1, side, packed), shape(frames, held, side, packed),
            shape((CACHE + frames) * held, side, packed), shape(side, packed),
        ),
        in_specs=[pl.BlockSpec(memory_space=pltpu.SMEM), vmem, vmem],
        out_specs=(vmem,) * 4,
        scratch_shapes=[pltpu.VMEM((frames, pairs, side, packed), bf16)],
        compiler_params=limit,
    )(frame_counts, slots, features)

    if blocks > 2:
        tail = joined_tail(tail)
        rest = lax.dynamic_slice_in_dim(
            tail[:-1].reshape(CACHE, pairs, side, packed), (1 - lower_part()) * (pairs - held), held, 1
        )
        theirs = jnp.concatenate([rest.reshape(tiles, side, packed), theirs[tiles:]], axis=0)
    straight, diagonal, across = [], [], []

    def index(block, h, core):
        return (block * tall + h) * cores + core

    for k in range(blocks - 1):
        for h in range(tall):
            for core in range(cores):
                straight.append((index(k, h, core), index(k + 1, h, core)))
    for h in range(tall - 1):
        for k in range(blocks):
            lower, upper = index(k, h, 0), index(k, h + 1, 1)
            across += [(lower, upper), (upper, lower)]
            if k + 1 < blocks:
                lower_next, upper_next = index(k + 1, h, 0), index(k + 1, h + 1, 1)
                diagonal += [(lower, upper_next), (upper, lower_next)]
    axes = ("tchunk", "ha", "wa")
    swap = [(0, 1), (1, 0)]
    tail_mine = lax.ppermute(tail, axes, straight)
    other = lax.ppermute(theirs, "wa", swap)
    tail_edge, own_edge = pl.pallas_call(
        border_kernel,
        out_shape=(shape(2 * CACHE, side, packed), shape(2, frames, side, packed)),
        in_specs=[vmem] * 3,
        out_specs=(vmem, vmem),
        compiler_params=limit,
        cost_estimate=cost(2**34, 2**20),
    )(tail, mine, other)
    own_edge = lax.ppermute(own_edge, axes, across)
    tail_edge = lax.ppermute(tail_edge, axes, diagonal)

    weights = (
        gain_first.reshape(1, channels), conv_first, bias_first.reshape(1, channels),
        gain_second.reshape(1, channels), conv_second, bias_second.reshape(1, channels),
    )
    products = -(-(frames - 2) * half * width // OWN)
    each = -(-(frames - 2) // products)
    done = each * (products - 2)
    first, late, raw = pl.pallas_call(
        own_kernel,
        out_shape=(
            shape(3, frames, half + 2, width, LANES), shape(3, done, half, width, LANES),
            jax.ShapeDtypeStruct((each, half, width, channels), jnp.float32),
        ),
        in_specs=[vmem] * 7,
        out_specs=(vmem,) * 3,
        compiler_params=limit,
        cost_estimate=cost(work * (frames - 2) * half, 4 * 2**20),
    )(marks, mine, other, *weights[:4])
    rest = pl.pallas_call(
        other_rows_kernel,
        out_shape=shape(tiles, side, packed),
        in_specs=[vmem, pl.BlockSpec(memory_space=pl.ANY)],
        out_specs=vmem,
        compiler_params=limit,
        cost_estimate=cost(1, 1),
    )(tail_mine, late)
    tail_other = lax.ppermute(rest, "wa", swap)
    strip, hidden, keep, send, border, late = pl.pallas_call(
        edge_kernel,
        out_shape=(
            shape(3, 2, 2, width, LANES), shape(3, 2, half + 2, width, LANES),
            shape(frames - CACHE, half - 2, side, channels), shape(frames - CACHE, half - 2, side, channels),
            jax.ShapeDtypeStruct((frames - CACHE, 2, width, channels), jnp.float32),
            shape(3, frames - 2, 4, width, LANES),
        ),
        in_specs=[vmem] * 13,
        out_specs=(vmem,) * 6,
        scratch_shapes=[
            pltpu.VMEM((3, frames, 4, width, LANES), bf16),
            pltpu.VMEM((3, frames - 2, half, width, LANES), bf16),
        ],
        compiler_params=limit,
        cost_estimate=cost(2**20, 2**20),
    )(marks, mine, other, own_edge, first, late, raw, *weights)
    tail_edge = pl.pallas_call(
        tail_edge_kernel,
        out_shape=shape(3, CACHE + 2, 2, width, LANES),
        in_specs=[vmem] * 3,
        out_specs=vmem,
        compiler_params=limit,
        cost_estimate=cost(2**30, 2**18),
    )(tail_edge, strip, weights[0])
    keep, send = pl.pallas_call(
        early_kernel,
        out_shape=(shape(frames, half, side, channels), shape(frames, half, side, channels)),
        in_specs=[vmem] * 18,
        out_specs=(vmem, vmem),
        scratch_shapes=[
            pltpu.VMEM((3, CACHE + 2, half + 4, width, LANES), bf16),
            pltpu.VMEM((3, CACHE + 2, half + 2, width, LANES), bf16),
        ],
        compiler_params=limit,
        cost_estimate=cost(work * CACHE * (2 * half + 2), 8 * 2**20),
    )(marks, tail_mine, tail_other, mine, other, tail_edge, first, hidden, keep, send, border, late, *weights)
    got = lax.ppermute(send, "wa", swap)
    hbm = pl.BlockSpec(memory_space=pltpu.HBM)
    kept = pl.pallas_call(
        keep_kernel,
        out_shape=shape(*features.shape),
        in_specs=[vmem],
        out_specs=hbm,
        scratch_shapes=[pltpu.SemaphoreType.DMA],
        compiler_params=limit,
        cost_estimate=cost(2**28, 2**20),
    )(keep)
    return pl.pallas_call(
        got_kernel,
        out_shape=shape(*features.shape),
        in_specs=[vmem, hbm],
        out_specs=hbm,
        input_output_aliases={1: 0},
        scratch_shapes=[pltpu.SemaphoreType.DMA],
        compiler_params=limit,
    )(got, kept)


def solution(mesh):
    return jax.shard_map(
        shards,
        mesh=mesh,
        in_specs=(
            P(("grp", "tchunk"), "ha", "wa", None),
            P(("grp", "tchunk")),
            P(), P(), P(), P(), P(), P(),
        ),
        out_specs=P(("grp", "tchunk"), "ha", "wa", None),
        check_vma=False,
    )
```

```python
import jax
import jax.numpy as jnp
from jax import lax
from jax.experimental import pallas as pl
from jax.experimental.pallas import tpu as pltpu
from jax.sharding import PartitionSpec as P

epsilon = 1e-06
CACHE = 4
TAPS = 3
LANES = 128
PRODUCT = 192
OWN = 128


def slots_kernel(slots_ref):
    slots_ref[...] = lax.broadcasted_iota(jnp.int32, slots_ref.shape, 0)


def lower_part():
    return 1 - lax.axis_index("wa")


def prepare_kernel(total_ref, slots_ref, raw, tail_ref, mine_ref, theirs_ref, marks_ref, pack):
    frames, rows = raw.shape[:2]
    pairs, held = rows // 2, mine_ref.shape[1]
    core = lower_part()
    total = total_ref[0]
    for frame in range(frames):
        for pair in range(pairs):
            first, second = raw[frame, 2 * pair], raw[frame, 2 * pair + 1]
            packed = jnp.concatenate(
                [first[:, :LANES], second[:, :LANES], first[:, LANES:], second[:, LANES:]], axis=-1
            )
            pack[frame, pair] = packed
    for slot in range(CACHE):
        frame = total - CACHE + slot
        value = pack[jnp.maximum(frame, 0)]
        tail_ref[slot * pairs:(slot + 1) * pairs] = jnp.where(frame >= 0, value, jnp.zeros_like(value))
        value = pack[jnp.maximum(frame, 0), pl.ds((1 - core) * (pairs - held), held)]
        theirs_ref[slot * held:(slot + 1) * held] = jnp.where(frame >= 0, value, jnp.zeros_like(value))
    for frame in range(frames):
        start = (CACHE + frame) * held
        value = pack[frame, pl.ds(core * (pairs - held), held)]
        mine_ref[frame] = jnp.where(frame < total, value, jnp.zeros_like(value))
        value = pack[frame, pl.ds((1 - core) * (pairs - held), held)]
        theirs_ref[start:start + held] = jnp.where(frame < total, value, jnp.zeros_like(value))
    slot = slots_ref[...]
    tail_ref[CACHE * pairs] = jnp.where(
        (slot < CACHE) & (total - CACHE + slot >= 0), 1.0, 0.0
    ).astype(tail_ref.dtype)
    marks_ref[...] = jnp.where(slot < total, 1.0, 0.0).astype(marks_ref.dtype)


def joined_tail(tail):
    count = lax.axis_size("tchunk")

    def pushed(value, held):
        return lax.dynamic_slice_in_dim(jnp.concatenate([value, jnp.zeros_like(value)], axis=0), held, CACHE, 0)

    step = 1
    while step < count - 1:
        early = lax.ppermute(tail, "tchunk", [(k, k + step) for k in range(count - step)])
        held = jnp.sum(tail[-1, :CACHE, 0].astype(jnp.int32))
        body = pushed(early[:-1].reshape((CACHE, -1) + tail.shape[1:]), held).reshape(tail[:-1].shape)
        marks = jnp.pad(pushed(early[-1, :CACHE], held), ((0, tail.shape[1] - CACHE), (0, 0)))
        tail = tail + jnp.concatenate([body, marks[None]], axis=0)
        step *= 2
    return tail


def silu(half):
    return half + half * jnp.tanh(half)


def lane_mask():
    return lax.broadcasted_iota(jnp.int32, (1, 1, 1, LANES), 3) < LANES // 2


def gains(gain_ref):
    low, high = 0.5 * gain_ref[:, :LANES], 0.5 * gain_ref[:, LANES:]
    return low.reshape(1, 1, 1, LANES), jnp.concatenate([high, high], axis=-1).reshape(1, 1, 1, LANES)


def rolled(values):
    shape = values.shape
    return pltpu.roll(values.reshape(-1, LANES), LANES // 2, 1).reshape(shape)


def first_rows(left, right, gain_ref, channels):
    raw = jnp.concatenate([left.astype(jnp.float32), right.astype(jnp.float32)], axis=2)
    front, back, high = raw[..., :LANES], raw[..., LANES:2 * LANES], raw[..., 2 * LANES:]
    lower = lane_mask()
    squared = high * high

    def inverse(low, mask):
        total = jnp.sum(low * low + jnp.where(mask, squared, 0.0), axis=-1, keepdims=True)
        return lax.rsqrt(total * (1.0 / channels) + epsilon)

    scale_front, scale_back = inverse(front, lower), inverse(back, jnp.logical_not(lower))
    gain_low, gain_high = gains(gain_ref)
    front = silu(front * scale_front * gain_low)
    back = silu(back * scale_back * gain_low)
    high = silu(high * jnp.where(lower, scale_front, scale_back) * gain_high)
    turned = rolled(high)
    one = [front, jnp.where(lower, high, 0.0), jnp.where(lower, 0.0, turned)]
    two = [back, jnp.where(lower, turned, 0.0), jnp.where(lower, 0.0, high)]
    return [[part.astype(jnp.bfloat16) for part in row] for row in (one, two)]


def second_rows(hidden, flag, gain_ref, channels):
    gain = 0.5 * gain_ref[...].reshape(1, 1, 1, channels)
    total = jnp.sum(hidden * hidden, axis=-1, keepdims=True)
    inverse = lax.rsqrt(total * (1.0 / channels) + epsilon) * flag
    values = silu(hidden * inverse * gain)
    rest = jnp.zeros(values.shape[:-1] + (LANES // 2,), jnp.float32)
    high = jnp.concatenate([values[..., LANES:], rest], axis=-1)
    parts = [values[..., :LANES], high, rolled(high)]
    return jnp.stack([part.astype(jnp.bfloat16) for part in parts])


def in_turn(steps, beside=None):
    waiting = None
    for product, then in steps:
        result = product()
        if waiting:
            waiting[1](waiting[0])
        elif beside:
            beside()
        waiting = (result, then)
    waiting[1](waiting[0])


def convolved(operand, weights_ref, bias_ref, frame, frames, rows, then, most=PRODUCT):
    products = -(-frames * rows * operand.shape[3] // most)
    step = -(-frames // products)

    def part(start):
        count = min(step, frames - start)
        return (
            lambda: convolved_part(operand, weights_ref, bias_ref, frame + start, count, rows),
            lambda result: then(start, count, result),
        )

    return [part(start) for start in range(0, frames, step)]


def convolved_part(operand, weights_ref, bias_ref, frame, frames, rows):
    width = operand.shape[3]
    channels = weights_ref.shape[-1]
    taps = [(a, i) for a in range(TAPS) for i in range(TAPS)]
    groups = [taps[start:start + 2] for start in range(0, len(taps), 2)]

    def window(tap, part):
        a, i = tap
        value = operand[part, frame + a:frame + a + frames, i:i + rows]
        return value.reshape(frames * rows * width, LANES)

    def operands(groups):
        pieces = []
        for group in groups:
            pieces += [window(tap, 0) for tap in group]
            high = window(group[0], 1)
            pieces.append(high + window(group[1], 2) if len(group) > 1 else high)
        return jnp.concatenate(pieces, axis=-1)

    def weights(groups, j, depth):
        rights = []
        for group in groups:
            held = [weights_ref[a, i, j] for a, i in group]
            rights += [weight[:LANES] for weight in held] + [weight[LANES:] for weight in held]
        rest = depth - sum(right.shape[0] for right in rights)
        if rest:
            rights.append(jnp.zeros((rest, channels), jnp.bfloat16))
        return jnp.concatenate(rights, axis=0)

    half = len(groups) // 2
    parts = [(part, operands(part)) for part in (groups[:half], groups[half:])]
    products = []
    for j in range(TAPS):
        total = None
        for part, left in parts if j % 2 == 0 else parts[::-1]:
            product = jnp.dot(left, weights(part, j, left.shape[1]), preferred_element_type=jnp.float32)
            total = product if total is None else total + product
        products.append(total.reshape(frames * rows, width, channels))
    column = lax.broadcasted_iota(jnp.int32, (1, width, 1), 1)
    before = jnp.where(column == 0, 0.0, pltpu.roll(products[0], 1, 1))
    after = jnp.where(column == width - 1, 0.0, pltpu.roll(products[2], width - 1, 1))
    result = products[1] + before + after + bias_ref[...].reshape(1, 1, channels)
    return result.reshape(frames, rows, width, channels)


def halves(core, mine, other):
    return jnp.where(core == 0, mine, other), jnp.where(core == 0, other, mine)


def frame_flags(marks, frames):
    values = marks.astype(jnp.float32)
    return [values[k:k + 1, 0:1].reshape(1, 1, 1, 1) for k in frames]


def fill_rows(operand, frame, row, mine, other, gain_ref):
    left, right = halves(lax.axis_index("wa"), mine, other)
    frames, pairs = mine.shape[:2]
    upper, lower = first_rows(left, right, gain_ref, gain_ref.shape[-1])
    for part in range(len(upper)):
        for pair in range(pairs):
            operand[part, frame:frame + frames, pl.ds(row + 2 * pair, 1)] = upper[part][:, pair:pair + 1]
            operand[part, frame:frame + frames, pl.ds(row + 2 * pair + 1, 1)] = lower[part][:, pair:pair + 1]


def border_kernel(tail_ref, mine_ref, other_ref, tail_edge_ref, own_edge_ref):
    frames, held = mine_ref.shape[:2]
    pairs = tail_ref.shape[0] // CACHE
    core = lower_part()
    pair = core * (held - 1)
    for slot in range(CACHE):
        tail_edge_ref[slot] = tail_ref[slot * pairs + core * (pairs - 1)]
        tail_edge_ref[CACHE + slot] = other_ref[slot * held + pair]
    for frame in range(frames):
        own_edge_ref[0, frame] = mine_ref[frame, pair]
        own_edge_ref[1, frame] = other_ref[(CACHE + frame) * held + pair]


def finish(mine_ref, other_ref, live, first, pairs, value, targets):
    _, held, side, _ = mine_ref.shape
    frames, channels = value.shape[0], value.shape[-1]
    start, count = pairs
    near, far = halves(lax.axis_index("wa"), value[:, :, :side], value[:, :, side:])
    for mine, value, target in ((True, near, targets[0]), (False, far, targets[1])):
        for frame in range(frames):
            for k in range(count):
                if mine:
                    raw = mine_ref[first + frame, start + k]
                else:
                    raw = other_ref[(CACHE + first + frame) * held + start + k]
                raw = raw.astype(jnp.float32)
                high = raw[:, 2 * LANES:]
                for row, tail in ((0, high), (1, pltpu.roll(high, LANES // 2, 1))):
                    low = raw[:, row * LANES:(row + 1) * LANES]
                    features = jnp.concatenate([low, tail[:, :channels - LANES]], axis=-1)
                    summed = features + value[frame, 2 * k + row]
                    kept = jnp.where(live[first + frame].reshape(1, 1) > 0.5, summed, 0.0)
                    target(first + frame, 2 * k + row, kept.astype(jnp.bfloat16))


def hide(operand, weights_ref, bias_ref, gain_ref, first, count, rows, flags, store, most=PRODUCT):
    channels = weights_ref.shape[-1]

    def then(begin, part, hidden):
        flag = jnp.concatenate(flags[begin:begin + part], axis=0)
        store(begin, begin + part, second_rows(hidden, flag, gain_ref, channels))

    return convolved(operand, weights_ref, bias_ref, first, count, rows, then, most)


def inside_flags(rows):
    core, place = lower_part(), lax.axis_index("ha")
    inside = jnp.where(core == 0, place > 0, place < lax.axis_size("ha") - 1)
    row = lax.broadcasted_iota(jnp.int32, (1, rows, 1, 1), 1)
    return jnp.where((row == (rows - 1) * core) & jnp.logical_not(inside), 0.0, 1.0)


def own_kernel(
    marks_ref, tail_ref, mine_ref, other_ref, gain1_ref, w1_ref, bias1_ref, gain2_ref,
    first_ref, late_ref, raw_ref, rest_ref,
):
    frames, pairs, side, packed = mine_ref.shape
    whole = tail_ref.shape[0] // CACHE
    place = (1 - lower_part()) * (whole - pairs)
    for slot in range(CACHE):
        rest_ref[slot * pairs:(slot + 1) * pairs] = tail_ref[pl.ds(slot * whole + place, pairs)]
    live = frame_flags(marks_ref[...], range(2, frames))

    def fill(start, end):
        other = other_ref[(CACHE + start) * pairs:(CACHE + end) * pairs].reshape(end - start, pairs, side, packed)
        fill_rows(first_ref, start, 0, mine_ref[start:end], other, gain1_ref)

    def store(begin, end, rows):
        late_ref[:, begin:end] = rows

    steps = hide(first_ref, w1_ref, bias1_ref, gain2_ref, 0, frames - 2, 2 * pairs - 2, live, store, OWN)
    each = -(-(frames - 2) // len(steps))

    position, result = 0, None
    for k, (product, _) in enumerate(steps[:-1]):
        fill(position, each * (k + 1) + 2)
        position = each * (k + 1) + 2
        before, result = result, product()
        if k:
            steps[k - 1][1](before)
    fill(position, frames)
    raw_ref[...] = result


def edge_kernel(
    marks_ref, mine_ref, other_ref, edge_ref, first_ref, done_ref, raw_ref,
    gain1_ref, w1_ref, bias1_ref, gain2_ref, w2_ref, bias2_ref,
    strip_ref, hidden_ref, keep_ref, send_ref, border_ref, operand, strip, late_ref,
):
    core = lower_part()
    frames, pairs = mine_ref.shape[:2]
    rows = 2 * pairs
    late = frames - CACHE
    outward, inward = pl.ds(2 * core, 2), pl.ds(2 * (1 - core), 2)
    live = frame_flags(marks_ref[...], range(frames))
    inside = inside_flags(2)
    done, made = done_ref.shape[1], done_ref.shape[1] + raw_ref.shape[0]

    def activate():
        fill_rows(strip, 0, 2 * core, edge_ref[1][:, None], edge_ref[0][:, None], gain1_ref)
        strip[:, :, inward] = first_ref[:, :, pl.ds((rows - 2) * core, 2)]
        late_ref[:, 0:done] = done_ref[...]
        flag = jnp.concatenate(live[2 + done:2 + made], axis=0)
        late_ref[:, done:made] = second_rows(raw_ref[...], flag, gain2_ref, gain2_ref.shape[-1])

    def store_last(begin, end, values):
        late_ref[:, made + begin:made + end] = values
        if made + end == frames - 2:
            operand[:, :, inward] = late_ref[:, :, pl.ds((rows - 4) * core, 2)]

    def store(begin, end, values):
        operand[:, begin:end, outward] = values

    def put(ref):
        def store(frame, row, value):
            ref[frame - CACHE, row] = value
        return store

    def middle(start, part, result):
        targets = (put(keep_ref), put(send_ref))
        finish(mine_ref, other_ref, live, CACHE + start, (1, pairs - 2), result, targets)

    def border(start, part, result):
        border_ref[start:start + part] = result

    flags = [flag * inside for flag in live[2:]]
    earlier = lax.axis_index("tchunk") > 0

    def steps():
        left = frames - 2 - made
        return (
            hide(first_ref, w1_ref, bias1_ref, gain2_ref, made, left, rows - 2, live[2 + made:], store_last, OWN)
            + hide(strip, w1_ref, bias1_ref, gain2_ref, 0, frames - 2, 2, flags, store)
            + convolved(late_ref, w2_ref, bias2_ref, 0, late, rows - 4, middle)
        )

    @pl.when(earlier)
    def _():
        in_turn(steps() + convolved(operand, w2_ref, bias2_ref, 0, late, 2, border), activate)

    @pl.when(jnp.logical_not(earlier))
    def _():
        in_turn(steps(), activate)

    strip_ref[...] = strip[:, 0:2, outward]
    hidden_ref[:, :, pl.ds(2 * (1 - core), rows - 2)] = late_ref[:, 0:2]
    hidden_ref[:, :, pl.ds((rows - 2) * core, 2)] = operand[:, 0:2, outward]


def tail_edge_kernel(edge_ref, strip_ref, gain_ref, rows_ref):
    rows_ref[:, CACHE:] = strip_ref[...]

    @pl.when(lax.axis_index("tchunk") > 0)
    def _():
        fill_rows(rows_ref, 0, 0, edge_ref[CACHE:2 * CACHE][:, None], edge_ref[0:CACHE][:, None], gain_ref)

    @pl.when(lax.axis_index("tchunk") == 0)
    def _():
        rows_ref[:, 0:CACHE] = jnp.zeros((rows_ref.shape[0], CACHE) + rows_ref.shape[2:], rows_ref.dtype)


def early_kernel(
    marks_ref, tail_mine_ref, tail_other_ref, mine_ref, other_ref, edge_ref, first_ref, hidden_ref,
    late_keep_ref, late_send_ref, late_border_ref, late_operand_ref, gain1_ref, w1_ref, bias1_ref, gain2_ref, w2_ref, bias2_ref,
    keep_ref, send_ref, plane, operand,
):
    core = lower_part()
    held = mine_ref.shape[1]
    rows = 2 * held
    pairs = tail_mine_ref.shape[0] // CACHE
    live = frame_flags(marks_ref[...], range(mine_ref.shape[0]))
    inside = inside_flags(rows)
    earlier = lax.axis_index("tchunk") > 0
    middle, border = 2 * (1 - core), rows * core

    def unpacked(ref, stride, first):
        return jnp.stack([ref[pl.ds(slot * stride + first, held)] for slot in range(CACHE)])

    plane[:, CACHE:, pl.ds(middle, rows)] = first_ref[:, 0:2]
    plane[:, :, pl.ds(border, 2)] = edge_ref[...]
    operand[:, CACHE:] = hidden_ref[...]

    def put(ref, offset=0):
        def store(frame, row, value):
            ref[frame, offset + row] = value
        return store

    def late_border(start, part, result):
        offset = (rows - 4) * core
        targets = (put(keep_ref, offset), put(send_ref, offset))
        finish(mine_ref, other_ref, live, CACHE + start, ((held - 1) * core, 1), result, targets)

    def late_middle():
        for source, target in ((late_keep_ref, keep_ref), (late_send_ref, send_ref)):
            target[CACHE:, pl.ds(2 * (1 - core), rows - 4)] = source[...]

    def hidden_steps(first, flags):
        def store(begin, end, values):
            operand[:, first + begin:first + end] = values

        flags = [flag * inside for flag in flags]
        return hide(plane, w1_ref, bias1_ref, gain2_ref, first, CACHE - first, rows, flags, store)

    def then(start, part, result):
        finish(mine_ref, other_ref, live, start, (core, held - 1), result, (put(keep_ref), put(send_ref)))

    def result_steps():
        return convolved(operand, w2_ref, bias2_ref, 0, CACHE, rows - 2, then)

    @pl.when(earlier)
    def _():
        fill_rows(
            plane, 0, middle, unpacked(tail_mine_ref, pairs, core * (pairs - held)),
            unpacked(tail_other_ref, held, 0), gain1_ref,
        )
        flags = frame_flags(tail_mine_ref[CACHE * pairs], range(CACHE - 2, CACHE)) + live[0:2]

        def beside():
            late_middle()
            late_border(0, late_border_ref.shape[0], late_border_ref[...])

        hidden, results = hidden_steps(0, flags), result_steps()
        if len(hidden) == 2 and len(results) == 2:
            in_turn(hidden[::-1] + results[::-1], beside)
        else:
            in_turn(hidden, beside)
            in_turn(results)

    @pl.when(jnp.logical_not(earlier))
    def _():
        plane[:, 2:CACHE, pl.ds(middle, rows)] = jnp.zeros(
            plane.shape[:1] + (CACHE - 2, rows) + plane.shape[3:], plane.dtype
        )
        operand[:, 0:2] = jnp.zeros(operand.shape[:1] + (2,) + operand.shape[2:], operand.dtype)
        border = convolved(late_operand_ref, w2_ref, bias2_ref, 0, late_border_ref.shape[0], 2, late_border)
        in_turn(hidden_steps(2, live[0:2]) + border + result_steps()[::-1], late_middle)


def keep_kernel(keep_ref, result_ref, arrived):
    half = keep_ref.shape[1]
    copy = pltpu.make_async_copy(keep_ref, result_ref.at[:, pl.ds(half * lower_part(), half)], arrived)
    copy.start()
    copy.wait()


def got_kernel(got_ref, kept_ref, result_ref, arrived):
    half = got_ref.shape[1]
    copy = pltpu.make_async_copy(got_ref, result_ref.at[:, pl.ds(half * (1 - lower_part()), half)], arrived)
    copy.start()
    copy.wait()


def shards(features, frame_counts, gain_first, conv_first, bias_first, gain_second, conv_second, bias_second):
    frames, rows, side, channels = features.shape
    pairs, half = rows // 2, rows // 2
    held = half // 2 + 1
    tall, cores, blocks = lax.axis_size("ha"), lax.axis_size("wa"), lax.axis_size("tchunk")
    packed, width, tiles = 3 * LANES, 2 * side, CACHE * held
    bf16 = jnp.bfloat16
    vmem = pl.BlockSpec(memory_space=pltpu.VMEM)
    limit = pltpu.CompilerParams(vmem_limit_bytes=20 * 2**20)
    work = 2 * TAPS**3 * channels * channels * width

    def shape(*extent):
        return jax.ShapeDtypeStruct(extent, bf16)

    def cost(flops, fetched):
        return pl.CostEstimate(flops=flops, bytes_accessed=fetched, transcendentals=0)

    slots = pl.pallas_call(
        slots_kernel,
        out_shape=jax.ShapeDtypeStruct((side, packed), jnp.int32),
        out_specs=vmem,
        compiler_params=limit,
        cost_estimate=cost(2**34, 2**20),
    )()
    slots, frame_counts = lax.optimization_barrier((slots, frame_counts))
    tail, mine, theirs, marks = pl.pallas_call(
        prepare_kernel,
        out_shape=(
            shape(CACHE * pairs + 1, side, packed), shape(frames, held, side, packed),
            shape((CACHE + frames) * held, side, packed), shape(side, packed),
        ),
        in_specs=[pl.BlockSpec(memory_space=pltpu.SMEM), vmem, vmem],
        out_specs=(vmem,) * 4,
        scratch_shapes=[pltpu.VMEM((frames, pairs, side, packed), bf16)],
        compiler_params=limit,
    )(frame_counts, slots, features)

    if blocks > 2:
        tail = joined_tail(tail)
        rest = lax.dynamic_slice_in_dim(
            tail[:-1].reshape(CACHE, pairs, side, packed), (1 - lower_part()) * (pairs - held), held, 1
        )
        theirs = jnp.concatenate([rest.reshape(tiles, side, packed), theirs[tiles:]], axis=0)
    straight, diagonal, across = [], [], []

    def index(block, h, core):
        return (block * tall + h) * cores + core

    for k in range(blocks - 1):
        for h in range(tall):
            for core in range(cores):
                straight.append((index(k, h, core), index(k + 1, h, core)))
    for h in range(tall - 1):
        for k in range(blocks):
            lower, upper = index(k, h, 0), index(k, h + 1, 1)
            across += [(lower, upper), (upper, lower)]
            if k + 1 < blocks:
                lower_next, upper_next = index(k + 1, h, 0), index(k + 1, h + 1, 1)
                diagonal += [(lower, upper_next), (upper, lower_next)]
    axes = ("tchunk", "ha", "wa")
    swap = [(0, 1), (1, 0)]
    tail_mine = lax.ppermute(tail, axes, straight)
    other = lax.ppermute(theirs, "wa", swap)
    tail_edge, own_edge = pl.pallas_call(
        border_kernel,
        out_shape=(shape(2 * CACHE, side, packed), shape(2, frames, side, packed)),
        in_specs=[vmem] * 3,
        out_specs=(vmem, vmem),
        compiler_params=limit,
        cost_estimate=cost(2**34, 2**20),
    )(tail, mine, other)
    own_edge = lax.ppermute(own_edge, axes, across)
    tail_edge = lax.ppermute(tail_edge, axes, diagonal)

    weights = (
        gain_first.reshape(1, channels), conv_first, bias_first.reshape(1, channels),
        gain_second.reshape(1, channels), conv_second, bias_second.reshape(1, channels),
    )
    products = -(-(frames - 2) * half * width // OWN)
    each = -(-(frames - 2) // products)
    done = each * (products - 2)
    first, late, raw, rest = pl.pallas_call(
        own_kernel,
        out_shape=(
            shape(3, frames, half + 2, width, LANES), shape(3, done, half, width, LANES),
            jax.ShapeDtypeStruct((each, half, width, channels), jnp.float32), shape(tiles, side, packed),
        ),
        in_specs=[vmem] * 8,
        out_specs=(vmem,) * 4,
        compiler_params=limit,
        cost_estimate=cost(work * (frames - 2) * half, 4 * 2**20),
    )(marks, tail_mine, mine, other, *weights[:4])
    tail_other = lax.ppermute(rest, "wa", swap)
    strip, hidden, keep, send, border, late = pl.pallas_call(
        edge_kernel,
        out_shape=(
            shape(3, 2, 2, width, LANES), shape(3, 2, half + 2, width, LANES),
            shape(frames - CACHE, half - 2, side, channels), shape(frames - CACHE, half - 2, side, channels),
            jax.ShapeDtypeStruct((frames - CACHE, 2, width, channels), jnp.float32),
            shape(3, frames - 2, 4, width, LANES),
        ),
        in_specs=[vmem] * 13,
        out_specs=(vmem,) * 6,
        scratch_shapes=[
            pltpu.VMEM((3, frames, 4, width, LANES), bf16),
            pltpu.VMEM((3, frames - 2, half, width, LANES), bf16),
        ],
        compiler_params=limit,
        cost_estimate=cost(2**20, 2**20),
    )(marks, mine, other, own_edge, first, late, raw, *weights)
    tail_edge = pl.pallas_call(
        tail_edge_kernel,
        out_shape=shape(3, CACHE + 2, 2, width, LANES),
        in_specs=[vmem] * 3,
        out_specs=vmem,
        compiler_params=limit,
        cost_estimate=cost(2**30, 2**18),
    )(tail_edge, strip, weights[0])
    keep, send = pl.pallas_call(
        early_kernel,
        out_shape=(shape(frames, half, side, channels), shape(frames, half, side, channels)),
        in_specs=[vmem] * 18,
        out_specs=(vmem, vmem),
        scratch_shapes=[
            pltpu.VMEM((3, CACHE + 2, half + 4, width, LANES), bf16),
            pltpu.VMEM((3, CACHE + 2, half + 2, width, LANES), bf16),
        ],
        compiler_params=limit,
        cost_estimate=cost(work * CACHE * (2 * half + 2), 8 * 2**20),
    )(marks, tail_mine, tail_other, mine, other, tail_edge, first, hidden, keep, send, border, late, *weights)
    got = lax.ppermute(send, "wa", swap)
    hbm = pl.BlockSpec(memory_space=pltpu.HBM)
    kept = pl.pallas_call(
        keep_kernel,
        out_shape=shape(*features.shape),
        in_specs=[vmem],
        out_specs=hbm,
        scratch_shapes=[pltpu.SemaphoreType.DMA],
        compiler_params=limit,
        cost_estimate=cost(2**28, 2**20),
    )(keep)
    return pl.pallas_call(
        got_kernel,
        out_shape=shape(*features.shape),
        in_specs=[vmem, hbm],
        out_specs=hbm,
        input_output_aliases={1: 0},
        scratch_shapes=[pltpu.SemaphoreType.DMA],
        compiler_params=limit,
    )(got, kept)


def solution(mesh):
    return jax.shard_map(
        shards,
        mesh=mesh,
        in_specs=(
            P(("grp", "tchunk"), "ha", "wa", None),
            P(("grp", "tchunk")),
            P(), P(), P(), P(), P(), P(),
        ),
        out_specs=P(("grp", "tchunk"), "ha", "wa", None),
        check_vma=False,
    )
```

```python
import jax
import jax.numpy as jnp
from jax import lax
from jax.experimental import pallas as pl
from jax.experimental.pallas import tpu as pltpu
from jax.sharding import PartitionSpec as P

epsilon = 1e-06
CACHE = 4
TAPS = 3
LANES = 128
PRODUCT = 192
OWN = 128


def slots_kernel(slots_ref):
    slots_ref[...] = lax.broadcasted_iota(jnp.int32, slots_ref.shape, 0)


def lower_part():
    return 1 - lax.axis_index("wa")


def prepare_kernel(total_ref, slots_ref, raw, tail_ref, mine_ref, theirs_ref, marks_ref, pack):
    frames, rows = raw.shape[:2]
    pairs, held = rows // 2, mine_ref.shape[1]
    core = lower_part()
    total = total_ref[0]
    for frame in range(frames):
        for pair in range(pairs):
            first, second = raw[frame, 2 * pair], raw[frame, 2 * pair + 1]
            packed = jnp.concatenate(
                [first[:, :LANES], second[:, :LANES], first[:, LANES:], second[:, LANES:]], axis=-1
            )
            pack[frame, pair] = packed
    for slot in range(CACHE):
        frame = total - CACHE + slot
        value = pack[jnp.maximum(frame, 0)]
        tail_ref[slot * pairs:(slot + 1) * pairs] = jnp.where(frame >= 0, value, jnp.zeros_like(value))
        value = pack[jnp.maximum(frame, 0), pl.ds((1 - core) * (pairs - held), held)]
        theirs_ref[slot * held:(slot + 1) * held] = jnp.where(frame >= 0, value, jnp.zeros_like(value))
    for frame in range(frames):
        start = (CACHE + frame) * held
        value = pack[frame, pl.ds(core * (pairs - held), held)]
        mine_ref[frame] = jnp.where(frame < total, value, jnp.zeros_like(value))
        value = pack[frame, pl.ds((1 - core) * (pairs - held), held)]
        theirs_ref[start:start + held] = jnp.where(frame < total, value, jnp.zeros_like(value))
    slot = slots_ref[...]
    tail_ref[CACHE * pairs] = jnp.where(
        (slot < CACHE) & (total - CACHE + slot >= 0), 1.0, 0.0
    ).astype(tail_ref.dtype)
    marks_ref[...] = jnp.where(slot < total, 1.0, 0.0).astype(marks_ref.dtype)


def joined_tail(tail):
    count = lax.axis_size("tchunk")

    def pushed(value, held):
        return lax.dynamic_slice_in_dim(jnp.concatenate([value, jnp.zeros_like(value)], axis=0), held, CACHE, 0)

    step = 1
    while step < count - 1:
        early = lax.ppermute(tail, "tchunk", [(k, k + step) for k in range(count - step)])
        held = jnp.sum(tail[-1, :CACHE, 0].astype(jnp.int32))
        body = pushed(early[:-1].reshape((CACHE, -1) + tail.shape[1:]), held).reshape(tail[:-1].shape)
        marks = jnp.pad(pushed(early[-1, :CACHE], held), ((0, tail.shape[1] - CACHE), (0, 0)))
        tail = tail + jnp.concatenate([body, marks[None]], axis=0)
        step *= 2
    return tail


def silu(half):
    return half + half * jnp.tanh(half)


def lane_mask():
    return lax.broadcasted_iota(jnp.int32, (1, 1, 1, LANES), 3) < LANES // 2


def gains(gain_ref):
    low, high = 0.5 * gain_ref[:, :LANES], 0.5 * gain_ref[:, LANES:]
    return low.reshape(1, 1, 1, LANES), jnp.concatenate([high, high], axis=-1).reshape(1, 1, 1, LANES)


def rolled(values):
    shape = values.shape
    return pltpu.roll(values.reshape(-1, LANES), LANES // 2, 1).reshape(shape)


def first_rows(left, right, gain_ref, channels):
    raw = jnp.concatenate([left.astype(jnp.float32), right.astype(jnp.float32)], axis=2)
    front, back, high = raw[..., :LANES], raw[..., LANES:2 * LANES], raw[..., 2 * LANES:]
    lower = lane_mask()
    squared = high * high

    def inverse(low, mask):
        total = jnp.sum(low * low + jnp.where(mask, squared, 0.0), axis=-1, keepdims=True)
        return lax.rsqrt(total * (1.0 / channels) + epsilon)

    scale_front, scale_back = inverse(front, lower), inverse(back, jnp.logical_not(lower))
    gain_low, gain_high = gains(gain_ref)
    front = silu(front * scale_front * gain_low)
    back = silu(back * scale_back * gain_low)
    high = silu(high * jnp.where(lower, scale_front, scale_back) * gain_high)
    turned = rolled(high)
    one = [front, jnp.where(lower, high, 0.0), jnp.where(lower, 0.0, turned)]
    two = [back, jnp.where(lower, turned, 0.0), jnp.where(lower, 0.0, high)]
    return [[part.astype(jnp.bfloat16) for part in row] for row in (one, two)]


def second_rows(hidden, flag, gain_ref, channels):
    gain = 0.5 * gain_ref[...].reshape(1, 1, 1, channels)
    total = jnp.sum(hidden * hidden, axis=-1, keepdims=True)
    inverse = lax.rsqrt(total * (1.0 / channels) + epsilon) * flag
    values = silu(hidden * inverse * gain)
    rest = jnp.zeros(values.shape[:-1] + (LANES // 2,), jnp.float32)
    high = jnp.concatenate([values[..., LANES:], rest], axis=-1)
    parts = [values[..., :LANES], high, rolled(high)]
    return jnp.stack([part.astype(jnp.bfloat16) for part in parts])


def in_turn(steps, beside=None):
    waiting = None
    for product, then in steps:
        result = product()
        if waiting:
            waiting[1](waiting[0])
        elif beside:
            beside()
        waiting = (result, then)
    waiting[1](waiting[0])


def convolved(operand, weights_ref, bias_ref, frame, frames, rows, then, most=PRODUCT):
    products = -(-frames * rows * operand.shape[3] // most)
    step = -(-frames // products)

    def part(start):
        count = min(step, frames - start)
        return (
            lambda: convolved_part(operand, weights_ref, bias_ref, frame + start, count, rows),
            lambda result: then(start, count, result),
        )

    return [part(start) for start in range(0, frames, step)]


def convolved_part(operand, weights_ref, bias_ref, frame, frames, rows):
    width = operand.shape[3]
    channels = weights_ref.shape[-1]
    taps = [(a, i) for a in range(TAPS) for i in range(TAPS)]
    groups = [taps[start:start + 2] for start in range(0, len(taps), 2)]

    def window(tap, part):
        a, i = tap
        value = operand[part, frame + a:frame + a + frames, i:i + rows]
        return value.reshape(frames * rows * width, LANES)

    def operands(groups):
        pieces = []
        for group in groups:
            pieces += [window(tap, 0) for tap in group]
            high = window(group[0], 1)
            pieces.append(high + window(group[1], 2) if len(group) > 1 else high)
        return jnp.concatenate(pieces, axis=-1)

    def weights(groups, j, depth):
        rights = []
        for group in groups:
            held = [weights_ref[a, i, j] for a, i in group]
            rights += [weight[:LANES] for weight in held] + [weight[LANES:] for weight in held]
        rest = depth - sum(right.shape[0] for right in rights)
        if rest:
            rights.append(jnp.zeros((rest, channels), jnp.bfloat16))
        return jnp.concatenate(rights, axis=0)

    half = len(groups) // 2
    parts = [(part, operands(part)) for part in (groups[:half], groups[half:])]
    products = []
    for j in range(TAPS):
        total = None
        for part, left in parts if j % 2 == 0 else parts[::-1]:
            product = jnp.dot(left, weights(part, j, left.shape[1]), preferred_element_type=jnp.float32)
            total = product if total is None else total + product
        products.append(total.reshape(frames * rows, width, channels))
    column = lax.broadcasted_iota(jnp.int32, (1, width, 1), 1)
    before = jnp.where(column == 0, 0.0, pltpu.roll(products[0], 1, 1))
    after = jnp.where(column == width - 1, 0.0, pltpu.roll(products[2], width - 1, 1))
    result = products[1] + before + after + bias_ref[...].reshape(1, 1, channels)
    return result.reshape(frames, rows, width, channels)


def halves(core, mine, other):
    return jnp.where(core == 0, mine, other), jnp.where(core == 0, other, mine)


def frame_flags(marks, frames):
    values = marks.astype(jnp.float32)
    return [values[k:k + 1, 0:1].reshape(1, 1, 1, 1) for k in frames]


def fill_rows(operand, frame, row, mine, other, gain_ref):
    left, right = halves(lax.axis_index("wa"), mine, other)
    frames, pairs = mine.shape[:2]
    upper, lower = first_rows(left, right, gain_ref, gain_ref.shape[-1])
    for part in range(len(upper)):
        for pair in range(pairs):
            operand[part, frame:frame + frames, pl.ds(row + 2 * pair, 1)] = upper[part][:, pair:pair + 1]
            operand[part, frame:frame + frames, pl.ds(row + 2 * pair + 1, 1)] = lower[part][:, pair:pair + 1]


def border_kernel(tail_ref, mine_ref, other_ref, tail_edge_ref, own_edge_ref):
    frames, held = mine_ref.shape[:2]
    pairs = tail_ref.shape[0] // CACHE
    core = lower_part()
    pair = core * (held - 1)
    for slot in range(CACHE):
        tail_edge_ref[slot] = tail_ref[slot * pairs + core * (pairs - 1)]
        tail_edge_ref[CACHE + slot] = other_ref[slot * held + pair]
    for frame in range(frames):
        own_edge_ref[0, frame] = mine_ref[frame, pair]
        own_edge_ref[1, frame] = other_ref[(CACHE + frame) * held + pair]


def finish(mine_ref, other_ref, live, first, pairs, value, targets):
    _, held, side, _ = mine_ref.shape
    frames, channels = value.shape[0], value.shape[-1]
    start, count = pairs
    near, far = halves(lax.axis_index("wa"), value[:, :, :side], value[:, :, side:])
    for mine, value, target in ((True, near, targets[0]), (False, far, targets[1])):
        for frame in range(frames):
            for k in range(count):
                if mine:
                    raw = mine_ref[first + frame, start + k]
                else:
                    raw = other_ref[(CACHE + first + frame) * held + start + k]
                raw = raw.astype(jnp.float32)
                high = raw[:, 2 * LANES:]
                for row, tail in ((0, high), (1, pltpu.roll(high, LANES // 2, 1))):
                    low = raw[:, row * LANES:(row + 1) * LANES]
                    features = jnp.concatenate([low, tail[:, :channels - LANES]], axis=-1)
                    summed = features + value[frame, 2 * k + row]
                    kept = jnp.where(live[first + frame].reshape(1, 1) > 0.5, summed, 0.0)
                    target(first + frame, 2 * k + row, kept.astype(jnp.bfloat16))


def hide(operand, weights_ref, bias_ref, gain_ref, first, count, rows, flags, store, most=PRODUCT):
    channels = weights_ref.shape[-1]

    def then(begin, part, hidden):
        flag = jnp.concatenate(flags[begin:begin + part], axis=0)
        store(begin, begin + part, second_rows(hidden, flag, gain_ref, channels))

    return convolved(operand, weights_ref, bias_ref, first, count, rows, then, most)


def inside_flags(rows):
    core, place = lower_part(), lax.axis_index("ha")
    inside = jnp.where(core == 0, place > 0, place < lax.axis_size("ha") - 1)
    row = lax.broadcasted_iota(jnp.int32, (1, rows, 1, 1), 1)
    return jnp.where((row == (rows - 1) * core) & jnp.logical_not(inside), 0.0, 1.0)


def own_kernel(
    marks_ref, tail_ref, mine_ref, other_ref, gain1_ref, w1_ref, bias1_ref, gain2_ref,
    first_ref, late_ref, raw_ref, rest_ref,
):
    frames, pairs, side, packed = mine_ref.shape
    whole = tail_ref.shape[0] // CACHE
    place = (1 - lower_part()) * (whole - pairs)
    for slot in range(CACHE):
        rest_ref[slot * pairs:(slot + 1) * pairs] = tail_ref[pl.ds(slot * whole + place, pairs)]
    live = frame_flags(marks_ref[...], range(2, frames))

    def fill(start, end):
        other = other_ref[(CACHE + start) * pairs:(CACHE + end) * pairs].reshape(end - start, pairs, side, packed)
        fill_rows(first_ref, start, 0, mine_ref[start:end], other, gain1_ref)

    def store(begin, end, rows):
        late_ref[:, begin:end] = rows

    steps = hide(first_ref, w1_ref, bias1_ref, gain2_ref, 0, frames - 2, 2 * pairs - 2, live, store, OWN)
    each = -(-(frames - 2) // len(steps))

    position, result = 0, None
    for k, (product, _) in enumerate(steps[:-1]):
        fill(position, each * (k + 1) + 2)
        position = each * (k + 1) + 2
        before, result = result, product()
        if k:
            steps[k - 1][1](before)
    fill(position, frames)
    raw_ref[...] = result


def edge_kernel(
    marks_ref, mine_ref, other_ref, edge_ref, first_ref, done_ref, raw_ref,
    gain1_ref, w1_ref, bias1_ref, gain2_ref, w2_ref, bias2_ref,
    strip_ref, hidden_ref, keep_ref, send_ref, border_ref, operand, strip, late_ref,
):
    core = lower_part()
    frames, pairs = mine_ref.shape[:2]
    rows = 2 * pairs
    late = frames - CACHE
    outward, inward = pl.ds(2 * core, 2), pl.ds(2 * (1 - core), 2)
    live = frame_flags(marks_ref[...], range(frames))
    inside = inside_flags(2)
    done, made = done_ref.shape[1], done_ref.shape[1] + raw_ref.shape[0]

    def activate():
        fill_rows(strip, 0, 2 * core, edge_ref[1][:, None], edge_ref[0][:, None], gain1_ref)
        strip[:, :, inward] = first_ref[:, :, pl.ds((rows - 2) * core, 2)]
        late_ref[:, 0:done] = done_ref[...]
        flag = jnp.concatenate(live[2 + done:2 + made], axis=0)
        late_ref[:, done:made] = second_rows(raw_ref[...], flag, gain2_ref, gain2_ref.shape[-1])
        strip_ref[...] = strip[:, 0:2, outward]
        hidden_ref[:, :, pl.ds(2 * (1 - core), rows - 2)] = late_ref[:, 0:2]

    def store_last(begin, end, values):
        late_ref[:, made + begin:made + end] = values
        if made + end == frames - 2:
            operand[:, :, inward] = late_ref[:, :, pl.ds((rows - 4) * core, 2)]

    def store(begin, end, values):
        operand[:, begin:end, outward] = values

    def put(ref):
        def store(frame, row, value):
            ref[frame - CACHE, row] = value
        return store

    def middle(start, part, result):
        targets = (put(keep_ref), put(send_ref))
        finish(mine_ref, other_ref, live, CACHE + start, (1, pairs - 2), result, targets)

    def border(start, part, result):
        border_ref[start:start + part] = result

    flags = [flag * inside for flag in live[2:]]
    earlier = lax.axis_index("tchunk") > 0

    def steps():
        left = frames - 2 - made
        return (
            hide(first_ref, w1_ref, bias1_ref, gain2_ref, made, left, rows - 2, live[2 + made:], store_last, OWN)
            + hide(strip, w1_ref, bias1_ref, gain2_ref, 0, frames - 2, 2, flags, store)
            + convolved(late_ref, w2_ref, bias2_ref, 0, late, rows - 4, middle)
        )

    @pl.when(earlier)
    def _():
        in_turn(steps() + convolved(operand, w2_ref, bias2_ref, 0, late, 2, border), activate)

    @pl.when(jnp.logical_not(earlier))
    def _():
        in_turn(steps(), activate)

    hidden_ref[:, :, pl.ds((rows - 2) * core, 2)] = operand[:, 0:2, outward]


def tail_edge_kernel(edge_ref, strip_ref, gain_ref, rows_ref):
    rows_ref[:, CACHE:] = strip_ref[...]

    @pl.when(lax.axis_index("tchunk") > 0)
    def _():
        fill_rows(rows_ref, 0, 0, edge_ref[CACHE:2 * CACHE][:, None], edge_ref[0:CACHE][:, None], gain_ref)

    @pl.when(lax.axis_index("tchunk") == 0)
    def _():
        rows_ref[:, 0:CACHE] = jnp.zeros((rows_ref.shape[0], CACHE) + rows_ref.shape[2:], rows_ref.dtype)


def early_kernel(
    marks_ref, tail_mine_ref, tail_other_ref, mine_ref, other_ref, edge_ref, first_ref, hidden_ref,
    late_keep_ref, late_send_ref, late_border_ref, late_operand_ref, gain1_ref, w1_ref, bias1_ref, gain2_ref, w2_ref, bias2_ref,
    keep_ref, send_ref, plane, operand,
):
    core = lower_part()
    held = mine_ref.shape[1]
    rows = 2 * held
    pairs = tail_mine_ref.shape[0] // CACHE
    live = frame_flags(marks_ref[...], range(mine_ref.shape[0]))
    inside = inside_flags(rows)
    earlier = lax.axis_index("tchunk") > 0
    middle, border = 2 * (1 - core), rows * core

    def unpacked(ref, stride, first):
        return jnp.stack([ref[pl.ds(slot * stride + first, held)] for slot in range(CACHE)])

    plane[:, CACHE:, pl.ds(middle, rows)] = first_ref[:, 0:2]
    plane[:, :, pl.ds(border, 2)] = edge_ref[...]

    def put(ref, offset=0):
        def store(frame, row, value):
            ref[frame, offset + row] = value
        return store

    def late_border(start, part, result):
        offset = (rows - 4) * core
        targets = (put(keep_ref, offset), put(send_ref, offset))
        finish(mine_ref, other_ref, live, CACHE + start, ((held - 1) * core, 1), result, targets)

    def late_middle():
        operand[:, CACHE:] = hidden_ref[...]
        for source, target in ((late_keep_ref, keep_ref), (late_send_ref, send_ref)):
            target[CACHE:, pl.ds(2 * (1 - core), rows - 4)] = source[...]

    def hidden_steps(first, flags):
        def store(begin, end, values):
            operand[:, first + begin:first + end] = values

        flags = [flag * inside for flag in flags]
        return hide(plane, w1_ref, bias1_ref, gain2_ref, first, CACHE - first, rows, flags, store)

    def then(start, part, result):
        finish(mine_ref, other_ref, live, start, (core, held - 1), result, (put(keep_ref), put(send_ref)))

    def result_steps():
        return convolved(operand, w2_ref, bias2_ref, 0, CACHE, rows - 2, then)

    @pl.when(earlier)
    def _():
        fill_rows(
            plane, 0, middle, unpacked(tail_mine_ref, pairs, core * (pairs - held)),
            unpacked(tail_other_ref, held, 0), gain1_ref,
        )
        flags = frame_flags(tail_mine_ref[CACHE * pairs], range(CACHE - 2, CACHE)) + live[0:2]

        def beside():
            late_middle()
            late_border(0, late_border_ref.shape[0], late_border_ref[...])

        hidden, results = hidden_steps(0, flags), result_steps()
        if len(hidden) == 2 and len(results) == 2:
            in_turn(hidden[::-1] + results[::-1], beside)
        else:
            in_turn(hidden, beside)
            in_turn(results)

    @pl.when(jnp.logical_not(earlier))
    def _():
        plane[:, 2:CACHE, pl.ds(middle, rows)] = jnp.zeros(
            plane.shape[:1] + (CACHE - 2, rows) + plane.shape[3:], plane.dtype
        )

        def beside():
            operand[:, 0:2] = jnp.zeros(operand.shape[:1] + (2,) + operand.shape[2:], operand.dtype)
            late_middle()

        border = convolved(late_operand_ref, w2_ref, bias2_ref, 0, late_border_ref.shape[0], 2, late_border)
        in_turn(hidden_steps(2, live[0:2]) + border + result_steps()[::-1], beside)


def keep_kernel(keep_ref, result_ref, arrived):
    half = keep_ref.shape[1]
    copy = pltpu.make_async_copy(keep_ref, result_ref.at[:, pl.ds(half * lower_part(), half)], arrived)
    copy.start()
    copy.wait()


def got_kernel(got_ref, kept_ref, result_ref, arrived):
    half = got_ref.shape[1]
    copy = pltpu.make_async_copy(got_ref, result_ref.at[:, pl.ds(half * (1 - lower_part()), half)], arrived)
    copy.start()
    copy.wait()


def shards(features, frame_counts, gain_first, conv_first, bias_first, gain_second, conv_second, bias_second):
    frames, rows, side, channels = features.shape
    pairs, half = rows // 2, rows // 2
    held = half // 2 + 1
    tall, cores, blocks = lax.axis_size("ha"), lax.axis_size("wa"), lax.axis_size("tchunk")
    packed, width, tiles = 3 * LANES, 2 * side, CACHE * held
    bf16 = jnp.bfloat16
    vmem = pl.BlockSpec(memory_space=pltpu.VMEM)
    limit = pltpu.CompilerParams(vmem_limit_bytes=20 * 2**20)
    work = 2 * TAPS**3 * channels * channels * width

    def shape(*extent):
        return jax.ShapeDtypeStruct(extent, bf16)

    def cost(flops, fetched):
        return pl.CostEstimate(flops=flops, bytes_accessed=fetched, transcendentals=0)

    slots = pl.pallas_call(
        slots_kernel,
        out_shape=jax.ShapeDtypeStruct((side, packed), jnp.int32),
        out_specs=vmem,
        compiler_params=limit,
        cost_estimate=cost(2**34, 2**20),
    )()
    slots, frame_counts = lax.optimization_barrier((slots, frame_counts))
    tail, mine, theirs, marks = pl.pallas_call(
        prepare_kernel,
        out_shape=(
            shape(CACHE * pairs + 1, side, packed), shape(frames, held, side, packed),
            shape((CACHE + frames) * held, side, packed), shape(side, packed),
        ),
        in_specs=[pl.BlockSpec(memory_space=pltpu.SMEM), vmem, vmem],
        out_specs=(vmem,) * 4,
        scratch_shapes=[pltpu.VMEM((frames, pairs, side, packed), bf16)],
        compiler_params=limit,
    )(frame_counts, slots, features)

    if blocks > 2:
        tail = joined_tail(tail)
        rest = lax.dynamic_slice_in_dim(
            tail[:-1].reshape(CACHE, pairs, side, packed), (1 - lower_part()) * (pairs - held), held, 1
        )
        theirs = jnp.concatenate([rest.reshape(tiles, side, packed), theirs[tiles:]], axis=0)
    straight, diagonal, across = [], [], []

    def index(block, h, core):
        return (block * tall + h) * cores + core

    for k in range(blocks - 1):
        for h in range(tall):
            for core in range(cores):
                straight.append((index(k, h, core), index(k + 1, h, core)))
    for h in range(tall - 1):
        for k in range(blocks):
            lower, upper = index(k, h, 0), index(k, h + 1, 1)
            across += [(lower, upper), (upper, lower)]
            if k + 1 < blocks:
                lower_next, upper_next = index(k + 1, h, 0), index(k + 1, h + 1, 1)
                diagonal += [(lower, upper_next), (upper, lower_next)]
    axes = ("tchunk", "ha", "wa")
    swap = [(0, 1), (1, 0)]
    tail_mine = lax.ppermute(tail, axes, straight)
    other = lax.ppermute(theirs, "wa", swap)
    tail_edge, own_edge = pl.pallas_call(
        border_kernel,
        out_shape=(shape(2 * CACHE, side, packed), shape(2, frames, side, packed)),
        in_specs=[vmem] * 3,
        out_specs=(vmem, vmem),
        compiler_params=limit,
        cost_estimate=cost(2**34, 2**20),
    )(tail, mine, other)
    own_edge = lax.ppermute(own_edge, axes, across)
    tail_edge = lax.ppermute(tail_edge, axes, diagonal)

    weights = (
        gain_first.reshape(1, channels), conv_first, bias_first.reshape(1, channels),
        gain_second.reshape(1, channels), conv_second, bias_second.reshape(1, channels),
    )
    products = -(-(frames - 2) * half * width // OWN)
    each = -(-(frames - 2) // products)
    done = each * (products - 2)
    first, late, raw, rest = pl.pallas_call(
        own_kernel,
        out_shape=(
            shape(3, frames, half + 2, width, LANES), shape(3, done, half, width, LANES),
            jax.ShapeDtypeStruct((each, half, width, channels), jnp.float32), shape(tiles, side, packed),
        ),
        in_specs=[vmem] * 8,
        out_specs=(vmem,) * 4,
        compiler_params=limit,
        cost_estimate=cost(work * (frames - 2) * half, 4 * 2**20),
    )(marks, tail_mine, mine, other, *weights[:4])
    tail_other = lax.ppermute(rest, "wa", swap)
    strip, hidden, keep, send, border, late = pl.pallas_call(
        edge_kernel,
        out_shape=(
            shape(3, 2, 2, width, LANES), shape(3, 2, half + 2, width, LANES),
            shape(frames - CACHE, half - 2, side, channels), shape(frames - CACHE, half - 2, side, channels),
            jax.ShapeDtypeStruct((frames - CACHE, 2, width, channels), jnp.float32),
            shape(3, frames - 2, 4, width, LANES),
        ),
        in_specs=[vmem] * 13,
        out_specs=(vmem,) * 6,
        scratch_shapes=[
            pltpu.VMEM((3, frames, 4, width, LANES), bf16),
            pltpu.VMEM((3, frames - 2, half, width, LANES), bf16),
        ],
        compiler_params=limit,
        cost_estimate=cost(2**20, 2**20),
    )(marks, mine, other, own_edge, first, late, raw, *weights)
    tail_edge = pl.pallas_call(
        tail_edge_kernel,
        out_shape=shape(3, CACHE + 2, 2, width, LANES),
        in_specs=[vmem] * 3,
        out_specs=vmem,
        compiler_params=limit,
        cost_estimate=cost(2**30, 2**18),
    )(tail_edge, strip, weights[0])
    keep, send = pl.pallas_call(
        early_kernel,
        out_shape=(shape(frames, half, side, channels), shape(frames, half, side, channels)),
        in_specs=[vmem] * 18,
        out_specs=(vmem, vmem),
        scratch_shapes=[
            pltpu.VMEM((3, CACHE + 2, half + 4, width, LANES), bf16),
            pltpu.VMEM((3, CACHE + 2, half + 2, width, LANES), bf16),
        ],
        compiler_params=limit,
        cost_estimate=cost(work * CACHE * (2 * half + 2), 8 * 2**20),
    )(marks, tail_mine, tail_other, mine, other, tail_edge, first, hidden, keep, send, border, late, *weights)
    got = lax.ppermute(send, "wa", swap)
    hbm = pl.BlockSpec(memory_space=pltpu.HBM)
    kept = pl.pallas_call(
        keep_kernel,
        out_shape=shape(*features.shape),
        in_specs=[vmem],
        out_specs=hbm,
        scratch_shapes=[pltpu.SemaphoreType.DMA],
        compiler_params=limit,
        cost_estimate=cost(2**28, 2**20),
    )(keep)
    return pl.pallas_call(
        got_kernel,
        out_shape=shape(*features.shape),
        in_specs=[vmem, hbm],
        out_specs=hbm,
        input_output_aliases={1: 0},
        scratch_shapes=[pltpu.SemaphoreType.DMA],
        compiler_params=limit,
    )(got, kept)


def solution(mesh):
    return jax.shard_map(
        shards,
        mesh=mesh,
        in_specs=(
            P(("grp", "tchunk"), "ha", "wa", None),
            P(("grp", "tchunk")),
            P(), P(), P(), P(), P(), P(),
        ),
        out_specs=P(("grp", "tchunk"), "ha", "wa", None),
        check_vma=False,
    )
```
